128 devices in a mesh: rows: 32 (over x, y, core), cols: 4 (over z).
Axes of the slice: x: 4, y: 4, z: 4, core: 2. Of those that a mesh axis runs over, the one named last changes fastest.
Arguments:
- features: bfloat16 [4, 128, 512, 256], P(None, 'rows', 'cols'), may hold values from -450 to 450
- conv_weight: bfloat16 [3, 3, 256, 512], replicated, may hold values from -0.125 to 0.125
- bn_gain: float32 [512], replicated, may hold values from 0.1 to 1.9
- bn_bias: float32 [512], replicated, may hold values from -3 to 3
- head_weight: bfloat16 [512, 4], replicated, may hold values from -0.25 to 0.25
- labels: int32 [4, 128, 512], P(None, 'rows', 'cols'), may hold values from 0 to 3
- raster: int32 [4, 128, 512], P(None, 'rows', 'cols'), may hold values 0 or 1
Outputs:
- grad_weight: float32 [3, 3, 256, 512], P(None, None, None, 'cols')
- grad_gain: float32 [512], P('cols')
- grad_bias: float32 [512], P('cols')
- grad_head: float32 [512, 4], P('cols')
- grad_input: float32 [4, 128, 512, 256], P(None, 'rows', 'cols')
The draws below stay inside these ranges and needn't reach their ends.
All inputs are finite; a program needn't handle non-finite values. No bound on the sum of `raster` on one device may be relied on, other than what follows from the above.
Results may differ from the reference program's by a relative error of at most 0.009.
Values may be sent and summed in bfloat16 or wider, within the bound.
A program may use at most 192 MiB of HBM per device.

```python
import math
import jax
import jax.numpy as jnp
from jax import lax

CIN = 256
COUT = 512
NCLASS = 4
BATCH = 4
HEIGHT = 128
WIDTH = 512


def draw_features(key, part):
    key = jax.random.fold_in(key, 11)
    key_noise, key_pixel, key_channel, key_offset = jax.random.split(key, 4)
    shape = (BATCH, HEIGHT, WIDTH, CIN)
    pixel = jnp.exp(jax.random.uniform(key_pixel, (BATCH, HEIGHT, WIDTH, 1), jnp.float32) * math.log(10.0))
    channel = jnp.exp(jax.random.uniform(key_channel, (CIN,), jnp.float32) * math.log(10.0))
    offset = jax.random.uniform(key_offset, (CIN,), jnp.float32, -1.0, 1.0)
    place = jnp.arange(HEIGHT, dtype=jnp.float32) / float(max(HEIGHT - 1, 1))
    noise = jnp.clip(jax.random.normal(key_noise, shape, jnp.float32), -4.0, 4.0)
    rising = 3.0 ** place
    values = rising[None, :, None, None] * pixel * channel * (noise + offset) / 10.0
    return values.astype(jnp.bfloat16)


def place_ends(drawn, own_key, low, top_value):
    longest = drawn.shape.index(max(drawn.shape))
    spots = []
    for shift in (0, 1):
        where = [jax.random.randint(jax.random.fold_in(own_key, axis), (), 0, length) for axis, length in enumerate(drawn.shape)]
        where[longest] = (where[longest] + shift) % drawn.shape[longest]
        spots.append(tuple(where))
    return drawn.at[spots[0]].set(low).at[spots[1]].set(top_value)


def normal_values(key, extent, scale, limit, held_as=jnp.bfloat16):
    entries = jax.random.normal(key, extent, jnp.float32) * scale
    return jnp.minimum(jnp.maximum(entries, -limit), limit).astype(held_as)


def setup_inputs(seed: int = 0) -> dict:
    splits = jax.random.split(jax.random.key(seed), 8)
    features = draw_features(jax.random.fold_in(splits[7], 71), 0)
    conv_weight = normal_values(splits[1], (3, 3, CIN, COUT), (9 * CIN) ** -0.5, 0.125)
    bn_gain = jnp.clip(1.0 + 0.18 * jax.random.normal(splits[2], (COUT,), jnp.float32), 0.1, 1.9)
    bn_bias = normal_values(splits[3], (COUT,), 0.5, 3.0, jnp.float32)
    head_weight = normal_values(splits[4], (COUT, NCLASS), COUT ** -0.5, 0.25)
    labels = place_ends(jax.random.randint(splits[5], (BATCH, HEIGHT, WIDTH), 0, NCLASS), jax.random.fold_in(splits[5], 1), 0, NCLASS - 1).astype(jnp.int32)
    raster = place_ends((jax.random.randint(splits[6], (BATCH, HEIGHT, WIDTH), 0, 3) < 1).astype(jnp.int32), jax.random.fold_in(splits[6], 1), 0, 1)
    return {"features": features, "conv_weight": conv_weight, "bn_gain": bn_gain, "bn_bias": bn_bias, "head_weight": head_weight, "labels": labels, "raster": raster}


HIGH = lax.Precision.HIGHEST

def shifted_conv(padded, kernel, height, width):
    total = jnp.zeros(padded.shape[:1] + (height, width, kernel.shape[3]), jnp.float32)
    for offset_row in range(3):
        for offset_col in range(3):
            window = padded[:, offset_row:offset_row + height, offset_col:offset_col + width]
            total = total + jnp.einsum('bhwc,co->bhwo', window, kernel[offset_row, offset_col], precision=HIGH)
    return total

def back_conv(padded_grad, kernel, height, width):
    total = jnp.zeros(padded_grad.shape[:1] + (height, width, kernel.shape[2]), jnp.float32)
    for offset_row in range(3):
        for offset_col in range(3):
            window = padded_grad[:, 2 - offset_row:2 - offset_row + height, 2 - offset_col:2 - offset_col + width]
            total = total + jnp.einsum('bhwo,co->bhwc', window, kernel[offset_row, offset_col], precision=HIGH)
    return total

def kernel_grad(padded, grad, height, width):
    layers = []
    for offset_row in range(3):
        line = []
        for offset_col in range(3):
            window = padded[:, offset_row:offset_row + height, offset_col:offset_col + width]
            line.append(jnp.einsum('bhwc,bhwo->co', window, grad, precision=HIGH))
        layers.append(jnp.stack(line))
    return jnp.stack(layers)

def reference(features, conv_weight, bn_gain, bn_bias, head_weight, labels, raster):
    batch, height, width, channels = features.shape
    count = float(batch * height * width)
    padded = jnp.pad(features.astype(jnp.float32), ((0, 0), (1, 1), (1, 1), (0, 0)))
    kernel = conv_weight.astype(jnp.float32)
    conv = shifted_conv(padded, kernel, height, width)
    mean = lax.optimization_barrier(jnp.sum(conv, axis=(0, 1, 2))) / count
    var = lax.optimization_barrier(jnp.sum((conv - mean) ** 2, axis=(0, 1, 2))) / count
    rstd = lax.rsqrt(var + 1e-05)
    normed = (conv - mean) * rstd
    preact = bn_gain * normed + bn_bias
    act = jnp.maximum(preact, 0.0).astype(jnp.bfloat16)
    head = head_weight.astype(jnp.float32)
    logits = jnp.einsum('bhwo,oq->bhwq', act.astype(jnp.float32), head, precision=HIGH)
    expo = jnp.exp(logits)
    probs = expo / lax.optimization_barrier(jnp.sum(expo, axis=-1, keepdims=True))
    onehot = (labels[..., None] == jnp.arange(logits.shape[-1], dtype=jnp.int32)).astype(jnp.float32)
    pixel_weight = (1 + raster).astype(jnp.float32)
    score_grad = (pixel_weight[..., None] * (probs - onehot) / float(batch)).astype(jnp.bfloat16)
    score32 = score_grad.astype(jnp.float32)
    grad_head = jnp.einsum('bhwo,bhwq->oq', act.astype(jnp.float32), score32, precision=HIGH)
    act_grad = jnp.einsum('bhwq,oq->bhwo', score32, head, precision=HIGH)
    pre_grad = jnp.where(preact > 0, act_grad, 0.0)
    grad_bias = lax.optimization_barrier(jnp.sum(pre_grad, axis=(0, 1, 2)))
    grad_gain = lax.optimization_barrier(jnp.sum(pre_grad * normed, axis=(0, 1, 2)))
    conv_grad = (bn_gain * rstd * (pre_grad - grad_bias / count - normed * grad_gain / count)).astype(jnp.bfloat16)
    grad32 = conv_grad.astype(jnp.float32)
    grad_weight = kernel_grad(padded, grad32, height, width)
    padded_grad = jnp.pad(grad32, ((0, 0), (1, 1), (1, 1), (0, 0)))
    grad_input = back_conv(padded_grad, kernel, height, width)
    return (grad_weight, grad_gain, grad_bias, grad_head, grad_input)
```

```python
import jax
import jax.numpy as jnp
from jax import lax
from jax.experimental import pallas as pl
from jax.experimental.pallas import tpu as pltpu
from jax.sharding import PartitionSpec as P

F32 = jnp.float32
BF16 = jnp.bfloat16
MESH = pl.DeviceIdType.MESH

B = 4
H = 4
W = 128
CI = 256
CO = 512
TAPS = 9
PIX = H * W
COUNT = 4.0 * 128.0 * 512.0
EPS = 1e-05
OWN = 1152
PART = 80


def part_start(j):
    return pl.multiple_of(((9 * j) // 2) * 16, 16)


def kernel(
    feat,
    wgt_hbm,
    gain_ref,
    bias_ref,
    head_ref,
    labels_ref,
    raster_ref,
    gw_out,
    gg_out,
    gb_out,
    gh_out,
    gi_out,
    wgt,
    wgt_t,
    xl,
    xc,
    xr,
    xt,
    conv,
    pgs,
    act,
    sgs,
    onehot,
    pixw,
    head_pad,
    head_tile,
    head_t,
    gl,
    gc,
    gr,
    xrow,
    xedge_out,
    xedge_in,
    grow,
    gedge_f,
    gedge_out,
    gedge_in,
    st_local,
    st8,
    st16,
    tot8,
    tot16,
    hd8,
    hd16,
    head_all,
    part,
    send_a,
    recv_a,
    send_b,
    recv_b,
    sum_c,
    send_c,
    recv_c,
    gath,
    gath_other,
    wsem,
    xrow_s,
    xrow_r,
    xedge_s,
    xedge_r,
    grow_s,
    grow_r,
    gedge_s,
    gedge_r,
    s8_s,
    s8_r,
    s16_s,
    s16_r,
    t8_s,
    t8_r,
    t16_s,
    t16_r,
    h8_s,
    h8_r,
    h16_s,
    h16_r,
    a_s,
    a_r,
    b_s,
    b_r,
    c_s,
    c_r,
    g_s,
    g_r,
    o_s,
    o_r,
):
    me = lax.axis_index("rows")
    z = lax.axis_index("cols")
    core = lax.rem(me, 2)
    chip = me // 2
    rank8 = z * 2 + core

    def dev8(j):
        return (chip * 2 + lax.rem(j, 2), j // 2)

    def dev16(j):
        return (j * 2 + core, z)

    other = (chip * 2 + 1 - core, z)
    up = lax.rem(me + 31, 32)
    down = lax.rem(me + 1, 32)
    west = lax.rem(z + 3, 4)
    east = lax.rem(z + 1, 4)
    beyond = lax.rem(me + 31 + 2 * core, 32)

    barrier = pltpu.get_barrier_semaphore()

    def greet(device):
        pl.semaphore_signal(barrier, inc=1, device_id=device, device_id_type=MESH)

    for k in range(1, 8):
        greet(dev8(lax.rem(rank8 + k, 8)))
    for col in (west, z, east):
        greet((beyond, col))

    def greet16(k, carry):
        greet(dev16(lax.rem(chip + k, 16)))
        return carry

    lax.fori_loop(1, 16, greet16, 0)

    wcopy = pltpu.make_async_copy(wgt_hbm, wgt, wsem)
    wcopy.start()

    row_id = lax.broadcasted_iota(jnp.int32, (16, CI), 0)
    left_edge = jnp.zeros((16, CI), F32)
    right_edge = jnp.zeros((16, CI), F32)
    for b in range(B):
        for h in range(H):
            low = feat[b, h, 0:16, :].astype(F32)[0:1, :]
            top = feat[b, h, W - 16 : W, :].astype(F32)[15:16, :]
            here = row_id == b * H + h
            left_edge = jnp.where(here, low, left_edge)
            right_edge = jnp.where(here, top, right_edge)
    xedge_out[0] = right_edge.astype(BF16)
    xedge_out[1] = left_edge.astype(BF16)

    pl.semaphore_wait(barrier, 25)

    def remote(src, dst, ssem, rsem, device):
        return pltpu.make_async_remote_copy(
            src_ref=src,
            dst_ref=dst,
            send_sem=ssem,
            recv_sem=rsem,
            device_id=device,
            device_id_type=MESH,
        )

    def row_sends(first, last, land, ssem, rsem):
        return [
            remote(last, land.at[0], ssem.at[0], rsem.at[0], (down, z)),
            remote(first, land.at[1], ssem.at[1], rsem.at[1], (up, z)),
        ]

    def edge_sends(out, land, ssem, rsem):
        copies = []
        for side, col in ((0, east), (1, west)):
            for slot, row in ((0, down), (1, me), (2, up)):
                index = side * 3 + slot
                copies.append(
                    remote(
                        out.at[side], land.at[index], ssem.at[index], rsem.at[index], (row, col)
                    )
                )
        return copies

    xrow_copies = row_sends(feat.at[:, 0], feat.at[:, H - 1], xrow, xrow_s, xrow_r)
    for copy in xrow_copies:
        copy.start()
    xedge_copies = edge_sends(xedge_out, xedge_in, xedge_s, xedge_r)
    for copy in xedge_copies:
        copy.start()

    head_pad[...] = jnp.zeros((CO, 128), F32)
    head_pad[:, 0:4] = head_ref[...].astype(F32)
    spread = head_pad[...]
    head_t[...] = jnp.transpose(spread).astype(BF16)
    for step in (4, 8, 16, 32, 64):
        spread = spread + pltpu.roll(spread, step, 1)
    head_tile[...] = spread.astype(BF16)

    west_ok = jnp.where(z > 0, 1.0, 0.0).astype(F32)
    east_ok = jnp.where(z < 3, 1.0, 0.0).astype(F32)
    up_ok = jnp.where(me > 0, 1.0, 0.0).astype(F32)
    down_ok = jnp.where(me < 31, 1.0, 0.0).astype(F32)

    def pick_row(ref, slot, index):
        block = ref[slot].astype(F32)
        ids = lax.broadcasted_iota(jnp.int32, block.shape, 0)
        return jnp.sum(jnp.where(ids == index, block, 0.0), axis=0, keepdims=True)

    def shifted(value, before, after):
        ids = lax.broadcasted_iota(jnp.int32, value.shape, 0)
        left = jnp.where(ids == 0, before, pltpu.roll(value, 1, 0))
        right = jnp.where(ids == W - 1, after, pltpu.roll(value, W - 1, 0))
        return left.astype(BF16), right.astype(BF16)

    for copy in xedge_copies:
        copy.wait_recv()

    def build_x(i, carry):
        b = i // H
        h = lax.rem(i, H)
        value = feat[b, h].astype(F32)
        left, right = shifted(
            value,
            pick_row(xedge_in, 1, i) * west_ok,
            pick_row(xedge_in, 4, i) * east_ok,
        )
        xl[b, h + 1] = left
        xc[b, h + 1] = feat[b, h]
        xr[b, h + 1] = right
        return carry

    lax.fori_loop(0, B * H, build_x, 0)

    for copy in xrow_copies:
        copy.wait_recv()

    def build_halo(land, edge_in, left_ref, mid_ref, right_ref):
        def body(b, carry):
            for side, line, ok, src in ((0, 0, up_ok, H - 1), (1, H + 1, down_ok, 0)):
                value = land[side, b].astype(F32) * ok
                slot = 2 * side
                left, right = shifted(
                    value,
                    pick_row(edge_in, slot, b * H + src) * (west_ok * ok),
                    pick_row(edge_in, slot + 3, b * H + src) * (east_ok * ok),
                )
                left_ref[b, line] = left
                mid_ref[b, line] = value.astype(BF16)
                right_ref[b, line] = right
            return carry

        lax.fori_loop(0, B, body, 0)

    build_halo(xrow, xedge_in, xl, xc, xr)
    wcopy.wait()

    def forward(b, carry):
        lhs = jnp.concatenate(
            [
                ref[b, r : r + H].reshape(PIX, CI)
                for r in range(3)
                for ref in (xl, xc, xr)
            ],
            axis=1,
        )
        value = jnp.dot(lhs, wgt[...], preferred_element_type=F32)
        conv[b] = value
        mid = jnp.sum(value, axis=0, keepdims=True) * (1.0 / PIX)
        st_local[b, 0:1] = mid
        st_local[b, 1:2] = jnp.sum((value - mid) ** 2, axis=0, keepdims=True)
        return carry

    lax.fori_loop(0, B, forward, 0)

    def combine(parts, count):
        total = parts[0][0:1]
        for item in parts[1:]:
            total = total + item[0:1]
        mid = total * (1.0 / len(parts))
        spread_sum = None
        for item in parts:
            term = item[1:2] + count * (item[0:1] - mid) ** 2
            spread_sum = term if spread_sum is None else spread_sum + term
        return mid, spread_sum

    def exchange(buf, rank, size, dev, ssem, rsem):
        def copy_to(k):
            return remote(
                buf.at[rank],
                buf.at[rank],
                ssem.at[k],
                rsem.at[rank],
                dev(lax.rem(rank + k, size)),
            )

        def start():
            def body(k, carry):
                copy_to(k).start()
                return carry

            lax.fori_loop(1, size, body, 0)

        def wait():
            def body(k, carry):
                j = lax.rem(rank + k, size)
                remote(buf.at[j], buf.at[j], ssem.at[k], rsem.at[j], dev(j)).wait_recv()
                return carry

            lax.fori_loop(1, size, body, 0)

        def finish():
            def body(k, carry):
                copy_to(k).wait_send()
                return carry

            lax.fori_loop(1, size, body, 0)

        return start, wait, finish

    st8_x = exchange(st8, rank8, 8, dev8, s8_s, s8_r)
    st16_x = exchange(st16, chip, 16, dev16, s16_s, s16_r)
    tot8_x = exchange(tot8, rank8, 8, dev8, t8_s, t8_r)
    tot16_x = exchange(tot16, chip, 16, dev16, t16_s, t16_r)
    hd8_x = exchange(hd8, rank8, 8, dev8, h8_s, h8_r)
    hd16_x = exchange(hd16, chip, 16, dev16, h16_s, h16_r)

    mid, m2 = combine([st_local[b] for b in range(B)], float(PIX))
    st8[rank8, 0:1] = mid
    st8[rank8, 1:2] = m2
    st8_x[0]()

    def transpose_x(i, carry):
        b = i // (H + 2)
        h = lax.rem(i, H + 2)
        for c, ref in enumerate((xl, xc, xr)):
            xt[b, h, c * CI : (c + 1) * CI, :] = jnp.transpose(ref[b, h])
        return carry

    lax.fori_loop(0, B * (H + 2), transpose_x, 0)

    st8_x[1]()
    mid, m2 = combine([st8[j] for j in range(8)], float(B * PIX))
    st16[chip, 0:1] = mid
    st16[chip, 1:2] = m2
    st16_x[0]()

    def transpose_w(t, carry):
        wgt_t[pl.ds(pl.multiple_of(t * CO, CO), CO), :] = jnp.transpose(
            wgt[pl.ds(pl.multiple_of((TAPS - 1 - t) * CI, CI), CI), :]
        )
        return carry

    lax.fori_loop(0, TAPS, transpose_w, 0)

    lane_class = lax.rem(lax.broadcasted_iota(jnp.int32, (W, 128), 1), 4).astype(F32)
    for b in range(B):
        for h in range(H):
            label = labels_ref[b, h : h + 1, :].astype(F32)
            weight = raster_ref[b, h : h + 1, :].astype(F32)
            label_t = jnp.transpose(jnp.broadcast_to(label, (128, W)))
            weight_t = jnp.transpose(jnp.broadcast_to(weight, (128, W)))
            onehot[b, h * W : (h + 1) * W] = jnp.where(label_t == lane_class, 1.0, 0.0)
            pixw[b, h * W : (h + 1) * W] = (1.0 + weight_t) * 0.25

    st16_x[1]()
    mean, m2 = combine([st16[j] for j in range(16)], float(8 * B * PIX))
    rstd = lax.rsqrt(m2 * (1.0 / COUNT) + EPS)
    gain = gain_ref[...]
    bias = bias_ref[...]
    scale = gain * rstd

    def middle(b, carry):
        sum_g, sum_gn = carry
        away = conv[b] - mean
        pre = away * scale + bias
        acted = jnp.maximum(pre, 0.0).astype(BF16)
        act[b] = acted
        logits = jnp.dot(acted, head_tile[...], preferred_element_type=F32)
        expo = jnp.exp(logits)
        total = expo + pltpu.roll(expo, 1, 1)
        total = total + pltpu.roll(total, 2, 1)
        score = (pixw[b] * (expo / total - onehot[b])).astype(BF16)
        sgs[b] = score
        act_grad = jnp.dot(score, head_t[...], preferred_element_type=F32)
        pre_grad = jnp.where(pre > 0.0, act_grad, 0.0)
        pgs[b] = pre_grad
        sum_g = sum_g + jnp.sum(pre_grad, axis=0, keepdims=True)
        sum_gn = sum_gn + jnp.sum(pre_grad * away, axis=0, keepdims=True)
        return sum_g, sum_gn

    zero_row = jnp.zeros((1, CO), F32)
    sum_g, sum_gn = lax.fori_loop(0, B, middle, (zero_row, zero_row))

    def add_up(buf, size):
        total = buf[0]
        for j in range(1, size):
            total = total + buf[j]
        return total

    tot8[rank8, 0:1] = sum_g
    tot8[rank8, 1:2] = sum_gn * rstd
    tot8_x[0]()

    def head_part(b, total):
        return total + lax.dot_general(
            sgs[b], act[b], (((0,), (0,)), ((), ())), preferred_element_type=F32
        )

    head_sum = lax.fori_loop(0, B, head_part, jnp.zeros((128, CO), F32))

    tot8_x[1]()
    tot16[chip] = add_up(tot8, 8)
    tot16_x[0]()
    hd8[rank8] = head_sum[0:4, :]
    hd8_x[0]()
    tot16_x[1]()
    totals = add_up(tot16, 16)
    off = totals[0:1] * (1.0 / COUNT)
    slope = rstd * totals[1:2] * (1.0 / COUNT)
    st_local[0] = totals
    gb_out[...] = st_local[0, 0:1, pl.ds(pl.multiple_of(z * 128, 128), 128)]
    gg_out[...] = st_local[0, 1:2, pl.ds(pl.multiple_of(z * 128, 128), 128)]

    def conv_grad(i, carry):
        b = lax.rem(i, B)
        h = lax.rem(3 * (i // B), H)
        spot = pl.ds(pl.multiple_of(h * W, W), W)
        away = conv[b, spot] - mean
        value = scale * (pgs[b, spot] - off - away * slope)
        gc[b, h + 1] = value.astype(BF16)
        gedge_f[0, pl.ds(b * H + h, 1)] = value[W - 1 : W, :]
        gedge_f[1, pl.ds(b * H + h, 1)] = value[0:1, :]
        return carry

    lax.fori_loop(0, 2 * B, conv_grad, 0)
    grow_copies = row_sends(gc.at[:, 1], gc.at[:, H], grow, grow_s, grow_r)
    for copy in grow_copies:
        copy.start()
    lax.fori_loop(2 * B, 4 * B, conv_grad, 0)
    gedge_out[...] = gedge_f[...].astype(BF16)
    gedge_copies = edge_sends(gedge_out, gedge_in, gedge_s, gedge_r)
    for copy in gedge_copies:
        copy.start()

    mine = pl.ds(pl.multiple_of(core * 128, 128), 128)
    theirs = pl.ds(pl.multiple_of((1 - core) * 128, 128), 128)
    a_copies = [remote(send_a.at[r], recv_a.at[r], a_s.at[r], a_r.at[r], other) for r in range(3)]

    def kernel_grad(r):
        lhs = jnp.concatenate([xt[b, h + r] for b in range(B) for h in range(H)], axis=1)
        grad = gc[:, 1 : H + 1].reshape(B * PIX, CO)
        part[r] = jnp.dot(lhs, grad, preferred_element_type=F32).reshape(3, CI, CO)
        send_a[r] = part[r, :, theirs, :].astype(BF16)
        a_copies[r].start()

    def b_copy(r, k):
        j = lax.rem(z + k, 4)
        return remote(send_b.at[r, j], recv_b.at[r, z], b_s.at[r, k], b_r.at[r, z], (me, j))

    def b_arrival(r, k):
        j = lax.rem(z + k, 4)
        return remote(send_b.at[r, j], recv_b.at[r, j], b_s.at[r, k], b_r.at[r, j], (me, j))

    def stage_b(r):
        a_copies[r].wait_recv()
        value = part[r, :, mine, :] + recv_a[r].astype(F32)
        part[r, :, mine, :] = value
        for j in range(4):
            send_b[r, j] = value[:, :, j * 128 : (j + 1) * 128].reshape(384, 128).astype(BF16)
        for k in range(1, 4):
            b_copy(r, k).start()

    kernel_grad(0)
    hd8_x[1]()
    hd16[chip] = add_up(hd8, 8)
    hd16_x[0]()
    kernel_grad(1)
    stage_b(0)
    kernel_grad(2)
    stage_b(1)

    for copy in gedge_copies:
        copy.wait_recv()

    def build_g(i, carry):
        b = i // H
        h = lax.rem(i, H)
        left, right = shifted(
            gc[b, h + 1].astype(F32),
            pick_row(gedge_in, 1, i) * west_ok,
            pick_row(gedge_in, 4, i) * east_ok,
        )
        gl[b, h + 1] = left
        gr[b, h + 1] = right
        return carry

    lax.fori_loop(0, B * H, build_g, 0)
    stage_b(2)
    for copy in grow_copies:
        copy.wait_recv()
    for copy in grow_copies:
        copy.wait_send()
    build_halo(grow, gedge_in, gl, gc, gr)

    def back(b, carry):
        lhs = jnp.concatenate(
            [
                ref[b, r : r + H].reshape(PIX, CO)
                for r in range(3)
                for ref in (gl, gc, gr)
            ],
            axis=1,
        )
        value = jnp.dot(lhs, wgt_t[...], preferred_element_type=F32)
        gi_out[b] = value.reshape(H, W, CI)
        return carry

    lax.fori_loop(0, B, back, 0)

    own_cols = pl.ds(pl.multiple_of(z * 128, 128), 128)
    for r in range(3):
        total = part[r, :, mine, own_cols].reshape(384, 128)
        for k in range(1, 4):
            b_arrival(r, k).wait_recv()
            total = total + recv_b[r, lax.rem(z + k, 4)].astype(F32)
        sum_c[r * 384 : (r + 1) * 384] = total
        send_c[r * 384 : (r + 1) * 384] = total.astype(BF16)

    def c_copy(k):
        j = lax.rem(chip + k, 16)
        return remote(
            send_c.at[pl.ds(part_start(j), PART)],
            recv_c.at[chip],
            c_s.at[k],
            c_r.at[chip],
            dev16(j),
        )

    def c_arrival(k):
        j = lax.rem(chip + k, 16)
        return remote(
            send_c.at[pl.ds(part_start(j), PART)], recv_c.at[j], c_s.at[k], c_r.at[j], dev16(j)
        )

    def loop16(action):
        def body(k, carry):
            action(k)
            return carry

        lax.fori_loop(1, 16, body, 0)

    loop16(lambda k: c_copy(k).start())
    hd16_x[1]()
    head_all[...] = add_up(hd16, 16)
    gh_out[...] = head_all[:, own_cols]
    loop16(lambda k: c_arrival(k).wait_recv())

    def add_c(k, total):
        return total + recv_c[lax.rem(chip + k, 16)].astype(F32)

    total = lax.fori_loop(1, 16, add_c, sum_c[pl.ds(part_start(chip), PART)])
    gath[chip] = total.astype(BF16)
    gath_x = exchange(gath, chip, 16, dev16, g_s, g_r)
    gath_x[0]()
    gath_x[1]()
    o_copy = remote(gath, gath_other, o_s, o_r, other)
    o_copy.start()

    def unpack(src, half):
        for i in range(72):
            pair, rest = divmod(i, 9)
            owner, at = (2 * pair, rest) if rest < 5 else (2 * pair + 1, rest - 4)
            spot = pl.ds(pl.multiple_of(half * 128 + (i % 8) * 16, 16), 16)
            gw_out[i // 8, spot, :] = src[owner, at * 16 : (at + 1) * 16, :].astype(F32)

    unpack(gath, core)
    o_copy.wait_recv()
    unpack(gath_other, 1 - core)

    for copy in xrow_copies + xedge_copies + gedge_copies + a_copies + [o_copy]:
        copy.wait_send()
    for exchanged in (st8_x, st16_x, tot8_x, tot16_x, hd8_x, hd16_x, gath_x):
        exchanged[2]()
    for r in range(3):
        for k in range(1, 4):
            b_copy(r, k).wait_send()
    loop16(lambda k: c_copy(k).wait_send())


def per_device(features, conv_weight, bn_gain, bn_bias, head_weight, labels, raster):
    dma = pltpu.SemaphoreType.DMA
    vmem = pltpu.VMEM
    whole = pl.BlockSpec(memory_space=pltpu.VMEM)
    outs = pl.pallas_call(
        kernel,
        out_shape=(
            jax.ShapeDtypeStruct((TAPS, CI, 128), F32),
            jax.ShapeDtypeStruct((1, 128), F32),
            jax.ShapeDtypeStruct((1, 128), F32),
            jax.ShapeDtypeStruct((4, 128), F32),
            jax.ShapeDtypeStruct((B, H, W, CI), F32),
        ),
        in_specs=[whole, pl.BlockSpec(memory_space=pl.ANY)] + [whole] * 5,
        out_specs=(whole,) * 5,
        scratch_shapes=[
            vmem((TAPS * CI, CO), BF16),
            vmem((TAPS * CO, CI), BF16),
            vmem((B, H + 2, W, CI), BF16),
            vmem((B, H + 2, W, CI), BF16),
            vmem((B, H + 2, W, CI), BF16),
            vmem((B, H + 2, 3 * CI, W), BF16),
            vmem((B, PIX, CO), F32),
            vmem((B, PIX, CO), F32),
            vmem((B, PIX, CO), BF16),
            vmem((B, PIX, 128), BF16),
            vmem((B, PIX, 128), F32),
            vmem((B, PIX, 128), F32),
            vmem((CO, 128), F32),
            vmem((CO, 128), BF16),
            vmem((128, CO), BF16),
            vmem((B, H + 2, W, CO), BF16),
            vmem((B, H + 2, W, CO), BF16),
            vmem((B, H + 2, W, CO), BF16),
            vmem((2, B, W, CI), BF16),
            vmem((2, 16, CI), BF16),
            vmem((6, 16, CI), BF16),
            vmem((2, B, W, CO), BF16),
            vmem((2, 16, CO), F32),
            vmem((2, 16, CO), BF16),
            vmem((6, 16, CO), BF16),
            vmem((B, 2, CO), F32),
            vmem((8, 2, CO), F32),
            vmem((16, 2, CO), F32),
            vmem((8, 2, CO), F32),
            vmem((16, 2, CO), F32),
            vmem((8, 4, CO), F32),
            vmem((16, 4, CO), F32),
            vmem((4, CO), F32),
            vmem((3, 3, CI, CO), F32),
            vmem((3, 3, 128, CO), BF16),
            vmem((3, 3, 128, CO), BF16),
            vmem((3, 4, 384, 128), BF16),
            vmem((3, 4, 384, 128), BF16),
            vmem((OWN, 128), F32),
            vmem((OWN, 128), BF16),
            vmem((16, PART, 128), BF16),
            vmem((16, PART, 128), BF16),
            vmem((16, PART, 128), BF16),
            dma,
            dma((2,)),
            dma((2,)),
            dma((6,)),
            dma((6,)),
            dma((2,)),
            dma((2,)),
            dma((6,)),
            dma((6,)),
        ]
        + [dma((n,)) for n in (8, 8, 16, 16) * 3]
        + [
            dma((3,)),
            dma((3,)),
            dma((3, 4)),
            dma((3, 4)),
            dma((16,)),
            dma((16,)),
            dma((16,)),
            dma((16,)),
            dma,
            dma,
        ],
        compiler_params=pltpu.CompilerParams(
            collective_id=0, has_side_effects=True, vmem_limit_bytes=60 * 1024 * 1024
        ),
        cost_estimate=pl.CostEstimate(
            flops=15_000_000_000, bytes_accessed=8_000_000, transcendentals=300_000
        ),
    )(
        features,
        conv_weight.reshape(TAPS * CI, CO),
        bn_gain.reshape(1, CO),
        bn_bias.reshape(1, CO),
        head_weight,
        labels,
        raster,
    )
    grad_weight, grad_gain, grad_bias, grad_head, grad_input = outs
    return (
        grad_weight.reshape(3, 3, CI, 128),
        grad_gain.reshape(128),
        grad_bias.reshape(128),
        jnp.transpose(grad_head),
        grad_input,
    )


def solution(mesh):
    in_specs = (
        P(None, "rows", "cols", None),
        P(),
        P(),
        P(),
        P(),
        P(None, "rows", "cols"),
        P(None, "rows", "cols"),
    )
    out_specs = (
        P(None, None, None, "cols"),
        P("cols"),
        P("cols"),
        P("cols", None),
        P(None, "rows", "cols", None),
    )
    return jax.shard_map(
        per_device, mesh=mesh, in_specs=in_specs, out_specs=out_specs, check_vma=False
    )
```

```python
import jax
import jax.numpy as jnp
from jax import lax
from jax.experimental import pallas as pl
from jax.experimental.pallas import tpu as pltpu
from jax.sharding import PartitionSpec as P

F32 = jnp.float32
BF16 = jnp.bfloat16
MESH = pl.DeviceIdType.MESH

B = 4
H = 4
W = 128
CI = 256
CO = 512
TAPS = 9
PIX = H * W
COUNT = 4.0 * 128.0 * 512.0
EPS = 1e-05


def kernel(
    feat,
    wgt_hbm,
    gain_ref,
    bias_ref,
    head_ref,
    labels_ref,
    raster_ref,
    gw_out,
    gg_out,
    gb_out,
    gh_out,
    gi_out,
    wgt,
    wgt_t,
    xl,
    xc,
    xr,
    xt,
    conv,
    pgs,
    act,
    sgs,
    onehot,
    pixw,
    head_pad,
    head_tile,
    head_t,
    gl,
    gc,
    gr,
    xrow,
    xedge_out,
    xedge_in,
    grow,
    gedge_f,
    gedge_out,
    gedge_in,
    st_local,
    st8,
    st16,
    tot8,
    tot16,
    hd8,
    hd16,
    head_all,
    part,
    send_a,
    recv_a,
    acc,
    ring1z_send,
    ring1x_send,
    ring1y_send,
    ring1z_recv,
    ring1x_recv,
    ring1y_recv,
    ring2z_send,
    ring2x_send,
    ring2y_send,
    ring2z_recv,
    ring2x_recv,
    ring2y_recv,
    two_own,
    two_send,
    two_recv,
    three_send,
    three_recv,
    gat3,
    gat2,
    gat_other,
    gi_buf,
    wsem,
    xrow_s,
    xrow_r,
    xedge_s,
    xedge_r,
    grow_s,
    grow_r,
    gedge_s,
    gedge_r,
    s8_s,
    s8_r,
    s16_s,
    s16_r,
    t8_s,
    t8_r,
    t16_s,
    t16_r,
    h8_s,
    h8_r,
    h16_s,
    h16_r,
    a_s,
    a_r,
    ring_s,
    ring_r,
    two_s,
    two_r,
    three_s,
    three_r,
    gat3_s,
    gat3_r,
    gat2_s,
    gat2_r,
    o_s,
    o_r,
    gi_sem,
):
    me = lax.axis_index("rows")
    z = lax.axis_index("cols")
    core = lax.rem(me, 2)
    chip = me // 2
    rank8 = z * 2 + core

    def dev8(j):
        return (chip * 2 + lax.rem(j, 2), j // 2)

    def dev16(j):
        return (j * 2 + core, z)

    other = (chip * 2 + 1 - core, z)
    up = lax.rem(me + 31, 32)
    down = lax.rem(me + 1, 32)
    west = lax.rem(z + 3, 4)
    east = lax.rem(z + 1, 4)
    beyond = lax.rem(me + 31 + 2 * core, 32)

    barrier = pltpu.get_barrier_semaphore()

    def greet(device):
        pl.semaphore_signal(barrier, inc=1, device_id=device, device_id_type=MESH)

    for k in range(1, 8):
        greet(dev8(lax.rem(rank8 + k, 8)))
    for col in (west, z, east):
        greet((beyond, col))

    def greet16(k, carry):
        greet(dev16(lax.rem(chip + k, 16)))
        return carry

    lax.fori_loop(1, 16, greet16, 0)

    wcopies = []
    for t in range(TAPS):
        rows = pl.ds(t * CI, CI)
        wcopies.append(pltpu.make_async_copy(wgt_hbm.at[rows], wgt.at[rows], wsem.at[t]))
    for copy in wcopies:
        copy.start()

    row_id = lax.broadcasted_iota(jnp.int32, (16, CI), 0)
    left_edge = jnp.zeros((16, CI), F32)
    right_edge = jnp.zeros((16, CI), F32)
    for b in range(B):
        for h in range(H):
            low = feat[b, h, 0:16, :].astype(F32)[0:1, :]
            top = feat[b, h, W - 16 : W, :].astype(F32)[15:16, :]
            here = row_id == h * B + b
            left_edge = jnp.where(here, low, left_edge)
            right_edge = jnp.where(here, top, right_edge)
    xedge_out[0] = right_edge.astype(BF16)
    xedge_out[1] = left_edge.astype(BF16)

    pl.semaphore_wait(barrier, 25)

    def remote(src, dst, ssem, rsem, device):
        return pltpu.make_async_remote_copy(
            src_ref=src,
            dst_ref=dst,
            send_sem=ssem,
            recv_sem=rsem,
            device_id=device,
            device_id_type=MESH,
        )

    def row_sends(first, last, land, ssem, rsem):
        return [
            remote(last, land.at[0], ssem.at[0], rsem.at[0], (down, z)),
            remote(first, land.at[1], ssem.at[1], rsem.at[1], (up, z)),
        ]

    def edge_sends(out, land, ssem, rsem):
        copies = []
        for side, col in ((0, east), (1, west)):
            for slot, row in ((0, down), (1, me), (2, up)):
                index = side * 3 + slot
                copies.append(
                    remote(
                        out.at[side], land.at[index], ssem.at[index], rsem.at[index], (row, col)
                    )
                )
        return copies

    xrow_copies = row_sends(feat.at[:, 0], feat.at[:, H - 1], xrow, xrow_s, xrow_r)
    for copy in xrow_copies:
        copy.start()
    xedge_copies = edge_sends(xedge_out, xedge_in, xedge_s, xedge_r)
    for copy in xedge_copies:
        copy.start()

    head_pad[...] = jnp.zeros((128, CO), F32)
    head_pad[0:4] = head_ref[...].astype(F32)
    head_t[...] = head_pad[...].astype(BF16)
    head_pad[4:8] = head_ref[...].astype(F32)
    head_tile[...] = jnp.transpose(jnp.concatenate([head_pad[0:8]] * 16, axis=0)).astype(BF16)

    west_ok = jnp.where(z > 0, 1.0, 0.0).astype(F32)
    east_ok = jnp.where(z < 3, 1.0, 0.0).astype(F32)
    up_ok = jnp.where(me > 0, 1.0, 0.0).astype(F32)
    down_ok = jnp.where(me < 31, 1.0, 0.0).astype(F32)

    def pick_row(ref, slot, index):
        block = ref[slot].astype(F32)
        ids = lax.broadcasted_iota(jnp.int32, block.shape, 0)
        return jnp.sum(jnp.where(ids == index, block, 0.0), axis=0, keepdims=True)

    def shifted(value, before, after):
        ids = lax.broadcasted_iota(jnp.int32, value.shape, 0)
        left = jnp.where(ids == 0, before, pltpu.roll(value, 1, 0))
        right = jnp.where(ids == W - 1, after, pltpu.roll(value, W - 1, 0))
        return left.astype(BF16), right.astype(BF16)

    for copy in xedge_copies:
        copy.wait_recv()

    def build_x(i, carry):
        h = i // B
        b = lax.rem(i, B)
        value = feat[b, h].astype(F32)
        left, right = shifted(
            value,
            pick_row(xedge_in, 1, i) * west_ok,
            pick_row(xedge_in, 4, i) * east_ok,
        )
        xl[h + 1, b] = left
        xc[h + 1, b] = feat[b, h]
        xr[h + 1, b] = right
        return carry

    lax.fori_loop(0, B * H, build_x, 0)

    def build_halo(land, edge_in, left_ref, mid_ref, right_ref):
        def body(b, carry):
            for side, line, ok, src in ((0, 0, up_ok, H - 1), (1, H + 1, down_ok, 0)):
                value = land[side, b].astype(F32) * ok
                slot = 2 * side
                left, right = shifted(
                    value,
                    pick_row(edge_in, slot, src * B + b) * (west_ok * ok),
                    pick_row(edge_in, slot + 3, src * B + b) * (east_ok * ok),
                )
                left_ref[line, b] = left
                mid_ref[line, b] = value.astype(BF16)
                right_ref[line, b] = right
            return carry

        lax.fori_loop(0, B, body, 0)

    for copy in wcopies:
        copy.wait()

    def conv_rows(h, first, count):
        lhs = jnp.concatenate(
            [
                ref[h + first + r].reshape(PIX, CI)
                for r in range(count)
                for ref in (xl, xc, xr)
            ],
            axis=1,
        )
        start = pl.multiple_of(first * 3 * CI, 3 * CI)
        return jnp.dot(lhs, wgt[pl.ds(start, count * 3 * CI), :], preferred_element_type=F32)

    def statistics(h, value):
        mid = jnp.sum(value, axis=0, keepdims=True) * (1.0 / PIX)
        st_local[h, 0:1] = mid
        st_local[h, 1:2] = jnp.sum((value - mid) ** 2, axis=0, keepdims=True)

    def transpose_x(line):
        for c, ref in enumerate((xl, xc, xr)):
            xt[line, c * CI : (c + 1) * CI, :] = jnp.transpose(ref[line].reshape(PIX, CI))

    def transpose_w(t):
        wgt_t[pl.ds(pl.multiple_of(t * CO, CO), CO), :] = jnp.transpose(
            wgt[pl.ds(pl.multiple_of((TAPS - 1 - t) * CI, CI), CI), :]
        )

    def inner_rows(i, carry):
        value = conv_rows(1 + i, 0, 3)
        conv[1 + i] = value
        transpose_x(1 + i)
        transpose_x(3 + i)
        statistics(1 + i, value)
        return carry

    lax.fori_loop(0, 2, inner_rows, 0)

    def outer_rows(i, carry):
        conv[3 * i] = conv_rows(3 * i, 1 - i, 2)
        for t in range(4):
            transpose_w(4 * i + t)
        return carry

    lax.fori_loop(0, 2, outer_rows, 0)

    for copy in xrow_copies:
        copy.wait_recv()
    build_halo(xrow, xedge_in, xl, xc, xr)

    def halo_rows(i, carry):
        value = conv[3 * i] + conv_rows(3 * i, 2 * i, 1)
        conv[3 * i] = value
        statistics(3 * i, value)
        return carry

    lax.fori_loop(0, 2, halo_rows, 0)

    def combine(parts, count):
        total = parts[0][0:1]
        for item in parts[1:]:
            total = total + item[0:1]
        mid = total * (1.0 / len(parts))
        spread_sum = None
        for item in parts:
            term = item[1:2] + count * (item[0:1] - mid) ** 2
            spread_sum = term if spread_sum is None else spread_sum + term
        return mid, spread_sum

    def exchange(buf, rank, size, dev, ssem, rsem):
        def copy_to(k):
            return remote(
                buf.at[rank],
                buf.at[rank],
                ssem.at[k],
                rsem.at[rank],
                dev(lax.rem(rank + k, size)),
            )

        def start():
            def body(k, carry):
                copy_to(k).start()
                return carry

            lax.fori_loop(1, size, body, 0)

        def wait():
            def body(k, carry):
                j = lax.rem(rank + k, size)
                remote(buf.at[j], buf.at[j], ssem.at[k], rsem.at[j], dev(j)).wait_recv()
                return carry

            lax.fori_loop(1, size, body, 0)

        def finish():
            def body(k, carry):
                copy_to(k).wait_send()
                return carry

            lax.fori_loop(1, size, body, 0)

        return start, wait, finish

    st8_x = exchange(st8, rank8, 8, dev8, s8_s, s8_r)
    st16_x = exchange(st16, chip, 16, dev16, s16_s, s16_r)
    tot8_x = exchange(tot8, rank8, 8, dev8, t8_s, t8_r)
    tot16_x = exchange(tot16, chip, 16, dev16, t16_s, t16_r)
    hd8_x = exchange(hd8, rank8, 8, dev8, h8_s, h8_r)
    hd16_x = exchange(hd16, chip, 16, dev16, h16_s, h16_r)

    mid, m2 = combine([st_local[h] for h in range(H)], float(PIX))
    st8[rank8, 0:1] = mid
    st8[rank8, 1:2] = m2
    st8_x[0]()

    transpose_x(0)
    transpose_x(H + 1)
    transpose_w(TAPS - 1)

    st8_x[1]()
    mid, m2 = combine([st8[j] for j in range(8)], float(B * PIX))
    st16[chip, 0:1] = mid
    st16[chip, 1:2] = m2
    st16_x[0]()

    lane_class = lax.rem(lax.broadcasted_iota(jnp.int32, (W, 128), 1), 4).astype(F32)
    for b in range(B):
        for h in range(H):
            label = labels_ref[b, h : h + 1, :].astype(F32)
            weight = raster_ref[b, h : h + 1, :].astype(F32)
            label_t = jnp.transpose(jnp.broadcast_to(label, (128, W)))
            weight_t = jnp.transpose(jnp.broadcast_to(weight, (128, W)))
            onehot[h, b * W : (b + 1) * W] = jnp.where(label_t == lane_class, 1.0, 0.0)
            pixw[h, b * W : (b + 1) * W] = (1.0 + weight_t) * 0.25

    st16_x[1]()
    mean, m2 = combine([st16[j] for j in range(16)], float(8 * B * PIX))
    rstd = lax.rsqrt(m2 * (1.0 / COUNT) + EPS)
    gain = gain_ref[...]
    bias = bias_ref[...]
    scale = gain * rstd

    def middle(b, carry):
        sum_g, sum_gn = carry
        away = conv[b] - mean
        pre = away * scale + bias
        acted = jnp.maximum(pre, 0.0).astype(BF16)
        act[b] = acted
        logits = jnp.dot(acted, head_tile[...], preferred_element_type=F32)
        expo = jnp.exp(logits)
        total = expo + pltpu.roll(expo, 1, 1)
        total = total + pltpu.roll(total, 2, 1)
        score = (pixw[b] * (expo / total - onehot[b])).astype(BF16)
        sgs[b] = score
        act_grad = jnp.dot(score, head_t[...], preferred_element_type=F32)
        pre_grad = jnp.where(pre > 0.0, act_grad, 0.0)
        pgs[b] = pre_grad
        sum_g = sum_g + jnp.sum(pre_grad, axis=0, keepdims=True)
        sum_gn = sum_gn + jnp.sum(pre_grad * away, axis=0, keepdims=True)
        return sum_g, sum_gn

    zero_row = jnp.zeros((1, CO), F32)
    sum_g, sum_gn = lax.fori_loop(0, B, middle, (zero_row, zero_row))

    def add_up(buf, size):
        total = buf[0]
        for j in range(1, size):
            total = total + buf[j]
        return total

    tot8[rank8, 0:1] = sum_g
    tot8[rank8, 1:2] = sum_gn * rstd
    tot8_x[0]()

    def head_part(b, total):
        return total + lax.dot_general(
            sgs[b], act[b], (((0,), (0,)), ((), ())), preferred_element_type=F32
        )

    head_sum = lax.fori_loop(0, B, head_part, jnp.zeros((128, CO), F32))

    tot8_x[1]()
    tot16[chip] = add_up(tot8, 8)
    tot16_x[0]()
    hd8[rank8] = head_sum[0:4, :]
    hd8_x[0]()
    tot16_x[1]()
    totals = add_up(tot16, 16)
    off = totals[0:1] * (1.0 / COUNT)
    slope = rstd * totals[1:2] * (1.0 / COUNT)
    st_local[0] = totals
    gb_out[...] = st_local[0, 0:1, pl.ds(pl.multiple_of(z * 128, 128), 128)]
    gg_out[...] = st_local[0, 1:2, pl.ds(pl.multiple_of(z * 128, 128), 128)]

    def conv_grad(i, carry):
        b = lax.rem(i, B)
        h = lax.rem(3 * (i // B), H)
        spot = pl.ds(pl.multiple_of(b * W, W), W)
        away = conv[h, spot] - mean
        value = scale * (pgs[h, spot] - off - away * slope)
        gc[h + 1, b] = value.astype(BF16)
        gedge_f[0, pl.ds(h * B + b, 1)] = value[W - 1 : W, :]
        gedge_f[1, pl.ds(h * B + b, 1)] = value[0:1, :]
        return carry

    lax.fori_loop(0, 2 * B, conv_grad, 0)
    grow_copies = row_sends(gc.at[1], gc.at[H], grow, grow_s, grow_r)
    for copy in grow_copies:
        copy.start()
    lax.fori_loop(2 * B, 4 * B, conv_grad, 0)
    gedge_out[...] = gedge_f[...].astype(BF16)
    gedge_copies = edge_sends(gedge_out, gedge_in, gedge_s, gedge_r)
    for copy in gedge_copies:
        copy.start()

    x = chip // 4
    y = lax.rem(chip, 4)
    coords = {"x": x, "y": y, "z": z}

    def on_axis(axis, j):
        j = lax.rem(j, 4)
        if axis == "z":
            return (me, j)
        if axis == "y":
            return ((x * 4 + j) * 2 + core, z)
        return ((j * 4 + y) * 2 + core, z)

    ORDERS = (("z", "y", "x"), ("x", "z", "y"), ("y", "z", "x"))
    mine = pl.ds(pl.multiple_of(core * 128, 128), 128)
    theirs = pl.ds(pl.multiple_of((1 - core) * 128, 128), 128)
    a_copies = [remote(send_a.at[r], recv_a.at[r], a_s.at[r], a_r.at[r], other) for r in range(3)]

    def build_g(i):
        h, b = divmod(i, B)
        value = gc[h + 1, b].astype(F32)
        gl[h + 1, b], gr[h + 1, b] = shifted(value, 0.0, 0.0)

    def kernel_grad(r):
        for i in ((0, 1, 2, 3, 4), (5, 6, 7, 8, 9), (10, 11, 12, 13, 14, 15))[r]:
            build_g(i)
        lhs = jnp.concatenate([xt[h + r] for h in range(H)], axis=1)
        grad = gc[1 : H + 1].reshape(B * PIX, CO)
        part[r] = jnp.dot(lhs, grad, preferred_element_type=F32).reshape(3, CI, CO)
        send_a[r] = part[r, :, theirs, :].astype(BF16)
        a_copies[r].start()

    ring1_send, ring1_recv = (ring1z_send, ring1x_send, ring1y_send), (
        ring1z_recv,
        ring1x_recv,
        ring1y_recv,
    )
    ring2_send, ring2_recv = (ring2z_send, ring2x_send, ring2y_send), (
        ring2z_recv,
        ring2x_recv,
        ring2y_recv,
    )

    def halves(r):
        return 192 if r == 0 else 48

    def block(r, q, low, high):
        q = lax.rem(q, 4)
        if r == 0:
            return acc[r, low:high, pl.ds(pl.multiple_of(q * 128, 128), 128)]
        return acc[r, pl.ds(pl.multiple_of(q * 96 + low, 16), high - low), :]

    def ring1_copies(r):
        axis = ORDERS[r][0]
        here = coords[axis]
        return [
            remote(
                ring1_send[r].at[way],
                ring1_recv[r].at[way],
                ring_s.at[r, way],
                ring_r.at[r, way],
                on_axis(axis, here + (1, 3)[way]),
            )
            for way in range(2)
        ]

    def ring2_copies(r):
        axis = ORDERS[r][0]
        here = coords[axis]
        return [
            remote(
                ring2_send[r].at[way],
                ring2_recv[r].at[way],
                ring_s.at[r, 2 + way],
                ring_r.at[r, 2 + way],
                on_axis(axis, here + (1, 3)[way]),
            )
            for way in range(2)
        ]

    def ring1(r):
        a_copies[r].wait_recv()
        acc[r] = part[r, :, mine, :].reshape(384, CO) + recv_a[r].reshape(384, CO).astype(F32)
        here, half = coords[ORDERS[r][0]], halves(r)
        ring1_send[r][0] = block(r, here + 2, 0, half).astype(BF16)
        ring1_send[r][1] = block(r, here + 2, half, 2 * half).astype(BF16)
        for copy in ring1_copies(r):
            copy.start()

    def ring2(r):
        for copy in ring1_copies(r):
            copy.wait_recv()
        here, half = coords[ORDERS[r][0]], halves(r)
        low = ring1_recv[r][0].astype(F32)
        high = ring1_recv[r][1].astype(F32)
        ring2_send[r][0, 0:half] = (block(r, here + 1, 0, half) + low).astype(BF16)
        ring2_send[r][0, half : 2 * half] = block(r, here + 1, half, 2 * half).astype(BF16)
        ring2_send[r][1, 0:half] = block(r, here + 3, 0, half).astype(BF16)
        ring2_send[r][1, half : 2 * half] = (
            block(r, here + 3, half, 2 * half) + high
        ).astype(BF16)
        for copy in ring2_copies(r):
            copy.start()

    def along(r, axis, send, recv, ssem, rsem, piece):
        here = coords[axis]

        def towards(k):
            j = lax.rem(here + k, 4)
            return remote(piece(send, j), recv.at[r, here], ssem.at[r, k], rsem.at[r, here], on_axis(axis, j))

        def arriving(k):
            j = lax.rem(here + k, 4)
            return remote(piece(send, j), recv.at[r, j], ssem.at[r, k], rsem.at[r, j], on_axis(axis, j))

        def start():
            for k in range(1, 4):
                towards(k).start()

        def wait():
            for k in range(1, 4):
                arriving(k).wait_recv()

        def finish():
            for k in range(1, 4):
                towards(k).wait_send()

        return start, wait, finish

    second = [
        along(r, ORDERS[r][1], two_send, two_recv, two_s, two_r, lambda ref, j, r=r: ref.at[r, j])
        for r in range(3)
    ]
    third = [
        along(
            r,
            ORDERS[r][2],
            three_send,
            three_recv,
            three_s,
            three_r,
            lambda ref, j, r=r: ref.at[r, j],
        )
        for r in range(3)
    ]
    row_axis = ("y", "x", "y")
    gather3 = [
        along(
            r,
            ORDERS[r][2],
            gat3,
            gat3,
            gat3_s,
            gat3_r,
            lambda ref, j, r=r: ref.at[r, coords[ORDERS[r][2]]],
        )
        for r in range(3)
    ]
    gather2 = [
        along(
            r,
            row_axis[r],
            gat2,
            gat2,
            gat2_s,
            gat2_r,
            lambda ref, j, r=r: ref.at[r, coords[row_axis[r]]],
        )
        for r in range(3)
    ]

    def stage2(r):
        for copy in ring2_copies(r):
            copy.wait_recv()
        here, half = coords[ORDERS[r][0]], halves(r)
        total = (
            block(r, here, 0, 2 * half)
            + ring2_recv[r][0].astype(F32)
            + ring2_recv[r][1].astype(F32)
        )
        for q in range(4):
            piece = (
                total[q * 96 : (q + 1) * 96] if r == 0 else total[:, q * 128 : (q + 1) * 128]
            )
            two_own[r, q] = piece
            two_send[r, q] = piece.astype(BF16)
        second[r][0]()

    def stage3(r):
        second[r][1]()
        here = coords[ORDERS[r][1]]
        total = two_own[r, here]
        for k in range(1, 4):
            total = total + two_recv[r, lax.rem(here + k, 4)].astype(F32)
        for q in range(4):
            three_send[r, q] = total[q * 24 : (q + 1) * 24]
        third[r][0]()

    def collect3(r):
        third[r][1]()
        here = coords[ORDERS[r][2]]
        total = three_send[r, here]
        for k in range(1, 4):
            total = total + three_recv[r, lax.rem(here + k, 4)]
        gat3[r, here] = total
        gather3[r][0]()

    def collect2(r):
        gather3[r][1]()
        here = coords[row_axis[r]]
        gat2[r, here] = jnp.concatenate([gat3[r, q] for q in range(4)], axis=0).astype(BF16)
        gather2[r][0]()

    o_copies = [remote(gat2.at[r], gat_other.at[r], o_s.at[r], o_r.at[r], other) for r in range(3)]

    def swap(r):
        gather2[r][1]()
        o_copies[r].start()
        unpack(r, gat2, core)

    def unpack(r, src, half):
        rows = src[r].reshape(384, 128)
        spot = pl.ds(pl.multiple_of(half * 128, 128), 128)
        for c in range(3):
            gw_out[3 * r + c, spot, :] = rows[c * 128 : (c + 1) * 128].astype(F32)

    def unpack_other(r):
        o_copies[r].wait_recv()
        unpack(r, gat_other, 1 - core)

    gi_copies = [
        pltpu.make_async_copy(gi_buf.at[h], gi_out.at[:, h], gi_sem.at[h]) for h in range(H)
    ]

    def back(h):
        lhs = jnp.concatenate(
            [
                ref[h + r].reshape(PIX, CO)
                for r in range(3)
                for ref in (gl, gc, gr)
            ],
            axis=1,
        )
        value = jnp.dot(lhs, wgt_t[...], preferred_element_type=F32)
        gi_buf[h] = value.reshape(B, W, CI)
        gi_copies[h].start()

    def set_edges(i, carry):
        h = i // B
        b = lax.rem(i, B)
        ids = lax.broadcasted_iota(jnp.int32, (16, CO), 0)
        low = pick_row(gedge_in, 1, i) * west_ok
        top = pick_row(gedge_in, 4, i) * east_ok
        block16 = gl[h + 1, b, 0:16].astype(F32)
        gl[h + 1, b, 0:16] = jnp.where(ids == 0, low, block16).astype(BF16)
        block16 = gr[h + 1, b, W - 16 : W].astype(F32)
        gr[h + 1, b, W - 16 : W] = jnp.where(ids == 15, top, block16).astype(BF16)
        return carry

    kernel_grad(0)
    hd8_x[1]()
    hd16[chip] = add_up(hd8, 8)
    hd16_x[0]()
    kernel_grad(1)
    ring1(0)
    kernel_grad(2)
    ring1(1)
    ring2(0)
    for copy in gedge_copies:
        copy.wait_recv()
    lax.fori_loop(0, B * H, set_edges, 0)
    ring1(2)
    ring2(1)
    stage2(0)
    back(1)
    ring2(2)
    stage2(1)
    stage3(0)
    back(2)
    stage2(2)
    stage3(1)
    collect3(0)
    for copy in grow_copies:
        copy.wait_recv()
    build_halo(grow, gedge_in, gl, gc, gr)
    back(0)
    stage3(2)
    collect3(1)
    collect2(0)
    back(3)
    collect3(2)
    collect2(1)
    swap(0)
    hd16_x[1]()
    head_all[...] = add_up(hd16, 16)
    gh_out[...] = head_all[:, pl.ds(pl.multiple_of(z * 128, 128), 128)]
    collect2(2)
    swap(1)
    unpack_other(0)
    swap(2)
    unpack_other(1)

    for copy in xrow_copies + xedge_copies + grow_copies + gedge_copies + a_copies:
        copy.wait_send()
    for exchanged in (st8_x, st16_x, tot8_x, tot16_x, hd8_x, hd16_x):
        exchanged[2]()
    for r in range(3):
        for copy in ring1_copies(r) + ring2_copies(r):
            copy.wait_send()
        for exchanged in (second[r], third[r], gather3[r], gather2[r]):
            exchanged[2]()
    for copy in gi_copies:
        copy.wait()
    unpack_other(2)
    for copy in o_copies:
        copy.wait_send()


def move_kernel(*refs):
    count = (len(refs) - 2) // 3
    in_sem, out_sem = refs[-2:]
    arrivals, leaves = [], []
    for src, dst, held in zip(refs[:count], refs[count : 2 * count], refs[2 * count : 3 * count]):
        size = src.shape[0] if len(src.shape) > 2 else 1
        for i in range(size):
            here, there, hold = (src.at[i], dst.at[i], held.at[i]) if size > 1 else (src, dst, held)
            slot = len(arrivals)
            arrivals.append(pltpu.make_async_copy(here, hold, in_sem.at[slot]))
            leaves.append(pltpu.make_async_copy(hold, there, out_sem.at[slot]))
    for copy in arrivals:
        copy.start()
    for arrival, leave in zip(arrivals, leaves):
        arrival.wait()
        leave.start()
    for leave in leaves:
        leave.wait()


def move_out(arrays):
    anywhere = pl.BlockSpec(memory_space=pl.ANY)
    return pl.pallas_call(
        move_kernel,
        out_shape=tuple(jax.ShapeDtypeStruct(a.shape, a.dtype) for a in arrays),
        in_specs=[anywhere] * len(arrays),
        out_specs=(anywhere,) * len(arrays),
        scratch_shapes=[pltpu.VMEM(a.shape, a.dtype) for a in arrays]
        + [pltpu.SemaphoreType.DMA((16,)), pltpu.SemaphoreType.DMA((16,))],
        compiler_params=pltpu.CompilerParams(vmem_limit_bytes=60 * 1024 * 1024),
    )(*arrays)


def per_device(features, conv_weight, bn_gain, bn_bias, head_weight, labels, raster):
    dma = pltpu.SemaphoreType.DMA
    vmem = pltpu.VMEM
    whole = pl.BlockSpec(memory_space=pltpu.VMEM)
    outs = pl.pallas_call(
        kernel,
        out_shape=(
            jax.ShapeDtypeStruct((TAPS, CI, 128), F32),
            jax.ShapeDtypeStruct((1, 128), F32),
            jax.ShapeDtypeStruct((1, 128), F32),
            jax.ShapeDtypeStruct((4, 128), F32),
            jax.ShapeDtypeStruct((B, H, W, CI), F32),
        ),
        in_specs=[whole, pl.BlockSpec(memory_space=pl.ANY)] + [whole] * 5,
        out_specs=(whole,) * 4 + (pl.BlockSpec(memory_space=pl.ANY),),
        scratch_shapes=[
            vmem((TAPS * CI, CO), BF16),
            vmem((TAPS * CO, CI), BF16),
            vmem((H + 2, B, W, CI), BF16),
            vmem((H + 2, B, W, CI), BF16),
            vmem((H + 2, B, W, CI), BF16),
            vmem((H + 2, 3 * CI, PIX), BF16),
            vmem((H, PIX, CO), F32),
            vmem((H, PIX, CO), F32),
            vmem((H, PIX, CO), BF16),
            vmem((H, PIX, 128), BF16),
            vmem((H, PIX, 128), F32),
            vmem((H, PIX, 128), F32),
            vmem((128, CO), F32),
            vmem((CO, 128), BF16),
            vmem((128, CO), BF16),
            vmem((H + 2, B, W, CO), BF16),
            vmem((H + 2, B, W, CO), BF16),
            vmem((H + 2, B, W, CO), BF16),
            vmem((2, B, W, CI), BF16),
            vmem((2, 16, CI), BF16),
            vmem((6, 16, CI), BF16),
            vmem((2, B, W, CO), BF16),
            vmem((2, 16, CO), F32),
            vmem((2, 16, CO), BF16),
            vmem((6, 16, CO), BF16),
            vmem((B, 2, CO), F32),
            vmem((8, 2, CO), F32),
            vmem((16, 2, CO), F32),
            vmem((8, 2, CO), F32),
            vmem((16, 2, CO), F32),
            vmem((8, 4, CO), F32),
            vmem((16, 4, CO), F32),
            vmem((4, CO), F32),
            vmem((3, 3, CI, CO), F32),
            vmem((3, 3, 128, CO), BF16),
            vmem((3, 3, 128, CO), BF16),
            vmem((3, 384, CO), F32),
            vmem((2, 192, 128), BF16),
            vmem((2, 48, CO), BF16),
            vmem((2, 48, CO), BF16),
            vmem((2, 192, 128), BF16),
            vmem((2, 48, CO), BF16),
            vmem((2, 48, CO), BF16),
            vmem((2, 384, 128), BF16),
            vmem((2, 96, CO), BF16),
            vmem((2, 96, CO), BF16),
            vmem((2, 384, 128), BF16),
            vmem((2, 96, CO), BF16),
            vmem((2, 96, CO), BF16),
            vmem((3, 4, 96, 128), F32),
            vmem((3, 4, 96, 128), BF16),
            vmem((3, 4, 96, 128), BF16),
            vmem((3, 4, 24, 128), F32),
            vmem((3, 4, 24, 128), F32),
            vmem((3, 4, 24, 128), F32),
            vmem((3, 4, 96, 128), BF16),
            vmem((3, 4, 96, 128), BF16),
            vmem((H, B, W, CI), F32),
            dma((TAPS,)),
            dma((2,)),
            dma((2,)),
            dma((6,)),
            dma((6,)),
            dma((2,)),
            dma((2,)),
            dma((6,)),
            dma((6,)),
        ]
        + [dma((n,)) for n in (8, 8, 16, 16) * 3]
        + [
            dma((3,)),
            dma((3,)),
            dma((3, 4)),
            dma((3, 4)),
            dma((3, 4)),
            dma((3, 4)),
            dma((3, 4)),
            dma((3, 4)),
            dma((3, 4)),
            dma((3, 4)),
            dma((3, 4)),
            dma((3, 4)),
            dma((3,)),
            dma((3,)),
            dma((H,)),
        ],
        compiler_params=pltpu.CompilerParams(
            collective_id=0, has_side_effects=True, vmem_limit_bytes=60 * 1024 * 1024
        ),
        cost_estimate=pl.CostEstimate(
            flops=15_000_000_000, bytes_accessed=8_000_000, transcendentals=300_000
        ),
    )(
        features,
        conv_weight.reshape(TAPS * CI, CO),
        bn_gain.reshape(1, CO),
        bn_bias.reshape(1, CO),
        jnp.transpose(head_weight),
        labels,
        raster,
    )
    grad_weight, grad_gain, grad_bias, grad_head, grad_input = move_out(outs)
    return (
        grad_weight.reshape(3, 3, CI, 128),
        grad_gain.reshape(128),
        grad_bias.reshape(128),
        jnp.transpose(grad_head),
        grad_input,
    )


def solution(mesh):
    in_specs = (
        P(None, "rows", "cols", None),
        P(),
        P(),
        P(),
        P(),
        P(None, "rows", "cols"),
        P(None, "rows", "cols"),
    )
    out_specs = (
        P(None, None, None, "cols"),
        P("cols"),
        P("cols"),
        P("cols", None),
        P(None, "rows", "cols", None),
    )
    return jax.shard_map(
        per_device, mesh=mesh, in_specs=in_specs, out_specs=out_specs, check_vma=False
    )
```

```python
import jax
import jax.numpy as jnp
from jax import lax
from jax.experimental import pallas as pl
from jax.experimental.pallas import tpu as pltpu
from jax.sharding import PartitionSpec as P

F32 = jnp.float32
BF16 = jnp.bfloat16
MESH = pl.DeviceIdType.MESH

B = 4
H = 4
W = 128
CI = 256
CO = 512
TAPS = 9
PIX = H * W
COUNT = 4.0 * 128.0 * 512.0
EPS = 1e-05


def kernel(
    feat,
    wgt_hbm,
    gain_ref,
    bias_ref,
    head_ref,
    labels_ref,
    raster_ref,
    gw_out,
    gg_out,
    gb_out,
    gh_out,
    gi_out,
    wgt,
    wgt_t,
    xl,
    xc,
    xr,
    xt,
    conv,
    pgs,
    act,
    sgs,
    onehot,
    pixw,
    head_pad,
    head_tile,
    head_t,
    gl,
    gc,
    gr,
    xrow,
    xedge_out,
    xedge_in,
    grow,
    gedge_f,
    gedge_out,
    gedge_in,
    st_local,
    st8,
    st16,
    tot8,
    tot16,
    hd2,
    hdz_send,
    hdz,
    hdy,
    hdx,
    part,
    send_a,
    recv_a,
    acc,
    ring1z_send,
    ring1x_send,
    ring1y_send,
    ring1z_recv,
    ring1x_recv,
    ring1y_recv,
    ring2z_send,
    ring2x_send,
    ring2y_send,
    ring2z_recv,
    ring2x_recv,
    ring2y_recv,
    two_own,
    two_send,
    two_recv,
    three_send,
    three_recv,
    gat3,
    gat2,
    gat_other,
    gi_buf,
    wsem,
    xrow_s,
    xrow_r,
    xedge_s,
    xedge_r,
    grow_s,
    grow_r,
    gedge_s,
    gedge_r,
    st_s,
    st_r,
    hd_s,
    hd_r,
    a_s,
    a_r,
    ring_s,
    ring_r,
    dir_s,
    dir_r,
    o_s,
    o_r,
    gi_sem,
):
    me = lax.axis_index("rows")
    z = lax.axis_index("cols")
    core = lax.rem(me, 2)
    chip = me // 2
    x = chip // 4
    y = lax.rem(chip, 4)
    rank8 = z * 2 + core
    coords = {"x": x, "y": y, "z": z}

    def flip(value, bits):
        return lax.bitwise_xor(value, jnp.int32(bits)) if bits else value

    def dev8(k):
        return (flip(me, k % 2), flip(z, k // 2))

    def dev16(k):
        return (flip(me, 2 * k), z)

    def on_axis(axis, k):
        return (me, flip(z, k)) if axis == "z" else (flip(me, (2 if axis == "y" else 8) * k), z)

    other = (flip(me, 1), z)
    up = lax.rem(me + 31, 32)
    down = lax.rem(me + 1, 32)
    west = lax.rem(z + 3, 4)
    east = lax.rem(z + 1, 4)
    beyond = lax.rem(me + 31 + 2 * core, 32)

    barrier = pltpu.get_barrier_semaphore()

    def greet(device):
        pl.semaphore_signal(barrier, inc=1, device_id=device, device_id_type=MESH)

    for k in range(1, 8):
        greet(dev8(k))
    for col in (west, z, east):
        greet((beyond, col))
    for k in range(1, 16):
        greet(dev16(k))

    wcopies = []
    for t in range(TAPS):
        rows = pl.ds(t * CI, CI)
        wcopies.append(pltpu.make_async_copy(wgt_hbm.at[rows], wgt.at[rows], wsem.at[t]))
    for copy in wcopies:
        copy.start()

    row_id = lax.broadcasted_iota(jnp.int32, (16, CI), 0)
    left_edge = jnp.zeros((16, CI), F32)
    right_edge = jnp.zeros((16, CI), F32)
    for b in range(B):
        for h in range(H):
            low = feat[b, h, 0:16, :].astype(F32)[0:1, :]
            top = feat[b, h, W - 16 : W, :].astype(F32)[15:16, :]
            here = row_id == h * B + b
            left_edge = jnp.where(here, low, left_edge)
            right_edge = jnp.where(here, top, right_edge)
    xedge_out[0] = right_edge.astype(BF16)
    xedge_out[1] = left_edge.astype(BF16)

    pl.semaphore_wait(barrier, 25)

    def remote(src, dst, ssem, rsem, device):
        return pltpu.make_async_remote_copy(
            src_ref=src,
            dst_ref=dst,
            send_sem=ssem,
            recv_sem=rsem,
            device_id=device,
            device_id_type=MESH,
        )

    def row_sends(first, last, land, ssem, rsem):
        return [
            remote(last, land.at[0], ssem.at[0], rsem.at[0], (down, z)),
            remote(first, land.at[1], ssem.at[1], rsem.at[1], (up, z)),
        ]

    def edge_sends(out, land, ssem, rsem):
        copies = []
        for side, col in ((0, east), (1, west)):
            for slot, row in ((0, down), (1, me), (2, up)):
                index = side * 3 + slot
                copies.append(
                    remote(
                        out.at[side], land.at[index], ssem.at[index], rsem.at[index], (row, col)
                    )
                )
        return copies

    xrow_copies = row_sends(feat.at[:, 0], feat.at[:, H - 1], xrow, xrow_s, xrow_r)
    for copy in xrow_copies:
        copy.start()
    xedge_copies = edge_sends(xedge_out, xedge_in, xedge_s, xedge_r)
    for copy in xedge_copies:
        copy.start()

    head_pad[...] = jnp.zeros((128, CO), F32)
    head_pad[0:4] = head_ref[...].astype(F32)
    head_t[...] = head_pad[...].astype(BF16)
    head_pad[4:8] = head_ref[...].astype(F32)
    head_tile[...] = jnp.transpose(jnp.concatenate([head_pad[0:8]] * 16, axis=0)).astype(BF16)

    west_ok = jnp.where(z > 0, 1.0, 0.0).astype(F32)
    east_ok = jnp.where(z < 3, 1.0, 0.0).astype(F32)
    up_ok = jnp.where(me > 0, 1.0, 0.0).astype(F32)
    down_ok = jnp.where(me < 31, 1.0, 0.0).astype(F32)

    def pick_row(ref, slot, index):
        block = ref[slot].astype(F32)
        ids = lax.broadcasted_iota(jnp.int32, block.shape, 0)
        return jnp.sum(jnp.where(ids == index, block, 0.0), axis=0, keepdims=True)

    def shifted(value, before, after):
        ids = lax.broadcasted_iota(jnp.int32, value.shape, 0)
        left = jnp.where(ids == 0, before, pltpu.roll(value, 1, 0))
        right = jnp.where(ids == W - 1, after, pltpu.roll(value, W - 1, 0))
        return left.astype(BF16), right.astype(BF16)

    for copy in xedge_copies:
        copy.wait_recv()

    def build_x(i, carry):
        h = i // B
        b = lax.rem(i, B)
        value = feat[b, h].astype(F32)
        left, right = shifted(
            value,
            pick_row(xedge_in, 1, i) * west_ok,
            pick_row(xedge_in, 4, i) * east_ok,
        )
        xl[h + 1, b] = left
        xc[h + 1, b] = feat[b, h]
        xr[h + 1, b] = right
        return carry

    lax.fori_loop(0, B * H, build_x, 0)

    def build_halo(land, edge_in, left_ref, mid_ref, right_ref):
        def body(b, carry):
            for side, line, ok, src in ((0, 0, up_ok, H - 1), (1, H + 1, down_ok, 0)):
                value = land[side, b].astype(F32) * ok
                slot = 2 * side
                left, right = shifted(
                    value,
                    pick_row(edge_in, slot, src * B + b) * (west_ok * ok),
                    pick_row(edge_in, slot + 3, src * B + b) * (east_ok * ok),
                )
                left_ref[line, b] = left
                mid_ref[line, b] = value.astype(BF16)
                right_ref[line, b] = right
            return carry

        lax.fori_loop(0, B, body, 0)

    for copy in wcopies:
        copy.wait()

    def conv_rows(h, first, count):
        lhs = jnp.concatenate(
            [
                ref[h + first + r].reshape(PIX, CI)
                for r in range(count)
                for ref in (xl, xc, xr)
            ],
            axis=1,
        )
        start = pl.multiple_of(first * 3 * CI, 3 * CI)
        return jnp.dot(lhs, wgt[pl.ds(start, count * 3 * CI), :], preferred_element_type=F32)

    def statistics(h, value):
        mid = jnp.sum(value, axis=0, keepdims=True) * (1.0 / PIX)
        st_local[h, 0:1] = mid
        st_local[h, 1:2] = jnp.sum((value - mid) ** 2, axis=0, keepdims=True)

    def transpose_x(line):
        for c, ref in enumerate((xl, xc, xr)):
            xt[line, c * CI : (c + 1) * CI, :] = jnp.transpose(ref[line].reshape(PIX, CI))

    def transpose_w(t):
        wgt_t[pl.ds(pl.multiple_of(t * CO, CO), CO), :] = jnp.transpose(
            wgt[pl.ds(pl.multiple_of((TAPS - 1 - t) * CI, CI), CI), :]
        )

    def inner_rows(i, carry):
        value = conv_rows(1 + i, 0, 3)
        conv[1 + i] = value
        transpose_x(1 + i)
        transpose_x(3 + i)
        statistics(1 + i, value)
        return carry

    lax.fori_loop(0, 2, inner_rows, 0)

    def outer_rows(i, carry):
        conv[3 * i] = conv_rows(3 * i, 1 - i, 2)
        for t in range(4):
            transpose_w(4 * i + t)
        return carry

    lax.fori_loop(0, 2, outer_rows, 0)

    for copy in xrow_copies:
        copy.wait_recv()
    build_halo(xrow, xedge_in, xl, xc, xr)

    def halo_rows(i, carry):
        value = conv[3 * i] + conv_rows(3 * i, 2 * i, 1)
        conv[3 * i] = value
        statistics(3 * i, value)
        return carry

    lax.fori_loop(0, 2, halo_rows, 0)

    def combine(parts, count):
        total = parts[0][0:1]
        for item in parts[1:]:
            total = total + item[0:1]
        mid = total * (1.0 / len(parts))
        spread_sum = None
        for item in parts:
            term = item[1:2] + count * (item[0:1] - mid) ** 2
            spread_sum = term if spread_sum is None else spread_sum + term
        return mid, spread_sum

    def exchange(size, devices, src_of, land, rank, ssem, rsem):
        def all_of(sem):
            few = land.at[0 : size - 1]
            return pltpu.make_async_copy(few, few, sem)

        def start():
            for k in range(1, size):
                remote(src_of(flip(rank, k)), land.at[rank], ssem, rsem, devices(k)).start()

        return start, lambda: all_of(rsem).wait(), lambda: all_of(ssem).wait()

    def share(size, devices, land, rank, ssem, rsem):
        return exchange(size, devices, lambda j: land.at[rank], land, rank, ssem, rsem)

    def along(axis, src_of, land, ssem, rsem):
        return exchange(
            4, lambda k: on_axis(axis, k), src_of, land, coords[axis], ssem, rsem
        )

    def share_along(axis, land, ssem, rsem):
        return along(axis, lambda j: land.at[coords[axis]], land, ssem, rsem)

    st8_x = share(8, dev8, st8, rank8, st_s.at[0], st_r.at[0])
    st16_x = share(16, dev16, st16, chip, st_s.at[1], st_r.at[1])
    tot8_x = share(8, dev8, tot8, rank8, st_s.at[2], st_r.at[2])
    tot16_x = share(16, dev16, tot16, chip, st_s.at[3], st_r.at[3])
    hd2_copy = remote(hd2.at[core], hd2.at[core], hd_s.at[0], hd_r.at[0], other)
    hdz_x = along("z", lambda j: hdz_send.at[j], hdz, hd_s.at[1], hd_r.at[1])
    hdy_x = share_along("y", hdy, hd_s.at[2], hd_r.at[2])
    hdx_x = share_along("x", hdx, hd_s.at[3], hd_r.at[3])

    mid, m2 = combine([st_local[h] for h in range(H)], float(PIX))
    st8[rank8, 0:1] = mid
    st8[rank8, 1:2] = m2
    st8_x[0]()

    transpose_x(0)
    transpose_x(H + 1)
    transpose_w(TAPS - 1)

    st8_x[1]()
    mid, m2 = combine([st8[j] for j in range(8)], float(B * PIX))
    st16[chip, 0:1] = mid
    st16[chip, 1:2] = m2
    st16_x[0]()

    lane_class = lax.rem(lax.broadcasted_iota(jnp.int32, (W, 128), 1), 4).astype(F32)
    for b in range(B):
        for h in range(H):
            label = labels_ref[b, h : h + 1, :].astype(F32)
            weight = raster_ref[b, h : h + 1, :].astype(F32)
            label_t = jnp.transpose(jnp.broadcast_to(label, (128, W)))
            weight_t = jnp.transpose(jnp.broadcast_to(weight, (128, W)))
            onehot[h, b * W : (b + 1) * W] = jnp.where(label_t == lane_class, 1.0, 0.0)
            pixw[h, b * W : (b + 1) * W] = (1.0 + weight_t) * 0.25

    st16_x[1]()
    mean, m2 = combine([st16[j] for j in range(16)], float(8 * B * PIX))
    rstd = lax.rsqrt(m2 * (1.0 / COUNT) + EPS)
    gain = gain_ref[...]
    bias = bias_ref[...]
    scale = gain * rstd

    def middle(b, carry):
        sum_g, sum_gn = carry
        away = conv[b] - mean
        pre = away * scale + bias
        acted = jnp.maximum(pre, 0.0).astype(BF16)
        act[b] = acted
        logits = jnp.dot(acted, head_tile[...], preferred_element_type=F32)
        expo = jnp.exp(logits)
        total = expo + pltpu.roll(expo, 1, 1)
        total = total + pltpu.roll(total, 2, 1)
        score = (pixw[b] * (expo / total - onehot[b])).astype(BF16)
        sgs[b] = score
        act_grad = jnp.dot(score, head_t[...], preferred_element_type=F32)
        pre_grad = jnp.where(pre > 0.0, act_grad, 0.0)
        pgs[b] = pre_grad
        sum_g = sum_g + jnp.sum(pre_grad, axis=0, keepdims=True)
        sum_gn = sum_gn + jnp.sum(pre_grad * away, axis=0, keepdims=True)
        return sum_g, sum_gn

    zero_row = jnp.zeros((1, CO), F32)
    sum_g, sum_gn = lax.fori_loop(0, B, middle, (zero_row, zero_row))

    def add_up(buf, size):
        total = buf[0]
        for j in range(1, size):
            total = total + buf[j]
        return total

    tot8[rank8, 0:1] = sum_g
    tot8[rank8, 1:2] = sum_gn * rstd
    tot8_x[0]()

    def head_part(b, total):
        return total + lax.dot_general(
            sgs[b], act[b], (((0,), (0,)), ((), ())), preferred_element_type=F32
        )

    head_sum = lax.fori_loop(0, B, head_part, jnp.zeros((128, CO), F32))

    tot8_x[1]()
    tot16[chip] = add_up(tot8, 8)
    tot16_x[0]()
    hd2[core] = head_sum[0:4, :]
    hd2_copy.start()
    st8_x[2]()
    st16_x[2]()
    for copy in xrow_copies + xedge_copies:
        copy.wait_send()
    tot16_x[1]()
    totals = add_up(tot16, 16)
    off = totals[0:1] * (1.0 / COUNT)
    slope = rstd * totals[1:2] * (1.0 / COUNT)
    st_local[0] = totals
    gb_out[...] = st_local[0, 0:1, pl.ds(pl.multiple_of(z * 128, 128), 128)]
    gg_out[...] = st_local[0, 1:2, pl.ds(pl.multiple_of(z * 128, 128), 128)]

    def conv_grad(i, carry):
        b = lax.rem(i, B)
        h = lax.rem(3 * (i // B), H)
        spot = pl.ds(pl.multiple_of(b * W, W), W)
        away = conv[h, spot] - mean
        value = scale * (pgs[h, spot] - off - away * slope)
        gc[h + 1, b] = value.astype(BF16)
        gedge_f[0, pl.ds(h * B + b, 1)] = value[W - 1 : W, :]
        gedge_f[1, pl.ds(h * B + b, 1)] = value[0:1, :]
        return carry

    lax.fori_loop(0, 2 * B, conv_grad, 0)
    grow_copies = row_sends(gc.at[1], gc.at[H], grow, grow_s, grow_r)
    for copy in grow_copies:
        copy.start()
    lax.fori_loop(2 * B, 4 * B, conv_grad, 0)
    gedge_out[...] = gedge_f[...].astype(BF16)
    gedge_copies = edge_sends(gedge_out, gedge_in, gedge_s, gedge_r)
    for copy in gedge_copies:
        copy.start()

    ORDERS = (("z", "y", "x"), ("x", "z", "y"), ("y", "z", "x"))
    mine = pl.ds(pl.multiple_of(core * 128, 128), 128)
    theirs = pl.ds(pl.multiple_of((1 - core) * 128, 128), 128)
    a_copies = [remote(send_a.at[r], recv_a.at[r], a_s.at[r], a_r.at[r], other) for r in range(3)]

    def build_g(i):
        h, b = divmod(i, B)
        value = gc[h + 1, b].astype(F32)
        gl[h + 1, b], gr[h + 1, b] = shifted(value, 0.0, 0.0)

    def kernel_grad(r):
        for i in ((0, 1, 2, 3, 4), (5, 6, 7, 8, 9), (10, 11, 12, 13, 14, 15))[r]:
            build_g(i)
        lhs = jnp.concatenate([xt[h + r] for h in range(H)], axis=1)
        grad = gc[1 : H + 1].reshape(B * PIX, CO)
        part[r] = jnp.dot(lhs, grad, preferred_element_type=F32).reshape(3, CI, CO)
        send_a[r] = part[r, :, theirs, :].astype(BF16)
        a_copies[r].start()

    ring1_send, ring1_recv = (ring1z_send, ring1x_send, ring1y_send), (
        ring1z_recv,
        ring1x_recv,
        ring1y_recv,
    )
    ring2_send, ring2_recv = (ring2z_send, ring2x_send, ring2y_send), (
        ring2z_recv,
        ring2x_recv,
        ring2y_recv,
    )

    def halves(r):
        return 192 if r == 0 else 48

    def block(r, q, low, high):
        q = lax.rem(q, 4)
        if r == 0:
            return acc[r, low:high, pl.ds(pl.multiple_of(q * 128, 128), 128)]
        return acc[r, pl.ds(pl.multiple_of(q * 96 + low, 16), high - low), :]

    def around(axis, way):
        step = 1 if way == 0 else 3
        if axis == "z":
            return (me, lax.rem(z + step, 4))
        stride = 2 if axis == "y" else 8
        here = coords[axis]
        return (me + stride * (lax.rem(here + step, 4) - here), z)

    def ring1_copies(r):
        axis = ORDERS[r][0]
        return [
            remote(
                ring1_send[r].at[way],
                ring1_recv[r].at[way],
                ring_s.at[r, way],
                ring_r.at[r, way],
                around(axis, way),
            )
            for way in range(2)
        ]

    def ring2_copies(r):
        axis = ORDERS[r][0]
        return [
            remote(
                ring2_send[r].at[way],
                ring2_recv[r].at[way],
                ring_s.at[r, 2 + way],
                ring_r.at[r, 2 + way],
                around(axis, way),
            )
            for way in range(2)
        ]

    def ring1(r):
        a_copies[r].wait_recv()
        acc[r] = part[r, :, mine, :].reshape(384, CO) + recv_a[r].reshape(384, CO).astype(F32)
        here, half = coords[ORDERS[r][0]], halves(r)
        ring1_send[r][0] = block(r, here + 2, 0, half).astype(BF16)
        ring1_send[r][1] = block(r, here + 2, half, 2 * half).astype(BF16)
        for copy in ring1_copies(r):
            copy.start()

    def ring2(r):
        for copy in ring1_copies(r):
            copy.wait_recv()
        here, half = coords[ORDERS[r][0]], halves(r)
        low = ring1_recv[r][0].astype(F32)
        high = ring1_recv[r][1].astype(F32)
        ring2_send[r][0, 0:half] = (block(r, here + 1, 0, half) + low).astype(BF16)
        ring2_send[r][0, half : 2 * half] = block(r, here + 1, half, 2 * half).astype(BF16)
        ring2_send[r][1, 0:half] = block(r, here + 3, 0, half).astype(BF16)
        ring2_send[r][1, half : 2 * half] = (
            block(r, here + 3, half, 2 * half) + high
        ).astype(BF16)
        for copy in ring2_copies(r):
            copy.start()

    row_axis = ("y", "x", "y")
    second, third, gather3, gather2 = [], [], [], []
    for r in range(3):
        second.append(
            along(
                ORDERS[r][1],
                lambda j, r=r: two_send.at[r, j],
                two_recv.at[r],
                dir_s.at[0, r],
                dir_r.at[0, r],
            )
        )
        third.append(
            along(
                ORDERS[r][2],
                lambda j, r=r: three_send.at[r, j],
                three_recv.at[r],
                dir_s.at[1, r],
                dir_r.at[1, r],
            )
        )
        gather3.append(share_along(ORDERS[r][2], gat3.at[r], dir_s.at[2, r], dir_r.at[2, r]))
        gather2.append(share_along(row_axis[r], gat2.at[r], dir_s.at[3, r], dir_r.at[3, r]))

    def stage2(r):
        for copy in ring2_copies(r):
            copy.wait_recv()
        here, half = coords[ORDERS[r][0]], halves(r)
        total = (
            block(r, here, 0, 2 * half)
            + ring2_recv[r][0].astype(F32)
            + ring2_recv[r][1].astype(F32)
        )
        for q in range(4):
            piece = (
                total[q * 96 : (q + 1) * 96] if r == 0 else total[:, q * 128 : (q + 1) * 128]
            )
            two_own[r, q] = piece
            two_send[r, q] = piece.astype(BF16)
        second[r][0]()

    def stage3(r):
        second[r][1]()
        here = coords[ORDERS[r][1]]
        total = two_own[r, here]
        for k in range(1, 4):
            total = total + two_recv[r, flip(here, k)].astype(F32)
        for q in range(4):
            three_send[r, q] = total[q * 24 : (q + 1) * 24]
        third[r][0]()

    def collect3(r):
        third[r][1]()
        here = coords[ORDERS[r][2]]
        total = three_send[r, here]
        for k in range(1, 4):
            total = total + three_recv[r, flip(here, k)]
        gat3[r, here] = total
        gather3[r][0]()

    def collect2(r):
        gather3[r][1]()
        here = coords[row_axis[r]]
        gat2[r, here] = jnp.concatenate([gat3[r, q] for q in range(4)], axis=0).astype(BF16)
        gather2[r][0]()

    o_copies = [remote(gat2.at[r], gat_other.at[r], o_s.at[r], o_r.at[r], other) for r in range(3)]

    def swap(r):
        gather2[r][1]()
        o_copies[r].start()
        unpack(r, gat2, core)

    def unpack(r, src, half):
        rows = src[r].reshape(384, 128)
        spot = pl.ds(pl.multiple_of(half * 128, 128), 128)
        for c in range(3):
            gw_out[3 * r + c, spot, :] = rows[c * 128 : (c + 1) * 128].astype(F32)

    def unpack_other(r):
        o_copies[r].wait_recv()
        unpack(r, gat_other, 1 - core)

    gi_copies = [
        pltpu.make_async_copy(gi_buf.at[h], gi_out.at[:, h], gi_sem.at[h]) for h in range(H)
    ]

    def back(h):
        lhs = jnp.concatenate(
            [
                ref[h + r].reshape(PIX, CO)
                for r in range(3)
                for ref in (gl, gc, gr)
            ],
            axis=1,
        )
        value = jnp.dot(lhs, wgt_t[...], preferred_element_type=F32)
        gi_buf[h] = value.reshape(B, W, CI)
        gi_copies[h].start()

    def set_edges(i, carry):
        h = i // B
        b = lax.rem(i, B)
        ids = lax.broadcasted_iota(jnp.int32, (16, CO), 0)
        low = pick_row(gedge_in, 1, i) * west_ok
        top = pick_row(gedge_in, 4, i) * east_ok
        block16 = gl[h + 1, b, 0:16].astype(F32)
        gl[h + 1, b, 0:16] = jnp.where(ids == 0, low, block16).astype(BF16)
        block16 = gr[h + 1, b, W - 16 : W].astype(F32)
        gr[h + 1, b, W - 16 : W] = jnp.where(ids == 15, top, block16).astype(BF16)
        return carry

    kernel_grad(0)
    hd2_copy.wait_recv()
    head_pair = hd2[0] + hd2[1]
    for q in range(4):
        hdz_send[q] = head_pair[:, q * 128 : (q + 1) * 128]
    hdz_x[0]()
    kernel_grad(1)
    ring1(0)
    hdz_x[1]()
    head_line = hdz_send[z]
    for k in range(1, 4):
        head_line = head_line + hdz[flip(z, k)]
    hdy[y] = head_line
    hdy_x[0]()
    kernel_grad(2)
    hdy_x[1]()
    hdx[x] = add_up(hdy, 4)
    hdx_x[0]()
    ring1(1)
    ring2(0)
    for copy in gedge_copies:
        copy.wait_recv()
    lax.fori_loop(0, B * H, set_edges, 0)
    ring1(2)
    ring2(1)
    stage2(0)
    back(1)
    hdx_x[1]()
    gh_out[...] = add_up(hdx, 4)
    ring2(2)
    stage2(1)
    stage3(0)
    back(2)
    stage2(2)
    stage3(1)
    collect3(0)
    for copy in grow_copies:
        copy.wait_recv()
    build_halo(grow, gedge_in, gl, gc, gr)
    back(0)
    stage3(2)
    collect3(1)
    collect2(0)
    back(3)
    collect3(2)
    collect2(1)
    swap(0)
    collect2(2)
    swap(1)
    unpack_other(0)
    swap(2)
    unpack_other(1)

    for copy in [hd2_copy] + grow_copies + gedge_copies + a_copies:
        copy.wait_send()
    for exchanged in [tot8_x, tot16_x, hdz_x, hdy_x, hdx_x] + second + third + gather3 + gather2:
        exchanged[2]()
    for r in range(3):
        for copy in ring1_copies(r) + ring2_copies(r):
            copy.wait_send()
    for copy in gi_copies:
        copy.wait()
    unpack_other(2)
    for copy in o_copies:
        copy.wait_send()


def move_kernel(*refs):
    count = (len(refs) - 2) // 3
    in_sem, out_sem = refs[-2:]
    arrivals, leaves = [], []
    for src, dst, held in zip(refs[:count], refs[count : 2 * count], refs[2 * count : 3 * count]):
        size = src.shape[0] if len(src.shape) > 2 else 1
        for i in range(size):
            here, there, hold = (src.at[i], dst.at[i], held.at[i]) if size > 1 else (src, dst, held)
            slot = len(arrivals)
            arrivals.append(pltpu.make_async_copy(here, hold, in_sem.at[slot]))
            leaves.append(pltpu.make_async_copy(hold, there, out_sem.at[slot]))
    for copy in arrivals:
        copy.start()
    for arrival, leave in zip(arrivals, leaves):
        arrival.wait()
        leave.start()
    for leave in leaves:
        leave.wait()


def move_out(arrays):
    anywhere = pl.BlockSpec(memory_space=pl.ANY)
    return pl.pallas_call(
        move_kernel,
        out_shape=tuple(jax.ShapeDtypeStruct(a.shape, a.dtype) for a in arrays),
        in_specs=[anywhere] * len(arrays),
        out_specs=(anywhere,) * len(arrays),
        scratch_shapes=[pltpu.VMEM(a.shape, a.dtype) for a in arrays]
        + [pltpu.SemaphoreType.DMA((16,)), pltpu.SemaphoreType.DMA((16,))],
        compiler_params=pltpu.CompilerParams(vmem_limit_bytes=60 * 1024 * 1024),
    )(*arrays)


def per_device(features, conv_weight, bn_gain, bn_bias, head_weight, labels, raster):
    dma = pltpu.SemaphoreType.DMA
    vmem = pltpu.VMEM
    whole = pl.BlockSpec(memory_space=pltpu.VMEM)
    outs = pl.pallas_call(
        kernel,
        out_shape=(
            jax.ShapeDtypeStruct((TAPS, CI, 128), F32),
            jax.ShapeDtypeStruct((1, 128), F32),
            jax.ShapeDtypeStruct((1, 128), F32),
            jax.ShapeDtypeStruct((4, 128), F32),
            jax.ShapeDtypeStruct((B, H, W, CI), F32),
        ),
        in_specs=[whole, pl.BlockSpec(memory_space=pl.ANY)] + [whole] * 5,
        out_specs=(whole,) * 4 + (pl.BlockSpec(memory_space=pl.ANY),),
        scratch_shapes=[
            vmem((TAPS * CI, CO), BF16),
            vmem((TAPS * CO, CI), BF16),
            vmem((H + 2, B, W, CI), BF16),
            vmem((H + 2, B, W, CI), BF16),
            vmem((H + 2, B, W, CI), BF16),
            vmem((H + 2, 3 * CI, PIX), BF16),
            vmem((H, PIX, CO), F32),
            vmem((H, PIX, CO), F32),
            vmem((H, PIX, CO), BF16),
            vmem((H, PIX, 128), BF16),
            vmem((H, PIX, 128), F32),
            vmem((H, PIX, 128), F32),
            vmem((128, CO), F32),
            vmem((CO, 128), BF16),
            vmem((128, CO), BF16),
            vmem((H + 2, B, W, CO), BF16),
            vmem((H + 2, B, W, CO), BF16),
            vmem((H + 2, B, W, CO), BF16),
            vmem((2, B, W, CI), BF16),
            vmem((2, 16, CI), BF16),
            vmem((6, 16, CI), BF16),
            vmem((2, B, W, CO), BF16),
            vmem((2, 16, CO), F32),
            vmem((2, 16, CO), BF16),
            vmem((6, 16, CO), BF16),
            vmem((B, 2, CO), F32),
            vmem((8, 2, CO), F32),
            vmem((16, 2, CO), F32),
            vmem((8, 2, CO), F32),
            vmem((16, 2, CO), F32),
            vmem((2, 4, CO), F32),
            vmem((4, 4, 128), F32),
            vmem((4, 4, 128), F32),
            vmem((4, 4, 128), F32),
            vmem((4, 4, 128), F32),
            vmem((3, 3, CI, CO), F32),
            vmem((3, 3, 128, CO), BF16),
            vmem((3, 3, 128, CO), BF16),
            vmem((3, 384, CO), F32),
            vmem((2, 192, 128), BF16),
            vmem((2, 48, CO), BF16),
            vmem((2, 48, CO), BF16),
            vmem((2, 192, 128), BF16),
            vmem((2, 48, CO), BF16),
            vmem((2, 48, CO), BF16),
            vmem((2, 384, 128), BF16),
            vmem((2, 96, CO), BF16),
            vmem((2, 96, CO), BF16),
            vmem((2, 384, 128), BF16),
            vmem((2, 96, CO), BF16),
            vmem((2, 96, CO), BF16),
            vmem((3, 4, 96, 128), F32),
            vmem((3, 4, 96, 128), BF16),
            vmem((3, 4, 96, 128), BF16),
            vmem((3, 4, 24, 128), F32),
            vmem((3, 4, 24, 128), F32),
            vmem((3, 4, 24, 128), F32),
            vmem((3, 4, 96, 128), BF16),
            vmem((3, 4, 96, 128), BF16),
            vmem((H, B, W, CI), F32),
            dma((TAPS,)),
            dma((2,)),
            dma((2,)),
            dma((6,)),
            dma((6,)),
            dma((2,)),
            dma((2,)),
            dma((6,)),
            dma((6,)),
        ]
        + [dma((4,))] * 4
        + [
            dma((3,)),
            dma((3,)),
            dma((3, 4)),
            dma((3, 4)),
            dma((4, 3)),
            dma((4, 3)),
            dma((3,)),
            dma((3,)),
            dma((H,)),
        ],
        compiler_params=pltpu.CompilerParams(
            collective_id=0, has_side_effects=True, vmem_limit_bytes=60 * 1024 * 1024
        ),
        cost_estimate=pl.CostEstimate(
            flops=15_000_000_000, bytes_accessed=8_000_000, transcendentals=300_000
        ),
    )(
        features,
        conv_weight.reshape(TAPS * CI, CO),
        bn_gain.reshape(1, CO),
        bn_bias.reshape(1, CO),
        jnp.transpose(head_weight),
        labels,
        raster,
    )
    grad_weight, grad_gain, grad_bias, grad_head, grad_input = move_out(outs)
    return (
        grad_weight.reshape(3, 3, CI, 128),
        grad_gain.reshape(128),
        grad_bias.reshape(128),
        jnp.transpose(grad_head),
        grad_input,
    )


def solution(mesh):
    in_specs = (
        P(None, "rows", "cols", None),
        P(),
        P(),
        P(),
        P(),
        P(None, "rows", "cols"),
        P(None, "rows", "cols"),
    )
    out_specs = (
        P(None, None, None, "cols"),
        P("cols"),
        P("cols"),
        P("cols", None),
        P(None, "rows", "cols", None),
    )
    return jax.shard_map(
        per_device, mesh=mesh, in_specs=in_specs, out_specs=out_specs, check_vma=False
    )
```

```python
import jax
import jax.numpy as jnp
from jax import lax
from jax.experimental import pallas as pl
from jax.experimental.pallas import tpu as pltpu
from jax.sharding import PartitionSpec as P

F32 = jnp.float32
BF16 = jnp.bfloat16
MESH = pl.DeviceIdType.MESH

B = 4
H = 4
W = 128
CI = 256
CO = 512
TAPS = 9
PIX = H * W
COUNT = 4.0 * 128.0 * 512.0
EPS = 1e-05


def kernel(
    feat,
    wgt_hbm,
    gain_ref,
    bias_ref,
    head_ref,
    labels_ref,
    raster_ref,
    gw_out,
    gg_out,
    gb_out,
    gh_out,
    gi_out,
    wgt,
    wgt_t,
    xl,
    xc,
    xr,
    xt,
    conv,
    pgs,
    act,
    sgs,
    onehot,
    pixw,
    head_pad,
    head_tile,
    head_t,
    gl,
    gc,
    gr,
    xrow,
    xedge_out,
    xedge_in,
    grow,
    gedge_f,
    gedge_out,
    gedge_in,
    st_local,
    st8,
    st16,
    tot8,
    tot16,
    hd2,
    hdz_send,
    hdz,
    hdy,
    hdx,
    part,
    with_conv,
    with_one,
    send_a,
    recv_a,
    ring1z_send,
    ring1x_send,
    ring1y_send,
    ring1z_recv,
    ring1x_recv,
    ring1y_recv,
    ring2z_send,
    ring2x_send,
    ring2y_send,
    ring2z_recv,
    ring2x_recv,
    ring2y_recv,
    two_own,
    two_send,
    two_recv,
    three_send,
    three_recv,
    gat3,
    gat2,
    gat_other,
    wsem,
    xrow_s,
    xrow_r,
    xedge_s,
    xedge_r,
    grow_s,
    grow_r,
    gedge_s,
    gedge_r,
    st_s,
    st_r,
    hd_s,
    hd_r,
    a_s,
    a_r,
    ring_s,
    ring_r,
    dir_s,
    dir_r,
    o_s,
    o_r,
    gi_sem,
):
    me = lax.axis_index("rows")
    z = lax.axis_index("cols")
    core = lax.rem(me, 2)
    chip = me // 2
    x = chip // 4
    y = lax.rem(chip, 4)
    rank8 = z * 2 + core
    coords = {"x": x, "y": y, "z": z}

    def flip(value, bits):
        return lax.bitwise_xor(value, jnp.int32(bits)) if bits else value

    def dev8(k):
        return (flip(me, k % 2), flip(z, k // 2))

    def dev16(k):
        return (flip(me, 2 * k), z)

    def on_axis(axis, k):
        return (me, flip(z, k)) if axis == "z" else (flip(me, (2 if axis == "y" else 8) * k), z)

    other = (flip(me, 1), z)
    up = lax.rem(me + 31, 32)
    down = lax.rem(me + 1, 32)
    west = lax.rem(z + 3, 4)
    east = lax.rem(z + 1, 4)
    beyond = lax.rem(me + 31 + 2 * core, 32)

    barrier = pltpu.get_barrier_semaphore()

    def greet(device):
        pl.semaphore_signal(barrier, inc=1, device_id=device, device_id_type=MESH)

    for k in range(1, 8):
        greet(dev8(k))
    for col in (west, z, east):
        greet((beyond, col))
    for k in range(1, 16):
        greet(dev16(k))

    wcopies = []
    for t in range(TAPS):
        rows = pl.ds(t * CI, CI)
        wcopies.append(pltpu.make_async_copy(wgt_hbm.at[rows], wgt.at[rows], wsem.at[t]))
    for copy in wcopies:
        copy.start()

    row_id = lax.broadcasted_iota(jnp.int32, (16, CI), 0)
    left_edge = jnp.zeros((16, CI), F32)
    right_edge = jnp.zeros((16, CI), F32)
    for b in range(B):
        for h in range(H):
            low = feat[b, h, 0:16, :].astype(F32)[0:1, :]
            top = feat[b, h, W - 16 : W, :].astype(F32)[15:16, :]
            here = row_id == h * B + b
            left_edge = jnp.where(here, low, left_edge)
            right_edge = jnp.where(here, top, right_edge)
    xedge_out[0] = right_edge.astype(BF16)
    xedge_out[1] = left_edge.astype(BF16)

    pl.semaphore_wait(barrier, 25)

    def remote(src, dst, ssem, rsem, device):
        return pltpu.make_async_remote_copy(
            src_ref=src,
            dst_ref=dst,
            send_sem=ssem,
            recv_sem=rsem,
            device_id=device,
            device_id_type=MESH,
        )

    def row_sends(first, last, land, ssem, rsem):
        return [
            remote(last, land.at[0], ssem.at[0], rsem.at[0], (down, z)),
            remote(first, land.at[1], ssem.at[1], rsem.at[1], (up, z)),
        ]

    def edge_sends(out, land, ssem, rsem):
        copies = []
        for side, col in ((0, east), (1, west)):
            for slot, row in ((0, down), (1, me), (2, up)):
                index = side * 3 + slot
                copies.append(
                    remote(
                        out.at[side], land.at[index], ssem.at[index], rsem.at[index], (row, col)
                    )
                )
        return copies

    xrow_copies = row_sends(feat.at[:, 0], feat.at[:, H - 1], xrow, xrow_s, xrow_r)
    for copy in xrow_copies:
        copy.start()
    xedge_copies = edge_sends(xedge_out, xedge_in, xedge_s, xedge_r)
    for copy in xedge_copies:
        copy.start()

    head_pad[...] = jnp.zeros((128, CO), F32)
    head_pad[0:4] = head_ref[...].astype(F32)
    head_t[...] = head_pad[...].astype(BF16)
    head_pad[4:8] = head_ref[...].astype(F32)
    head_tile[...] = jnp.transpose(jnp.concatenate([head_pad[0:8]] * 16, axis=0)).astype(BF16)

    lane_class = lax.rem(lax.broadcasted_iota(jnp.int32, (W, 128), 1), 4).astype(F32)
    for b in range(B):
        for h in range(H):
            label = labels_ref[b, h : h + 1, :].astype(F32)
            weight = raster_ref[b, h : h + 1, :].astype(F32)
            label_t = jnp.transpose(jnp.broadcast_to(label, (128, W)))
            weight_t = jnp.transpose(jnp.broadcast_to(weight, (128, W)))
            marks = jnp.where(label_t == lane_class, 1.0, 0.0)
            onehot[h, b * W : (b + 1) * W] = marks.astype(BF16)
            pixw[h, b * W : (b + 1) * W] = ((1.0 + weight_t) * 0.25).astype(BF16)

    west_ok = jnp.where(z > 0, 1.0, 0.0).astype(F32)
    east_ok = jnp.where(z < 3, 1.0, 0.0).astype(F32)
    up_ok = jnp.where(me > 0, 1.0, 0.0).astype(F32)
    down_ok = jnp.where(me < 31, 1.0, 0.0).astype(F32)

    def pick_row(ref, slot, index):
        block = ref[slot].astype(F32)
        ids = lax.broadcasted_iota(jnp.int32, block.shape, 0)
        return jnp.sum(jnp.where(ids == index, block, 0.0), axis=0, keepdims=True)

    def shifted(value, before, after):
        ids = lax.broadcasted_iota(jnp.int32, value.shape, 0)
        left = jnp.where(ids == 0, before, pltpu.roll(value, 1, 0))
        right = jnp.where(ids == W - 1, after, pltpu.roll(value, W - 1, 0))
        return left.astype(BF16), right.astype(BF16)

    for copy in xedge_copies:
        copy.wait_recv()

    def build_x(i, carry):
        h = i // B
        b = lax.rem(i, B)
        value = feat[b, h].astype(F32)
        left, right = shifted(
            value,
            pick_row(xedge_in, 1, i) * west_ok,
            pick_row(xedge_in, 4, i) * east_ok,
        )
        xl[h + 1, b] = left
        xc[h + 1, b] = feat[b, h]
        xr[h + 1, b] = right
        return carry

    lax.fori_loop(0, B * H, build_x, 0)

    def build_halo(land, edge_in, left_ref, mid_ref, right_ref):
        def body(b, carry):
            for side, line, ok, src in ((0, 0, up_ok, H - 1), (1, H + 1, down_ok, 0)):
                value = land[side, b].astype(F32) * ok
                slot = 2 * side
                left, right = shifted(
                    value,
                    pick_row(edge_in, slot, src * B + b) * (west_ok * ok),
                    pick_row(edge_in, slot + 3, src * B + b) * (east_ok * ok),
                )
                left_ref[line, b] = left
                mid_ref[line, b] = value.astype(BF16)
                right_ref[line, b] = right
            return carry

        lax.fori_loop(0, B, body, 0)

    for copy in wcopies:
        copy.wait()

    def conv_rows(h, first, count):
        lhs = jnp.concatenate(
            [
                ref[h + first + r].reshape(PIX, CI)
                for r in range(count)
                for ref in (xl, xc, xr)
            ],
            axis=1,
        )
        start = pl.multiple_of(first * 3 * CI, 3 * CI)
        return jnp.dot(lhs, wgt[pl.ds(start, count * 3 * CI), :], preferred_element_type=F32)

    def statistics(h, value):
        mid = jnp.sum(value, axis=0, keepdims=True) * (1.0 / PIX)
        st_local[h, 0:1] = mid
        st_local[h, 1:2] = jnp.sum((value - mid) ** 2, axis=0, keepdims=True)

    def transpose_x(line):
        for c, ref in enumerate((xl, xc, xr)):
            xt[line, c * CI : (c + 1) * CI, :] = jnp.transpose(ref[line].reshape(PIX, CI))

    def transpose_w(t):
        wgt_t[pl.ds(pl.multiple_of(t * CO, CO), CO), :] = jnp.transpose(
            wgt[pl.ds(pl.multiple_of((TAPS - 1 - t) * CI, CI), CI), :]
        )

    def inner_rows(i, carry):
        value = conv_rows(1 + i, 0, 3)
        conv[1 + i] = value
        transpose_x(1 + i)
        transpose_x(3 + i)
        statistics(1 + i, value)
        return carry

    lax.fori_loop(0, 2, inner_rows, 0)

    def outer_rows(i, carry):
        conv[3 * i] = conv_rows(3 * i, 1 - i, 2)
        for t in range(4):
            transpose_w(4 * i + t)
        return carry

    lax.fori_loop(0, 2, outer_rows, 0)

    for copy in xrow_copies:
        copy.wait_recv()
    build_halo(xrow, xedge_in, xl, xc, xr)

    def halo_rows(i, carry):
        value = conv[3 * i] + conv_rows(3 * i, 2 * i, 1)
        conv[3 * i] = value
        statistics(3 * i, value)
        return carry

    lax.fori_loop(0, 2, halo_rows, 0)

    def combine(parts, count):
        total = parts[0][0:1]
        for item in parts[1:]:
            total = total + item[0:1]
        mid = total * (1.0 / len(parts))
        spread_sum = None
        for item in parts:
            term = item[1:2] + count * (item[0:1] - mid) ** 2
            spread_sum = term if spread_sum is None else spread_sum + term
        return mid, spread_sum

    def exchange(size, devices, src_of, land, rank, ssem, rsem):
        def all_of(sem):
            few = land.at[0 : size - 1]
            return pltpu.make_async_copy(few, few, sem)

        def start():
            for k in range(1, size):
                remote(src_of(flip(rank, k)), land.at[rank], ssem, rsem, devices(k)).start()

        return start, lambda: all_of(rsem).wait(), lambda: all_of(ssem).wait()

    def share(size, devices, land, rank, ssem, rsem):
        return exchange(size, devices, lambda j: land.at[rank], land, rank, ssem, rsem)

    def along(axis, src_of, land, ssem, rsem):
        return exchange(
            4, lambda k: on_axis(axis, k), src_of, land, coords[axis], ssem, rsem
        )

    def share_along(axis, land, ssem, rsem):
        return along(axis, lambda j: land.at[coords[axis]], land, ssem, rsem)

    st8_x = share(8, dev8, st8, rank8, st_s.at[0], st_r.at[0])
    st16_x = share(16, dev16, st16, chip, st_s.at[1], st_r.at[1])
    tot8_x = share(8, dev8, tot8, rank8, st_s.at[2], st_r.at[2])
    tot16_x = share(16, dev16, tot16, chip, st_s.at[3], st_r.at[3])
    hd2_copy = remote(hd2.at[core], hd2.at[core], hd_s.at[0], hd_r.at[0], other)
    hdz_x = along("z", lambda j: hdz_send.at[j], hdz, hd_s.at[1], hd_r.at[1])
    hdy_x = share_along("y", hdy, hd_s.at[2], hd_r.at[2])
    hdx_x = share_along("x", hdx, hd_s.at[3], hd_r.at[3])

    mid, m2 = combine([st_local[h] for h in range(H)], float(PIX))
    st8[rank8, 0:1] = mid
    st8[rank8, 1:2] = m2
    st8_x[0]()

    local_mean = mid
    transpose_x(0)
    transpose_x(H + 1)

    def center(h, carry):
        act[h] = (conv[h] - local_mean).astype(BF16)
        return carry

    lax.fori_loop(0, H, center, 0)

    def features_of(r):
        return jnp.concatenate([xt[h + r] for h in range(H)], axis=1)

    def cross_conv(r, carry):
        lhs = features_of(r)
        with_conv[r] = jnp.dot(lhs, act[...].reshape(B * PIX, CO), preferred_element_type=F32)
        with_one[r] = jnp.dot(lhs, jnp.ones((B * PIX, 128), BF16), preferred_element_type=F32)
        return carry

    lax.fori_loop(0, 1, cross_conv, 0)
    st8_x[1]()
    mid, m2 = combine([st8[j] for j in range(8)], float(B * PIX))
    st16[chip, 0:1] = mid
    st16[chip, 1:2] = m2
    st16_x[0]()
    lax.fori_loop(1, 3, cross_conv, 0)
    transpose_w(TAPS - 1)
    st16_x[1]()
    mean, m2 = combine([st16[j] for j in range(16)], float(8 * B * PIX))
    rstd = lax.rsqrt(m2 * (1.0 / COUNT) + EPS)
    gain = gain_ref[...]
    bias = bias_ref[...]
    scale = gain * rstd

    def middle(b, carry):
        sum_g, sum_gn = carry
        away = conv[b] - mean
        pre = away * scale + bias
        acted = jnp.maximum(pre, 0.0).astype(BF16)
        act[b] = acted
        logits = jnp.dot(acted, head_tile[...], preferred_element_type=F32)
        expo = jnp.exp(logits)
        total = expo + pltpu.roll(expo, 1, 1)
        total = total + pltpu.roll(total, 2, 1)
        score = (pixw[b].astype(F32) * (expo / total - onehot[b].astype(F32))).astype(BF16)
        sgs[b] = score
        act_grad = jnp.dot(score, head_t[...], preferred_element_type=F32)
        pre_grad = jnp.where(pre > 0.0, act_grad, 0.0)
        pgs[b] = pre_grad
        gc[b + 1] = pre_grad.astype(BF16).reshape(B, W, CO)
        sum_g = sum_g + jnp.sum(pre_grad, axis=0, keepdims=True)
        sum_gn = sum_gn + jnp.sum(pre_grad * away, axis=0, keepdims=True)
        return sum_g, sum_gn

    zero_row = jnp.zeros((1, CO), F32)
    sum_g, sum_gn = lax.fori_loop(0, B, middle, (zero_row, zero_row))

    def add_up(buf, size):
        total = buf[0]
        for j in range(1, size):
            total = total + buf[j]
        return total

    tot8[rank8, 0:1] = sum_g
    tot8[rank8, 1:2] = sum_gn * rstd
    tot8_x[0]()

    def cross_grad(r, carry):
        part[r] = jnp.dot(
            features_of(r),
            gc[1 : H + 1].reshape(B * PIX, CO),
            preferred_element_type=F32,
        ).reshape(3, CI, CO)
        return carry

    def head_part(b, total):
        return total + lax.dot_general(
            sgs[b], act[b], (((0,), (0,)), ((), ())), preferred_element_type=F32
        )

    lax.fori_loop(0, 1, cross_grad, 0)
    tot8_x[1]()
    tot16[chip] = add_up(tot8, 8)
    tot16_x[0]()
    lax.fori_loop(1, 3, cross_grad, 0)
    head_sum = lax.fori_loop(0, B, head_part, jnp.zeros((128, CO), F32))
    hd2[core] = head_sum[0:4, :]
    hd2_copy.start()
    st8_x[2]()
    st16_x[2]()
    for copy in xrow_copies + xedge_copies:
        copy.wait_send()
    tot16_x[1]()
    totals = add_up(tot16, 16)
    off = totals[0:1] * (1.0 / COUNT)
    slope = rstd * totals[1:2] * (1.0 / COUNT)
    st_local[0] = totals
    gb_out[...] = st_local[0, 0:1, pl.ds(pl.multiple_of(z * 128, 128), 128)]
    gg_out[...] = st_local[0, 1:2, pl.ds(pl.multiple_of(z * 128, 128), 128)]

    ORDERS = (("z", "y", "x"), ("x", "z", "y"), ("y", "z", "x"))
    a_copies = [remote(send_a.at[r], recv_a.at[r], a_s.at[r], a_r.at[r], other) for r in range(3)]

    shift = scale * (off + slope * (local_mean - mean))
    turn = scale * slope

    def kernel_grad(r, half):
        pieces = []
        for c in range(3):
            rows = pl.ds(pl.multiple_of(c * CI + half * 128, 128), 128)
            ones = jnp.concatenate([with_one[r, rows, :]] * 4, axis=1)
            pieces.append(
                part[r, c, pl.ds(pl.multiple_of(half * 128, 128), 128), :] * scale
                - with_conv[r, rows, :] * turn
                - ones * shift
            )
        return pieces

    for r in range(3):
        for c, piece in enumerate(kernel_grad(r, 1 - core)):
            send_a[r, c] = piece.astype(BF16)
        a_copies[r].start()

    def conv_grad(i, carry):
        b = lax.rem(i, B)
        h = lax.rem(3 * (i // B), H)
        spot = pl.ds(pl.multiple_of(b * W, W), W)
        away = conv[h, spot] - mean
        value = scale * (pgs[h, spot] - off - away * slope)
        gc[h + 1, b] = value.astype(BF16)
        gl[h + 1, b], gr[h + 1, b] = shifted(value, 0.0, 0.0)
        gedge_f[0, pl.ds(h * B + b, 1)] = value[W - 1 : W, :]
        gedge_f[1, pl.ds(h * B + b, 1)] = value[0:1, :]
        return carry

    ring1_send, ring1_recv = (ring1z_send, ring1x_send, ring1y_send), (
        ring1z_recv,
        ring1x_recv,
        ring1y_recv,
    )
    ring2_send, ring2_recv = (ring2z_send, ring2x_send, ring2y_send), (
        ring2z_recv,
        ring2x_recv,
        ring2y_recv,
    )

    def halves(r):
        return 192 if r == 0 else 48

    def block(r, q, low, high):
        q = lax.rem(q, 4)
        if r == 0:
            return with_conv[r, low:high, pl.ds(pl.multiple_of(q * 128, 128), 128)]
        return with_conv[r, pl.ds(pl.multiple_of(q * 96 + low, 16), high - low), :]

    def around(axis, way):
        step = 1 if way == 0 else 3
        if axis == "z":
            return (me, lax.rem(z + step, 4))
        stride = 2 if axis == "y" else 8
        here = coords[axis]
        return (me + stride * (lax.rem(here + step, 4) - here), z)

    def ring1_copies(r):
        axis = ORDERS[r][0]
        return [
            remote(
                ring1_send[r].at[way],
                ring1_recv[r].at[way],
                ring_s.at[r, way],
                ring_r.at[r, way],
                around(axis, way),
            )
            for way in range(2)
        ]

    def ring2_copies(r):
        axis = ORDERS[r][0]
        return [
            remote(
                ring2_send[r].at[way],
                ring2_recv[r].at[way],
                ring_s.at[r, 2 + way],
                ring_r.at[r, 2 + way],
                around(axis, way),
            )
            for way in range(2)
        ]

    def ring1(r):
        a_copies[r].wait_recv()
        for c, piece in enumerate(kernel_grad(r, core)):
            with_conv[r, c * 128 : (c + 1) * 128] = piece + recv_a[r, c].astype(F32)
        here, half = coords[ORDERS[r][0]], halves(r)
        ring1_send[r][0] = block(r, here + 2, 0, half).astype(BF16)
        ring1_send[r][1] = block(r, here + 2, half, 2 * half).astype(BF16)
        for copy in ring1_copies(r):
            copy.start()

    def ring2(r):
        for copy in ring1_copies(r):
            copy.wait_recv()
        here, half = coords[ORDERS[r][0]], halves(r)
        low = ring1_recv[r][0].astype(F32)
        high = ring1_recv[r][1].astype(F32)
        ring2_send[r][0, 0:half] = (block(r, here + 1, 0, half) + low).astype(BF16)
        ring2_send[r][0, half : 2 * half] = block(r, here + 1, half, 2 * half).astype(BF16)
        ring2_send[r][1, 0:half] = block(r, here + 3, 0, half).astype(BF16)
        ring2_send[r][1, half : 2 * half] = (
            block(r, here + 3, half, 2 * half) + high
        ).astype(BF16)
        for copy in ring2_copies(r):
            copy.start()

    row_axis = ("y", "x", "y")
    second, third, gather3, gather2 = [], [], [], []
    for r in range(3):
        second.append(
            along(
                ORDERS[r][1],
                lambda j, r=r: two_send.at[r, j],
                two_recv.at[r],
                dir_s.at[0, r],
                dir_r.at[0, r],
            )
        )
        third.append(
            along(
                ORDERS[r][2],
                lambda j, r=r: three_send.at[r, j],
                three_recv.at[r],
                dir_s.at[1, r],
                dir_r.at[1, r],
            )
        )
        gather3.append(share_along(ORDERS[r][2], gat3.at[r], dir_s.at[2, r], dir_r.at[2, r]))
        gather2.append(share_along(row_axis[r], gat2.at[r], dir_s.at[3, r], dir_r.at[3, r]))

    def stage2(r):
        for copy in ring2_copies(r):
            copy.wait_recv()
        here, half = coords[ORDERS[r][0]], halves(r)
        total = (
            block(r, here, 0, 2 * half)
            + ring2_recv[r][0].astype(F32)
            + ring2_recv[r][1].astype(F32)
        )
        for q in range(4):
            piece = (
                total[q * 96 : (q + 1) * 96] if r == 0 else total[:, q * 128 : (q + 1) * 128]
            )
            two_own[r, q] = piece
            two_send[r, q] = piece.astype(BF16)
        second[r][0]()

    def stage3(r):
        second[r][1]()
        here = coords[ORDERS[r][1]]
        total = two_own[r, here]
        for k in range(1, 4):
            total = total + two_recv[r, flip(here, k)].astype(F32)
        for q in range(4):
            three_send[r, q] = total[q * 24 : (q + 1) * 24]
        third[r][0]()

    def collect3(r):
        third[r][1]()
        here = coords[ORDERS[r][2]]
        total = three_send[r, here]
        for k in range(1, 4):
            total = total + three_recv[r, flip(here, k)]
        gat3[r, here] = total
        gather3[r][0]()

    def collect2(r):
        gather3[r][1]()
        here = coords[row_axis[r]]
        gat2[r, here] = jnp.concatenate([gat3[r, q] for q in range(4)], axis=0).astype(BF16)
        gather2[r][0]()

    o_copies = [remote(gat2.at[r], gat_other.at[r], o_s.at[r], o_r.at[r], other) for r in range(3)]

    def swap(r):
        gather2[r][1]()
        o_copies[r].start()
        unpack(r, gat2, core)

    def unpack(r, src, half):
        rows = src[r].reshape(384, 128)
        spot = pl.ds(pl.multiple_of(half * 128, 128), 128)
        for c in range(3):
            gw_out[3 * r + c, spot, :] = rows[c * 128 : (c + 1) * 128].astype(F32)

    def unpack_other(r):
        o_copies[r].wait_recv()
        unpack(r, gat_other, 1 - core)

    gi_copies = [
        [
            pltpu.make_async_copy(
                pgs.at[h, pl.ds(b * W, W), pl.ds(0, CI)], gi_out.at[b, h], gi_sem.at[h, b]
            )
            for b in range(B)
        ]
        for h in range(H)
    ]

    def back(h):
        lhs = jnp.concatenate(
            [
                ref[h + r].reshape(PIX, CO)
                for r in range(3)
                for ref in (gl, gc, gr)
            ],
            axis=1,
        )
        value = jnp.dot(lhs, wgt_t[...], preferred_element_type=F32)
        pgs[h, :, 0:CI] = value
        for copy in gi_copies[h]:
            copy.start()

    def set_edges(i, carry):
        h = i // B
        b = lax.rem(i, B)
        ids = lax.broadcasted_iota(jnp.int32, (16, CO), 0)
        low = pick_row(gedge_in, 1, i) * west_ok
        top = pick_row(gedge_in, 4, i) * east_ok
        block16 = gl[h + 1, b, 0:16].astype(F32)
        gl[h + 1, b, 0:16] = jnp.where(ids == 0, low, block16).astype(BF16)
        block16 = gr[h + 1, b, W - 16 : W].astype(F32)
        gr[h + 1, b, W - 16 : W] = jnp.where(ids == 15, top, block16).astype(BF16)
        return carry

    lax.fori_loop(0, 2 * B, conv_grad, 0)
    grow_copies = row_sends(gc.at[1], gc.at[H], grow, grow_s, grow_r)
    for copy in grow_copies:
        copy.start()
    ring1(0)
    lax.fori_loop(2 * B, 4 * B, conv_grad, 0)
    gedge_out[...] = gedge_f[...].astype(BF16)
    gedge_copies = edge_sends(gedge_out, gedge_in, gedge_s, gedge_r)
    for copy in gedge_copies:
        copy.start()
    ring1(1)
    ring1(2)
    hd2_copy.wait_recv()
    head_pair = hd2[0] + hd2[1]
    for q in range(4):
        hdz_send[q] = head_pair[:, q * 128 : (q + 1) * 128]
    hdz_x[0]()
    ring2(0)
    ring2(1)
    ring2(2)
    for copy in gedge_copies:
        copy.wait_recv()
    lax.fori_loop(0, B * H, set_edges, 0)
    hdz_x[1]()
    head_line = hdz_send[z]
    for k in range(1, 4):
        head_line = head_line + hdz[flip(z, k)]
    hdy[y] = head_line
    hdy_x[0]()
    back(1)
    stage2(0)
    stage2(1)
    stage2(2)
    hdy_x[1]()
    hdx[x] = add_up(hdy, 4)
    hdx_x[0]()
    back(2)
    stage3(0)
    stage3(1)
    stage3(2)
    for copy in grow_copies:
        copy.wait_recv()
    build_halo(grow, gedge_in, gl, gc, gr)
    hdx_x[1]()
    gh_out[...] = add_up(hdx, 4)
    collect3(0)
    collect3(1)
    collect3(2)
    back(0)
    collect2(0)
    collect2(1)
    collect2(2)
    back(3)
    swap(0)
    swap(1)
    swap(2)
    unpack_other(0)
    unpack_other(1)

    for copy in [hd2_copy] + grow_copies + gedge_copies + a_copies:
        copy.wait_send()
    for exchanged in [tot8_x, tot16_x, hdz_x, hdy_x, hdx_x] + second + third + gather3 + gather2:
        exchanged[2]()
    for r in range(3):
        for copy in ring1_copies(r) + ring2_copies(r):
            copy.wait_send()
    for line in gi_copies:
        for copy in line:
            copy.wait()
    unpack_other(2)
    for copy in o_copies:
        copy.wait_send()


def move_kernel(*refs):
    count = (len(refs) - 2) // 3
    in_sem, out_sem = refs[-2:]
    arrivals, leaves = [], []
    for src, dst, held in zip(refs[:count], refs[count : 2 * count], refs[2 * count : 3 * count]):
        size = src.shape[0] if len(src.shape) > 2 else 1
        for i in range(size):
            here, there, hold = (src.at[i], dst.at[i], held.at[i]) if size > 1 else (src, dst, held)
            slot = len(arrivals)
            arrivals.append(pltpu.make_async_copy(here, hold, in_sem.at[slot]))
            leaves.append(pltpu.make_async_copy(hold, there, out_sem.at[slot]))
    for copy in arrivals:
        copy.start()
    for arrival, leave in zip(arrivals, leaves):
        arrival.wait()
        leave.start()
    for leave in leaves:
        leave.wait()


def move_out(arrays):
    anywhere = pl.BlockSpec(memory_space=pl.ANY)
    return pl.pallas_call(
        move_kernel,
        out_shape=tuple(jax.ShapeDtypeStruct(a.shape, a.dtype) for a in arrays),
        in_specs=[anywhere] * len(arrays),
        out_specs=(anywhere,) * len(arrays),
        scratch_shapes=[pltpu.VMEM(a.shape, a.dtype) for a in arrays]
        + [pltpu.SemaphoreType.DMA((16,)), pltpu.SemaphoreType.DMA((16,))],
        compiler_params=pltpu.CompilerParams(vmem_limit_bytes=60 * 1024 * 1024),
    )(*arrays)


def per_device(features, conv_weight, bn_gain, bn_bias, head_weight, labels, raster):
    dma = pltpu.SemaphoreType.DMA
    vmem = pltpu.VMEM
    whole = pl.BlockSpec(memory_space=pltpu.VMEM)
    outs = pl.pallas_call(
        kernel,
        out_shape=(
            jax.ShapeDtypeStruct((TAPS, CI, 128), F32),
            jax.ShapeDtypeStruct((1, 128), F32),
            jax.ShapeDtypeStruct((1, 128), F32),
            jax.ShapeDtypeStruct((4, 128), F32),
            jax.ShapeDtypeStruct((B, H, W, CI), F32),
        ),
        in_specs=[whole, pl.BlockSpec(memory_space=pl.ANY)] + [whole] * 5,
        out_specs=(whole,) * 4 + (pl.BlockSpec(memory_space=pl.ANY),),
        scratch_shapes=[
            vmem((TAPS * CI, CO), BF16),
            vmem((TAPS * CO, CI), BF16),
            vmem((H + 2, B, W, CI), BF16),
            vmem((H + 2, B, W, CI), BF16),
            vmem((H + 2, B, W, CI), BF16),
            vmem((H + 2, 3 * CI, PIX), BF16),
            vmem((H, PIX, CO), F32),
            vmem((H, PIX, CO), F32),
            vmem((H, PIX, CO), BF16),
            vmem((H, PIX, 128), BF16),
            vmem((H, PIX, 128), BF16),
            vmem((H, PIX, 128), BF16),
            vmem((128, CO), F32),
            vmem((CO, 128), BF16),
            vmem((128, CO), BF16),
            vmem((H + 2, B, W, CO), BF16),
            vmem((H + 2, B, W, CO), BF16),
            vmem((H + 2, B, W, CO), BF16),
            vmem((2, B, W, CI), BF16),
            vmem((2, 16, CI), BF16),
            vmem((6, 16, CI), BF16),
            vmem((2, B, W, CO), BF16),
            vmem((2, 16, CO), F32),
            vmem((2, 16, CO), BF16),
            vmem((6, 16, CO), BF16),
            vmem((B, 2, CO), F32),
            vmem((8, 2, CO), F32),
            vmem((16, 2, CO), F32),
            vmem((8, 2, CO), F32),
            vmem((16, 2, CO), F32),
            vmem((2, 4, CO), F32),
            vmem((4, 4, 128), F32),
            vmem((4, 4, 128), F32),
            vmem((4, 4, 128), F32),
            vmem((4, 4, 128), F32),
            vmem((3, 3, CI, CO), F32),
            vmem((3, 3 * CI, CO), F32),
            vmem((3, 3 * CI, 128), F32),
            vmem((3, 3, 128, CO), BF16),
            vmem((3, 3, 128, CO), BF16),
            vmem((2, 192, 128), BF16),
            vmem((2, 48, CO), BF16),
            vmem((2, 48, CO), BF16),
            vmem((2, 192, 128), BF16),
            vmem((2, 48, CO), BF16),
            vmem((2, 48, CO), BF16),
            vmem((2, 384, 128), BF16),
            vmem((2, 96, CO), BF16),
            vmem((2, 96, CO), BF16),
            vmem((2, 384, 128), BF16),
            vmem((2, 96, CO), BF16),
            vmem((2, 96, CO), BF16),
            vmem((3, 4, 96, 128), F32),
            vmem((3, 4, 96, 128), BF16),
            vmem((3, 4, 96, 128), BF16),
            vmem((3, 4, 24, 128), F32),
            vmem((3, 4, 24, 128), F32),
            vmem((3, 4, 24, 128), F32),
            vmem((3, 4, 96, 128), BF16),
            vmem((3, 4, 96, 128), BF16),
            dma((TAPS,)),
            dma((2,)),
            dma((2,)),
            dma((6,)),
            dma((6,)),
            dma((2,)),
            dma((2,)),
            dma((6,)),
            dma((6,)),
        ]
        + [dma((4,))] * 4
        + [
            dma((3,)),
            dma((3,)),
            dma((3, 4)),
            dma((3, 4)),
            dma((4, 3)),
            dma((4, 3)),
            dma((3,)),
            dma((3,)),
            dma((H, B)),
        ],
        compiler_params=pltpu.CompilerParams(
            collective_id=0, has_side_effects=True, vmem_limit_bytes=60 * 1024 * 1024
        ),
        cost_estimate=pl.CostEstimate(
            flops=15_000_000_000, bytes_accessed=8_000_000, transcendentals=300_000
        ),
    )(
        features,
        conv_weight.reshape(TAPS * CI, CO),
        bn_gain.reshape(1, CO),
        bn_bias.reshape(1, CO),
        jnp.transpose(head_weight),
        labels,
        raster,
    )
    grad_weight, grad_gain, grad_bias, grad_head, grad_input = move_out(outs)
    return (
        grad_weight.reshape(3, 3, CI, 128),
        grad_gain.reshape(128),
        grad_bias.reshape(128),
        jnp.transpose(grad_head),
        grad_input,
    )


def solution(mesh):
    in_specs = (
        P(None, "rows", "cols", None),
        P(),
        P(),
        P(),
        P(),
        P(None, "rows", "cols"),
        P(None, "rows", "cols"),
    )
    out_specs = (
        P(None, None, None, "cols"),
        P("cols"),
        P("cols"),
        P("cols", None),
        P(None, "rows", "cols", None),
    )
    return jax.shard_map(
        per_device, mesh=mesh, in_specs=in_specs, out_specs=out_specs, check_vma=False
    )
```

```python
import jax
import jax.numpy as jnp
from jax import lax
from jax.experimental import pallas as pl
from jax.experimental.pallas import tpu as pltpu
from jax.sharding import PartitionSpec as P

F32 = jnp.float32
BF16 = jnp.bfloat16
MESH = pl.DeviceIdType.MESH

B = 4
H = 4
W = 128
CI = 256
CO = 512
TAPS = 9
PIX = H * W
COUNT = 4.0 * 128.0 * 512.0
EPS = 1e-05


def kernel(
    feat,
    wgt_hbm,
    gain_ref,
    bias_ref,
    head_ref,
    labels_ref,
    raster_ref,
    gw_out,
    gg_out,
    gb_out,
    gh_out,
    gi_out,
    wgt,
    wgt_t,
    x3,
    xt,
    conv,
    pgs,
    act,
    sgs,
    onehot,
    pixw,
    head_pad,
    head_tile,
    head_t,
    gl,
    gc,
    gr,
    xrow,
    xedge_out,
    xedge_in,
    grow,
    gedge_f,
    gedge_out,
    gedge_in,
    st_local,
    st8,
    st16,
    tot8,
    tot16,
    hd2,
    hdz_send,
    hdz,
    hdy,
    hdx,
    part,
    with_conv,
    with_one,
    send_a,
    recv_a,
    ring1z_send,
    ring1x_send,
    ring1y_send,
    ring1z_recv,
    ring1x_recv,
    ring1y_recv,
    ring2z_send,
    ring2x_send,
    ring2y_send,
    ring2z_recv,
    ring2x_recv,
    ring2y_recv,
    two_own,
    two_send,
    two_recv,
    three_send,
    three_recv,
    gat3,
    gat2,
    gat_other,
    wsem,
    xrow_s,
    xrow_r,
    xedge_s,
    xedge_r,
    grow_s,
    grow_r,
    gedge_s,
    gedge_r,
    st_s,
    st_r,
    hd_s,
    hd_r,
    a_s,
    a_r,
    ring_s,
    ring_r,
    dir_s,
    dir_r,
    o_s,
    o_r,
    gi_sem,
):
    me = lax.axis_index("rows")
    z = lax.axis_index("cols")
    core = lax.rem(me, 2)
    chip = me // 2
    x = chip // 4
    y = lax.rem(chip, 4)
    rank8 = z * 2 + core
    coords = {"x": x, "y": y, "z": z}

    def flip(value, bits):
        return lax.bitwise_xor(value, jnp.int32(bits)) if bits else value

    def dev8(k):
        return (flip(me, k % 2), flip(z, k // 2))

    def dev16(k):
        return (flip(me, 2 * k), z)

    def on_axis(axis, k):
        return (me, flip(z, k)) if axis == "z" else (flip(me, (2 if axis == "y" else 8) * k), z)

    other = (flip(me, 1), z)
    up = lax.rem(me + 31, 32)
    down = lax.rem(me + 1, 32)
    west = lax.rem(z + 3, 4)
    east = lax.rem(z + 1, 4)
    beyond = lax.rem(me + 31 + 2 * core, 32)

    barrier = pltpu.get_barrier_semaphore()

    def greet(device):
        pl.semaphore_signal(barrier, inc=1, device_id=device, device_id_type=MESH)

    for k in range(1, 8):
        greet(dev8(k))
    for col in (west, z, east):
        greet((beyond, col))
    for k in range(1, 16):
        greet(dev16(k))

    wcopies = []
    for t in range(TAPS):
        rows = pl.ds(t * CI, CI)
        wcopies.append(pltpu.make_async_copy(wgt_hbm.at[rows], wgt.at[rows], wsem.at[t]))
    for copy in wcopies:
        copy.start()

    row_id = lax.broadcasted_iota(jnp.int32, (16, CI), 0)
    left_edge = jnp.zeros((16, CI), F32)
    right_edge = jnp.zeros((16, CI), F32)
    for b in range(B):
        for h in range(H):
            low = feat[b, h, 0:16, :].astype(F32)[0:1, :]
            top = feat[b, h, W - 16 : W, :].astype(F32)[15:16, :]
            here = row_id == h * B + b
            left_edge = jnp.where(here, low, left_edge)
            right_edge = jnp.where(here, top, right_edge)
    xedge_out[0] = right_edge.astype(BF16)
    xedge_out[1] = left_edge.astype(BF16)

    pl.semaphore_wait(barrier, 25)

    def remote(src, dst, ssem, rsem, device):
        return pltpu.make_async_remote_copy(
            src_ref=src,
            dst_ref=dst,
            send_sem=ssem,
            recv_sem=rsem,
            device_id=device,
            device_id_type=MESH,
        )

    def row_sends(first, last, land, ssem, rsem):
        return [
            remote(last, land.at[0], ssem.at[0], rsem.at[0], (down, z)),
            remote(first, land.at[1], ssem.at[1], rsem.at[1], (up, z)),
        ]

    def edge_sends(out, land, ssem, rsem):
        copies = []
        for side, col in ((0, east), (1, west)):
            for slot, row in ((0, down), (1, me), (2, up)):
                index = side * 3 + slot
                copies.append(
                    remote(
                        out.at[side], land.at[index], ssem.at[index], rsem.at[index], (row, col)
                    )
                )
        return copies

    xrow_copies = row_sends(feat.at[:, 0], feat.at[:, H - 1], xrow, xrow_s, xrow_r)
    for copy in xrow_copies:
        copy.start()
    xedge_copies = edge_sends(xedge_out, xedge_in, xedge_s, xedge_r)
    for copy in xedge_copies:
        copy.start()

    head_pad[...] = jnp.zeros((128, CO), F32)
    head_pad[0:4] = head_ref[...].astype(F32)
    head_t[...] = head_pad[...].astype(BF16)
    head_pad[4:8] = head_ref[...].astype(F32)
    head_tile[...] = jnp.transpose(jnp.concatenate([head_pad[0:8]] * 16, axis=0)).astype(BF16)

    lane_class = lax.rem(lax.broadcasted_iota(jnp.int32, (W, 128), 1), 4).astype(F32)

    def class_marks(i, carry):
        b = i // H
        h = lax.rem(i, H)
        spot = pl.ds(pl.multiple_of(b * W, W), W)
        label = labels_ref[b, pl.ds(h, 1), :].astype(F32)
        weight = raster_ref[b, pl.ds(h, 1), :].astype(F32)
        label_t = jnp.transpose(jnp.broadcast_to(label, (128, W)))
        weight_t = jnp.transpose(jnp.broadcast_to(weight, (128, W)))
        onehot[h, spot] = jnp.where(label_t == lane_class, 1.0, 0.0).astype(BF16)
        pixw[h, spot] = ((1.0 + weight_t) * 0.25).astype(BF16)
        return carry

    lax.fori_loop(0, B * H, class_marks, 0)

    west_ok = jnp.where(z > 0, 1.0, 0.0).astype(F32)
    east_ok = jnp.where(z < 3, 1.0, 0.0).astype(F32)
    up_ok = jnp.where(me > 0, 1.0, 0.0).astype(F32)
    down_ok = jnp.where(me < 31, 1.0, 0.0).astype(F32)

    def pick_row(ref, slot, index):
        block = ref[slot].astype(F32)
        ids = lax.broadcasted_iota(jnp.int32, block.shape, 0)
        return jnp.sum(jnp.where(ids == index, block, 0.0), axis=0, keepdims=True)

    def shifted(value, before, after):
        ids = lax.broadcasted_iota(jnp.int32, value.shape, 0)
        left = jnp.where(ids == 0, before, pltpu.roll(value, 1, 0))
        right = jnp.where(ids == W - 1, after, pltpu.roll(value, W - 1, 0))
        return left.astype(BF16), right.astype(BF16)

    def clear(h, carry):
        conv[h] = jnp.zeros((PIX, CO), F32)
        return carry

    lax.fori_loop(0, H, clear, 0)
    for copy in xedge_copies:
        copy.wait_recv()

    def build_x(i, carry):
        h = i // B
        b = lax.rem(i, B)
        value = feat[b, h].astype(F32)
        left, right = shifted(
            value,
            pick_row(xedge_in, 1, i) * west_ok,
            pick_row(xedge_in, 4, i) * east_ok,
        )
        x3[0, h + 1, b] = left
        x3[1, h + 1, b] = feat[b, h]
        x3[2, h + 1, b] = right
        return carry

    lax.fori_loop(0, B * H, build_x, 0)

    def build_halo(land, edge_in, store):
        def body(b, carry):
            for side, line, ok, src in ((0, 0, up_ok, H - 1), (1, H + 1, down_ok, 0)):
                value = land[side, b].astype(F32) * ok
                slot = 2 * side
                left, right = shifted(
                    value,
                    pick_row(edge_in, slot, src * B + b) * (west_ok * ok),
                    pick_row(edge_in, slot + 3, src * B + b) * (east_ok * ok),
                )
                store(line, b, left, value.astype(BF16), right)
            return carry

        lax.fori_loop(0, B, body, 0)

    for copy in wcopies:
        copy.wait()

    def store_x(line, b, left, value, right):
        x3[0, line, b] = left
        x3[1, line, b] = value
        x3[2, line, b] = right

    def transpose_x(c, line):
        rows = pl.ds(pl.multiple_of(c * CI, CI), CI)
        xt[line, rows, :] = jnp.transpose(x3[c, line].reshape(PIX, CI))

    def transpose_w(t):
        wgt_t[pl.ds(pl.multiple_of(t * CO, CO), CO), :] = jnp.transpose(
            wgt[pl.ds(pl.multiple_of((TAPS - 1 - t) * CI, CI), CI), :]
        )

    def forward(k, carry):
        q = k // 4
        flipped = lax.rem(q, 2)
        h = 3 * flipped + (1 - 2 * flipped) * lax.rem(k, 4)
        r = lax.rem(2 * q + 1, 3)

        @pl.when(k == 7)
        def _():
            for copy in xrow_copies:
                copy.wait_recv()
            build_halo(xrow, xedge_in, store_x)

        lhs = jnp.concatenate([x3[c, h + r].reshape(PIX, CI) for c in range(3)], axis=1)
        rows = pl.ds(pl.multiple_of(r * 3 * CI, 3 * CI), 3 * CI)
        conv[h] += jnp.dot(lhs, wgt[rows, :], preferred_element_type=F32)
        transpose_x(lax.rem(k, 3), 1 + k // 3)
        transpose_w(lax.rem(k, TAPS))
        return carry

    lax.fori_loop(0, 12, forward, 0)

    def statistics(h, carry):
        value = conv[h]
        mid = jnp.sum(value, axis=0, keepdims=True) * (1.0 / PIX)
        st_local[h, 0:1] = mid
        st_local[h, 1:2] = jnp.sum((value - mid) ** 2, axis=0, keepdims=True)
        return carry

    lax.fori_loop(0, H, statistics, 0)

    def combine(parts, count):
        total = parts[0][0:1]
        for item in parts[1:]:
            total = total + item[0:1]
        mid = total * (1.0 / len(parts))
        spread_sum = None
        for item in parts:
            term = item[1:2] + count * (item[0:1] - mid) ** 2
            spread_sum = term if spread_sum is None else spread_sum + term
        return mid, spread_sum

    def exchange(size, devices, src_of, land, rank, ssem, rsem):
        def all_of(sem):
            few = land.at[0 : size - 1]
            return pltpu.make_async_copy(few, few, sem)

        def start():
            for k in range(1, size):
                remote(src_of(flip(rank, k)), land.at[rank], ssem, rsem, devices(k)).start()

        return start, lambda: all_of(rsem).wait(), lambda: all_of(ssem).wait()

    def share(size, devices, land, rank, ssem, rsem):
        return exchange(size, devices, lambda j: land.at[rank], land, rank, ssem, rsem)

    def along(axis, src_of, land, ssem, rsem):
        return exchange(
            4, lambda k: on_axis(axis, k), src_of, land, coords[axis], ssem, rsem
        )

    def share_along(axis, land, ssem, rsem):
        return along(axis, lambda j: land.at[coords[axis]], land, ssem, rsem)

    st8_x = share(8, dev8, st8, rank8, st_s.at[0], st_r.at[0])
    st16_x = share(16, dev16, st16, chip, st_s.at[1], st_r.at[1])
    tot8_x = share(8, dev8, tot8, rank8, st_s.at[2], st_r.at[2])
    tot16_x = share(16, dev16, tot16, chip, st_s.at[3], st_r.at[3])
    hd2_copy = remote(hd2.at[core], hd2.at[core], hd_s.at[0], hd_r.at[0], other)
    hdz_x = along("z", lambda j: hdz_send.at[j], hdz, hd_s.at[1], hd_r.at[1])
    hdy_x = share_along("y", hdy, hd_s.at[2], hd_r.at[2])
    hdx_x = share_along("x", hdx, hd_s.at[3], hd_r.at[3])

    mid, m2 = combine([st_local[h] for h in range(H)], float(PIX))
    st8[rank8, 0:1] = mid
    st8[rank8, 1:2] = m2
    st8_x[0]()

    local_mean = mid

    def transpose_outer(i, carry):
        transpose_x(lax.rem(i, 3), (H + 1) * (i // 3))
        return carry

    lax.fori_loop(0, 6, transpose_outer, 0)

    def center(h, carry):
        act[h] = (conv[h] - local_mean).astype(BF16)
        return carry

    lax.fori_loop(0, H, center, 0)

    def features_of(r):
        return jnp.concatenate([xt[h + r] for h in range(H)], axis=1)

    def half_cols(i):
        return pl.ds(pl.multiple_of(lax.rem(i, 2) * 256, 256), 256)

    def with_ones(r, carry):
        with_one[r] = jnp.dot(
            features_of(r), jnp.ones((B * PIX, 128), BF16), preferred_element_type=F32
        )
        return carry

    def cross_conv(i, carry):
        @pl.when(i == 2)
        def _():
            st8_x[1]()
            first, second_moment = combine([st8[j] for j in range(8)], float(B * PIX))
            st16[chip, 0:1] = first
            st16[chip, 1:2] = second_moment
            st16_x[0]()

        with_conv[i // 2, :, half_cols(i)] = jnp.dot(
            features_of(i // 2),
            act[:, :, half_cols(i)].reshape(B * PIX, 256),
            preferred_element_type=F32,
        )
        return carry

    lax.fori_loop(0, 6, cross_conv, 0)
    lax.fori_loop(0, 3, with_ones, 0)

    st16_x[1]()
    mean, m2 = combine([st16[j] for j in range(16)], float(8 * B * PIX))
    rstd = lax.rsqrt(m2 * (1.0 / COUNT) + EPS)
    gain = gain_ref[...]
    bias = bias_ref[...]
    scale = gain * rstd

    def middle(b, carry):
        sum_g, sum_gn = carry
        away = conv[b] - mean
        pre = away * scale + bias
        acted = jnp.maximum(pre, 0.0).astype(BF16)
        act[b] = acted
        logits = jnp.dot(acted, head_tile[...], preferred_element_type=F32)
        expo = jnp.exp(logits)
        total = expo + pltpu.roll(expo, 1, 1)
        total = total + pltpu.roll(total, 2, 1)
        score = (pixw[b].astype(F32) * (expo / total - onehot[b].astype(F32))).astype(BF16)
        sgs[b] = score
        act_grad = jnp.dot(score, head_t[...], preferred_element_type=F32)
        pre_grad = jnp.where(pre > 0.0, act_grad, 0.0)
        pgs[b] = pre_grad
        gc[b + 1] = pre_grad.astype(BF16).reshape(B, W, CO)
        sum_g = sum_g + jnp.sum(pre_grad, axis=0, keepdims=True)
        sum_gn = sum_gn + jnp.sum(pre_grad * away, axis=0, keepdims=True)
        return sum_g, sum_gn

    zero_row = jnp.zeros((1, CO), F32)
    sum_g, sum_gn = lax.fori_loop(0, B, middle, (zero_row, zero_row))

    def add_up(buf, size):
        total = buf[0]
        for j in range(1, size):
            total = total + buf[j]
        return total

    tot8[rank8, 0:1] = sum_g
    tot8[rank8, 1:2] = sum_gn * rstd
    tot8_x[0]()

    def cross_grad(i, carry):
        @pl.when(i == 2)
        def _():
            tot8_x[1]()
            tot16[chip] = add_up(tot8, 8)
            tot16_x[0]()

        part[i // 2, :, :, half_cols(i)] = jnp.dot(
            features_of(i // 2),
            gc[1 : H + 1, :, :, half_cols(i)].reshape(B * PIX, 256),
            preferred_element_type=F32,
        ).reshape(3, CI, 256)
        return carry

    def head_part(b, total):
        return total + lax.dot_general(
            sgs[b], act[b], (((0,), (0,)), ((), ())), preferred_element_type=F32
        )

    lax.fori_loop(0, 6, cross_grad, 0)
    head_sum = lax.fori_loop(0, B, head_part, jnp.zeros((128, CO), F32))
    hd2[core] = head_sum[0:4, :]
    hd2_copy.start()
    st8_x[2]()
    st16_x[2]()
    for copy in xrow_copies + xedge_copies:
        copy.wait_send()
    tot16_x[1]()
    totals = add_up(tot16, 16)
    off = totals[0:1] * (1.0 / COUNT)
    slope = rstd * totals[1:2] * (1.0 / COUNT)
    st_local[0] = totals
    gb_out[...] = st_local[0, 0:1, pl.ds(pl.multiple_of(z * 128, 128), 128)]
    gg_out[...] = st_local[0, 1:2, pl.ds(pl.multiple_of(z * 128, 128), 128)]

    ORDERS = (("z", "y", "x"), ("x", "z", "y"), ("y", "z", "x"))

    def a_copy(r):
        return remote(send_a.at[r], recv_a.at[r], a_s.at[r], a_r.at[r], other)


    shift = scale * (off + slope * (local_mean - mean))
    turn = scale * slope

    def kernel_grad(r, half):
        pieces = []
        for c in range(3):
            rows = pl.ds(pl.multiple_of(c * CI + half * 128, 128), 128)
            ones = jnp.concatenate([with_one[r, rows, :]] * 4, axis=1)
            pieces.append(
                part[r, c, pl.ds(pl.multiple_of(half * 128, 128), 128), :] * scale
                - with_conv[r, rows, :] * turn
                - ones * shift
            )
        return pieces

    def for_other(r, carry):
        for c, piece in enumerate(kernel_grad(r, 1 - core)):
            send_a[r, c] = piece.astype(BF16)
        a_copy(r).start()
        return carry

    lax.fori_loop(0, 3, for_other, 0)

    def for_own(r, carry):
        pieces = kernel_grad(r, core)
        a_copy(r).wait_recv()
        for c, piece in enumerate(pieces):
            with_conv[r, c * 128 : (c + 1) * 128] = piece + recv_a[r, c].astype(F32)
        return carry

    def store_g(line, b, left, value, right):
        gl[line, b] = left
        gc[line, b] = value
        gr[line, b] = right

    def conv_grad(i, carry):
        b = lax.rem(i, B)
        h = lax.rem(3 * (i // B), H)
        spot = pl.ds(pl.multiple_of(b * W, W), W)
        away = conv[h, spot] - mean
        value = scale * (pgs[h, spot] - off - away * slope)
        gc[h + 1, b] = value.astype(BF16)
        gl[h + 1, b], gr[h + 1, b] = shifted(value, 0.0, 0.0)
        gedge_f[0, pl.ds(h * B + b, 1)] = value[W - 1 : W, :]
        gedge_f[1, pl.ds(h * B + b, 1)] = value[0:1, :]
        return carry

    ring1_send, ring1_recv = (ring1z_send, ring1x_send, ring1y_send), (
        ring1z_recv,
        ring1x_recv,
        ring1y_recv,
    )
    ring2_send, ring2_recv = (ring2z_send, ring2x_send, ring2y_send), (
        ring2z_recv,
        ring2x_recv,
        ring2y_recv,
    )

    def halves(r):
        return 192 if r == 0 else 48

    def block(r, q, low, high):
        q = lax.rem(q, 4)
        if r == 0:
            return with_conv[r, low:high, pl.ds(pl.multiple_of(q * 128, 128), 128)]
        return with_conv[r, pl.ds(pl.multiple_of(q * 96 + low, 16), high - low), :]

    def around(axis, way):
        step = 1 if way == 0 else 3
        if axis == "z":
            return (me, lax.rem(z + step, 4))
        stride = 2 if axis == "y" else 8
        here = coords[axis]
        return (me + stride * (lax.rem(here + step, 4) - here), z)

    def ring1_copies(r):
        axis = ORDERS[r][0]
        return [
            remote(
                ring1_send[r].at[way],
                ring1_recv[r].at[way],
                ring_s.at[r, way],
                ring_r.at[r, way],
                around(axis, way),
            )
            for way in range(2)
        ]

    def ring2_copies(r):
        axis = ORDERS[r][0]
        return [
            remote(
                ring2_send[r].at[way],
                ring2_recv[r].at[way],
                ring_s.at[r, 2 + way],
                ring_r.at[r, 2 + way],
                around(axis, way),
            )
            for way in range(2)
        ]

    def ring1(r):
        here, half = coords[ORDERS[r][0]], halves(r)
        ring1_send[r][0] = block(r, here + 2, 0, half).astype(BF16)
        ring1_send[r][1] = block(r, here + 2, half, 2 * half).astype(BF16)
        for copy in ring1_copies(r):
            copy.start()

    def ring2(r):
        for copy in ring1_copies(r):
            copy.wait_recv()
        here, half = coords[ORDERS[r][0]], halves(r)
        low = ring1_recv[r][0].astype(F32)
        high = ring1_recv[r][1].astype(F32)
        ring2_send[r][0, 0:half] = (block(r, here + 1, 0, half) + low).astype(BF16)
        ring2_send[r][0, half : 2 * half] = block(r, here + 1, half, 2 * half).astype(BF16)
        ring2_send[r][1, 0:half] = block(r, here + 3, 0, half).astype(BF16)
        ring2_send[r][1, half : 2 * half] = (
            block(r, here + 3, half, 2 * half) + high
        ).astype(BF16)
        for copy in ring2_copies(r):
            copy.start()

    row_axis = ("y", "x", "y")
    second, third, gather3, gather2 = [], [], [], []
    for r in range(3):
        second.append(
            along(
                ORDERS[r][1],
                lambda j, r=r: two_send.at[r, j],
                two_recv.at[r],
                dir_s.at[0, r],
                dir_r.at[0, r],
            )
        )
        third.append(
            along(
                ORDERS[r][2],
                lambda j, r=r: three_send.at[r, j],
                three_recv.at[r],
                dir_s.at[1, r],
                dir_r.at[1, r],
            )
        )
        gather3.append(share_along(ORDERS[r][2], gat3.at[r], dir_s.at[2, r], dir_r.at[2, r]))
        gather2.append(share_along(row_axis[r], gat2.at[r], dir_s.at[3, r], dir_r.at[3, r]))

    def stage2(r):
        for copy in ring2_copies(r):
            copy.wait_recv()
        here, half = coords[ORDERS[r][0]], halves(r)
        total = (
            block(r, here, 0, 2 * half)
            + ring2_recv[r][0].astype(F32)
            + ring2_recv[r][1].astype(F32)
        )
        for q in range(4):
            piece = (
                total[q * 96 : (q + 1) * 96] if r == 0 else total[:, q * 128 : (q + 1) * 128]
            )
            two_own[r, q] = piece
            two_send[r, q] = piece.astype(BF16)
        second[r][0]()

    def stage3(r):
        second[r][1]()
        here = coords[ORDERS[r][1]]
        total = two_own[r, here]
        for k in range(1, 4):
            total = total + two_recv[r, flip(here, k)].astype(F32)
        for q in range(4):
            three_send[r, q] = total[q * 24 : (q + 1) * 24]
        third[r][0]()

    def collect3(r):
        third[r][1]()
        here = coords[ORDERS[r][2]]
        total = three_send[r, here]
        for k in range(1, 4):
            total = total + three_recv[r, flip(here, k)]
        gat3[r, here] = total
        gather3[r][0]()

    def collect2(r):
        gather3[r][1]()
        here = coords[row_axis[r]]
        gat2[r, here] = jnp.concatenate([gat3[r, q] for q in range(4)], axis=0).astype(BF16)
        gather2[r][0]()

    o_copies = [remote(gat2.at[r], gat_other.at[r], o_s.at[r], o_r.at[r], other) for r in range(3)]

    def swap(r):
        gather2[r][1]()
        o_copies[r].start()
        unpack(r, gat2, core)

    def unpack(r, src, half):
        rows = src[r].reshape(384, 128)
        spot = pl.ds(pl.multiple_of(half * 128, 128), 128)
        for c in range(3):
            gw_out[3 * r + c, spot, :] = rows[c * 128 : (c + 1) * 128].astype(F32)

    def unpack_other(r):
        o_copies[r].wait_recv()
        unpack(r, gat_other, 1 - core)

    def gi_copies(h):
        return [
            pltpu.make_async_copy(
                pgs.at[h, pl.ds(b * W, W), pl.ds(0, CI)], gi_out.at[b, h], gi_sem.at[h, b]
            )
            for b in range(B)
        ]

    def back(h):
        def kernel_row(r, total):
            lhs = jnp.concatenate(
                [ref[h + r].reshape(PIX, CO) for ref in (gl, gc, gr)], axis=1
            )
            rows = pl.ds(pl.multiple_of(r * 3 * CO, 3 * CO), 3 * CO)
            pgs[h, :, 0:CI] += jnp.dot(lhs, wgt_t[rows, :], preferred_element_type=F32)
            return total

        pgs[h, :, 0:CI] = jnp.zeros((PIX, CI), F32)
        lax.fori_loop(0, 3, kernel_row, 0)
        for copy in gi_copies(h):
            copy.start()

    def set_edges(i, carry):
        h = i // B
        b = lax.rem(i, B)
        ids = lax.broadcasted_iota(jnp.int32, (16, CO), 0)
        low = pick_row(gedge_in, 1, i) * west_ok
        top = pick_row(gedge_in, 4, i) * east_ok
        block16 = gl[h + 1, b, 0:16].astype(F32)
        gl[h + 1, b, 0:16] = jnp.where(ids == 0, low, block16).astype(BF16)
        block16 = gr[h + 1, b, W - 16 : W].astype(F32)
        gr[h + 1, b, W - 16 : W] = jnp.where(ids == 15, top, block16).astype(BF16)
        return carry

    lax.fori_loop(0, 2 * B, conv_grad, 0)
    grow_copies = row_sends(gc.at[1], gc.at[H], grow, grow_s, grow_r)
    for copy in grow_copies:
        copy.start()
    lax.fori_loop(0, 3, for_own, 0)
    ring1(0)
    ring1(1)
    ring1(2)
    lax.fori_loop(2 * B, 4 * B, conv_grad, 0)
    gedge_out[...] = gedge_f[...].astype(BF16)
    gedge_copies = edge_sends(gedge_out, gedge_in, gedge_s, gedge_r)
    for copy in gedge_copies:
        copy.start()
    hd2_copy.wait_recv()
    head_pair = hd2[0] + hd2[1]
    for q in range(4):
        hdz_send[q] = head_pair[:, q * 128 : (q + 1) * 128]
    hdz_x[0]()
    ring2(0)
    ring2(1)
    ring2(2)
    for copy in gedge_copies:
        copy.wait_recv()
    lax.fori_loop(0, B * H, set_edges, 0)
    hdz_x[1]()
    head_line = hdz_send[z]
    for k in range(1, 4):
        head_line = head_line + hdz[flip(z, k)]
    hdy[y] = head_line
    hdy_x[0]()

    def back_rows(i, carry):
        @pl.when(i == 1)
        def _():
            stage2(0)
            stage2(1)
            stage2(2)
            hdy_x[1]()
            hdx[x] = add_up(hdy, 4)
            hdx_x[0]()

        @pl.when(i == 2)
        def _():
            stage3(0)
            stage3(1)
            stage3(2)
            for copy in grow_copies:
                copy.wait_recv()
            build_halo(grow, gedge_in, store_g)

        @pl.when(i == 3)
        def _():
            collect3(0)
            collect3(1)
            collect3(2)
            hdx_x[1]()
            gh_out[...] = add_up(hdx, 4)

        back(lax.rem(i + 1, 4))
        return carry

    lax.fori_loop(0, H, back_rows, 0)
    collect2(0)
    collect2(1)
    collect2(2)
    swap(0)
    swap(1)
    swap(2)
    unpack_other(0)
    unpack_other(1)

    for copy in [hd2_copy] + grow_copies + gedge_copies + [a_copy(r) for r in range(3)]:
        copy.wait_send()
    for exchanged in [tot8_x, tot16_x, hdz_x, hdy_x, hdx_x] + second + third + gather3 + gather2:
        exchanged[2]()
    for r in range(3):
        for copy in ring1_copies(r) + ring2_copies(r):
            copy.wait_send()
    for h in range(H):
        for copy in gi_copies(h):
            copy.wait()
    unpack_other(2)
    for copy in o_copies:
        copy.wait_send()


def move_kernel(*refs):
    count = (len(refs) - 2) // 3
    in_sem, out_sem = refs[-2:]
    arrivals, leaves = [], []
    for src, dst, held in zip(refs[:count], refs[count : 2 * count], refs[2 * count : 3 * count]):
        size = src.shape[0] if len(src.shape) > 2 else 1
        for i in range(size):
            here, there, hold = (src.at[i], dst.at[i], held.at[i]) if size > 1 else (src, dst, held)
            slot = len(arrivals)
            arrivals.append(pltpu.make_async_copy(here, hold, in_sem.at[slot]))
            leaves.append(pltpu.make_async_copy(hold, there, out_sem.at[slot]))
    for copy in arrivals:
        copy.start()
    for arrival, leave in zip(arrivals, leaves):
        arrival.wait()
        leave.start()
    for leave in leaves:
        leave.wait()


def move_out(arrays):
    anywhere = pl.BlockSpec(memory_space=pl.ANY)
    return pl.pallas_call(
        move_kernel,
        out_shape=tuple(jax.ShapeDtypeStruct(a.shape, a.dtype) for a in arrays),
        in_specs=[anywhere] * len(arrays),
        out_specs=(anywhere,) * len(arrays),
        scratch_shapes=[pltpu.VMEM(a.shape, a.dtype) for a in arrays]
        + [pltpu.SemaphoreType.DMA((16,)), pltpu.SemaphoreType.DMA((16,))],
        compiler_params=pltpu.CompilerParams(vmem_limit_bytes=60 * 1024 * 1024),
    )(*arrays)


def per_device(features, conv_weight, bn_gain, bn_bias, head_weight, labels, raster):
    dma = pltpu.SemaphoreType.DMA
    vmem = pltpu.VMEM
    whole = pl.BlockSpec(memory_space=pltpu.VMEM)
    outs = pl.pallas_call(
        kernel,
        out_shape=(
            jax.ShapeDtypeStruct((TAPS, CI, 128), F32),
            jax.ShapeDtypeStruct((1, 128), F32),
            jax.ShapeDtypeStruct((1, 128), F32),
            jax.ShapeDtypeStruct((4, 128), F32),
            jax.ShapeDtypeStruct((B, H, W, CI), F32),
        ),
        in_specs=[whole, pl.BlockSpec(memory_space=pl.ANY)] + [whole] * 5,
        out_specs=(whole,) * 4 + (pl.BlockSpec(memory_space=pl.ANY),),
        scratch_shapes=[
            vmem((TAPS * CI, CO), BF16),
            vmem((TAPS * CO, CI), BF16),
            vmem((3, H + 2, B, W, CI), BF16),
            vmem((H + 2, 3 * CI, PIX), BF16),
            vmem((H, PIX, CO), F32),
            vmem((H, PIX, CO), F32),
            vmem((H, PIX, CO), BF16),
            vmem((H, PIX, 128), BF16),
            vmem((H, PIX, 128), BF16),
            vmem((H, PIX, 128), BF16),
            vmem((128, CO), F32),
            vmem((CO, 128), BF16),
            vmem((128, CO), BF16),
            vmem((H + 2, B, W, CO), BF16),
            vmem((H + 2, B, W, CO), BF16),
            vmem((H + 2, B, W, CO), BF16),
            vmem((2, B, W, CI), BF16),
            vmem((2, 16, CI), BF16),
            vmem((6, 16, CI), BF16),
            vmem((2, B, W, CO), BF16),
            vmem((2, 16, CO), F32),
            vmem((2, 16, CO), BF16),
            vmem((6, 16, CO), BF16),
            vmem((B, 2, CO), F32),
            vmem((8, 2, CO), F32),
            vmem((16, 2, CO), F32),
            vmem((8, 2, CO), F32),
            vmem((16, 2, CO), F32),
            vmem((2, 4, CO), F32),
            vmem((4, 4, 128), F32),
            vmem((4, 4, 128), F32),
            vmem((4, 4, 128), F32),
            vmem((4, 4, 128), F32),
            vmem((3, 3, CI, CO), F32),
            vmem((3, 3 * CI, CO), F32),
            vmem((3, 3 * CI, 128), F32),
            vmem((3, 3, 128, CO), BF16),
            vmem((3, 3, 128, CO), BF16),
            vmem((2, 192, 128), BF16),
            vmem((2, 48, CO), BF16),
            vmem((2, 48, CO), BF16),
            vmem((2, 192, 128), BF16),
            vmem((2, 48, CO), BF16),
            vmem((2, 48, CO), BF16),
            vmem((2, 384, 128), BF16),
            vmem((2, 96, CO), BF16),
            vmem((2, 96, CO), BF16),
            vmem((2, 384, 128), BF16),
            vmem((2, 96, CO), BF16),
            vmem((2, 96, CO), BF16),
            vmem((3, 4, 96, 128), F32),
            vmem((3, 4, 96, 128), BF16),
            vmem((3, 4, 96, 128), BF16),
            vmem((3, 4, 24, 128), F32),
            vmem((3, 4, 24, 128), F32),
            vmem((3, 4, 24, 128), F32),
            vmem((3, 4, 96, 128), BF16),
            vmem((3, 4, 96, 128), BF16),
            dma((TAPS,)),
            dma((2,)),
            dma((2,)),
            dma((6,)),
            dma((6,)),
            dma((2,)),
            dma((2,)),
            dma((6,)),
            dma((6,)),
        ]
        + [dma((4,))] * 4
        + [
            dma((3,)),
            dma((3,)),
            dma((3, 4)),
            dma((3, 4)),
            dma((4, 3)),
            dma((4, 3)),
            dma((3,)),
            dma((3,)),
            dma((H, B)),
        ],
        compiler_params=pltpu.CompilerParams(
            collective_id=0, has_side_effects=True, vmem_limit_bytes=60 * 1024 * 1024
        ),
        cost_estimate=pl.CostEstimate(
            flops=15_000_000_000, bytes_accessed=8_000_000, transcendentals=300_000
        ),
    )(
        features,
        conv_weight.reshape(TAPS * CI, CO),
        bn_gain.reshape(1, CO),
        bn_bias.reshape(1, CO),
        jnp.transpose(head_weight),
        labels,
        raster,
    )
    grad_weight, grad_gain, grad_bias, grad_head, grad_input = move_out(outs)
    return (
        grad_weight.reshape(3, 3, CI, 128),
        grad_gain.reshape(128),
        grad_bias.reshape(128),
        jnp.transpose(grad_head),
        grad_input,
    )


def solution(mesh):
    in_specs = (
        P(None, "rows", "cols", None),
        P(),
        P(),
        P(),
        P(),
        P(None, "rows", "cols"),
        P(None, "rows", "cols"),
    )
    out_specs = (
        P(None, None, None, "cols"),
        P("cols"),
        P("cols"),
        P("cols", None),
        P(None, "rows", "cols", None),
    )
    return jax.shard_map(
        per_device, mesh=mesh, in_specs=in_specs, out_specs=out_specs, check_vma=False
    )
```

```python
import jax
import jax.numpy as jnp
from jax import lax
from jax.experimental import pallas as pl
from jax.experimental.pallas import tpu as pltpu
from jax.sharding import PartitionSpec as P

F32 = jnp.float32
BF16 = jnp.bfloat16
MESH = pl.DeviceIdType.MESH

B = 4
H = 4
W = 128
CI = 256
CO = 512
TAPS = 9
PIX = H * W
COUNT = 4.0 * 128.0 * 512.0
EPS = 1e-05


def kernel(
    feat,
    wgt_hbm,
    gain_ref,
    bias_ref,
    head_ref,
    labels_ref,
    raster_ref,
    gw_out,
    gg_out,
    gb_out,
    gh_out,
    gi_out,
    wgt,
    wgt_t,
    xl,
    xc,
    xr,
    xt,
    conv,
    pgs,
    act,
    sgs,
    onehot,
    pixw,
    head_pad,
    head_tile,
    head_t,
    gl,
    gc,
    gr,
    xrow,
    xedge_out,
    xedge_in,
    grow,
    gedge_f,
    gedge_out,
    gedge_in,
    st_local,
    st8,
    sty,
    stx,
    tot8,
    toty,
    totx,
    hd2,
    hdz_send,
    hdz,
    hdy,
    hdx,
    part,
    with_conv,
    with_one,
    send_a,
    recv_a,
    ring1z_send,
    ring1x_send,
    ring1y_send,
    ring1z_recv,
    ring1x_recv,
    ring1y_recv,
    ring2z_send,
    ring2x_send,
    ring2y_send,
    ring2z_recv,
    ring2x_recv,
    ring2y_recv,
    two_own,
    two_send,
    two_recv,
    three_send,
    three_recv,
    gat3,
    gat2,
    gat_other,
    wsem,
    xrow_s,
    xrow_r,
    xedge_s,
    xedge_r,
    grow_s,
    grow_r,
    gedge_s,
    gedge_r,
    st_s,
    st_r,
    hd_s,
    hd_r,
    a_s,
    a_r,
    ring_s,
    ring_r,
    dir_s,
    dir_r,
    o_s,
    o_r,
    gi_sem,
):
    me = lax.axis_index("rows")
    z = lax.axis_index("cols")
    core = lax.rem(me, 2)
    chip = me // 2
    x = chip // 4
    y = lax.rem(chip, 4)
    rank8 = z * 2 + core
    coords = {"x": x, "y": y, "z": z}

    def flip(value, bits):
        return lax.bitwise_xor(value, jnp.int32(bits)) if bits else value

    def dev8(k):
        return (flip(me, k % 2), flip(z, k // 2))

    def on_axis(axis, k):
        return (me, flip(z, k)) if axis == "z" else (flip(me, (2 if axis == "y" else 8) * k), z)

    other = (flip(me, 1), z)
    up = lax.rem(me + 31, 32)
    down = lax.rem(me + 1, 32)
    west = lax.rem(z + 3, 4)
    east = lax.rem(z + 1, 4)
    beyond = lax.rem(me + 31 + 2 * core, 32)

    barrier = pltpu.get_barrier_semaphore()

    def greet(device):
        pl.semaphore_signal(barrier, inc=1, device_id=device, device_id_type=MESH)

    for k in range(1, 8):
        greet(dev8(k))
    for col in (west, z, east):
        greet((beyond, col))
    for k in range(1, 4):
        greet(on_axis("y", k))
        greet(on_axis("x", k))

    wcopies = []
    for t in range(TAPS):
        rows = pl.ds(t * CI, CI)
        wcopies.append(pltpu.make_async_copy(wgt_hbm.at[rows], wgt.at[rows], wsem.at[t]))
    for copy in wcopies:
        copy.start()

    row_id = lax.broadcasted_iota(jnp.int32, (16, CI), 0)
    left_edge = jnp.zeros((16, CI), F32)
    right_edge = jnp.zeros((16, CI), F32)
    for b in range(B):
        for h in range(H):
            low = feat[b, h, 0:16, :].astype(F32)[0:1, :]
            top = feat[b, h, W - 16 : W, :].astype(F32)[15:16, :]
            here = row_id == h * B + b
            left_edge = jnp.where(here, low, left_edge)
            right_edge = jnp.where(here, top, right_edge)
    xedge_out[0] = right_edge.astype(BF16)
    xedge_out[1] = left_edge.astype(BF16)

    pl.semaphore_wait(barrier, 16)

    def remote(src, dst, ssem, rsem, device):
        return pltpu.make_async_remote_copy(
            src_ref=src,
            dst_ref=dst,
            send_sem=ssem,
            recv_sem=rsem,
            device_id=device,
            device_id_type=MESH,
        )

    def row_sends(first, last, land, ssem, rsem):
        return [
            remote(last, land.at[0], ssem.at[0], rsem.at[0], (down, z)),
            remote(first, land.at[1], ssem.at[1], rsem.at[1], (up, z)),
        ]

    def edge_sends(out, land, ssem, rsem):
        copies = []
        for side, col in ((0, east), (1, west)):
            for slot, row in ((0, down), (1, me), (2, up)):
                index = side * 3 + slot
                copies.append(
                    remote(
                        out.at[side], land.at[index], ssem.at[index], rsem.at[index], (row, col)
                    )
                )
        return copies

    xrow_copies = row_sends(feat.at[:, 0], feat.at[:, H - 1], xrow, xrow_s, xrow_r)
    for copy in xrow_copies:
        copy.start()
    xedge_copies = edge_sends(xedge_out, xedge_in, xedge_s, xedge_r)
    for copy in xedge_copies:
        copy.start()

    head_pad[...] = jnp.zeros((128, CO), F32)
    head_pad[0:4] = head_ref[...].astype(F32)
    head_t[...] = head_pad[...].astype(BF16)
    head_pad[4:8] = head_ref[...].astype(F32)
    head_tile[...] = jnp.transpose(jnp.concatenate([head_pad[0:8]] * 16, axis=0)).astype(BF16)

    lane_class = lax.rem(lax.broadcasted_iota(jnp.int32, (W, 128), 1), 4).astype(F32)
    for b in range(B):
        for h in range(H):
            label = labels_ref[b, h : h + 1, :].astype(F32)
            weight = raster_ref[b, h : h + 1, :].astype(F32)
            label_t = jnp.transpose(jnp.broadcast_to(label, (128, W)))
            weight_t = jnp.transpose(jnp.broadcast_to(weight, (128, W)))
            marks = jnp.where(label_t == lane_class, 1.0, 0.0)
            onehot[h, b * W : (b + 1) * W] = marks.astype(BF16)
            pixw[h, b * W : (b + 1) * W] = ((1.0 + weight_t) * 0.25).astype(BF16)

    west_ok = jnp.where(z > 0, 1.0, 0.0).astype(F32)
    east_ok = jnp.where(z < 3, 1.0, 0.0).astype(F32)
    up_ok = jnp.where(me > 0, 1.0, 0.0).astype(F32)
    down_ok = jnp.where(me < 31, 1.0, 0.0).astype(F32)

    def pick_row(ref, slot, index):
        block = ref[slot].astype(F32)
        ids = lax.broadcasted_iota(jnp.int32, block.shape, 0)
        return jnp.sum(jnp.where(ids == index, block, 0.0), axis=0, keepdims=True)

    def shifted(value, before, after):
        ids = lax.broadcasted_iota(jnp.int32, value.shape, 0)
        left = jnp.where(ids == 0, before, pltpu.roll(value, 1, 0))
        right = jnp.where(ids == W - 1, after, pltpu.roll(value, W - 1, 0))
        return left.astype(BF16), right.astype(BF16)

    for copy in xedge_copies:
        copy.wait_recv()

    def build_x(i, carry):
        h = i // B
        b = lax.rem(i, B)
        value = feat[b, h].astype(F32)
        left, right = shifted(
            value,
            pick_row(xedge_in, 1, i) * west_ok,
            pick_row(xedge_in, 4, i) * east_ok,
        )
        xl[h + 1, b] = left
        xc[h + 1, b] = feat[b, h]
        xr[h + 1, b] = right
        return carry

    lax.fori_loop(0, B * H, build_x, 0)

    def build_halo(land, edge_in, left_ref, mid_ref, right_ref):
        def body(b, carry):
            for side, line, ok, src in ((0, 0, up_ok, H - 1), (1, H + 1, down_ok, 0)):
                value = land[side, b].astype(F32) * ok
                slot = 2 * side
                left, right = shifted(
                    value,
                    pick_row(edge_in, slot, src * B + b) * (west_ok * ok),
                    pick_row(edge_in, slot + 3, src * B + b) * (east_ok * ok),
                )
                left_ref[line, b] = left
                mid_ref[line, b] = value.astype(BF16)
                right_ref[line, b] = right
            return carry

        lax.fori_loop(0, B, body, 0)

    for copy in wcopies:
        copy.wait()

    def conv_rows(h, first, count):
        lhs = jnp.concatenate(
            [
                ref[h + first + r].reshape(PIX, CI)
                for r in range(count)
                for ref in (xl, xc, xr)
            ],
            axis=1,
        )
        start = pl.multiple_of(first * 3 * CI, 3 * CI)
        return jnp.dot(lhs, wgt[pl.ds(start, count * 3 * CI), :], preferred_element_type=F32)

    def statistics(h, value):
        mid = jnp.sum(value, axis=0, keepdims=True) * (1.0 / PIX)
        st_local[h, 0:1] = mid
        st_local[h, 1:2] = jnp.sum((value - mid) ** 2, axis=0, keepdims=True)

    def transpose_x(line):
        for c, ref in enumerate((xl, xc, xr)):
            xt[line, c * CI : (c + 1) * CI, :] = jnp.transpose(ref[line].reshape(PIX, CI))

    def transpose_w(t):
        wgt_t[pl.ds(pl.multiple_of(t * CO, CO), CO), :] = jnp.transpose(
            wgt[pl.ds(pl.multiple_of((TAPS - 1 - t) * CI, CI), CI), :]
        )

    def inner_rows(i, carry):
        value = conv_rows(1 + i, 0, 3)
        conv[1 + i] = value
        transpose_x(1 + i)
        transpose_x(3 + i)
        statistics(1 + i, value)
        return carry

    lax.fori_loop(0, 2, inner_rows, 0)

    def outer_rows(i, carry):
        conv[3 * i] = conv_rows(3 * i, 1 - i, 2)
        for t in range(4):
            transpose_w(4 * i + t)
        return carry

    lax.fori_loop(0, 2, outer_rows, 0)

    for copy in xrow_copies:
        copy.wait_recv()
    build_halo(xrow, xedge_in, xl, xc, xr)

    def halo_rows(i, carry):
        value = conv[3 * i] + conv_rows(3 * i, 2 * i, 1)
        conv[3 * i] = value
        statistics(3 * i, value)
        return carry

    lax.fori_loop(0, 2, halo_rows, 0)

    def combine(parts, count):
        total = parts[0][0:1]
        for item in parts[1:]:
            total = total + item[0:1]
        mid = total * (1.0 / len(parts))
        spread_sum = None
        for item in parts:
            term = item[1:2] + count * (item[0:1] - mid) ** 2
            spread_sum = term if spread_sum is None else spread_sum + term
        return mid, spread_sum

    def exchange(size, devices, src_of, land, rank, ssem, rsem):
        def all_of(sem):
            few = land.at[0 : size - 1]
            return pltpu.make_async_copy(few, few, sem)

        def start():
            for k in range(1, size):
                remote(src_of(flip(rank, k)), land.at[rank], ssem, rsem, devices(k)).start()

        return start, lambda: all_of(rsem).wait(), lambda: all_of(ssem).wait()

    def share(size, devices, land, rank, ssem, rsem):
        return exchange(size, devices, lambda j: land.at[rank], land, rank, ssem, rsem)

    def along(axis, src_of, land, ssem, rsem):
        return exchange(
            4, lambda k: on_axis(axis, k), src_of, land, coords[axis], ssem, rsem
        )

    def share_along(axis, land, ssem, rsem):
        return along(axis, lambda j: land.at[coords[axis]], land, ssem, rsem)

    st8_x = share(8, dev8, st8, rank8, st_s.at[0], st_r.at[0])
    sty_x = share_along("y", sty, st_s.at[1], st_r.at[1])
    stx_x = share_along("x", stx, st_s.at[2], st_r.at[2])
    tot8_x = share(8, dev8, tot8, rank8, st_s.at[3], st_r.at[3])
    toty_x = share_along("y", toty, st_s.at[4], st_r.at[4])
    totx_x = share_along("x", totx, st_s.at[5], st_r.at[5])
    hd2_copy = remote(hd2.at[core], hd2.at[core], hd_s.at[0], hd_r.at[0], other)
    hdz_x = along("z", lambda j: hdz_send.at[j], hdz, hd_s.at[1], hd_r.at[1])
    hdy_x = share_along("y", hdy, hd_s.at[2], hd_r.at[2])
    hdx_x = share_along("x", hdx, hd_s.at[3], hd_r.at[3])

    mid, m2 = combine([st_local[h] for h in range(H)], float(PIX))
    st8[rank8, 0:1] = mid
    st8[rank8, 1:2] = m2
    st8_x[0]()

    local_mean = mid
    transpose_x(0)
    transpose_x(H + 1)

    def center(h, carry):
        act[h] = (conv[h] - local_mean).astype(BF16)
        return carry

    lax.fori_loop(0, H, center, 0)

    def features_of(r):
        return jnp.concatenate([xt[h + r] for h in range(H)], axis=1)

    def cross_conv(r, carry):
        lhs = features_of(r)
        with_conv[r] = jnp.dot(lhs, act[...].reshape(B * PIX, CO), preferred_element_type=F32)
        with_one[r] = jnp.dot(lhs, jnp.ones((B * PIX, 128), BF16), preferred_element_type=F32)
        return carry

    lax.fori_loop(0, 1, cross_conv, 0)
    st8_x[1]()
    mid, m2 = combine([st8[j] for j in range(8)], float(B * PIX))
    sty[y, 0:1] = mid
    sty[y, 1:2] = m2
    sty_x[0]()
    lax.fori_loop(1, 2, cross_conv, 0)
    sty_x[1]()
    mid, m2 = combine([sty[j] for j in range(4)], float(8 * B * PIX))
    stx[x, 0:1] = mid
    stx[x, 1:2] = m2
    stx_x[0]()
    lax.fori_loop(2, 3, cross_conv, 0)
    transpose_w(TAPS - 1)
    stx_x[1]()
    mean, m2 = combine([stx[j] for j in range(4)], float(32 * B * PIX))
    rstd = lax.rsqrt(m2 * (1.0 / COUNT) + EPS)
    gain = gain_ref[...]
    bias = bias_ref[...]
    scale = gain * rstd

    def middle(b, carry):
        sum_g, sum_gn = carry
        away = conv[b] - mean
        pre = away * scale + bias
        acted = jnp.maximum(pre, 0.0).astype(BF16)
        act[b] = acted
        logits = jnp.dot(acted, head_tile[...], preferred_element_type=F32)
        expo = jnp.exp(logits)
        total = expo + pltpu.roll(expo, 1, 1)
        total = total + pltpu.roll(total, 2, 1)
        score = (pixw[b].astype(F32) * (expo / total - onehot[b].astype(F32))).astype(BF16)
        sgs[b] = score
        act_grad = jnp.dot(score, head_t[...], preferred_element_type=F32)
        pre_grad = jnp.where(pre > 0.0, act_grad, 0.0)
        pgs[b] = pre_grad
        gc[b + 1] = pre_grad.astype(BF16).reshape(B, W, CO)
        sum_g = sum_g + jnp.sum(pre_grad, axis=0, keepdims=True)
        sum_gn = sum_gn + jnp.sum(pre_grad * away, axis=0, keepdims=True)
        return sum_g, sum_gn

    zero_row = jnp.zeros((1, CO), F32)
    sum_g, sum_gn = lax.fori_loop(0, B, middle, (zero_row, zero_row))

    def add_up(buf, size):
        total = buf[0]
        for j in range(1, size):
            total = total + buf[j]
        return total

    tot8[rank8, 0:1] = sum_g
    tot8[rank8, 1:2] = sum_gn * rstd
    tot8_x[0]()

    def cross_grad(r, carry):
        part[r] = jnp.dot(
            features_of(r),
            gc[1 : H + 1].reshape(B * PIX, CO),
            preferred_element_type=F32,
        ).reshape(3, CI, CO)
        return carry

    def head_part(b, total):
        return total + lax.dot_general(
            sgs[b], act[b], (((0,), (0,)), ((), ())), preferred_element_type=F32
        )

    lax.fori_loop(0, 1, cross_grad, 0)
    tot8_x[1]()
    toty[y] = add_up(tot8, 8)
    toty_x[0]()
    lax.fori_loop(1, 2, cross_grad, 0)
    toty_x[1]()
    totx[x] = add_up(toty, 4)
    totx_x[0]()
    lax.fori_loop(2, 3, cross_grad, 0)
    head_sum = lax.fori_loop(0, B, head_part, jnp.zeros((128, CO), F32))
    hd2[core] = head_sum[0:4, :]
    hd2_copy.start()
    st8_x[2]()
    sty_x[2]()
    stx_x[2]()
    for copy in xrow_copies + xedge_copies:
        copy.wait_send()
    totx_x[1]()
    totals = add_up(totx, 4)
    off = totals[0:1] * (1.0 / COUNT)
    slope = rstd * totals[1:2] * (1.0 / COUNT)
    st_local[0] = totals
    gb_out[...] = st_local[0, 0:1, pl.ds(pl.multiple_of(z * 128, 128), 128)]
    gg_out[...] = st_local[0, 1:2, pl.ds(pl.multiple_of(z * 128, 128), 128)]

    ORDERS = (("z", "y", "x"), ("x", "z", "y"), ("y", "z", "x"))
    a_copies = [remote(send_a.at[r], recv_a.at[r], a_s.at[r], a_r.at[r], other) for r in range(3)]

    shift = scale * (off + slope * (local_mean - mean))
    turn = scale * slope

    def kernel_grad(r, half):
        pieces = []
        for c in range(3):
            rows = pl.ds(pl.multiple_of(c * CI + half * 128, 128), 128)
            ones = jnp.concatenate([with_one[r, rows, :]] * 4, axis=1)
            pieces.append(
                part[r, c, pl.ds(pl.multiple_of(half * 128, 128), 128), :] * scale
                - with_conv[r, rows, :] * turn
                - ones * shift
            )
        return pieces

    for r in range(3):
        for c, piece in enumerate(kernel_grad(r, 1 - core)):
            send_a[r, c] = piece.astype(BF16)
        a_copies[r].start()

    def conv_grad(i, carry):
        b = lax.rem(i, B)
        h = lax.rem(3 * (i // B), H)
        spot = pl.ds(pl.multiple_of(b * W, W), W)
        away = conv[h, spot] - mean
        value = scale * (pgs[h, spot] - off - away * slope)
        gc[h + 1, b] = value.astype(BF16)
        gl[h + 1, b], gr[h + 1, b] = shifted(value, 0.0, 0.0)
        gedge_f[0, pl.ds(h * B + b, 1)] = value[W - 1 : W, :]
        gedge_f[1, pl.ds(h * B + b, 1)] = value[0:1, :]
        return carry

    ring1_send, ring1_recv = (ring1z_send, ring1x_send, ring1y_send), (
        ring1z_recv,
        ring1x_recv,
        ring1y_recv,
    )
    ring2_send, ring2_recv = (ring2z_send, ring2x_send, ring2y_send), (
        ring2z_recv,
        ring2x_recv,
        ring2y_recv,
    )

    def halves(r):
        return 192 if r == 0 else 48

    def block(r, q, low, high):
        q = lax.rem(q, 4)
        if r == 0:
            return with_conv[r, low:high, pl.ds(pl.multiple_of(q * 128, 128), 128)]
        return with_conv[r, pl.ds(pl.multiple_of(q * 96 + low, 16), high - low), :]

    def around(axis, way):
        step = 1 if way == 0 else 3
        if axis == "z":
            return (me, lax.rem(z + step, 4))
        stride = 2 if axis == "y" else 8
        here = coords[axis]
        return (me + stride * (lax.rem(here + step, 4) - here), z)

    def ring1_copies(r):
        axis = ORDERS[r][0]
        return [
            remote(
                ring1_send[r].at[way],
                ring1_recv[r].at[way],
                ring_s.at[r, way],
                ring_r.at[r, way],
                around(axis, way),
            )
            for way in range(2)
        ]

    def ring2_copies(r):
        axis = ORDERS[r][0]
        return [
            remote(
                ring2_send[r].at[way],
                ring2_recv[r].at[way],
                ring_s.at[r, 2 + way],
                ring_r.at[r, 2 + way],
                around(axis, way),
            )
            for way in range(2)
        ]

    def ring1(r):
        a_copies[r].wait_recv()
        for c, piece in enumerate(kernel_grad(r, core)):
            with_conv[r, c * 128 : (c + 1) * 128] = piece + recv_a[r, c].astype(F32)
        here, half = coords[ORDERS[r][0]], halves(r)
        ring1_send[r][0] = block(r, here + 2, 0, half).astype(BF16)
        ring1_send[r][1] = block(r, here + 2, half, 2 * half).astype(BF16)
        for copy in ring1_copies(r):
            copy.start()

    def ring2(r):
        for copy in ring1_copies(r):
            copy.wait_recv()
        here, half = coords[ORDERS[r][0]], halves(r)
        low = ring1_recv[r][0].astype(F32)
        high = ring1_recv[r][1].astype(F32)
        ring2_send[r][0, 0:half] = (block(r, here + 1, 0, half) + low).astype(BF16)
        ring2_send[r][0, half : 2 * half] = block(r, here + 1, half, 2 * half).astype(BF16)
        ring2_send[r][1, 0:half] = block(r, here + 3, 0, half).astype(BF16)
        ring2_send[r][1, half : 2 * half] = (
            block(r, here + 3, half, 2 * half) + high
        ).astype(BF16)
        for copy in ring2_copies(r):
            copy.start()

    row_axis = ("y", "x", "y")
    second, third, gather3, gather2 = [], [], [], []
    for r in range(3):
        second.append(
            along(
                ORDERS[r][1],
                lambda j, r=r: two_send.at[r, j],
                two_recv.at[r],
                dir_s.at[0, r],
                dir_r.at[0, r],
            )
        )
        third.append(
            along(
                ORDERS[r][2],
                lambda j, r=r: three_send.at[r, j],
                three_recv.at[r],
                dir_s.at[1, r],
                dir_r.at[1, r],
            )
        )
        gather3.append(share_along(ORDERS[r][2], gat3.at[r], dir_s.at[2, r], dir_r.at[2, r]))
        gather2.append(share_along(row_axis[r], gat2.at[r], dir_s.at[3, r], dir_r.at[3, r]))

    def stage2(r):
        for copy in ring2_copies(r):
            copy.wait_recv()
        here, half = coords[ORDERS[r][0]], halves(r)
        total = (
            block(r, here, 0, 2 * half)
            + ring2_recv[r][0].astype(F32)
            + ring2_recv[r][1].astype(F32)
        )
        for q in range(4):
            piece = (
                total[q * 96 : (q + 1) * 96] if r == 0 else total[:, q * 128 : (q + 1) * 128]
            )
            two_own[r, q] = piece
            two_send[r, q] = piece.astype(BF16)
        second[r][0]()

    def stage3(r):
        second[r][1]()
        here = coords[ORDERS[r][1]]
        total = two_own[r, here]
        for k in range(1, 4):
            total = total + two_recv[r, flip(here, k)].astype(F32)
        for q in range(4):
            three_send[r, q] = total[q * 24 : (q + 1) * 24]
        third[r][0]()

    def collect3(r):
        third[r][1]()
        here = coords[ORDERS[r][2]]
        total = three_send[r, here]
        for k in range(1, 4):
            total = total + three_recv[r, flip(here, k)]
        gat3[r, here] = total
        gather3[r][0]()

    def collect2(r):
        gather3[r][1]()
        here = coords[row_axis[r]]
        gat2[r, here] = jnp.concatenate([gat3[r, q] for q in range(4)], axis=0).astype(BF16)
        gather2[r][0]()

    o_copies = [remote(gat2.at[r], gat_other.at[r], o_s.at[r], o_r.at[r], other) for r in range(3)]

    def swap(r):
        gather2[r][1]()
        o_copies[r].start()
        unpack(r, gat2, core)

    def unpack(r, src, half):
        rows = src[r].reshape(384, 128)
        spot = pl.ds(pl.multiple_of(half * 128, 128), 128)
        for c in range(3):
            gw_out[3 * r + c, spot, :] = rows[c * 128 : (c + 1) * 128].astype(F32)

    def unpack_other(r):
        o_copies[r].wait_recv()
        unpack(r, gat_other, 1 - core)

    gi_copies = [
        [
            pltpu.make_async_copy(
                pgs.at[h, pl.ds(b * W, W), pl.ds(0, CI)], gi_out.at[b, h], gi_sem.at[h, b]
            )
            for b in range(B)
        ]
        for h in range(H)
    ]

    def back(h):
        lhs = jnp.concatenate(
            [
                ref[h + r].reshape(PIX, CO)
                for r in range(3)
                for ref in (gl, gc, gr)
            ],
            axis=1,
        )
        value = jnp.dot(lhs, wgt_t[...], preferred_element_type=F32)
        pgs[h, :, 0:CI] = value
        for copy in gi_copies[h]:
            copy.start()

    def set_edges(i, carry):
        h = i // B
        b = lax.rem(i, B)
        ids = lax.broadcasted_iota(jnp.int32, (16, CO), 0)
        low = pick_row(gedge_in, 1, i) * west_ok
        top = pick_row(gedge_in, 4, i) * east_ok
        block16 = gl[h + 1, b, 0:16].astype(F32)
        gl[h + 1, b, 0:16] = jnp.where(ids == 0, low, block16).astype(BF16)
        block16 = gr[h + 1, b, W - 16 : W].astype(F32)
        gr[h + 1, b, W - 16 : W] = jnp.where(ids == 15, top, block16).astype(BF16)
        return carry

    lax.fori_loop(0, 2 * B, conv_grad, 0)
    grow_copies = row_sends(gc.at[1], gc.at[H], grow, grow_s, grow_r)
    for copy in grow_copies:
        copy.start()
    ring1(0)
    lax.fori_loop(2 * B, 4 * B, conv_grad, 0)
    gedge_out[...] = gedge_f[...].astype(BF16)
    gedge_copies = edge_sends(gedge_out, gedge_in, gedge_s, gedge_r)
    for copy in gedge_copies:
        copy.start()
    ring1(1)
    ring1(2)
    hd2_copy.wait_recv()
    head_pair = hd2[0] + hd2[1]
    for q in range(4):
        hdz_send[q] = head_pair[:, q * 128 : (q + 1) * 128]
    hdz_x[0]()
    ring2(0)
    ring2(1)
    ring2(2)
    for copy in gedge_copies:
        copy.wait_recv()
    lax.fori_loop(0, B * H, set_edges, 0)
    hdz_x[1]()
    head_line = hdz_send[z]
    for k in range(1, 4):
        head_line = head_line + hdz[flip(z, k)]
    hdy[y] = head_line
    hdy_x[0]()
    back(1)
    stage2(0)
    stage2(1)
    stage2(2)
    hdy_x[1]()
    hdx[x] = add_up(hdy, 4)
    hdx_x[0]()
    back(2)
    stage3(0)
    stage3(1)
    stage3(2)
    for copy in grow_copies:
        copy.wait_recv()
    build_halo(grow, gedge_in, gl, gc, gr)
    hdx_x[1]()
    gh_out[...] = add_up(hdx, 4)
    collect3(0)
    collect3(1)
    collect3(2)
    back(0)
    collect2(0)
    collect2(1)
    collect2(2)
    back(3)
    swap(0)
    swap(1)
    swap(2)
    unpack_other(0)
    unpack_other(1)

    for copy in [hd2_copy] + grow_copies + gedge_copies + a_copies:
        copy.wait_send()
    for exchanged in [tot8_x, toty_x, totx_x, hdz_x, hdy_x, hdx_x] + second + third + gather3 + gather2:
        exchanged[2]()
    for r in range(3):
        for copy in ring1_copies(r) + ring2_copies(r):
            copy.wait_send()
    for line in gi_copies:
        for copy in line:
            copy.wait()
    unpack_other(2)
    for copy in o_copies:
        copy.wait_send()


def move_kernel(*refs):
    count = (len(refs) - 2) // 3
    in_sem, out_sem = refs[-2:]
    arrivals, leaves = [], []
    for src, dst, held in zip(refs[:count], refs[count : 2 * count], refs[2 * count : 3 * count]):
        size = src.shape[0] if len(src.shape) > 2 else 1
        for i in range(size):
            here, there, hold = (src.at[i], dst.at[i], held.at[i]) if size > 1 else (src, dst, held)
            slot = len(arrivals)
            arrivals.append(pltpu.make_async_copy(here, hold, in_sem.at[slot]))
            leaves.append(pltpu.make_async_copy(hold, there, out_sem.at[slot]))
    for copy in arrivals:
        copy.start()
    for arrival, leave in zip(arrivals, leaves):
        arrival.wait()
        leave.start()
    for leave in leaves:
        leave.wait()


def move_out(arrays):
    anywhere = pl.BlockSpec(memory_space=pl.ANY)
    return pl.pallas_call(
        move_kernel,
        out_shape=tuple(jax.ShapeDtypeStruct(a.shape, a.dtype) for a in arrays),
        in_specs=[anywhere] * len(arrays),
        out_specs=(anywhere,) * len(arrays),
        scratch_shapes=[pltpu.VMEM(a.shape, a.dtype) for a in arrays]
        + [pltpu.SemaphoreType.DMA((16,)), pltpu.SemaphoreType.DMA((16,))],
        compiler_params=pltpu.CompilerParams(vmem_limit_bytes=60 * 1024 * 1024),
    )(*arrays)


def per_device(features, conv_weight, bn_gain, bn_bias, head_weight, labels, raster):
    dma = pltpu.SemaphoreType.DMA
    vmem = pltpu.VMEM
    whole = pl.BlockSpec(memory_space=pltpu.VMEM)
    outs = pl.pallas_call(
        kernel,
        out_shape=(
            jax.ShapeDtypeStruct((TAPS, CI, 128), F32),
            jax.ShapeDtypeStruct((1, 128), F32),
            jax.ShapeDtypeStruct((1, 128), F32),
            jax.ShapeDtypeStruct((4, 128), F32),
            jax.ShapeDtypeStruct((B, H, W, CI), F32),
        ),
        in_specs=[whole, pl.BlockSpec(memory_space=pl.ANY)] + [whole] * 5,
        out_specs=(whole,) * 4 + (pl.BlockSpec(memory_space=pl.ANY),),
        scratch_shapes=[
            vmem((TAPS * CI, CO), BF16),
            vmem((TAPS * CO, CI), BF16),
            vmem((H + 2, B, W, CI), BF16),
            vmem((H + 2, B, W, CI), BF16),
            vmem((H + 2, B, W, CI), BF16),
            vmem((H + 2, 3 * CI, PIX), BF16),
            vmem((H, PIX, CO), F32),
            vmem((H, PIX, CO), F32),
            vmem((H, PIX, CO), BF16),
            vmem((H, PIX, 128), BF16),
            vmem((H, PIX, 128), BF16),
            vmem((H, PIX, 128), BF16),
            vmem((128, CO), F32),
            vmem((CO, 128), BF16),
            vmem((128, CO), BF16),
            vmem((H + 2, B, W, CO), BF16),
            vmem((H + 2, B, W, CO), BF16),
            vmem((H + 2, B, W, CO), BF16),
            vmem((2, B, W, CI), BF16),
            vmem((2, 16, CI), BF16),
            vmem((6, 16, CI), BF16),
            vmem((2, B, W, CO), BF16),
            vmem((2, 16, CO), F32),
            vmem((2, 16, CO), BF16),
            vmem((6, 16, CO), BF16),
            vmem((B, 2, CO), F32),
            vmem((8, 2, CO), F32),
            vmem((4, 2, CO), F32),
            vmem((4, 2, CO), F32),
            vmem((8, 2, CO), F32),
            vmem((4, 2, CO), F32),
            vmem((4, 2, CO), F32),
            vmem((2, 4, CO), F32),
            vmem((4, 4, 128), F32),
            vmem((4, 4, 128), F32),
            vmem((4, 4, 128), F32),
            vmem((4, 4, 128), F32),
            vmem((3, 3, CI, CO), F32),
            vmem((3, 3 * CI, CO), F32),
            vmem((3, 3 * CI, 128), F32),
            vmem((3, 3, 128, CO), BF16),
            vmem((3, 3, 128, CO), BF16),
            vmem((2, 192, 128), BF16),
            vmem((2, 48, CO), BF16),
            vmem((2, 48, CO), BF16),
            vmem((2, 192, 128), BF16),
            vmem((2, 48, CO), BF16),
            vmem((2, 48, CO), BF16),
            vmem((2, 384, 128), BF16),
            vmem((2, 96, CO), BF16),
            vmem((2, 96, CO), BF16),
            vmem((2, 384, 128), BF16),
            vmem((2, 96, CO), BF16),
            vmem((2, 96, CO), BF16),
            vmem((3, 4, 96, 128), F32),
            vmem((3, 4, 96, 128), BF16),
            vmem((3, 4, 96, 128), BF16),
            vmem((3, 4, 24, 128), F32),
            vmem((3, 4, 24, 128), F32),
            vmem((3, 4, 24, 128), F32),
            vmem((3, 4, 96, 128), BF16),
            vmem((3, 4, 96, 128), BF16),
            dma((TAPS,)),
            dma((2,)),
            dma((2,)),
            dma((6,)),
            dma((6,)),
            dma((2,)),
            dma((2,)),
            dma((6,)),
            dma((6,)),
        ]
        + [dma((6,))] * 2
        + [dma((4,))] * 2
        + [
            dma((3,)),
            dma((3,)),
            dma((3, 4)),
            dma((3, 4)),
            dma((4, 3)),
            dma((4, 3)),
            dma((3,)),
            dma((3,)),
            dma((H, B)),
        ],
        compiler_params=pltpu.CompilerParams(
            collective_id=0, has_side_effects=True, vmem_limit_bytes=60 * 1024 * 1024
        ),
        cost_estimate=pl.CostEstimate(
            flops=15_000_000_000, bytes_accessed=8_000_000, transcendentals=300_000
        ),
    )(
        features,
        conv_weight.reshape(TAPS * CI, CO),
        bn_gain.reshape(1, CO),
        bn_bias.reshape(1, CO),
        jnp.transpose(head_weight),
        labels,
        raster,
    )
    grad_weight, grad_gain, grad_bias, grad_head, grad_input = move_out(outs)
    return (
        grad_weight.reshape(3, 3, CI, 128),
        grad_gain.reshape(128),
        grad_bias.reshape(128),
        jnp.transpose(grad_head),
        grad_input,
    )


def solution(mesh):
    in_specs = (
        P(None, "rows", "cols", None),
        P(),
        P(),
        P(),
        P(),
        P(None, "rows", "cols"),
        P(None, "rows", "cols"),
    )
    out_specs = (
        P(None, None, None, "cols"),
        P("cols"),
        P("cols"),
        P("cols", None),
        P(None, "rows", "cols", None),
    )
    return jax.shard_map(
        per_device, mesh=mesh, in_specs=in_specs, out_specs=out_specs, check_vma=False
    )
```

```python
import jax
import jax.numpy as jnp
from jax import lax
from jax.experimental import pallas as pl
from jax.experimental.pallas import tpu as pltpu
from jax.sharding import PartitionSpec as P

F32 = jnp.float32
BF16 = jnp.bfloat16
MESH = pl.DeviceIdType.MESH

B = 4
H = 4
W = 128
CI = 256
CO = 512
TAPS = 9
PIX = H * W
COUNT = 4.0 * 128.0 * 512.0
EPS = 1e-05


def kernel(
    feat,
    wgt_hbm,
    gain_ref,
    bias_ref,
    head_ref,
    labels_ref,
    raster_ref,
    gw_out,
    gg_out,
    gb_out,
    gh_out,
    gc,
    edges_to,
    wgt,
    xl,
    xc,
    xr,
    xt,
    conv,
    pgs,
    act,
    sgs,
    onehot,
    pixw,
    head_pad,
    head_tile,
    head_t,
    xrow,
    xedge_out,
    xedge_in,
    grow,
    gedge_f,
    gedge_out,
    gedge_in,
    st_local,
    st8,
    st16,
    tot8,
    tot16,
    hd2,
    hdz_send,
    hdz,
    hdy,
    hdx,
    part,
    with_conv,
    with_one,
    send_a,
    recv_a,
    ring1z_send,
    ring1x_send,
    ring1y_send,
    ring1z_recv,
    ring1x_recv,
    ring1y_recv,
    ring2z_send,
    ring2x_send,
    ring2y_send,
    ring2z_recv,
    ring2x_recv,
    ring2y_recv,
    two_own,
    two_send,
    two_recv,
    three_send,
    three_recv,
    gat3,
    gat2,
    gat_other,
    wsem,
    xrow_s,
    xrow_r,
    xedge_s,
    xedge_r,
    grow_s,
    grow_r,
    gedge_s,
    gedge_r,
    st_s,
    st_r,
    hd_s,
    hd_r,
    a_s,
    a_r,
    ring_s,
    ring_r,
    dir_s,
    dir_r,
    o_s,
    o_r,
):
    me = lax.axis_index("rows")
    z = lax.axis_index("cols")
    core = lax.rem(me, 2)
    chip = me // 2
    x = chip // 4
    y = lax.rem(chip, 4)
    rank8 = z * 2 + core
    coords = {"x": x, "y": y, "z": z}

    def flip(value, bits):
        return lax.bitwise_xor(value, jnp.int32(bits)) if bits else value

    def dev8(k):
        return (flip(me, k % 2), flip(z, k // 2))

    def dev16(k):
        return (flip(me, 2 * k), z)

    def on_axis(axis, k):
        return (me, flip(z, k)) if axis == "z" else (flip(me, (2 if axis == "y" else 8) * k), z)

    other = (flip(me, 1), z)
    up = lax.rem(me + 31, 32)
    down = lax.rem(me + 1, 32)
    west = lax.rem(z + 3, 4)
    east = lax.rem(z + 1, 4)
    beyond = lax.rem(me + 31 + 2 * core, 32)

    barrier = pltpu.get_barrier_semaphore()

    def greet(device):
        pl.semaphore_signal(barrier, inc=1, device_id=device, device_id_type=MESH)

    for k in range(1, 8):
        greet(dev8(k))
    for col in (west, z, east):
        greet((beyond, col))
    for k in range(1, 16):
        greet(dev16(k))

    wcopies = []
    for t in range(TAPS):
        rows = pl.ds(t * CI, CI)
        wcopies.append(pltpu.make_async_copy(wgt_hbm.at[rows], wgt.at[rows], wsem.at[t]))
    for copy in wcopies:
        copy.start()

    row_id = lax.broadcasted_iota(jnp.int32, (16, CI), 0)
    left_edge = jnp.zeros((16, CI), F32)
    right_edge = jnp.zeros((16, CI), F32)
    for b in range(B):
        for h in range(H):
            low = feat[b, h, 0:16, :].astype(F32)[0:1, :]
            top = feat[b, h, W - 16 : W, :].astype(F32)[15:16, :]
            here = row_id == h * B + b
            left_edge = jnp.where(here, low, left_edge)
            right_edge = jnp.where(here, top, right_edge)
    xedge_out[0] = right_edge.astype(BF16)
    xedge_out[1] = left_edge.astype(BF16)

    pl.semaphore_wait(barrier, 25)

    def remote(src, dst, ssem, rsem, device):
        return pltpu.make_async_remote_copy(
            src_ref=src,
            dst_ref=dst,
            send_sem=ssem,
            recv_sem=rsem,
            device_id=device,
            device_id_type=MESH,
        )

    def row_sends(first, last, land, ssem, rsem):
        return [
            remote(last, land.at[0], ssem.at[0], rsem.at[0], (down, z)),
            remote(first, land.at[1], ssem.at[1], rsem.at[1], (up, z)),
        ]

    def edge_sends(out, land, ssem, rsem):
        copies = []
        for side, col in ((0, east), (1, west)):
            for slot, row in ((0, down), (1, me), (2, up)):
                index = side * 3 + slot
                copies.append(
                    remote(
                        out.at[side], land.at[index], ssem.at[index], rsem.at[index], (row, col)
                    )
                )
        return copies

    xrow_copies = row_sends(feat.at[:, 0], feat.at[:, H - 1], xrow, xrow_s, xrow_r)
    for copy in xrow_copies:
        copy.start()
    xedge_copies = edge_sends(xedge_out, xedge_in, xedge_s, xedge_r)
    for copy in xedge_copies:
        copy.start()

    head_pad[...] = jnp.zeros((128, CO), F32)
    head_pad[0:4] = head_ref[...].astype(F32)
    head_t[...] = head_pad[...].astype(BF16)
    head_pad[4:8] = head_ref[...].astype(F32)
    head_tile[...] = jnp.transpose(jnp.concatenate([head_pad[0:8]] * 16, axis=0)).astype(BF16)

    lane_class = lax.rem(lax.broadcasted_iota(jnp.int32, (W, 128), 1), 4).astype(F32)
    for b in range(B):
        for h in range(H):
            label = labels_ref[b, h : h + 1, :].astype(F32)
            weight = raster_ref[b, h : h + 1, :].astype(F32)
            label_t = jnp.transpose(jnp.broadcast_to(label, (128, W)))
            weight_t = jnp.transpose(jnp.broadcast_to(weight, (128, W)))
            marks = jnp.where(label_t == lane_class, 1.0, 0.0)
            onehot[h, b * W : (b + 1) * W] = marks.astype(BF16)
            pixw[h, b * W : (b + 1) * W] = ((1.0 + weight_t) * 0.25).astype(BF16)

    west_ok = jnp.where(z > 0, 1.0, 0.0).astype(F32)
    east_ok = jnp.where(z < 3, 1.0, 0.0).astype(F32)
    up_ok = jnp.where(me > 0, 1.0, 0.0).astype(F32)
    down_ok = jnp.where(me < 31, 1.0, 0.0).astype(F32)

    def pick_row(ref, slot, index):
        block = ref[slot].astype(F32)
        ids = lax.broadcasted_iota(jnp.int32, block.shape, 0)
        return jnp.sum(jnp.where(ids == index, block, 0.0), axis=0, keepdims=True)

    def shifted(value, before, after):
        ids = lax.broadcasted_iota(jnp.int32, value.shape, 0)
        left = jnp.where(ids == 0, before, pltpu.roll(value, 1, 0))
        right = jnp.where(ids == W - 1, after, pltpu.roll(value, W - 1, 0))
        return left.astype(BF16), right.astype(BF16)

    for copy in xedge_copies:
        copy.wait_recv()

    def build_x(i, carry):
        h = i // B
        b = lax.rem(i, B)
        value = feat[b, h].astype(F32)
        left, right = shifted(
            value,
            pick_row(xedge_in, 1, i) * west_ok,
            pick_row(xedge_in, 4, i) * east_ok,
        )
        xl[h + 1, b] = left
        xc[h + 1, b] = feat[b, h]
        xr[h + 1, b] = right
        return carry

    lax.fori_loop(0, B * H, build_x, 0)

    def build_halo(land, edge_in, left_ref, mid_ref, right_ref):
        def body(b, carry):
            for side, line, ok, src in ((0, 0, up_ok, H - 1), (1, H + 1, down_ok, 0)):
                value = land[side, b].astype(F32) * ok
                slot = 2 * side
                left, right = shifted(
                    value,
                    pick_row(edge_in, slot, src * B + b) * (west_ok * ok),
                    pick_row(edge_in, slot + 3, src * B + b) * (east_ok * ok),
                )
                left_ref[line, b] = left
                mid_ref[line, b] = value.astype(BF16)
                right_ref[line, b] = right
            return carry

        lax.fori_loop(0, B, body, 0)

    for copy in wcopies:
        copy.wait()

    def conv_rows(h, first, count):
        lhs = jnp.concatenate(
            [
                ref[h + first + r].reshape(PIX, CI)
                for r in range(count)
                for ref in (xl, xc, xr)
            ],
            axis=1,
        )
        start = pl.multiple_of(first * 3 * CI, 3 * CI)
        return jnp.dot(lhs, wgt[pl.ds(start, count * 3 * CI), :], preferred_element_type=F32)

    def statistics(h, value):
        mid = jnp.sum(value, axis=0, keepdims=True) * (1.0 / PIX)
        st_local[h, 0:1] = mid
        st_local[h, 1:2] = jnp.sum((value - mid) ** 2, axis=0, keepdims=True)

    def transpose_x(line):
        for c, ref in enumerate((xl, xc, xr)):
            xt[line, c * CI : (c + 1) * CI, :] = jnp.transpose(ref[line].reshape(PIX, CI))

    def inner_rows(i, carry):
        value = conv_rows(1 + i, 0, 3)
        conv[1 + i] = value
        transpose_x(1 + i)
        transpose_x(3 + i)
        statistics(1 + i, value)
        return carry

    lax.fori_loop(0, 2, inner_rows, 0)

    def outer_rows(i, carry):
        conv[3 * i] = conv_rows(3 * i, 1 - i, 2)
        return carry

    lax.fori_loop(0, 2, outer_rows, 0)

    for copy in xrow_copies:
        copy.wait_recv()
    build_halo(xrow, xedge_in, xl, xc, xr)

    def halo_rows(i, carry):
        value = conv[3 * i] + conv_rows(3 * i, 2 * i, 1)
        conv[3 * i] = value
        statistics(3 * i, value)
        return carry

    lax.fori_loop(0, 2, halo_rows, 0)

    def combine(parts, count):
        total = parts[0][0:1]
        for item in parts[1:]:
            total = total + item[0:1]
        mid = total * (1.0 / len(parts))
        spread_sum = None
        for item in parts:
            term = item[1:2] + count * (item[0:1] - mid) ** 2
            spread_sum = term if spread_sum is None else spread_sum + term
        return mid, spread_sum

    def exchange(size, devices, src_of, land, rank, ssem, rsem):
        def all_of(sem):
            few = land.at[0 : size - 1]
            return pltpu.make_async_copy(few, few, sem)

        def start():
            for k in range(1, size):
                remote(src_of(flip(rank, k)), land.at[rank], ssem, rsem, devices(k)).start()

        return start, lambda: all_of(rsem).wait(), lambda: all_of(ssem).wait()

    def share(size, devices, land, rank, ssem, rsem):
        return exchange(size, devices, lambda j: land.at[rank], land, rank, ssem, rsem)

    def along(axis, src_of, land, ssem, rsem):
        return exchange(
            4, lambda k: on_axis(axis, k), src_of, land, coords[axis], ssem, rsem
        )

    def share_along(axis, land, ssem, rsem):
        return along(axis, lambda j: land.at[coords[axis]], land, ssem, rsem)

    st8_x = share(8, dev8, st8, rank8, st_s.at[0], st_r.at[0])
    st16_x = share(16, dev16, st16, chip, st_s.at[1], st_r.at[1])
    tot8_x = share(8, dev8, tot8, rank8, st_s.at[2], st_r.at[2])
    tot16_x = share(16, dev16, tot16, chip, st_s.at[3], st_r.at[3])
    hd2_copy = remote(hd2.at[core], hd2.at[core], hd_s.at[0], hd_r.at[0], other)
    hdz_x = along("z", lambda j: hdz_send.at[j], hdz, hd_s.at[1], hd_r.at[1])
    hdy_x = share_along("y", hdy, hd_s.at[2], hd_r.at[2])
    hdx_x = share_along("x", hdx, hd_s.at[3], hd_r.at[3])

    mid, m2 = combine([st_local[h] for h in range(H)], float(PIX))
    st8[rank8, 0:1] = mid
    st8[rank8, 1:2] = m2
    st8_x[0]()

    local_mean = mid
    transpose_x(0)
    transpose_x(H + 1)

    def center(h, carry):
        act[h] = (conv[h] - local_mean).astype(BF16)
        return carry

    lax.fori_loop(0, H, center, 0)

    def features_of(r):
        return jnp.concatenate([xt[h + r] for h in range(H)], axis=1)

    def cross_conv(r, carry):
        lhs = features_of(r)
        with_conv[r] = jnp.dot(lhs, act[...].reshape(B * PIX, CO), preferred_element_type=F32)
        with_one[r] = jnp.dot(lhs, jnp.ones((B * PIX, 128), BF16), preferred_element_type=F32)
        return carry

    lax.fori_loop(0, 1, cross_conv, 0)
    st8_x[1]()
    mid, m2 = combine([st8[j] for j in range(8)], float(B * PIX))
    st16[chip, 0:1] = mid
    st16[chip, 1:2] = m2
    st16_x[0]()
    lax.fori_loop(1, 3, cross_conv, 0)
    st16_x[1]()
    mean, m2 = combine([st16[j] for j in range(16)], float(8 * B * PIX))
    rstd = lax.rsqrt(m2 * (1.0 / COUNT) + EPS)
    gain = gain_ref[...]
    bias = bias_ref[...]
    scale = gain * rstd

    def middle(b, carry):
        sum_g, sum_gn = carry
        away = conv[b] - mean
        pre = away * scale + bias
        acted = jnp.maximum(pre, 0.0).astype(BF16)
        act[b] = acted
        logits = jnp.dot(acted, head_tile[...], preferred_element_type=F32)
        expo = jnp.exp(logits)
        total = expo + pltpu.roll(expo, 1, 1)
        total = total + pltpu.roll(total, 2, 1)
        score = (pixw[b].astype(F32) * (expo / total - onehot[b].astype(F32))).astype(BF16)
        sgs[b] = score
        act_grad = jnp.dot(score, head_t[...], preferred_element_type=F32)
        pre_grad = jnp.where(pre > 0.0, act_grad, 0.0)
        pgs[b] = pre_grad
        gc[b + 1] = pre_grad.astype(BF16).reshape(B, W, CO)
        sum_g = sum_g + jnp.sum(pre_grad, axis=0, keepdims=True)
        sum_gn = sum_gn + jnp.sum(pre_grad * away, axis=0, keepdims=True)
        return sum_g, sum_gn

    zero_row = jnp.zeros((1, CO), F32)
    sum_g, sum_gn = lax.fori_loop(0, B, middle, (zero_row, zero_row))

    def add_up(buf, size):
        total = buf[0]
        for j in range(1, size):
            total = total + buf[j]
        return total

    tot8[rank8, 0:1] = sum_g
    tot8[rank8, 1:2] = sum_gn * rstd
    tot8_x[0]()

    def cross_grad(r, carry):
        part[r] = jnp.dot(
            features_of(r),
            gc[1 : H + 1].reshape(B * PIX, CO),
            preferred_element_type=F32,
        ).reshape(3, CI, CO)
        return carry

    def head_part(b, total):
        return total + lax.dot_general(
            sgs[b], act[b], (((0,), (0,)), ((), ())), preferred_element_type=F32
        )

    lax.fori_loop(0, 1, cross_grad, 0)
    tot8_x[1]()
    tot16[chip] = add_up(tot8, 8)
    tot16_x[0]()
    lax.fori_loop(1, 3, cross_grad, 0)
    head_sum = lax.fori_loop(0, B, head_part, jnp.zeros((128, CO), F32))
    hd2[core] = head_sum[0:4, :]
    hd2_copy.start()
    st8_x[2]()
    st16_x[2]()
    for copy in xrow_copies + xedge_copies:
        copy.wait_send()
    tot16_x[1]()
    totals = add_up(tot16, 16)
    off = totals[0:1] * (1.0 / COUNT)
    slope = rstd * totals[1:2] * (1.0 / COUNT)
    st_local[0] = totals
    gb_out[...] = st_local[0, 0:1, pl.ds(pl.multiple_of(z * 128, 128), 128)]
    gg_out[...] = st_local[0, 1:2, pl.ds(pl.multiple_of(z * 128, 128), 128)]

    ORDERS = (("z", "y", "x"), ("x", "z", "y"), ("y", "z", "x"))
    a_copies = [remote(send_a.at[r], recv_a.at[r], a_s.at[r], a_r.at[r], other) for r in range(3)]

    shift = scale * (off + slope * (local_mean - mean))
    turn = scale * slope

    def kernel_grad(r, half):
        pieces = []
        for c in range(3):
            rows = pl.ds(pl.multiple_of(c * CI + half * 128, 128), 128)
            ones = jnp.concatenate([with_one[r, rows, :]] * 4, axis=1)
            pieces.append(
                part[r, c, pl.ds(pl.multiple_of(half * 128, 128), 128), :] * scale
                - with_conv[r, rows, :] * turn
                - ones * shift
            )
        return pieces

    for r in range(3):
        for c, piece in enumerate(kernel_grad(r, 1 - core)):
            send_a[r, c] = piece.astype(BF16)
        a_copies[r].start()

    def conv_grad(i, carry):
        b = lax.rem(i, B)
        h = lax.rem(3 * (i // B), H)
        spot = pl.ds(pl.multiple_of(b * W, W), W)
        away = conv[h, spot] - mean
        value = scale * (pgs[h, spot] - off - away * slope)
        gc[h + 1, b] = value.astype(BF16)
        gedge_f[0, pl.ds(h * B + b, 1)] = value[W - 1 : W, :]
        gedge_f[1, pl.ds(h * B + b, 1)] = value[0:1, :]
        return carry

    ring1_send, ring1_recv = (ring1z_send, ring1x_send, ring1y_send), (
        ring1z_recv,
        ring1x_recv,
        ring1y_recv,
    )
    ring2_send, ring2_recv = (ring2z_send, ring2x_send, ring2y_send), (
        ring2z_recv,
        ring2x_recv,
        ring2y_recv,
    )

    def halves(r):
        return 192 if r == 0 else 48

    def block(r, q, low, high):
        q = lax.rem(q, 4)
        if r == 0:
            return with_conv[r, low:high, pl.ds(pl.multiple_of(q * 128, 128), 128)]
        return with_conv[r, pl.ds(pl.multiple_of(q * 96 + low, 16), high - low), :]

    def around(axis, way):
        step = 1 if way == 0 else 3
        if axis == "z":
            return (me, lax.rem(z + step, 4))
        stride = 2 if axis == "y" else 8
        here = coords[axis]
        return (me + stride * (lax.rem(here + step, 4) - here), z)

    def ring1_copies(r):
        axis = ORDERS[r][0]
        return [
            remote(
                ring1_send[r].at[way],
                ring1_recv[r].at[way],
                ring_s.at[r, way],
                ring_r.at[r, way],
                around(axis, way),
            )
            for way in range(2)
        ]

    def ring2_copies(r):
        axis = ORDERS[r][0]
        return [
            remote(
                ring2_send[r].at[way],
                ring2_recv[r].at[way],
                ring_s.at[r, 2 + way],
                ring_r.at[r, 2 + way],
                around(axis, way),
            )
            for way in range(2)
        ]

    def ring1(r):
        a_copies[r].wait_recv()
        for c, piece in enumerate(kernel_grad(r, core)):
            with_conv[r, c * 128 : (c + 1) * 128] = piece + recv_a[r, c].astype(F32)
        here, half = coords[ORDERS[r][0]], halves(r)
        ring1_send[r][0] = block(r, here + 2, 0, half).astype(BF16)
        ring1_send[r][1] = block(r, here + 2, half, 2 * half).astype(BF16)
        for copy in ring1_copies(r):
            copy.start()

    def ring2(r):
        for copy in ring1_copies(r):
            copy.wait_recv()
        here, half = coords[ORDERS[r][0]], halves(r)
        low = ring1_recv[r][0].astype(F32)
        high = ring1_recv[r][1].astype(F32)
        ring2_send[r][0, 0:half] = (block(r, here + 1, 0, half) + low).astype(BF16)
        ring2_send[r][0, half : 2 * half] = block(r, here + 1, half, 2 * half).astype(BF16)
        ring2_send[r][1, 0:half] = block(r, here + 3, 0, half).astype(BF16)
        ring2_send[r][1, half : 2 * half] = (
            block(r, here + 3, half, 2 * half) + high
        ).astype(BF16)
        for copy in ring2_copies(r):
            copy.start()

    row_axis = ("y", "x", "y")
    second, third, gather3, gather2 = [], [], [], []
    for r in range(3):
        second.append(
            along(
                ORDERS[r][1],
                lambda j, r=r: two_send.at[r, j],
                two_recv.at[r],
                dir_s.at[0, r],
                dir_r.at[0, r],
            )
        )
        third.append(
            along(
                ORDERS[r][2],
                lambda j, r=r: three_send.at[r, j],
                three_recv.at[r],
                dir_s.at[1, r],
                dir_r.at[1, r],
            )
        )
        gather3.append(share_along(ORDERS[r][2], gat3.at[r], dir_s.at[2, r], dir_r.at[2, r]))
        gather2.append(share_along(row_axis[r], gat2.at[r], dir_s.at[3, r], dir_r.at[3, r]))

    def stage2(r):
        for copy in ring2_copies(r):
            copy.wait_recv()
        here, half = coords[ORDERS[r][0]], halves(r)
        total = (
            block(r, here, 0, 2 * half)
            + ring2_recv[r][0].astype(F32)
            + ring2_recv[r][1].astype(F32)
        )
        for q in range(4):
            piece = (
                total[q * 96 : (q + 1) * 96] if r == 0 else total[:, q * 128 : (q + 1) * 128]
            )
            two_own[r, q] = piece
            two_send[r, q] = piece.astype(BF16)
        second[r][0]()

    def stage3(r):
        second[r][1]()
        here = coords[ORDERS[r][1]]
        total = two_own[r, here]
        for k in range(1, 4):
            total = total + two_recv[r, flip(here, k)].astype(F32)
        for q in range(4):
            three_send[r, q] = total[q * 24 : (q + 1) * 24]
        third[r][0]()

    def collect3(r):
        third[r][1]()
        here = coords[ORDERS[r][2]]
        total = three_send[r, here]
        for k in range(1, 4):
            total = total + three_recv[r, flip(here, k)]
        gat3[r, here] = total
        gather3[r][0]()

    def collect2(r):
        gather3[r][1]()
        here = coords[row_axis[r]]
        gat2[r, here] = jnp.concatenate([gat3[r, q] for q in range(4)], axis=0).astype(BF16)
        gather2[r][0]()

    o_copies = [remote(gat2.at[r], gat_other.at[r], o_s.at[r], o_r.at[r], other) for r in range(3)]

    def swap(r):
        gather2[r][1]()
        o_copies[r].start()
        unpack(r, gat2, core)

    def unpack(r, src, half):
        rows = src[r].reshape(384, 128)
        spot = pl.ds(pl.multiple_of(half * 128, 128), 128)
        for c in range(3):
            gw_out[3 * r + c, spot, :] = rows[c * 128 : (c + 1) * 128].astype(F32)

    def unpack_other(r):
        o_copies[r].wait_recv()
        unpack(r, gat_other, 1 - core)

    lax.fori_loop(0, 2 * B, conv_grad, 0)
    grow_copies = row_sends(gc.at[1], gc.at[H], grow, grow_s, grow_r)
    for copy in grow_copies:
        copy.start()
    ring1(0)
    lax.fori_loop(2 * B, 4 * B, conv_grad, 0)
    gedge_out[...] = gedge_f[...].astype(BF16)
    gedge_copies = edge_sends(gedge_out, gedge_in, gedge_s, gedge_r)
    for copy in gedge_copies:
        copy.start()
    ring1(1)
    ring1(2)
    hd2_copy.wait_recv()
    head_pair = hd2[0] + hd2[1]
    for q in range(4):
        hdz_send[q] = head_pair[:, q * 128 : (q + 1) * 128]
    hdz_x[0]()
    ring2(0)
    ring2(1)
    ring2(2)
    hdz_x[1]()
    head_line = hdz_send[z]
    for k in range(1, 4):
        head_line = head_line + hdz[flip(z, k)]
    hdy[y] = head_line
    hdy_x[0]()
    stage2(0)
    stage2(1)
    stage2(2)
    for copy in gedge_copies:
        copy.wait_recv()
    edges_to[...] = gedge_in[...]
    hdy_x[1]()
    hdx[x] = add_up(hdy, 4)
    hdx_x[0]()
    stage3(0)
    stage3(1)
    stage3(2)
    for copy in grow_copies:
        copy.wait_recv()
    gc[0] = (grow[0].astype(F32) * up_ok).astype(BF16)
    gc[H + 1] = (grow[1].astype(F32) * down_ok).astype(BF16)
    collect3(0)
    collect3(1)
    collect3(2)
    hdx_x[1]()
    gh_out[...] = add_up(hdx, 4)
    collect2(0)
    collect2(1)
    collect2(2)
    swap(0)
    swap(1)
    swap(2)
    unpack_other(0)
    unpack_other(1)

    for copy in [hd2_copy] + grow_copies + gedge_copies + a_copies:
        copy.wait_send()
    for exchanged in [tot8_x, tot16_x, hdz_x, hdy_x, hdx_x] + second + third + gather3 + gather2:
        exchanged[2]()
    for r in range(3):
        for copy in ring1_copies(r) + ring2_copies(r):
            copy.wait_send()
    unpack_other(2)
    for copy in o_copies:
        copy.wait_send()


def back_kernel(gc, edges, wgt, *refs):
    small_in, small_out, gi_out = refs[0:4], refs[4:8], refs[8]
    held = refs[9:13]
    gl, gr, wgt_t, gi_buf, in_sem, out_sem, gi_sem = refs[13:]
    me = lax.axis_index("rows")
    z = lax.axis_index("cols")
    west_ok = jnp.where(z > 0, 1.0, 0.0).astype(F32)
    east_ok = jnp.where(z < 3, 1.0, 0.0).astype(F32)
    up_ok = jnp.where(me > 0, 1.0, 0.0).astype(F32)
    down_ok = jnp.where(me < 31, 1.0, 0.0).astype(F32)
    arrivals = [pltpu.make_async_copy(a, b, in_sem.at[i]) for i, (a, b) in enumerate(zip(small_in, held))]
    leaves = [pltpu.make_async_copy(a, b, out_sem.at[i]) for i, (a, b) in enumerate(zip(held, small_out))]
    for copy in arrivals:
        copy.start()

    def transpose_w(t, carry):
        wgt_t[pl.ds(pl.multiple_of(t * CO, CO), CO), :] = jnp.transpose(
            wgt[pl.ds(pl.multiple_of((TAPS - 1 - t) * CI, CI), CI), :]
        )
        return carry

    lax.fori_loop(0, TAPS, transpose_w, 0)
    for arrival, leave in zip(arrivals, leaves):
        arrival.wait()
        leave.start()

    def pick_row(slot, index):
        block = edges[slot].astype(F32)
        ids = lax.broadcasted_iota(jnp.int32, block.shape, 0)
        return jnp.sum(jnp.where(ids == index, block, 0.0), axis=0, keepdims=True)

    def build(line, b, slot, index, ok):
        value = gc[line, b].astype(F32)
        ids = lax.broadcasted_iota(jnp.int32, value.shape, 0)
        before = pick_row(slot, index) * (west_ok * ok)
        after = pick_row(slot + 3, index) * (east_ok * ok)
        left = jnp.where(ids == 0, before, pltpu.roll(value, 1, 0))
        right = jnp.where(ids == W - 1, after, pltpu.roll(value, W - 1, 0))
        gl[line, b] = left.astype(BF16)
        gr[line, b] = right.astype(BF16)

    def build_inner(i, carry):
        build(1 + i // B, lax.rem(i, B), 1, i, 1.0)
        return carry

    def build_outer(b, carry):
        build(0, b, 0, (H - 1) * B + b, up_ok)
        build(H + 1, b, 2, b, down_ok)
        return carry

    lax.fori_loop(0, B * H, build_inner, 0)
    lax.fori_loop(0, B, build_outer, 0)

    def gi_copy(h):
        return pltpu.make_async_copy(gi_buf.at[h], gi_out.at[:, h], gi_sem.at[h])

    def back(h, carry):
        lhs = jnp.concatenate(
            [ref[h + r].reshape(PIX, CO) for r in range(3) for ref in (gl, gc, gr)], axis=1
        )
        value = jnp.dot(lhs, wgt_t[...], preferred_element_type=F32)
        gi_buf[h] = value.reshape(B, W, CI)
        gi_copy(h).start()
        return carry

    lax.fori_loop(0, H, back, 0)
    for leave in leaves:
        leave.wait()
    for h in range(H):
        gi_copy(h).wait()


def back_convolution(grad, edges, weights, arrays):
    anywhere = pl.BlockSpec(memory_space=pl.ANY)
    whole = pl.BlockSpec(memory_space=pltpu.VMEM)
    dma = pltpu.SemaphoreType.DMA
    return pl.pallas_call(
        back_kernel,
        out_shape=tuple(jax.ShapeDtypeStruct(a.shape, a.dtype) for a in arrays)
        + (jax.ShapeDtypeStruct((B, H, W, CI), F32),),
        in_specs=[whole] * 3 + [anywhere] * 4,
        out_specs=(anywhere,) * 5,
        scratch_shapes=[pltpu.VMEM(a.shape, a.dtype) for a in arrays]
        + [
            pltpu.VMEM((H + 2, B, W, CO), BF16),
            pltpu.VMEM((H + 2, B, W, CO), BF16),
            pltpu.VMEM((TAPS * CO, CI), BF16),
            pltpu.VMEM((H, B, W, CI), F32),
            dma((4,)),
            dma((4,)),
            dma((H,)),
        ],
        compiler_params=pltpu.CompilerParams(vmem_limit_bytes=60 * 1024 * 1024),
    )(grad, edges, weights, *arrays)


def per_device(features, conv_weight, bn_gain, bn_bias, head_weight, labels, raster):
    dma = pltpu.SemaphoreType.DMA
    vmem = pltpu.VMEM
    whole = pl.BlockSpec(memory_space=pltpu.VMEM)
    outs = pl.pallas_call(
        kernel,
        out_shape=(
            jax.ShapeDtypeStruct((TAPS, CI, 128), F32),
            jax.ShapeDtypeStruct((1, 128), F32),
            jax.ShapeDtypeStruct((1, 128), F32),
            jax.ShapeDtypeStruct((4, 128), F32),
            jax.ShapeDtypeStruct((H + 2, B, W, CO), BF16),
            jax.ShapeDtypeStruct((6, 16, CO), BF16),
        ),
        in_specs=[whole, pl.BlockSpec(memory_space=pl.ANY)] + [whole] * 5,
        out_specs=(whole,) * 6,
        scratch_shapes=[
            vmem((TAPS * CI, CO), BF16),
            vmem((H + 2, B, W, CI), BF16),
            vmem((H + 2, B, W, CI), BF16),
            vmem((H + 2, B, W, CI), BF16),
            vmem((H + 2, 3 * CI, PIX), BF16),
            vmem((H, PIX, CO), F32),
            vmem((H, PIX, CO), F32),
            vmem((H, PIX, CO), BF16),
            vmem((H, PIX, 128), BF16),
            vmem((H, PIX, 128), BF16),
            vmem((H, PIX, 128), BF16),
            vmem((128, CO), F32),
            vmem((CO, 128), BF16),
            vmem((128, CO), BF16),
            vmem((2, B, W, CI), BF16),
            vmem((2, 16, CI), BF16),
            vmem((6, 16, CI), BF16),
            vmem((2, B, W, CO), BF16),
            vmem((2, 16, CO), F32),
            vmem((2, 16, CO), BF16),
            vmem((6, 16, CO), BF16),
            vmem((B, 2, CO), F32),
            vmem((8, 2, CO), F32),
            vmem((16, 2, CO), F32),
            vmem((8, 2, CO), F32),
            vmem((16, 2, CO), F32),
            vmem((2, 4, CO), F32),
            vmem((4, 4, 128), F32),
            vmem((4, 4, 128), F32),
            vmem((4, 4, 128), F32),
            vmem((4, 4, 128), F32),
            vmem((3, 3, CI, CO), F32),
            vmem((3, 3 * CI, CO), F32),
            vmem((3, 3 * CI, 128), F32),
            vmem((3, 3, 128, CO), BF16),
            vmem((3, 3, 128, CO), BF16),
            vmem((2, 192, 128), BF16),
            vmem((2, 48, CO), BF16),
            vmem((2, 48, CO), BF16),
            vmem((2, 192, 128), BF16),
            vmem((2, 48, CO), BF16),
            vmem((2, 48, CO), BF16),
            vmem((2, 384, 128), BF16),
            vmem((2, 96, CO), BF16),
            vmem((2, 96, CO), BF16),
            vmem((2, 384, 128), BF16),
            vmem((2, 96, CO), BF16),
            vmem((2, 96, CO), BF16),
            vmem((3, 4, 96, 128), F32),
            vmem((3, 4, 96, 128), BF16),
            vmem((3, 4, 96, 128), BF16),
            vmem((3, 4, 24, 128), F32),
            vmem((3, 4, 24, 128), F32),
            vmem((3, 4, 24, 128), F32),
            vmem((3, 4, 96, 128), BF16),
            vmem((3, 4, 96, 128), BF16),
            dma((TAPS,)),
            dma((2,)),
            dma((2,)),
            dma((6,)),
            dma((6,)),
            dma((2,)),
            dma((2,)),
            dma((6,)),
            dma((6,)),
        ]
        + [dma((4,))] * 4
        + [
            dma((3,)),
            dma((3,)),
            dma((3, 4)),
            dma((3, 4)),
            dma((4, 3)),
            dma((4, 3)),
            dma((3,)),
            dma((3,)),
        ],
        compiler_params=pltpu.CompilerParams(
            collective_id=0, has_side_effects=True, vmem_limit_bytes=60 * 1024 * 1024
        ),
        cost_estimate=pl.CostEstimate(
            flops=15_000_000_000, bytes_accessed=8_000_000, transcendentals=300_000
        ),
    )(
        features,
        conv_weight.reshape(TAPS * CI, CO),
        bn_gain.reshape(1, CO),
        bn_bias.reshape(1, CO),
        jnp.transpose(head_weight),
        labels,
        raster,
    )
    grad_weight, grad_gain, grad_bias, grad_head, grad_input = back_convolution(
        outs[4], outs[5], conv_weight.reshape(TAPS * CI, CO), outs[:4]
    )
    return (
        grad_weight.reshape(3, 3, CI, 128),
        grad_gain.reshape(128),
        grad_bias.reshape(128),
        jnp.transpose(grad_head),
        grad_input,
    )


def solution(mesh):
    in_specs = (
        P(None, "rows", "cols", None),
        P(),
        P(),
        P(),
        P(),
        P(None, "rows", "cols"),
        P(None, "rows", "cols"),
    )
    out_specs = (
        P(None, None, None, "cols"),
        P("cols"),
        P("cols"),
        P("cols", None),
        P(None, "rows", "cols", None),
    )
    return jax.shard_map(
        per_device, mesh=mesh, in_specs=in_specs, out_specs=out_specs, check_vma=False
    )
```

```python
import jax
import jax.numpy as jnp
from jax import lax
from jax.experimental import pallas as pl
from jax.experimental.pallas import tpu as pltpu
from jax.sharding import PartitionSpec as P

F32 = jnp.float32
BF16 = jnp.bfloat16
MESH = pl.DeviceIdType.MESH

B = 4
H = 4
W = 128
CI = 256
CO = 512
TAPS = 9
PIX = H * W
COUNT = 4.0 * 128.0 * 512.0
EPS = 1e-05


def kernel(
    feat,
    wgt_hbm,
    gain_ref,
    bias_ref,
    head_ref,
    labels_ref,
    raster_ref,
    gw_out,
    gg_out,
    gb_out,
    gh_out,
    gi_out,
    wgt,
    identity,
    xl,
    xc,
    xr,
    xt,
    conv,
    pgs,
    act,
    sgs,
    onehot,
    pixw,
    head_pad,
    head_tile,
    head_t,
    gl,
    gc,
    gr,
    xrow,
    xedge_out,
    xedge_in,
    grow,
    gedge_f,
    gedge_out,
    gedge_in,
    st_local,
    st8,
    st16,
    tot8,
    tot16,
    hd2,
    hdz_send,
    hdz,
    hdy,
    hdx,
    part,
    with_conv,
    with_one,
    send_a,
    recv_a,
    ring1z_send,
    ring1x_send,
    ring1y_send,
    ring1z_recv,
    ring1x_recv,
    ring1y_recv,
    ring2z_send,
    ring2x_send,
    ring2y_send,
    ring2z_recv,
    ring2x_recv,
    ring2y_recv,
    two_own,
    two_send,
    two_recv,
    three_send,
    three_recv,
    gat3,
    gat2,
    gat_other,
    wsem,
    xrow_s,
    xrow_r,
    xedge_s,
    xedge_r,
    grow_s,
    grow_r,
    gedge_s,
    gedge_r,
    st_s,
    st_r,
    hd_s,
    hd_r,
    a_s,
    a_r,
    ring_s,
    ring_r,
    dir_s,
    dir_r,
    o_s,
    o_r,
    gi_sem,
):
    me = lax.axis_index("rows")
    z = lax.axis_index("cols")
    core = lax.rem(me, 2)
    chip = me // 2
    x = chip // 4
    y = lax.rem(chip, 4)
    rank8 = z * 2 + core
    coords = {"x": x, "y": y, "z": z}

    def flip(value, bits):
        return lax.bitwise_xor(value, jnp.int32(bits)) if bits else value

    def dev8(k):
        return (flip(me, k % 2), flip(z, k // 2))

    def dev16(k):
        return (flip(me, 2 * k), z)

    def on_axis(axis, k):
        return (me, flip(z, k)) if axis == "z" else (flip(me, (2 if axis == "y" else 8) * k), z)

    other = (flip(me, 1), z)
    up = lax.rem(me + 31, 32)
    down = lax.rem(me + 1, 32)
    west = lax.rem(z + 3, 4)
    east = lax.rem(z + 1, 4)
    beyond = lax.rem(me + 31 + 2 * core, 32)

    barrier = pltpu.get_barrier_semaphore()

    def greet(device):
        pl.semaphore_signal(barrier, inc=1, device_id=device, device_id_type=MESH)

    for k in range(1, 8):
        greet(dev8(k))
    for col in (west, z, east):
        greet((beyond, col))
    for k in range(1, 16):
        greet(dev16(k))

    wcopies = []
    for t in range(TAPS):
        rows = pl.ds(t * CI, CI)
        wcopies.append(pltpu.make_async_copy(wgt_hbm.at[rows], wgt.at[rows], wsem.at[t]))
    for copy in wcopies:
        copy.start()

    row_id = lax.broadcasted_iota(jnp.int32, (16, CI), 0)
    left_edge = jnp.zeros((16, CI), F32)
    right_edge = jnp.zeros((16, CI), F32)
    for b in range(B):
        for h in range(H):
            low = feat[b, h, 0:16, :].astype(F32)[0:1, :]
            top = feat[b, h, W - 16 : W, :].astype(F32)[15:16, :]
            here = row_id == h * B + b
            left_edge = jnp.where(here, low, left_edge)
            right_edge = jnp.where(here, top, right_edge)
    xedge_out[0] = right_edge.astype(BF16)
    xedge_out[1] = left_edge.astype(BF16)

    pl.semaphore_wait(barrier, 25)

    def remote(src, dst, ssem, rsem, device):
        return pltpu.make_async_remote_copy(
            src_ref=src,
            dst_ref=dst,
            send_sem=ssem,
            recv_sem=rsem,
            device_id=device,
            device_id_type=MESH,
        )

    def row_sends(first, last, land, ssem, rsem):
        return [
            remote(last, land.at[0], ssem.at[0], rsem.at[0], (down, z)),
            remote(first, land.at[1], ssem.at[1], rsem.at[1], (up, z)),
        ]

    def edge_sends(out, land, ssem, rsem):
        copies = []
        for side, col in ((0, east), (1, west)):
            for slot, row in ((0, down), (1, me), (2, up)):
                index = side * 3 + slot
                copies.append(
                    remote(
                        out.at[side], land.at[index], ssem.at[index], rsem.at[index], (row, col)
                    )
                )
        return copies

    xrow_copies = row_sends(feat.at[:, 0], feat.at[:, H - 1], xrow, xrow_s, xrow_r)
    for copy in xrow_copies:
        copy.start()
    xedge_copies = edge_sends(xedge_out, xedge_in, xedge_s, xedge_r)
    for copy in xedge_copies:
        copy.start()

    head_pad[...] = jnp.zeros((128, CO), F32)
    head_pad[0:4] = head_ref[...].astype(F32)
    head_t[...] = head_pad[...].astype(BF16)
    head_pad[4:8] = head_ref[...].astype(F32)
    head_tile[...] = jnp.transpose(jnp.concatenate([head_pad[0:8]] * 16, axis=0)).astype(BF16)

    lane_class = lax.rem(lax.broadcasted_iota(jnp.int32, (W, 128), 1), 4).astype(F32)
    identity[...] = jnp.where(
        lax.broadcasted_iota(jnp.int32, (256, 256), 0)
        == lax.broadcasted_iota(jnp.int32, (256, 256), 1),
        1.0,
        0.0,
    ).astype(BF16)

    def turned(value):
        size = value.shape[1]
        return lax.dot_general(
            identity[0:size, 0:size],
            value,
            (((1,), (1,)), ((), ())),
            preferred_element_type=F32,
        )

    def class_marks(i, carry):
        b = i // H
        h = lax.rem(i, H)
        spot = pl.ds(pl.multiple_of(b * W, W), W)
        code = labels_ref[b, pl.ds(h, 1), :] + 4 * raster_ref[b, pl.ds(h, 1), :]
        code = turned(jnp.broadcast_to(code.astype(F32), (128, W)).astype(BF16))
        weight = jnp.where(code > 3.5, 1.0, 0.0)
        marks = jnp.where(code - 4.0 * weight == lane_class, 1.0, 0.0)
        onehot[h, spot] = marks.astype(BF16)
        pixw[h, spot] = ((1.0 + weight) * 0.25).astype(BF16)
        return carry

    lax.fori_loop(0, B * H, class_marks, 0)

    west_ok = jnp.where(z > 0, 1.0, 0.0).astype(F32)
    east_ok = jnp.where(z < 3, 1.0, 0.0).astype(F32)
    up_ok = jnp.where(me > 0, 1.0, 0.0).astype(F32)
    down_ok = jnp.where(me < 31, 1.0, 0.0).astype(F32)

    def pick_row(ref, slot, index):
        block = ref[slot].astype(F32)
        ids = lax.broadcasted_iota(jnp.int32, block.shape, 0)
        return jnp.sum(jnp.where(ids == index, block, 0.0), axis=0, keepdims=True)

    def shifted(value, before, after):
        ids = lax.broadcasted_iota(jnp.int32, value.shape, 0)
        left = jnp.where(ids == 0, before, pltpu.roll(value, 1, 0))
        right = jnp.where(ids == W - 1, after, pltpu.roll(value, W - 1, 0))
        return left.astype(BF16), right.astype(BF16)

    for copy in xedge_copies:
        copy.wait_recv()

    def build_x(i, carry):
        h = i // B
        b = lax.rem(i, B)
        value = feat[b, h].astype(F32)
        left, right = shifted(
            value,
            pick_row(xedge_in, 1, i) * west_ok,
            pick_row(xedge_in, 4, i) * east_ok,
        )
        xl[h + 1, b] = left
        xc[h + 1, b] = feat[b, h]
        xr[h + 1, b] = right
        return carry

    lax.fori_loop(0, B * H, build_x, 0)

    def build_halo(land, edge_in, left_ref, mid_ref, right_ref):
        def body(b, carry):
            for side, line, ok, src in ((0, 0, up_ok, H - 1), (1, H + 1, down_ok, 0)):
                value = land[side, b].astype(F32) * ok
                slot = 2 * side
                left, right = shifted(
                    value,
                    pick_row(edge_in, slot, src * B + b) * (west_ok * ok),
                    pick_row(edge_in, slot + 3, src * B + b) * (east_ok * ok),
                )
                left_ref[line, b] = left
                mid_ref[line, b] = value.astype(BF16)
                right_ref[line, b] = right
            return carry

        lax.fori_loop(0, B, body, 0)

    for copy in wcopies:
        copy.wait()

    def conv_rows(h, first, count):
        lhs = jnp.concatenate(
            [
                ref[h + first + r].reshape(PIX, CI)
                for r in range(count)
                for ref in (xl, xc, xr)
            ],
            axis=1,
        )
        start = pl.multiple_of(first * 3 * CI, 3 * CI)
        return jnp.dot(lhs, wgt[pl.ds(start, count * 3 * CI), :], preferred_element_type=F32)

    def statistics(h, value):
        mid = jnp.sum(value, axis=0, keepdims=True) * (1.0 / PIX)
        st_local[h, 0:1] = mid
        st_local[h, 1:2] = jnp.sum((value - mid) ** 2, axis=0, keepdims=True)

    def transpose_x(line):
        for c, ref in enumerate((xl, xc, xr)):
            xt[line, c * CI : (c + 1) * CI, :] = turned(ref[line].reshape(PIX, CI)).astype(BF16)

    def inner_rows(i, carry):
        value = conv_rows(1 + i, 0, 3)
        conv[1 + i] = value
        transpose_x(1 + i)
        transpose_x(3 + i)
        statistics(1 + i, value)
        return carry

    lax.fori_loop(0, 2, inner_rows, 0)

    def outer_rows(i, carry):
        conv[3 * i] = conv_rows(3 * i, 1 - i, 2)
        return carry

    lax.fori_loop(0, 2, outer_rows, 0)

    for copy in xrow_copies:
        copy.wait_recv()
    build_halo(xrow, xedge_in, xl, xc, xr)

    def halo_rows(i, carry):
        value = conv[3 * i] + conv_rows(3 * i, 2 * i, 1)
        conv[3 * i] = value
        statistics(3 * i, value)
        return carry

    lax.fori_loop(0, 2, halo_rows, 0)

    def combine(parts, count):
        total = parts[0][0:1]
        for item in parts[1:]:
            total = total + item[0:1]
        mid = total * (1.0 / len(parts))
        spread_sum = None
        for item in parts:
            term = item[1:2] + count * (item[0:1] - mid) ** 2
            spread_sum = term if spread_sum is None else spread_sum + term
        return mid, spread_sum

    def exchange(size, devices, src_of, land, rank, ssem, rsem):
        def all_of(sem):
            few = land.at[0 : size - 1]
            return pltpu.make_async_copy(few, few, sem)

        def start():
            for k in range(1, size):
                remote(src_of(flip(rank, k)), land.at[rank], ssem, rsem, devices(k)).start()

        return start, lambda: all_of(rsem).wait(), lambda: all_of(ssem).wait()

    def share(size, devices, land, rank, ssem, rsem):
        return exchange(size, devices, lambda j: land.at[rank], land, rank, ssem, rsem)

    def along(axis, src_of, land, ssem, rsem):
        return exchange(
            4, lambda k: on_axis(axis, k), src_of, land, coords[axis], ssem, rsem
        )

    def share_along(axis, land, ssem, rsem):
        return along(axis, lambda j: land.at[coords[axis]], land, ssem, rsem)

    st8_x = share(8, dev8, st8, rank8, st_s.at[0], st_r.at[0])
    st16_x = share(16, dev16, st16, chip, st_s.at[1], st_r.at[1])
    tot8_x = share(8, dev8, tot8, rank8, st_s.at[2], st_r.at[2])
    tot16_x = share(16, dev16, tot16, chip, st_s.at[3], st_r.at[3])
    hd2_copy = remote(hd2.at[core], hd2.at[core], hd_s.at[0], hd_r.at[0], other)
    hdz_x = along("z", lambda j: hdz_send.at[j], hdz, hd_s.at[1], hd_r.at[1])
    hdy_x = share_along("y", hdy, hd_s.at[2], hd_r.at[2])
    hdx_x = share_along("x", hdx, hd_s.at[3], hd_r.at[3])

    mid, m2 = combine([st_local[h] for h in range(H)], float(PIX))
    st8[rank8, 0:1] = mid
    st8[rank8, 1:2] = m2
    st8_x[0]()

    local_mean = mid
    transpose_x(0)
    transpose_x(H + 1)

    def center(h, carry):
        act[h] = (conv[h] - local_mean).astype(BF16)
        return carry

    lax.fori_loop(0, H, center, 0)

    def features_of(r):
        return jnp.concatenate([xt[h + r] for h in range(H)], axis=1)

    def cross_conv(r, carry):
        lhs = features_of(r)
        with_conv[r] = jnp.dot(lhs, act[...].reshape(B * PIX, CO), preferred_element_type=F32)
        with_one[r] = jnp.dot(lhs, jnp.ones((B * PIX, 128), BF16), preferred_element_type=F32)
        return carry

    lax.fori_loop(0, 1, cross_conv, 0)
    st8_x[1]()
    mid, m2 = combine([st8[j] for j in range(8)], float(B * PIX))
    st16[chip, 0:1] = mid
    st16[chip, 1:2] = m2
    st16_x[0]()
    lax.fori_loop(1, 3, cross_conv, 0)
    st16_x[1]()
    mean, m2 = combine([st16[j] for j in range(16)], float(8 * B * PIX))
    rstd = lax.rsqrt(m2 * (1.0 / COUNT) + EPS)
    gain = gain_ref[...]
    bias = bias_ref[...]
    scale = gain * rstd

    def middle(b, carry):
        sum_g, sum_gn = carry
        away = conv[b] - mean
        pre = away * scale + bias
        acted = jnp.maximum(pre, 0.0).astype(BF16)
        act[b] = acted
        logits = jnp.dot(acted, head_tile[...], preferred_element_type=F32)
        expo = jnp.exp(logits)
        total = expo + pltpu.roll(expo, 1, 1)
        total = total + pltpu.roll(total, 2, 1)
        score = (pixw[b].astype(F32) * (expo / total - onehot[b].astype(F32))).astype(BF16)
        sgs[b] = score
        act_grad = jnp.dot(score, head_t[...], preferred_element_type=F32)
        pre_grad = jnp.where(pre > 0.0, act_grad, 0.0)
        pgs[b] = pre_grad
        gc[b + 1] = pre_grad.astype(BF16).reshape(B, W, CO)
        sum_g = sum_g + jnp.sum(pre_grad, axis=0, keepdims=True)
        sum_gn = sum_gn + jnp.sum(pre_grad * away, axis=0, keepdims=True)
        return sum_g, sum_gn

    zero_row = jnp.zeros((1, CO), F32)
    sum_g, sum_gn = lax.fori_loop(0, B, middle, (zero_row, zero_row))

    def add_up(buf, size):
        total = buf[0]
        for j in range(1, size):
            total = total + buf[j]
        return total

    tot8[rank8, 0:1] = sum_g
    tot8[rank8, 1:2] = sum_gn * rstd
    tot8_x[0]()

    def cross_grad(r, carry):
        part[r] = jnp.dot(
            features_of(r),
            gc[1 : H + 1].reshape(B * PIX, CO),
            preferred_element_type=F32,
        ).reshape(3, CI, CO)
        return carry

    def head_part(b, total):
        return total + lax.dot_general(
            sgs[b], act[b], (((0,), (0,)), ((), ())), preferred_element_type=F32
        )

    lax.fori_loop(0, 1, cross_grad, 0)
    tot8_x[1]()
    tot16[chip] = add_up(tot8, 8)
    tot16_x[0]()
    lax.fori_loop(1, 3, cross_grad, 0)
    head_sum = lax.fori_loop(0, B, head_part, jnp.zeros((128, CO), F32))
    hd2[core] = head_sum[0:4, :]
    hd2_copy.start()
    st8_x[2]()
    st16_x[2]()
    for copy in xrow_copies + xedge_copies:
        copy.wait_send()
    tot16_x[1]()
    totals = add_up(tot16, 16)
    off = totals[0:1] * (1.0 / COUNT)
    slope = rstd * totals[1:2] * (1.0 / COUNT)
    st_local[0] = totals
    gb_out[...] = st_local[0, 0:1, pl.ds(pl.multiple_of(z * 128, 128), 128)]
    gg_out[...] = st_local[0, 1:2, pl.ds(pl.multiple_of(z * 128, 128), 128)]

    ORDERS = (("z", "y", "x"), ("x", "z", "y"), ("y", "z", "x"))
    a_copies = [remote(send_a.at[r], recv_a.at[r], a_s.at[r], a_r.at[r], other) for r in range(3)]

    shift = scale * (off + slope * (local_mean - mean))
    turn = scale * slope

    def kernel_grad(r, half):
        pieces = []
        for c in range(3):
            rows = pl.ds(pl.multiple_of(c * CI + half * 128, 128), 128)
            ones = jnp.concatenate([with_one[r, rows, :]] * 4, axis=1)
            pieces.append(
                part[r, c, pl.ds(pl.multiple_of(half * 128, 128), 128), :] * scale
                - with_conv[r, rows, :] * turn
                - ones * shift
            )
        return pieces

    for r in range(3):
        for c, piece in enumerate(kernel_grad(r, 1 - core)):
            send_a[r, c] = piece.astype(BF16)
        a_copies[r].start()

    def conv_grad(i, carry):
        b = lax.rem(i, B)
        h = lax.rem(3 * (i // B), H)
        spot = pl.ds(pl.multiple_of(b * W, W), W)
        away = conv[h, spot] - mean
        value = scale * (pgs[h, spot] - off - away * slope)
        gc[h + 1, b] = value.astype(BF16)
        gl[h + 1, b], gr[h + 1, b] = shifted(value, 0.0, 0.0)
        gedge_f[0, pl.ds(h * B + b, 1)] = value[W - 1 : W, :]
        gedge_f[1, pl.ds(h * B + b, 1)] = value[0:1, :]
        return carry

    ring1_send, ring1_recv = (ring1z_send, ring1x_send, ring1y_send), (
        ring1z_recv,
        ring1x_recv,
        ring1y_recv,
    )
    ring2_send, ring2_recv = (ring2z_send, ring2x_send, ring2y_send), (
        ring2z_recv,
        ring2x_recv,
        ring2y_recv,
    )

    def halves(r):
        return 192 if r == 0 else 48

    def block(r, q, low, high):
        q = lax.rem(q, 4)
        if r == 0:
            return with_conv[r, low:high, pl.ds(pl.multiple_of(q * 128, 128), 128)]
        return with_conv[r, pl.ds(pl.multiple_of(q * 96 + low, 16), high - low), :]

    def around(axis, way):
        step = 1 if way == 0 else 3
        if axis == "z":
            return (me, lax.rem(z + step, 4))
        stride = 2 if axis == "y" else 8
        here = coords[axis]
        return (me + stride * (lax.rem(here + step, 4) - here), z)

    def ring1_copies(r):
        axis = ORDERS[r][0]
        return [
            remote(
                ring1_send[r].at[way],
                ring1_recv[r].at[way],
                ring_s.at[r, way],
                ring_r.at[r, way],
                around(axis, way),
            )
            for way in range(2)
        ]

    def ring2_copies(r):
        axis = ORDERS[r][0]
        return [
            remote(
                ring2_send[r].at[way],
                ring2_recv[r].at[way],
                ring_s.at[r, 2 + way],
                ring_r.at[r, 2 + way],
                around(axis, way),
            )
            for way in range(2)
        ]

    def ring1(r):
        a_copies[r].wait_recv()
        for c, piece in enumerate(kernel_grad(r, core)):
            with_conv[r, c * 128 : (c + 1) * 128] = piece + recv_a[r, c].astype(F32)
        here, half = coords[ORDERS[r][0]], halves(r)
        ring1_send[r][0] = block(r, here + 2, 0, half).astype(BF16)
        ring1_send[r][1] = block(r, here + 2, half, 2 * half).astype(BF16)
        for copy in ring1_copies(r):
            copy.start()

    def ring2(r):
        for copy in ring1_copies(r):
            copy.wait_recv()
        here, half = coords[ORDERS[r][0]], halves(r)
        low = ring1_recv[r][0].astype(F32)
        high = ring1_recv[r][1].astype(F32)
        ring2_send[r][0, 0:half] = (block(r, here + 1, 0, half) + low).astype(BF16)
        ring2_send[r][0, half : 2 * half] = block(r, here + 1, half, 2 * half).astype(BF16)
        ring2_send[r][1, 0:half] = block(r, here + 3, 0, half).astype(BF16)
        ring2_send[r][1, half : 2 * half] = (
            block(r, here + 3, half, 2 * half) + high
        ).astype(BF16)
        for copy in ring2_copies(r):
            copy.start()

    row_axis = ("y", "x", "y")
    second, third, gather3, gather2 = [], [], [], []
    for r in range(3):
        second.append(
            along(
                ORDERS[r][1],
                lambda j, r=r: two_send.at[r, j],
                two_recv.at[r],
                dir_s.at[0, r],
                dir_r.at[0, r],
            )
        )
        third.append(
            along(
                ORDERS[r][2],
                lambda j, r=r: three_send.at[r, j],
                three_recv.at[r],
                dir_s.at[1, r],
                dir_r.at[1, r],
            )
        )
        gather3.append(share_along(ORDERS[r][2], gat3.at[r], dir_s.at[2, r], dir_r.at[2, r]))
        gather2.append(share_along(row_axis[r], gat2.at[r], dir_s.at[3, r], dir_r.at[3, r]))

    def stage2(r):
        for copy in ring2_copies(r):
            copy.wait_recv()
        here, half = coords[ORDERS[r][0]], halves(r)
        total = (
            block(r, here, 0, 2 * half)
            + ring2_recv[r][0].astype(F32)
            + ring2_recv[r][1].astype(F32)
        )
        for q in range(4):
            piece = (
                total[q * 96 : (q + 1) * 96] if r == 0 else total[:, q * 128 : (q + 1) * 128]
            )
            two_own[r, q] = piece
            two_send[r, q] = piece.astype(BF16)
        second[r][0]()

    def stage3(r):
        second[r][1]()
        here = coords[ORDERS[r][1]]
        total = two_own[r, here]
        for k in range(1, 4):
            total = total + two_recv[r, flip(here, k)].astype(F32)
        for q in range(4):
            three_send[r, q] = total[q * 24 : (q + 1) * 24]
        third[r][0]()

    def collect3(r):
        third[r][1]()
        here = coords[ORDERS[r][2]]
        total = three_send[r, here]
        for k in range(1, 4):
            total = total + three_recv[r, flip(here, k)]
        gat3[r, here] = total
        gather3[r][0]()

    def collect2(r):
        gather3[r][1]()
        here = coords[row_axis[r]]
        gat2[r, here] = jnp.concatenate([gat3[r, q] for q in range(4)], axis=0).astype(BF16)
        gather2[r][0]()

    o_copies = [remote(gat2.at[r], gat_other.at[r], o_s.at[r], o_r.at[r], other) for r in range(3)]

    def swap(r):
        gather2[r][1]()
        o_copies[r].start()
        unpack(r, gat2, core)

    def unpack(r, src, half):
        rows = src[r].reshape(384, 128)
        spot = pl.ds(pl.multiple_of(half * 128, 128), 128)
        for c in range(3):
            gw_out[3 * r + c, spot, :] = rows[c * 128 : (c + 1) * 128].astype(F32)

    def unpack_other(r):
        o_copies[r].wait_recv()
        unpack(r, gat_other, 1 - core)

    gi_copies = [
        [
            pltpu.make_async_copy(
                pgs.at[h, pl.ds(b * W, W), pl.ds(0, CI)], gi_out.at[b, h], gi_sem.at[h, b]
            )
            for b in range(B)
        ]
        for h in range(H)
    ]

    def back(h):
        lhs = jnp.concatenate(
            [
                ref[h + r].reshape(PIX, CO)
                for r in range(3)
                for ref in (gl, gc, gr)
            ],
            axis=1,
        )
        flipped = jnp.concatenate(
            [wgt[(TAPS - 1 - t) * CI : (TAPS - t) * CI, :] for t in range(TAPS)], axis=1
        )
        value = lax.dot_general(
            lhs, flipped, (((1,), (1,)), ((), ())), preferred_element_type=F32
        )
        pgs[h, :, 0:CI] = value
        for copy in gi_copies[h]:
            copy.start()

    def set_edges(i, carry):
        h = i // B
        b = lax.rem(i, B)
        ids = lax.broadcasted_iota(jnp.int32, (16, CO), 0)
        low = pick_row(gedge_in, 1, i) * west_ok
        top = pick_row(gedge_in, 4, i) * east_ok
        block16 = gl[h + 1, b, 0:16].astype(F32)
        gl[h + 1, b, 0:16] = jnp.where(ids == 0, low, block16).astype(BF16)
        block16 = gr[h + 1, b, W - 16 : W].astype(F32)
        gr[h + 1, b, W - 16 : W] = jnp.where(ids == 15, top, block16).astype(BF16)
        return carry

    lax.fori_loop(0, 2 * B, conv_grad, 0)
    grow_copies = row_sends(gc.at[1], gc.at[H], grow, grow_s, grow_r)
    for copy in grow_copies:
        copy.start()
    ring1(0)
    lax.fori_loop(2 * B, 4 * B, conv_grad, 0)
    gedge_out[...] = gedge_f[...].astype(BF16)
    gedge_copies = edge_sends(gedge_out, gedge_in, gedge_s, gedge_r)
    for copy in gedge_copies:
        copy.start()
    ring1(1)
    ring1(2)
    hd2_copy.wait_recv()
    head_pair = hd2[0] + hd2[1]
    for q in range(4):
        hdz_send[q] = head_pair[:, q * 128 : (q + 1) * 128]
    hdz_x[0]()
    ring2(0)
    ring2(1)
    ring2(2)
    for copy in gedge_copies:
        copy.wait_recv()
    lax.fori_loop(0, B * H, set_edges, 0)
    hdz_x[1]()
    head_line = hdz_send[z]
    for k in range(1, 4):
        head_line = head_line + hdz[flip(z, k)]
    hdy[y] = head_line
    hdy_x[0]()
    back(1)
    stage2(0)
    stage2(1)
    stage2(2)
    hdy_x[1]()
    hdx[x] = add_up(hdy, 4)
    hdx_x[0]()
    back(2)
    stage3(0)
    stage3(1)
    stage3(2)
    for copy in grow_copies:
        copy.wait_recv()
    build_halo(grow, gedge_in, gl, gc, gr)
    hdx_x[1]()
    gh_out[...] = add_up(hdx, 4)
    collect3(0)
    collect3(1)
    collect3(2)
    back(0)
    collect2(0)
    collect2(1)
    collect2(2)
    back(3)
    swap(0)
    swap(1)
    swap(2)
    unpack_other(0)
    unpack_other(1)

    for copy in [hd2_copy] + grow_copies + gedge_copies + a_copies:
        copy.wait_send()
    for exchanged in [tot8_x, tot16_x, hdz_x, hdy_x, hdx_x] + second + third + gather3 + gather2:
        exchanged[2]()
    for r in range(3):
        for copy in ring1_copies(r) + ring2_copies(r):
            copy.wait_send()
    for line in gi_copies:
        for copy in line:
            copy.wait()
    unpack_other(2)
    for copy in o_copies:
        copy.wait_send()


def move_kernel(*refs):
    count = (len(refs) - 2) // 3
    in_sem, out_sem = refs[-2:]
    arrivals, leaves = [], []
    for src, dst, held in zip(refs[:count], refs[count : 2 * count], refs[2 * count : 3 * count]):
        size = src.shape[0] if len(src.shape) > 2 else 1
        for i in range(size):
            here, there, hold = (src.at[i], dst.at[i], held.at[i]) if size > 1 else (src, dst, held)
            slot = len(arrivals)
            arrivals.append(pltpu.make_async_copy(here, hold, in_sem.at[slot]))
            leaves.append(pltpu.make_async_copy(hold, there, out_sem.at[slot]))
    for copy in arrivals:
        copy.start()
    for arrival, leave in zip(arrivals, leaves):
        arrival.wait()
        leave.start()
    for leave in leaves:
        leave.wait()


def move_out(arrays):
    anywhere = pl.BlockSpec(memory_space=pl.ANY)
    return pl.pallas_call(
        move_kernel,
        out_shape=tuple(jax.ShapeDtypeStruct(a.shape, a.dtype) for a in arrays),
        in_specs=[anywhere] * len(arrays),
        out_specs=(anywhere,) * len(arrays),
        scratch_shapes=[pltpu.VMEM(a.shape, a.dtype) for a in arrays]
        + [pltpu.SemaphoreType.DMA((16,)), pltpu.SemaphoreType.DMA((16,))],
        compiler_params=pltpu.CompilerParams(vmem_limit_bytes=60 * 1024 * 1024),
    )(*arrays)


def per_device(features, conv_weight, bn_gain, bn_bias, head_weight, labels, raster):
    dma = pltpu.SemaphoreType.DMA
    vmem = pltpu.VMEM
    whole = pl.BlockSpec(memory_space=pltpu.VMEM)
    outs = pl.pallas_call(
        kernel,
        out_shape=(
            jax.ShapeDtypeStruct((TAPS, CI, 128), F32),
            jax.ShapeDtypeStruct((1, 128), F32),
            jax.ShapeDtypeStruct((1, 128), F32),
            jax.ShapeDtypeStruct((4, 128), F32),
            jax.ShapeDtypeStruct((B, H, W, CI), F32),
        ),
        in_specs=[whole, pl.BlockSpec(memory_space=pl.ANY)] + [whole] * 5,
        out_specs=(whole,) * 4 + (pl.BlockSpec(memory_space=pl.ANY),),
        scratch_shapes=[
            vmem((TAPS * CI, CO), BF16),
            vmem((256, 256), BF16),
            vmem((H + 2, B, W, CI), BF16),
            vmem((H + 2, B, W, CI), BF16),
            vmem((H + 2, B, W, CI), BF16),
            vmem((H + 2, 3 * CI, PIX), BF16),
            vmem((H, PIX, CO), F32),
            vmem((H, PIX, CO), F32),
            vmem((H, PIX, CO), BF16),
            vmem((H, PIX, 128), BF16),
            vmem((H, PIX, 128), BF16),
            vmem((H, PIX, 128), BF16),
            vmem((128, CO), F32),
            vmem((CO, 128), BF16),
            vmem((128, CO), BF16),
            vmem((H + 2, B, W, CO), BF16),
            vmem((H + 2, B, W, CO), BF16),
            vmem((H + 2, B, W, CO), BF16),
            vmem((2, B, W, CI), BF16),
            vmem((2, 16, CI), BF16),
            vmem((6, 16, CI), BF16),
            vmem((2, B, W, CO), BF16),
            vmem((2, 16, CO), F32),
            vmem((2, 16, CO), BF16),
            vmem((6, 16, CO), BF16),
            vmem((B, 2, CO), F32),
            vmem((8, 2, CO), F32),
            vmem((16, 2, CO), F32),
            vmem((8, 2, CO), F32),
            vmem((16, 2, CO), F32),
            vmem((2, 4, CO), F32),
            vmem((4, 4, 128), F32),
            vmem((4, 4, 128), F32),
            vmem((4, 4, 128), F32),
            vmem((4, 4, 128), F32),
            vmem((3, 3, CI, CO), F32),
            vmem((3, 3 * CI, CO), F32),
            vmem((3, 3 * CI, 128), F32),
            vmem((3, 3, 128, CO), BF16),
            vmem((3, 3, 128, CO), BF16),
            vmem((2, 192, 128), BF16),
            vmem((2, 48, CO), BF16),
            vmem((2, 48, CO), BF16),
            vmem((2, 192, 128), BF16),
            vmem((2, 48, CO), BF16),
            vmem((2, 48, CO), BF16),
            vmem((2, 384, 128), BF16),
            vmem((2, 96, CO), BF16),
            vmem((2, 96, CO), BF16),
            vmem((2, 384, 128), BF16),
            vmem((2, 96, CO), BF16),
            vmem((2, 96, CO), BF16),
            vmem((3, 4, 96, 128), F32),
            vmem((3, 4, 96, 128), BF16),
            vmem((3, 4, 96, 128), BF16),
            vmem((3, 4, 24, 128), F32),
            vmem((3, 4, 24, 128), F32),
            vmem((3, 4, 24, 128), F32),
            vmem((3, 4, 96, 128), BF16),
            vmem((3, 4, 96, 128), BF16),
            dma((TAPS,)),
            dma((2,)),
            dma((2,)),
            dma((6,)),
            dma((6,)),
            dma((2,)),
            dma((2,)),
            dma((6,)),
            dma((6,)),
        ]
        + [dma((4,))] * 4
        + [
            dma((3,)),
            dma((3,)),
            dma((3, 4)),
            dma((3, 4)),
            dma((4, 3)),
            dma((4, 3)),
            dma((3,)),
            dma((3,)),
            dma((H, B)),
        ],
        compiler_params=pltpu.CompilerParams(
            collective_id=0, has_side_effects=True, vmem_limit_bytes=60 * 1024 * 1024
        ),
        cost_estimate=pl.CostEstimate(
            flops=15_000_000_000, bytes_accessed=8_000_000, transcendentals=300_000
        ),
    )(
        features,
        conv_weight.reshape(TAPS * CI, CO),
        bn_gain.reshape(1, CO),
        bn_bias.reshape(1, CO),
        jnp.transpose(head_weight),
        labels,
        raster,
    )
    grad_weight, grad_gain, grad_bias, grad_head, grad_input = move_out(outs)
    return (
        grad_weight.reshape(3, 3, CI, 128),
        grad_gain.reshape(128),
        grad_bias.reshape(128),
        jnp.transpose(grad_head),
        grad_input,
    )


def solution(mesh):
    in_specs = (
        P(None, "rows", "cols", None),
        P(),
        P(),
        P(),
        P(),
        P(None, "rows", "cols"),
        P(None, "rows", "cols"),
    )
    out_specs = (
        P(None, None, None, "cols"),
        P("cols"),
        P("cols"),
        P("cols", None),
        P(None, "rows", "cols", None),
    )
    return jax.shard_map(
        per_device, mesh=mesh, in_specs=in_specs, out_specs=out_specs, check_vma=False
    )
```

```python
import jax
import jax.numpy as jnp
from jax import lax
from jax.experimental import pallas as pl
from jax.experimental.pallas import tpu as pltpu
from jax.sharding import PartitionSpec as P

F32 = jnp.float32
BF16 = jnp.bfloat16
MESH = pl.DeviceIdType.MESH

B = 4
H = 4
W = 128
CI = 256
CO = 512
TAPS = 9
PIX = H * W
COUNT = 4.0 * 128.0 * 512.0
EPS = 1e-05


def kernel(
    feat,
    wgt_hbm,
    gain_ref,
    bias_ref,
    head_ref,
    labels_ref,
    raster_ref,
    gw_out,
    gg_out,
    gb_out,
    gh_out,
    gi_out,
    wgt,
    identity,
    line_one,
    edge_f,
    edge_part,
    xl,
    xc,
    xr,
    xt,
    conv,
    pgs,
    act,
    sgs,
    onehot,
    pixw,
    head_pad,
    head_tile,
    head_t,
    gl,
    gc,
    gr,
    xrow,
    xedge_out,
    xedge_in,
    grow,
    gedge_f,
    gedge_out,
    gedge_in,
    st_local,
    st8,
    st16,
    tot8,
    tot16,
    hd2,
    hdz_send,
    hdz,
    hdy,
    hdx,
    part,
    with_conv,
    with_one,
    send_a,
    recv_a,
    ring1z_send,
    ring1x_send,
    ring1y_send,
    ring1z_recv,
    ring1x_recv,
    ring1y_recv,
    ring2z_send,
    ring2x_send,
    ring2y_send,
    ring2z_recv,
    ring2x_recv,
    ring2y_recv,
    two_own,
    two_send,
    two_recv,
    three_send,
    three_recv,
    gat3,
    gat2,
    gat_other,
    wsem,
    xrow_s,
    xrow_r,
    xedge_s,
    xedge_r,
    grow_s,
    grow_r,
    gedge_s,
    gedge_r,
    st_s,
    st_r,
    hd_s,
    hd_r,
    a_s,
    a_r,
    ring_s,
    ring_r,
    dir_s,
    dir_r,
    o_s,
    o_r,
    gi_sem,
):
    me = lax.axis_index("rows")
    z = lax.axis_index("cols")
    core = lax.rem(me, 2)
    chip = me // 2
    x = chip // 4
    y = lax.rem(chip, 4)
    rank8 = z * 2 + core
    coords = {"x": x, "y": y, "z": z}

    def flip(value, bits):
        return lax.bitwise_xor(value, jnp.int32(bits)) if bits else value

    def dev8(k):
        return (flip(me, k % 2), flip(z, k // 2))

    def dev16(k):
        return (flip(me, 2 * k), z)

    def on_axis(axis, k):
        return (me, flip(z, k)) if axis == "z" else (flip(me, (2 if axis == "y" else 8) * k), z)

    other = (flip(me, 1), z)
    up = lax.rem(me + 31, 32)
    down = lax.rem(me + 1, 32)
    west = lax.rem(z + 3, 4)
    east = lax.rem(z + 1, 4)
    beyond = lax.rem(me + 31 + 2 * core, 32)

    barrier = pltpu.get_barrier_semaphore()

    def greet(device):
        pl.semaphore_signal(barrier, inc=1, device_id=device, device_id_type=MESH)

    for k in range(1, 8):
        greet(dev8(k))
    for col in (west, z, east):
        greet((beyond, col))
    for k in range(1, 16):
        greet(dev16(k))

    wcopies = []
    for t in range(TAPS):
        rows = pl.ds(t * CI, CI)
        wcopies.append(pltpu.make_async_copy(wgt_hbm.at[rows], wgt.at[rows], wsem.at[t]))
    for copy in wcopies:
        copy.start()

    row_id = lax.broadcasted_iota(jnp.int32, (16, CI), 0)
    left_edge = jnp.zeros((16, CI), F32)
    right_edge = jnp.zeros((16, CI), F32)
    for b in range(B):
        for h in range(H):
            low = feat[b, h, 0:16, :].astype(F32)[0:1, :]
            top = feat[b, h, W - 16 : W, :].astype(F32)[15:16, :]
            here = row_id == h * B + b
            left_edge = jnp.where(here, low, left_edge)
            right_edge = jnp.where(here, top, right_edge)
    xedge_out[0] = right_edge.astype(BF16)
    xedge_out[1] = left_edge.astype(BF16)

    def pick_row(ref, slot, index):
        block = ref[slot].astype(F32)
        ids = lax.broadcasted_iota(jnp.int32, block.shape, 0)
        return jnp.sum(jnp.where(ids == index, block, 0.0), axis=0, keepdims=True)

    def shifted(value, before, after):
        ids = lax.broadcasted_iota(jnp.int32, value.shape, 0)
        left = jnp.where(ids == 0, before, pltpu.roll(value, 1, 0))
        right = jnp.where(ids == W - 1, after, pltpu.roll(value, W - 1, 0))
        return left.astype(BF16), right.astype(BF16)

    def build_x(i, carry):
        b = i // H
        h = lax.rem(i, H)
        left, right = shifted(feat[b, h].astype(F32), 0.0, 0.0)
        xl[h + 1, b] = left
        xc[h + 1, b] = feat[b, h]
        xr[h + 1, b] = right
        return carry

    lax.fori_loop(0, B * H, build_x, 0)

    pl.semaphore_wait(barrier, 25)

    def remote(src, dst, ssem, rsem, device):
        return pltpu.make_async_remote_copy(
            src_ref=src,
            dst_ref=dst,
            send_sem=ssem,
            recv_sem=rsem,
            device_id=device,
            device_id_type=MESH,
        )

    def row_sends(first, last, land, ssem, rsem):
        return [
            remote(last, land.at[0], ssem.at[0], rsem.at[0], (down, z)),
            remote(first, land.at[1], ssem.at[1], rsem.at[1], (up, z)),
        ]

    def edge_sends(out, land, ssem, rsem):
        copies = []
        for side, col in ((0, east), (1, west)):
            for slot, row in ((0, down), (1, me), (2, up)):
                index = side * 3 + slot
                copies.append(
                    remote(
                        out.at[side], land.at[index], ssem.at[index], rsem.at[index], (row, col)
                    )
                )
        return copies

    xrow_copies = row_sends(feat.at[:, 0], feat.at[:, H - 1], xrow, xrow_s, xrow_r)
    for copy in xrow_copies:
        copy.start()
    xedge_copies = edge_sends(xedge_out, xedge_in, xedge_s, xedge_r)
    for copy in xedge_copies:
        copy.start()

    head_pad[...] = jnp.zeros((128, CO), F32)
    head_pad[0:4] = head_ref[...].astype(F32)
    head_t[...] = head_pad[...].astype(BF16)
    head_pad[4:8] = head_ref[...].astype(F32)
    head_tile[...] = jnp.transpose(jnp.concatenate([head_pad[0:8]] * 16, axis=0)).astype(BF16)

    lane_class = lax.rem(lax.broadcasted_iota(jnp.int32, (W, 128), 1), 4).astype(F32)
    identity[...] = jnp.where(
        lax.broadcasted_iota(jnp.int32, (256, 256), 0)
        == lax.broadcasted_iota(jnp.int32, (256, 256), 1),
        1.0,
        0.0,
    ).astype(BF16)

    def turned(value):
        size = value.shape[1]
        return lax.dot_general(
            identity[0:size, 0:size],
            value,
            (((1,), (1,)), ((), ())),
            preferred_element_type=F32,
        )

    def class_marks(i, carry):
        b = i // H
        h = lax.rem(i, H)
        spot = pl.ds(pl.multiple_of(b * W, W), W)
        code = labels_ref[b, pl.ds(h, 1), :] + 4 * raster_ref[b, pl.ds(h, 1), :]
        code = turned(jnp.broadcast_to(code.astype(F32), (128, W)).astype(BF16))
        weight = jnp.where(code > 3.5, 1.0, 0.0)
        marks = jnp.where(code - 4.0 * weight == lane_class, 1.0, 0.0)
        onehot[h, spot] = marks.astype(BF16)
        pixw[h, spot] = ((1.0 + weight) * 0.25).astype(BF16)
        return carry

    lax.fori_loop(0, B * H, class_marks, 0)

    west_ok = jnp.where(z > 0, 1.0, 0.0).astype(F32)
    east_ok = jnp.where(z < 3, 1.0, 0.0).astype(F32)
    up_ok = jnp.where(me > 0, 1.0, 0.0).astype(F32)
    down_ok = jnp.where(me < 31, 1.0, 0.0).astype(F32)

    def build_halo(land, edge_in, left_ref, mid_ref, right_ref):
        def body(b, carry):
            for side, line, ok, src in ((0, 0, up_ok, H - 1), (1, H + 1, down_ok, 0)):
                value = land[side, b].astype(F32) * ok
                slot = 2 * side
                left, right = shifted(
                    value,
                    pick_row(edge_in, slot, src * B + b) * (west_ok * ok),
                    pick_row(edge_in, slot + 3, src * B + b) * (east_ok * ok),
                )
                left_ref[line, b] = left
                mid_ref[line, b] = value.astype(BF16)
                right_ref[line, b] = right
            return carry

        lax.fori_loop(0, B, body, 0)

    for copy in wcopies:
        copy.wait()

    def conv_rows(h, first, count):
        lhs = jnp.concatenate(
            [
                ref[h + first + r].reshape(PIX, CI)
                for r in range(count)
                for ref in (xl, xc, xr)
            ],
            axis=1,
        )
        start = pl.multiple_of(first * 3 * CI, 3 * CI)
        return jnp.dot(lhs, wgt[pl.ds(start, count * 3 * CI), :], preferred_element_type=F32)

    def statistics(h, carry):
        value = conv[h]
        mid = jnp.sum(value, axis=0, keepdims=True) * (1.0 / PIX)
        st_local[h, 0:1] = mid
        st_local[h, 1:2] = jnp.sum((value - mid) ** 2, axis=0, keepdims=True)
        return carry

    def transpose_x(line):
        for c, ref in enumerate((xl, xc, xr)):
            xt[line, c * CI : (c + 1) * CI, :] = turned(ref[line].reshape(PIX, CI)).astype(BF16)
        line_one[line] = jnp.dot(
            xt[line], jnp.ones((PIX, 128), BF16), preferred_element_type=F32
        )

    def set_edges_of(left_ref, right_ref, edge_in, channels):
        def body(i, carry):
            h = i // B
            b = lax.rem(i, B)
            ids = lax.broadcasted_iota(jnp.int32, (16, channels), 0)
            low = pick_row(edge_in, 1, i) * west_ok
            top = pick_row(edge_in, 4, i) * east_ok
            block16 = left_ref[h + 1, b, 0:16].astype(F32)
            left_ref[h + 1, b, 0:16] = jnp.where(ids == 0, low, block16).astype(BF16)
            block16 = right_ref[h + 1, b, W - 16 : W].astype(F32)
            right_ref[h + 1, b, W - 16 : W] = jnp.where(ids == 15, top, block16).astype(BF16)
            return carry

        lax.fori_loop(0, B * H, body, 0)

    def inner_rows(i, carry):
        conv[1 + i] = conv_rows(1 + i, 0, 3)
        return carry

    lax.fori_loop(0, 2, inner_rows, 0)

    def outer_rows(i, carry):
        conv[3 * i] = conv_rows(3 * i, 1 - i, 2)
        return carry

    lax.fori_loop(0, 2, outer_rows, 0)

    for copy in xedge_copies:
        copy.wait_recv()
    set_edges_of(xl, xr, xedge_in, CI)
    for side, ok, c, spot in ((0, west_ok, 0, 0), (1, east_ok, 2, W - 1)):
        edge_f[...] = jnp.zeros((24, CI), F32)
        edge_f[B : B + 16] = xedge_in[3 * side + 1].astype(F32) * ok
        lhs = jnp.concatenate([edge_f[B * r : B * r + 16] for r in range(3)], axis=1)
        taps = jnp.concatenate(
            [wgt[(3 * r + c) * CI : (3 * r + c + 1) * CI, :] for r in range(3)], axis=0
        )
        edge_part[...] = jnp.dot(lhs.astype(BF16), taps, preferred_element_type=F32)

        def add_edges(i, carry, spot=spot):
            h = i // B
            place = pl.ds(lax.rem(i, B) * W + spot, 1)
            conv[h, place] += edge_part[pl.ds(i, 1)]
            return carry

        lax.fori_loop(0, B * H, add_edges, 0)

    def transpose_inner(line, carry):
        transpose_x(line)
        return carry

    lax.fori_loop(1, H + 1, transpose_inner, 0)
    for copy in xrow_copies:
        copy.wait_recv()
    build_halo(xrow, xedge_in, xl, xc, xr)

    def halo_rows(i, carry):
        conv[3 * i] += conv_rows(3 * i, 2 * i, 1)
        return carry

    lax.fori_loop(0, 2, halo_rows, 0)
    lax.fori_loop(0, H, statistics, 0)

    def combine(parts, count):
        total = parts[0][0:1]
        for item in parts[1:]:
            total = total + item[0:1]
        mid = total * (1.0 / len(parts))
        spread_sum = None
        for item in parts:
            term = item[1:2] + count * (item[0:1] - mid) ** 2
            spread_sum = term if spread_sum is None else spread_sum + term
        return mid, spread_sum

    def exchange(size, devices, src_of, land, rank, ssem, rsem):
        def all_of(sem):
            few = land.at[0 : size - 1]
            return pltpu.make_async_copy(few, few, sem)

        def start():
            for k in range(1, size):
                remote(src_of(flip(rank, k)), land.at[rank], ssem, rsem, devices(k)).start()

        return start, lambda: all_of(rsem).wait(), lambda: all_of(ssem).wait()

    def share(size, devices, land, rank, ssem, rsem):
        return exchange(size, devices, lambda j: land.at[rank], land, rank, ssem, rsem)

    def along(axis, src_of, land, ssem, rsem):
        return exchange(
            4, lambda k: on_axis(axis, k), src_of, land, coords[axis], ssem, rsem
        )

    def share_along(axis, land, ssem, rsem):
        return along(axis, lambda j: land.at[coords[axis]], land, ssem, rsem)

    st8_x = share(8, dev8, st8, rank8, st_s.at[0], st_r.at[0])
    st16_x = share(16, dev16, st16, chip, st_s.at[1], st_r.at[1])
    tot8_x = share(8, dev8, tot8, rank8, st_s.at[2], st_r.at[2])
    tot16_x = share(16, dev16, tot16, chip, st_s.at[3], st_r.at[3])
    hd2_copy = remote(hd2.at[core], hd2.at[core], hd_s.at[0], hd_r.at[0], other)
    hdz_x = along("z", lambda j: hdz_send.at[j], hdz, hd_s.at[1], hd_r.at[1])
    hdy_x = share_along("y", hdy, hd_s.at[2], hd_r.at[2])
    hdx_x = share_along("x", hdx, hd_s.at[3], hd_r.at[3])

    mid, m2 = combine([st_local[h] for h in range(H)], float(PIX))
    st8[rank8, 0:1] = mid
    st8[rank8, 1:2] = m2
    st8_x[0]()

    local_mean = mid
    transpose_x(0)
    transpose_x(H + 1)

    def center(h, carry):
        act[h] = (conv[h] - local_mean).astype(BF16)
        return carry

    lax.fori_loop(0, H, center, 0)

    def features_of(r):
        return jnp.concatenate([xt[h + r] for h in range(H)], axis=1)

    def cross_conv(r, carry):
        lhs = features_of(r)
        with_conv[r] = jnp.dot(lhs, act[...].reshape(B * PIX, CO), preferred_element_type=F32)
        with_one[r] = line_one[r] + line_one[r + 1] + line_one[r + 2] + line_one[r + 3]
        return carry

    lax.fori_loop(0, 1, cross_conv, 0)
    st8_x[1]()
    mid, m2 = combine([st8[j] for j in range(8)], float(B * PIX))
    st16[chip, 0:1] = mid
    st16[chip, 1:2] = m2
    st16_x[0]()
    lax.fori_loop(1, 3, cross_conv, 0)
    st16_x[1]()
    mean, m2 = combine([st16[j] for j in range(16)], float(8 * B * PIX))
    rstd = lax.rsqrt(m2 * (1.0 / COUNT) + EPS)
    gain = gain_ref[...]
    bias = bias_ref[...]
    scale = gain * rstd

    def middle(b, carry):
        sum_g, sum_gn = carry
        away = conv[b] - mean
        pre = away * scale + bias
        acted = jnp.maximum(pre, 0.0).astype(BF16)
        act[b] = acted
        logits = jnp.dot(acted, head_tile[...], preferred_element_type=F32)
        expo = jnp.exp(logits)
        total = expo + pltpu.roll(expo, 1, 1)
        total = total + pltpu.roll(total, 2, 1)
        score = (pixw[b].astype(F32) * (expo / total - onehot[b].astype(F32))).astype(BF16)
        sgs[b] = score
        act_grad = jnp.dot(score, head_t[...], preferred_element_type=F32)
        pre_grad = jnp.where(pre > 0.0, act_grad, 0.0)
        pgs[b] = pre_grad
        gc[b + 1] = pre_grad.astype(BF16).reshape(B, W, CO)
        sum_g = sum_g + jnp.sum(pre_grad, axis=0, keepdims=True)
        sum_gn = sum_gn + jnp.sum(pre_grad * away, axis=0, keepdims=True)
        return sum_g, sum_gn

    zero_row = jnp.zeros((1, CO), F32)
    sum_g, sum_gn = lax.fori_loop(0, B, middle, (zero_row, zero_row))

    def add_up(buf, size):
        total = buf[0]
        for j in range(1, size):
            total = total + buf[j]
        return total

    tot8[rank8, 0:1] = sum_g
    tot8[rank8, 1:2] = sum_gn * rstd
    tot8_x[0]()

    def cross_grad(r, carry):
        part[r] = jnp.dot(
            features_of(r),
            gc[1 : H + 1].reshape(B * PIX, CO),
            preferred_element_type=F32,
        ).reshape(3, CI, CO)
        return carry

    def head_part(b, total):
        return total + lax.dot_general(
            sgs[b], act[b], (((0,), (0,)), ((), ())), preferred_element_type=F32
        )

    lax.fori_loop(0, 1, cross_grad, 0)
    tot8_x[1]()
    tot16[chip] = add_up(tot8, 8)
    tot16_x[0]()
    lax.fori_loop(1, 3, cross_grad, 0)
    head_sum = lax.fori_loop(0, B, head_part, jnp.zeros((128, CO), F32))
    hd2[core] = head_sum[0:4, :]
    hd2_copy.start()
    st8_x[2]()
    st16_x[2]()
    for copy in xrow_copies + xedge_copies:
        copy.wait_send()
    tot16_x[1]()
    totals = add_up(tot16, 16)
    off = totals[0:1] * (1.0 / COUNT)
    slope = rstd * totals[1:2] * (1.0 / COUNT)
    st_local[0] = totals
    gb_out[...] = st_local[0, 0:1, pl.ds(pl.multiple_of(z * 128, 128), 128)]
    gg_out[...] = st_local[0, 1:2, pl.ds(pl.multiple_of(z * 128, 128), 128)]

    ORDERS = (("z", "y", "x"), ("x", "z", "y"), ("y", "z", "x"))
    a_copies = [remote(send_a.at[r], recv_a.at[r], a_s.at[r], a_r.at[r], other) for r in range(3)]

    shift = scale * (off + slope * (local_mean - mean))
    turn = scale * slope

    def kernel_grad(r, half):
        pieces = []
        for c in range(3):
            rows = pl.ds(pl.multiple_of(c * CI + half * 128, 128), 128)
            ones = jnp.concatenate([with_one[r, rows, :]] * 4, axis=1)
            pieces.append(
                part[r, c, pl.ds(pl.multiple_of(half * 128, 128), 128), :] * scale
                - with_conv[r, rows, :] * turn
                - ones * shift
            )
        return pieces

    for r in range(3):
        for c, piece in enumerate(kernel_grad(r, 1 - core)):
            send_a[r, c] = piece.astype(BF16)
        a_copies[r].start()

    def conv_grad(i, carry):
        b = lax.rem(i, B)
        h = lax.rem(3 * (i // B), H)
        spot = pl.ds(pl.multiple_of(b * W, W), W)
        away = conv[h, spot] - mean
        value = scale * (pgs[h, spot] - off - away * slope)
        gc[h + 1, b] = value.astype(BF16)
        gl[h + 1, b], gr[h + 1, b] = shifted(value, 0.0, 0.0)
        gedge_f[0, pl.ds(h * B + b, 1)] = value[W - 1 : W, :]
        gedge_f[1, pl.ds(h * B + b, 1)] = value[0:1, :]
        return carry

    ring1_send, ring1_recv = (ring1z_send, ring1x_send, ring1y_send), (
        ring1z_recv,
        ring1x_recv,
        ring1y_recv,
    )
    ring2_send, ring2_recv = (ring2z_send, ring2x_send, ring2y_send), (
        ring2z_recv,
        ring2x_recv,
        ring2y_recv,
    )

    def halves(r):
        return 192 if r == 0 else 48

    def block(r, q, low, high):
        q = lax.rem(q, 4)
        if r == 0:
            return with_conv[r, low:high, pl.ds(pl.multiple_of(q * 128, 128), 128)]
        return with_conv[r, pl.ds(pl.multiple_of(q * 96 + low, 16), high - low), :]

    def around(axis, way):
        step = 1 if way == 0 else 3
        if axis == "z":
            return (me, lax.rem(z + step, 4))
        stride = 2 if axis == "y" else 8
        here = coords[axis]
        return (me + stride * (lax.rem(here + step, 4) - here), z)

    def ring1_copies(r):
        axis = ORDERS[r][0]
        return [
            remote(
                ring1_send[r].at[way],
                ring1_recv[r].at[way],
                ring_s.at[r, way],
                ring_r.at[r, way],
                around(axis, way),
            )
            for way in range(2)
        ]

    def ring2_copies(r):
        axis = ORDERS[r][0]
        return [
            remote(
                ring2_send[r].at[way],
                ring2_recv[r].at[way],
                ring_s.at[r, 2 + way],
                ring_r.at[r, 2 + way],
                around(axis, way),
            )
            for way in range(2)
        ]

    def ring1(r):
        a_copies[r].wait_recv()
        for c, piece in enumerate(kernel_grad(r, core)):
            with_conv[r, c * 128 : (c + 1) * 128] = piece + recv_a[r, c].astype(F32)
        here, half = coords[ORDERS[r][0]], halves(r)
        ring1_send[r][0] = block(r, here + 2, 0, half).astype(BF16)
        ring1_send[r][1] = block(r, here + 2, half, 2 * half).astype(BF16)
        for copy in ring1_copies(r):
            copy.start()

    def ring2(r):
        for copy in ring1_copies(r):
            copy.wait_recv()
        here, half = coords[ORDERS[r][0]], halves(r)
        low = ring1_recv[r][0].astype(F32)
        high = ring1_recv[r][1].astype(F32)
        ring2_send[r][0, 0:half] = (block(r, here + 1, 0, half) + low).astype(BF16)
        ring2_send[r][0, half : 2 * half] = block(r, here + 1, half, 2 * half).astype(BF16)
        ring2_send[r][1, 0:half] = block(r, here + 3, 0, half).astype(BF16)
        ring2_send[r][1, half : 2 * half] = (
            block(r, here + 3, half, 2 * half) + high
        ).astype(BF16)
        for copy in ring2_copies(r):
            copy.start()

    row_axis = ("y", "x", "y")
    second, third, gather3, gather2 = [], [], [], []
    for r in range(3):
        second.append(
            along(
                ORDERS[r][1],
                lambda j, r=r: two_send.at[r, j],
                two_recv.at[r],
                dir_s.at[0, r],
                dir_r.at[0, r],
            )
        )
        third.append(
            along(
                ORDERS[r][2],
                lambda j, r=r: three_send.at[r, j],
                three_recv.at[r],
                dir_s.at[1, r],
                dir_r.at[1, r],
            )
        )
        gather3.append(share_along(ORDERS[r][2], gat3.at[r], dir_s.at[2, r], dir_r.at[2, r]))
        gather2.append(share_along(row_axis[r], gat2.at[r], dir_s.at[3, r], dir_r.at[3, r]))

    def stage2(r):
        for copy in ring2_copies(r):
            copy.wait_recv()
        here, half = coords[ORDERS[r][0]], halves(r)
        total = (
            block(r, here, 0, 2 * half)
            + ring2_recv[r][0].astype(F32)
            + ring2_recv[r][1].astype(F32)
        )
        for q in range(4):
            piece = (
                total[q * 96 : (q + 1) * 96] if r == 0 else total[:, q * 128 : (q + 1) * 128]
            )
            two_own[r, q] = piece
            two_send[r, q] = piece.astype(BF16)
        second[r][0]()

    def stage3(r):
        second[r][1]()
        here = coords[ORDERS[r][1]]
        total = two_own[r, here]
        for k in range(1, 4):
            total = total + two_recv[r, flip(here, k)].astype(F32)
        for q in range(4):
            three_send[r, q] = total[q * 24 : (q + 1) * 24]
        third[r][0]()

    def collect3(r):
        third[r][1]()
        here = coords[ORDERS[r][2]]
        total = three_send[r, here]
        for k in range(1, 4):
            total = total + three_recv[r, flip(here, k)]
        gat3[r, here] = total
        gather3[r][0]()

    def collect2(r):
        gather3[r][1]()
        here = coords[row_axis[r]]
        gat2[r, here] = jnp.concatenate([gat3[r, q] for q in range(4)], axis=0).astype(BF16)
        gather2[r][0]()

    o_copies = [remote(gat2.at[r], gat_other.at[r], o_s.at[r], o_r.at[r], other) for r in range(3)]

    def swap(r):
        gather2[r][1]()
        o_copies[r].start()
        unpack(r, gat2, core)

    def unpack(r, src, half):
        rows = src[r].reshape(384, 128)
        spot = pl.ds(pl.multiple_of(half * 128, 128), 128)
        for c in range(3):
            gw_out[3 * r + c, spot, :] = rows[c * 128 : (c + 1) * 128].astype(F32)

    def unpack_other(r):
        o_copies[r].wait_recv()
        unpack(r, gat_other, 1 - core)

    gi_copies = [
        [
            pltpu.make_async_copy(
                pgs.at[h, pl.ds(b * W, W), pl.ds(0, CI)], gi_out.at[b, h], gi_sem.at[h, b]
            )
            for b in range(B)
        ]
        for h in range(H)
    ]

    def back(h):
        lhs = jnp.concatenate(
            [
                ref[h + r].reshape(PIX, CO)
                for r in range(3)
                for ref in (gl, gc, gr)
            ],
            axis=1,
        )
        flipped = jnp.concatenate(
            [wgt[(TAPS - 1 - t) * CI : (TAPS - t) * CI, :] for t in range(TAPS)], axis=1
        )
        value = lax.dot_general(
            lhs, flipped, (((1,), (1,)), ((), ())), preferred_element_type=F32
        )
        pgs[h, :, 0:CI] = value
        for copy in gi_copies[h]:
            copy.start()

    lax.fori_loop(0, 2 * B, conv_grad, 0)
    grow_copies = row_sends(gc.at[1], gc.at[H], grow, grow_s, grow_r)
    for copy in grow_copies:
        copy.start()
    ring1(0)
    lax.fori_loop(2 * B, 4 * B, conv_grad, 0)
    gedge_out[...] = gedge_f[...].astype(BF16)
    gedge_copies = edge_sends(gedge_out, gedge_in, gedge_s, gedge_r)
    for copy in gedge_copies:
        copy.start()
    ring1(1)
    ring1(2)
    hd2_copy.wait_recv()
    head_pair = hd2[0] + hd2[1]
    for q in range(4):
        hdz_send[q] = head_pair[:, q * 128 : (q + 1) * 128]
    hdz_x[0]()
    ring2(0)
    ring2(1)
    ring2(2)
    for copy in gedge_copies:
        copy.wait_recv()
    set_edges_of(gl, gr, gedge_in, CO)
    hdz_x[1]()
    head_line = hdz_send[z]
    for k in range(1, 4):
        head_line = head_line + hdz[flip(z, k)]
    hdy[y] = head_line
    hdy_x[0]()
    back(1)
    stage2(0)
    stage2(1)
    stage2(2)
    hdy_x[1]()
    hdx[x] = add_up(hdy, 4)
    hdx_x[0]()
    back(2)
    stage3(0)
    stage3(1)
    stage3(2)
    for copy in grow_copies:
        copy.wait_recv()
    build_halo(grow, gedge_in, gl, gc, gr)
    hdx_x[1]()
    gh_out[...] = add_up(hdx, 4)
    collect3(0)
    collect3(1)
    collect3(2)
    back(0)
    collect2(0)
    collect2(1)
    collect2(2)
    back(3)
    swap(0)
    swap(1)
    swap(2)
    unpack_other(0)
    unpack_other(1)

    for copy in [hd2_copy] + grow_copies + gedge_copies + a_copies:
        copy.wait_send()
    for exchanged in [tot8_x, tot16_x, hdz_x, hdy_x, hdx_x] + second + third + gather3 + gather2:
        exchanged[2]()
    for r in range(3):
        for copy in ring1_copies(r) + ring2_copies(r):
            copy.wait_send()
    for line in gi_copies:
        for copy in line:
            copy.wait()
    unpack_other(2)
    for copy in o_copies:
        copy.wait_send()


def move_kernel(*refs):
    count = (len(refs) - 2) // 3
    in_sem, out_sem = refs[-2:]
    arrivals, leaves = [], []
    for src, dst, held in zip(refs[:count], refs[count : 2 * count], refs[2 * count : 3 * count]):
        size = src.shape[0] if len(src.shape) > 2 else 1
        for i in range(size):
            here, there, hold = (src.at[i], dst.at[i], held.at[i]) if size > 1 else (src, dst, held)
            slot = len(arrivals)
            arrivals.append(pltpu.make_async_copy(here, hold, in_sem.at[slot]))
            leaves.append(pltpu.make_async_copy(hold, there, out_sem.at[slot]))
    for copy in arrivals:
        copy.start()
    for arrival, leave in zip(arrivals, leaves):
        arrival.wait()
        leave.start()
    for leave in leaves:
        leave.wait()


def move_out(arrays):
    anywhere = pl.BlockSpec(memory_space=pl.ANY)
    return pl.pallas_call(
        move_kernel,
        out_shape=tuple(jax.ShapeDtypeStruct(a.shape, a.dtype) for a in arrays),
        in_specs=[anywhere] * len(arrays),
        out_specs=(anywhere,) * len(arrays),
        scratch_shapes=[pltpu.VMEM(a.shape, a.dtype) for a in arrays]
        + [pltpu.SemaphoreType.DMA((16,)), pltpu.SemaphoreType.DMA((16,))],
        compiler_params=pltpu.CompilerParams(vmem_limit_bytes=60 * 1024 * 1024),
    )(*arrays)


def per_device(features, conv_weight, bn_gain, bn_bias, head_weight, labels, raster):
    dma = pltpu.SemaphoreType.DMA
    vmem = pltpu.VMEM
    whole = pl.BlockSpec(memory_space=pltpu.VMEM)
    outs = pl.pallas_call(
        kernel,
        out_shape=(
            jax.ShapeDtypeStruct((TAPS, CI, 128), F32),
            jax.ShapeDtypeStruct((1, 128), F32),
            jax.ShapeDtypeStruct((1, 128), F32),
            jax.ShapeDtypeStruct((4, 128), F32),
            jax.ShapeDtypeStruct((B, H, W, CI), F32),
        ),
        in_specs=[whole, pl.BlockSpec(memory_space=pl.ANY)] + [whole] * 5,
        out_specs=(whole,) * 4 + (pl.BlockSpec(memory_space=pl.ANY),),
        scratch_shapes=[
            vmem((TAPS * CI, CO), BF16),
            vmem((256, 256), BF16),
            vmem((H + 2, 3 * CI, 128), F32),
            vmem((24, CI), F32),
            vmem((16, CO), F32),
            vmem((H + 2, B, W, CI), BF16),
            vmem((H + 2, B, W, CI), BF16),
            vmem((H + 2, B, W, CI), BF16),
            vmem((H + 2, 3 * CI, PIX), BF16),
            vmem((H, PIX, CO), F32),
            vmem((H, PIX, CO), F32),
            vmem((H, PIX, CO), BF16),
            vmem((H, PIX, 128), BF16),
            vmem((H, PIX, 128), BF16),
            vmem((H, PIX, 128), BF16),
            vmem((128, CO), F32),
            vmem((CO, 128), BF16),
            vmem((128, CO), BF16),
            vmem((H + 2, B, W, CO), BF16),
            vmem((H + 2, B, W, CO), BF16),
            vmem((H + 2, B, W, CO), BF16),
            vmem((2, B, W, CI), BF16),
            vmem((2, 16, CI), BF16),
            vmem((6, 16, CI), BF16),
            vmem((2, B, W, CO), BF16),
            vmem((2, 16, CO), F32),
            vmem((2, 16, CO), BF16),
            vmem((6, 16, CO), BF16),
            vmem((B, 2, CO), F32),
            vmem((8, 2, CO), F32),
            vmem((16, 2, CO), F32),
            vmem((8, 2, CO), F32),
            vmem((16, 2, CO), F32),
            vmem((2, 4, CO), F32),
            vmem((4, 4, 128), F32),
            vmem((4, 4, 128), F32),
            vmem((4, 4, 128), F32),
            vmem((4, 4, 128), F32),
            vmem((3, 3, CI, CO), F32),
            vmem((3, 3 * CI, CO), F32),
            vmem((3, 3 * CI, 128), F32),
            vmem((3, 3, 128, CO), BF16),
            vmem((3, 3, 128, CO), BF16),
            vmem((2, 192, 128), BF16),
            vmem((2, 48, CO), BF16),
            vmem((2, 48, CO), BF16),
            vmem((2, 192, 128), BF16),
            vmem((2, 48, CO), BF16),
            vmem((2, 48, CO), BF16),
            vmem((2, 384, 128), BF16),
            vmem((2, 96, CO), BF16),
            vmem((2, 96, CO), BF16),
            vmem((2, 384, 128), BF16),
            vmem((2, 96, CO), BF16),
            vmem((2, 96, CO), BF16),
            vmem((3, 4, 96, 128), F32),
            vmem((3, 4, 96, 128), BF16),
            vmem((3, 4, 96, 128), BF16),
            vmem((3, 4, 24, 128), F32),
            vmem((3, 4, 24, 128), F32),
            vmem((3, 4, 24, 128), F32),
            vmem((3, 4, 96, 128), BF16),
            vmem((3, 4, 96, 128), BF16),
            dma((TAPS,)),
            dma((2,)),
            dma((2,)),
            dma((6,)),
            dma((6,)),
            dma((2,)),
            dma((2,)),
            dma((6,)),
            dma((6,)),
        ]
        + [dma((4,))] * 4
        + [
            dma((3,)),
            dma((3,)),
            dma((3, 4)),
            dma((3, 4)),
            dma((4, 3)),
            dma((4, 3)),
            dma((3,)),
            dma((3,)),
            dma((H, B)),
        ],
        compiler_params=pltpu.CompilerParams(
            collective_id=0, has_side_effects=True, vmem_limit_bytes=60 * 1024 * 1024
        ),
        cost_estimate=pl.CostEstimate(
            flops=15_000_000_000, bytes_accessed=8_000_000, transcendentals=300_000
        ),
    )(
        features,
        conv_weight.reshape(TAPS * CI, CO),
        bn_gain.reshape(1, CO),
        bn_bias.reshape(1, CO),
        jnp.transpose(head_weight),
        labels,
        raster,
    )
    grad_weight, grad_gain, grad_bias, grad_head, grad_input = move_out(outs)
    return (
        grad_weight.reshape(3, 3, CI, 128),
        grad_gain.reshape(128),
        grad_bias.reshape(128),
        jnp.transpose(grad_head),
        grad_input,
    )


def solution(mesh):
    in_specs = (
        P(None, "rows", "cols", None),
        P(),
        P(),
        P(),
        P(),
        P(None, "rows", "cols"),
        P(None, "rows", "cols"),
    )
    out_specs = (
        P(None, None, None, "cols"),
        P("cols"),
        P("cols"),
        P("cols", None),
        P(None, "rows", "cols", None),
    )
    return jax.shard_map(
        per_device, mesh=mesh, in_specs=in_specs, out_specs=out_specs, check_vma=False
    )
```

```python
import jax
import jax.numpy as jnp
from jax import lax
from jax.experimental import pallas as pl
from jax.experimental.pallas import tpu as pltpu
from jax.sharding import PartitionSpec as P

F32 = jnp.float32
BF16 = jnp.bfloat16
MESH = pl.DeviceIdType.MESH

B = 4
H = 4
W = 128
CI = 256
CO = 512
TAPS = 9
PIX = H * W
COUNT = 4.0 * 128.0 * 512.0
EPS = 1e-05


def kernel(
    feat,
    wgt_hbm,
    gain_ref,
    bias_ref,
    head_ref,
    labels_ref,
    raster_ref,
    gw_out,
    gg_out,
    gb_out,
    gh_out,
    gi_out,
    wgt,
    identity,
    line_one,
    edge_f,
    edge_part,
    xl,
    xc,
    xr,
    xt,
    conv,
    pgs,
    act,
    sgs,
    onehot,
    pixw,
    head_pad,
    head_tile,
    head_t,
    gl,
    gc,
    gr,
    xrow,
    xedge_out,
    xedge_in,
    grow,
    gedge_f,
    gedge_out,
    gedge_in,
    st_local,
    st8,
    st16,
    tot8,
    tot16,
    hd2,
    hdz_send,
    hdz,
    hdy,
    hdx,
    part,
    with_conv,
    with_one,
    send_a,
    recv_a,
    ring1z_send,
    ring1x_send,
    ring1y_send,
    ring1z_recv,
    ring1x_recv,
    ring1y_recv,
    ring2z_send,
    ring2x_send,
    ring2y_send,
    ring2z_recv,
    ring2x_recv,
    ring2y_recv,
    two_own,
    two_send,
    two_recv,
    three_send,
    three_recv,
    gat3,
    gat2,
    gat_other,
    wsem,
    xrow_s,
    xrow_r,
    xedge_s,
    xedge_r,
    grow_s,
    grow_r,
    gedge_s,
    gedge_r,
    st_s,
    st_r,
    hd_s,
    hd_r,
    a_s,
    a_r,
    ring_s,
    ring_r,
    dir_s,
    dir_r,
    o_s,
    o_r,
    gi_sem,
):
    me = lax.axis_index("rows")
    z = lax.axis_index("cols")
    core = lax.rem(me, 2)
    chip = me // 2
    x = chip // 4
    y = lax.rem(chip, 4)
    rank8 = z * 2 + core
    coords = {"x": x, "y": y, "z": z}

    def flip(value, bits):
        return lax.bitwise_xor(value, jnp.int32(bits)) if bits else value

    def dev8(k):
        return (flip(me, k % 2), flip(z, k // 2))

    def dev16(k):
        return (flip(me, 2 * k), z)

    def on_axis(axis, k):
        return (me, flip(z, k)) if axis == "z" else (flip(me, (2 if axis == "y" else 8) * k), z)

    other = (flip(me, 1), z)
    up = lax.rem(me + 31, 32)
    down = lax.rem(me + 1, 32)
    west = lax.rem(z + 3, 4)
    east = lax.rem(z + 1, 4)
    beyond = lax.rem(me + 31 + 2 * core, 32)

    barrier = pltpu.get_barrier_semaphore()

    def greet(device):
        pl.semaphore_signal(barrier, inc=1, device_id=device, device_id_type=MESH)

    for k in range(1, 8):
        greet(dev8(k))
    for col in (west, z, east):
        greet((beyond, col))
    for k in range(1, 16):
        greet(dev16(k))

    wcopies = []
    for t in range(TAPS):
        rows = pl.ds(t * CI, CI)
        wcopies.append(pltpu.make_async_copy(wgt_hbm.at[rows], wgt.at[rows], wsem.at[t]))
    for copy in wcopies:
        copy.start()

    row_id = lax.broadcasted_iota(jnp.int32, (16, CI), 0)
    left_edge = jnp.zeros((16, CI), F32)
    right_edge = jnp.zeros((16, CI), F32)
    for b in range(B):
        for h in range(H):
            low = feat[b, h, 0:16, :].astype(F32)[0:1, :]
            top = feat[b, h, W - 16 : W, :].astype(F32)[15:16, :]
            here = row_id == h * B + b
            left_edge = jnp.where(here, low, left_edge)
            right_edge = jnp.where(here, top, right_edge)
    xedge_out[0] = right_edge.astype(BF16)
    xedge_out[1] = left_edge.astype(BF16)

    def pick_row(ref, slot, index):
        block = ref[slot].astype(F32)
        ids = lax.broadcasted_iota(jnp.int32, block.shape, 0)
        return jnp.sum(jnp.where(ids == index, block, 0.0), axis=0, keepdims=True)

    def shifted(value, before, after):
        ids = lax.broadcasted_iota(jnp.int32, value.shape, 0)
        left = jnp.where(ids == 0, before, pltpu.roll(value, 1, 0))
        right = jnp.where(ids == W - 1, after, pltpu.roll(value, W - 1, 0))
        return left.astype(BF16), right.astype(BF16)

    def build_x(i, carry):
        b = i // H
        h = lax.rem(i, H)
        left, right = shifted(feat[b, h].astype(F32), 0.0, 0.0)
        xl[h + 1, b] = left
        xc[h + 1, b] = feat[b, h]
        xr[h + 1, b] = right
        return carry

    lax.fori_loop(0, B * H, build_x, 0)

    pl.semaphore_wait(barrier, 25)

    def remote(src, dst, ssem, rsem, device):
        return pltpu.make_async_remote_copy(
            src_ref=src,
            dst_ref=dst,
            send_sem=ssem,
            recv_sem=rsem,
            device_id=device,
            device_id_type=MESH,
        )

    def row_sends(first, last, land, ssem, rsem):
        return [
            remote(last, land.at[0], ssem.at[0], rsem.at[0], (down, z)),
            remote(first, land.at[1], ssem.at[1], rsem.at[1], (up, z)),
        ]

    def edge_sends(out, land, ssem, rsem):
        copies = []
        for side, col in ((0, east), (1, west)):
            for slot, row in ((0, down), (1, me), (2, up)):
                index = side * 3 + slot
                copies.append(
                    remote(
                        out.at[side], land.at[index], ssem.at[index], rsem.at[index], (row, col)
                    )
                )
        return copies

    xrow_copies = row_sends(feat.at[:, 0], feat.at[:, H - 1], xrow, xrow_s, xrow_r)
    for copy in xrow_copies:
        copy.start()
    xedge_copies = edge_sends(xedge_out, xedge_in, xedge_s, xedge_r)
    for copy in xedge_copies:
        copy.start()

    head_pad[...] = jnp.zeros((128, CO), F32)
    head_pad[0:4] = head_ref[...].astype(F32)
    head_t[...] = head_pad[...].astype(BF16)
    head_pad[4:8] = head_ref[...].astype(F32)
    head_tile[...] = jnp.transpose(jnp.concatenate([head_pad[0:8]] * 16, axis=0)).astype(BF16)

    lane_class = lax.rem(lax.broadcasted_iota(jnp.int32, (W, 128), 1), 4).astype(F32)
    identity[...] = jnp.where(
        lax.broadcasted_iota(jnp.int32, (256, 256), 0)
        == lax.broadcasted_iota(jnp.int32, (256, 256), 1),
        1.0,
        0.0,
    ).astype(BF16)

    def turned(value):
        size = value.shape[1]
        return lax.dot_general(
            identity[0:size, 0:size],
            value,
            (((1,), (1,)), ((), ())),
            preferred_element_type=F32,
        )

    def class_marks(i, carry):
        b = i // H
        h = lax.rem(i, H)
        spot = pl.ds(pl.multiple_of(b * W, W), W)
        code = labels_ref[b, pl.ds(h, 1), :] + 4 * raster_ref[b, pl.ds(h, 1), :]
        code = turned(jnp.broadcast_to(code.astype(F32), (128, W)).astype(BF16))
        weight = jnp.where(code > 3.5, 1.0, 0.0)
        marks = jnp.where(code - 4.0 * weight == lane_class, 1.0, 0.0)
        onehot[h, spot] = marks.astype(BF16)
        pixw[h, spot] = ((1.0 + weight) * 0.25).astype(BF16)
        return carry

    lax.fori_loop(0, B * H, class_marks, 0)

    west_ok = jnp.where(z > 0, 1.0, 0.0).astype(F32)
    east_ok = jnp.where(z < 3, 1.0, 0.0).astype(F32)
    up_ok = jnp.where(me > 0, 1.0, 0.0).astype(F32)
    down_ok = jnp.where(me < 31, 1.0, 0.0).astype(F32)

    def build_halo(land, edge_in, left_ref, mid_ref, right_ref):
        def body(b, carry):
            for side, line, ok, src in ((0, 0, up_ok, H - 1), (1, H + 1, down_ok, 0)):
                value = land[side, b].astype(F32) * ok
                slot = 2 * side
                left, right = shifted(
                    value,
                    pick_row(edge_in, slot, src * B + b) * (west_ok * ok),
                    pick_row(edge_in, slot + 3, src * B + b) * (east_ok * ok),
                )
                left_ref[line, b] = left
                mid_ref[line, b] = value.astype(BF16)
                right_ref[line, b] = right
            return carry

        lax.fori_loop(0, B, body, 0)

    for copy in wcopies:
        copy.wait()

    def conv_rows(h, first, count):
        lhs = jnp.concatenate(
            [
                ref[h + first + r].reshape(PIX, CI)
                for r in range(count)
                for ref in (xl, xc, xr)
            ],
            axis=1,
        )
        start = pl.multiple_of(first * 3 * CI, 3 * CI)
        return jnp.dot(lhs, wgt[pl.ds(start, count * 3 * CI), :], preferred_element_type=F32)

    def statistics(h, carry):
        value = conv[h]
        mid = jnp.sum(value, axis=0, keepdims=True) * (1.0 / PIX)
        st_local[h, 0:1] = mid
        st_local[h, 1:2] = jnp.sum((value - mid) ** 2, axis=0, keepdims=True)
        return carry

    def transpose_x(line):
        for c, ref in enumerate((xl, xc, xr)):
            xt[line, c * CI : (c + 1) * CI, :] = turned(ref[line].reshape(PIX, CI)).astype(BF16)
        line_one[line] = jnp.dot(
            xt[line], jnp.ones((PIX, 128), BF16), preferred_element_type=F32
        )

    def set_edges_of(left_ref, right_ref, edge_in, channels):
        def body(i, carry):
            h = i // B
            b = lax.rem(i, B)
            ids = lax.broadcasted_iota(jnp.int32, (16, channels), 0)
            low = pick_row(edge_in, 1, i) * west_ok
            top = pick_row(edge_in, 4, i) * east_ok
            block16 = left_ref[h + 1, b, 0:16].astype(F32)
            left_ref[h + 1, b, 0:16] = jnp.where(ids == 0, low, block16).astype(BF16)
            block16 = right_ref[h + 1, b, W - 16 : W].astype(F32)
            right_ref[h + 1, b, W - 16 : W] = jnp.where(ids == 15, top, block16).astype(BF16)
            return carry

        lax.fori_loop(0, B * H, body, 0)

    def inner_rows(i, carry):
        conv[1 + i] = conv_rows(1 + i, 0, 3)
        return carry

    lax.fori_loop(0, 2, inner_rows, 0)

    def outer_rows(i, carry):
        conv[3 * i] = conv_rows(3 * i, 1 - i, 2)
        return carry

    lax.fori_loop(0, 2, outer_rows, 0)

    for copy in xedge_copies:
        copy.wait_recv()
    set_edges_of(xl, xr, xedge_in, CI)
    for side, ok, c, spot in ((0, west_ok, 0, 0), (1, east_ok, 2, W - 1)):
        edge_f[...] = jnp.zeros((24, CI), F32)
        edge_f[B : B + 16] = xedge_in[3 * side + 1].astype(F32) * ok
        lhs = jnp.concatenate([edge_f[B * r : B * r + 16] for r in range(3)], axis=1)
        taps = jnp.concatenate(
            [wgt[(3 * r + c) * CI : (3 * r + c + 1) * CI, :] for r in range(3)], axis=0
        )
        edge_part[...] = jnp.dot(lhs.astype(BF16), taps, preferred_element_type=F32)

        def add_edges(i, carry, spot=spot):
            h = i // B
            place = pl.ds(lax.rem(i, B) * W + spot, 1)
            conv[h, place] += edge_part[pl.ds(i, 1)]
            return carry

        lax.fori_loop(0, B * H, add_edges, 0)

    def transpose_inner(line, carry):
        transpose_x(line)
        return carry

    lax.fori_loop(1, H + 1, transpose_inner, 0)
    for copy in xrow_copies:
        copy.wait_recv()
    build_halo(xrow, xedge_in, xl, xc, xr)

    def halo_rows(i, carry):
        conv[3 * i] += conv_rows(3 * i, 2 * i, 1)
        return carry

    lax.fori_loop(0, 2, halo_rows, 0)
    lax.fori_loop(0, H, statistics, 0)

    def combine(parts, count):
        total = parts[0][0:1]
        for item in parts[1:]:
            total = total + item[0:1]
        mid = total * (1.0 / len(parts))
        spread_sum = None
        for item in parts:
            term = item[1:2] + count * (item[0:1] - mid) ** 2
            spread_sum = term if spread_sum is None else spread_sum + term
        return mid, spread_sum

    def exchange(size, devices, src_of, land, rank, ssem, rsem):
        def all_of(sem):
            few = land.at[0 : size - 1]
            return pltpu.make_async_copy(few, few, sem)

        def start():
            for k in range(1, size):
                remote(src_of(flip(rank, k)), land.at[rank], ssem, rsem, devices(k)).start()

        return start, lambda: all_of(rsem).wait(), lambda: all_of(ssem).wait()

    def share(size, devices, land, rank, ssem, rsem):
        return exchange(size, devices, lambda j: land.at[rank], land, rank, ssem, rsem)

    def along(axis, src_of, land, ssem, rsem):
        return exchange(
            4, lambda k: on_axis(axis, k), src_of, land, coords[axis], ssem, rsem
        )

    def share_along(axis, land, ssem, rsem):
        return along(axis, lambda j: land.at[coords[axis]], land, ssem, rsem)

    st8_x = share(8, dev8, st8, rank8, st_s.at[0], st_r.at[0])
    st16_x = share(16, dev16, st16, chip, st_s.at[1], st_r.at[1])
    tot8_x = share(8, dev8, tot8, rank8, st_s.at[2], st_r.at[2])
    tot16_x = share(16, dev16, tot16, chip, st_s.at[3], st_r.at[3])
    hd2_copy = remote(hd2.at[core], hd2.at[core], hd_s.at[0], hd_r.at[0], other)
    hdz_x = along("z", lambda j: hdz_send.at[j], hdz, hd_s.at[1], hd_r.at[1])
    hdy_x = share_along("y", hdy, hd_s.at[2], hd_r.at[2])
    hdx_x = share_along("x", hdx, hd_s.at[3], hd_r.at[3])

    mid, m2 = combine([st_local[h] for h in range(H)], float(PIX))
    st8[rank8, 0:1] = mid
    st8[rank8, 1:2] = m2
    st8_x[0]()

    local_mean = mid
    transpose_x(0)
    transpose_x(H + 1)

    def center(h, carry):
        act[h] = (conv[h] - local_mean).astype(BF16)
        return carry

    lax.fori_loop(0, H, center, 0)

    def features_of(r):
        return jnp.concatenate([xt[h + r] for h in range(H)], axis=1)

    def cross_conv(r, carry):
        lhs = features_of(r)
        with_conv[r] = jnp.dot(lhs, act[...].reshape(B * PIX, CO), preferred_element_type=F32)
        with_one[r] = line_one[r] + line_one[r + 1] + line_one[r + 2] + line_one[r + 3]
        return carry

    lax.fori_loop(0, 1, cross_conv, 0)
    st8_x[1]()
    mid, m2 = combine([st8[j] for j in range(8)], float(B * PIX))
    st16[chip, 0:1] = mid
    st16[chip, 1:2] = m2
    st16_x[0]()
    lax.fori_loop(1, 3, cross_conv, 0)
    st16_x[1]()
    mean, m2 = combine([st16[j] for j in range(16)], float(8 * B * PIX))
    rstd = lax.rsqrt(m2 * (1.0 / COUNT) + EPS)
    gain = gain_ref[...]
    bias = bias_ref[...]
    scale = gain * rstd

    def middle(b, carry):
        sum_g, sum_gn = carry
        away = conv[b] - mean
        pre = away * scale + bias
        acted = jnp.maximum(pre, 0.0).astype(BF16)
        act[b] = acted
        logits = jnp.dot(acted, head_tile[...], preferred_element_type=F32)
        expo = jnp.exp(logits)
        total = expo + pltpu.roll(expo, 1, 1)
        total = total + pltpu.roll(total, 2, 1)
        score = (pixw[b].astype(F32) * (expo / total - onehot[b].astype(F32))).astype(BF16)
        sgs[b] = score
        act_grad = jnp.dot(score, head_t[...], preferred_element_type=F32)
        pre_grad = jnp.where(pre > 0.0, act_grad, 0.0)
        pgs[b] = pre_grad
        gc[b + 1] = pre_grad.astype(BF16).reshape(B, W, CO)
        sum_g = sum_g + jnp.sum(pre_grad, axis=0, keepdims=True)
        sum_gn = sum_gn + jnp.sum(pre_grad * away, axis=0, keepdims=True)
        return sum_g, sum_gn

    zero_row = jnp.zeros((1, CO), F32)
    sum_g, sum_gn = lax.fori_loop(0, B, middle, (zero_row, zero_row))

    def add_up(buf, size):
        total = buf[0]
        for j in range(1, size):
            total = total + buf[j]
        return total

    tot8[rank8, 0:1] = sum_g
    tot8[rank8, 1:2] = sum_gn * rstd
    tot8_x[0]()

    def cross_grad(r, carry):
        part[r] = jnp.dot(
            features_of(r),
            gc[1 : H + 1].reshape(B * PIX, CO),
            preferred_element_type=F32,
        ).reshape(3, CI, CO)
        return carry

    def head_part(b, total):
        return total + lax.dot_general(
            sgs[b], act[b], (((0,), (0,)), ((), ())), preferred_element_type=F32
        )

    lax.fori_loop(0, 1, cross_grad, 0)
    tot8_x[1]()
    tot16[chip] = add_up(tot8, 8)
    tot16_x[0]()
    lax.fori_loop(1, 3, cross_grad, 0)
    head_sum = lax.fori_loop(0, B, head_part, jnp.zeros((128, CO), F32))
    hd2[core] = head_sum[0:4, :]
    hd2_copy.start()
    st8_x[2]()
    st16_x[2]()
    for copy in xrow_copies + xedge_copies:
        copy.wait_send()
    tot16_x[1]()
    totals = add_up(tot16, 16)
    off = totals[0:1] * (1.0 / COUNT)
    slope = rstd * totals[1:2] * (1.0 / COUNT)
    st_local[0] = totals
    gb_out[...] = st_local[0, 0:1, pl.ds(pl.multiple_of(z * 128, 128), 128)]
    gg_out[...] = st_local[0, 1:2, pl.ds(pl.multiple_of(z * 128, 128), 128)]

    ORDERS = (("z", "y", "x"), ("x", "z", "y"), ("y", "z", "x"))
    a_copies = [remote(send_a.at[r], recv_a.at[r], a_s.at[r], a_r.at[r], other) for r in range(3)]

    shift = scale * (off + slope * (local_mean - mean))
    turn = scale * slope

    def kernel_grad(r, half):
        pieces = []
        for c in range(3):
            rows = pl.ds(pl.multiple_of(c * CI + half * 128, 128), 128)
            ones = jnp.concatenate([with_one[r, rows, :]] * 4, axis=1)
            pieces.append(
                part[r, c, pl.ds(pl.multiple_of(half * 128, 128), 128), :] * scale
                - with_conv[r, rows, :] * turn
                - ones * shift
            )
        return pieces

    for r in range(3):
        for c, piece in enumerate(kernel_grad(r, 1 - core)):
            send_a[r, c] = piece.astype(BF16)
        a_copies[r].start()

    def conv_grad(i, carry):
        b = lax.rem(i, B)
        h = lax.rem(3 * (i // B), H)
        spot = pl.ds(pl.multiple_of(b * W, W), W)
        away = conv[h, spot] - mean
        value = scale * (pgs[h, spot] - off - away * slope)
        gc[h + 1, b] = value.astype(BF16)
        gl[h + 1, b], gr[h + 1, b] = shifted(value, 0.0, 0.0)
        gedge_f[0, pl.ds(h * B + b, 1)] = value[W - 1 : W, :]
        gedge_f[1, pl.ds(h * B + b, 1)] = value[0:1, :]
        return carry

    ring1_send, ring1_recv = (ring1z_send, ring1x_send, ring1y_send), (
        ring1z_recv,
        ring1x_recv,
        ring1y_recv,
    )
    ring2_send, ring2_recv = (ring2z_send, ring2x_send, ring2y_send), (
        ring2z_recv,
        ring2x_recv,
        ring2y_recv,
    )

    def halves(r):
        return 192 if r == 0 else 48

    def block(r, q, low, high):
        q = lax.rem(q, 4)
        if r == 0:
            return with_conv[r, low:high, pl.ds(pl.multiple_of(q * 128, 128), 128)]
        return with_conv[r, pl.ds(pl.multiple_of(q * 96 + low, 16), high - low), :]

    def around(axis, way):
        step = 1 if way == 0 else 3
        if axis == "z":
            return (me, lax.rem(z + step, 4))
        stride = 2 if axis == "y" else 8
        here = coords[axis]
        return (me + stride * (lax.rem(here + step, 4) - here), z)

    def ring1_copies(r):
        axis = ORDERS[r][0]
        return [
            remote(
                ring1_send[r].at[way],
                ring1_recv[r].at[way],
                ring_s.at[r, way],
                ring_r.at[r, way],
                around(axis, way),
            )
            for way in range(2)
        ]

    def ring2_copies(r):
        axis = ORDERS[r][0]
        return [
            remote(
                ring2_send[r].at[way],
                ring2_recv[r].at[way],
                ring_s.at[r, 2 + way],
                ring_r.at[r, 2 + way],
                around(axis, way),
            )
            for way in range(2)
        ]

    def ring1(r):
        a_copies[r].wait_recv()
        for c, piece in enumerate(kernel_grad(r, core)):
            with_conv[r, c * 128 : (c + 1) * 128] = piece + recv_a[r, c].astype(F32)
        here, half = coords[ORDERS[r][0]], halves(r)
        ring1_send[r][0] = block(r, here + 2, 0, half).astype(BF16)
        ring1_send[r][1] = block(r, here + 2, half, 2 * half).astype(BF16)
        for copy in ring1_copies(r):
            copy.start()

    def ring2(r):
        for copy in ring1_copies(r):
            copy.wait_recv()
        here, half = coords[ORDERS[r][0]], halves(r)
        low = ring1_recv[r][0].astype(F32)
        high = ring1_recv[r][1].astype(F32)
        ring2_send[r][0, 0:half] = (block(r, here + 1, 0, half) + low).astype(BF16)
        ring2_send[r][0, half : 2 * half] = block(r, here + 1, half, 2 * half).astype(BF16)
        ring2_send[r][1, 0:half] = block(r, here + 3, 0, half).astype(BF16)
        ring2_send[r][1, half : 2 * half] = (
            block(r, here + 3, half, 2 * half) + high
        ).astype(BF16)
        for copy in ring2_copies(r):
            copy.start()

    row_axis = ("y", "x", "y")
    second, third, gather3, gather2 = [], [], [], []
    for r in range(3):
        second.append(
            along(
                ORDERS[r][1],
                lambda j, r=r: two_send.at[r, j],
                two_recv.at[r],
                dir_s.at[0, r],
                dir_r.at[0, r],
            )
        )
        third.append(
            along(
                ORDERS[r][2],
                lambda j, r=r: three_send.at[r, j],
                three_recv.at[r],
                dir_s.at[1, r],
                dir_r.at[1, r],
            )
        )
        gather3.append(share_along(ORDERS[r][2], gat3.at[r], dir_s.at[2, r], dir_r.at[2, r]))
        gather2.append(share_along(row_axis[r], gat2.at[r], dir_s.at[3, r], dir_r.at[3, r]))

    def stage2(r):
        for copy in ring2_copies(r):
            copy.wait_recv()
        here, half = coords[ORDERS[r][0]], halves(r)
        total = (
            block(r, here, 0, 2 * half)
            + ring2_recv[r][0].astype(F32)
            + ring2_recv[r][1].astype(F32)
        )
        for q in range(4):
            piece = (
                total[q * 96 : (q + 1) * 96] if r == 0 else total[:, q * 128 : (q + 1) * 128]
            )
            two_own[r, q] = piece
            two_send[r, q] = piece.astype(BF16)
        second[r][0]()

    def stage3(r):
        second[r][1]()
        here = coords[ORDERS[r][1]]
        total = two_own[r, here]
        for k in range(1, 4):
            total = total + two_recv[r, flip(here, k)].astype(F32)
        for q in range(4):
            three_send[r, q] = total[q * 24 : (q + 1) * 24]
        third[r][0]()

    def collect3(r):
        third[r][1]()
        here = coords[ORDERS[r][2]]
        total = three_send[r, here]
        for k in range(1, 4):
            total = total + three_recv[r, flip(here, k)]
        gat3[r, here] = total
        gather3[r][0]()

    def collect2(r):
        gather3[r][1]()
        here = coords[row_axis[r]]
        gat2[r, here] = jnp.concatenate([gat3[r, q] for q in range(4)], axis=0).astype(BF16)
        gather2[r][0]()

    o_copies = [remote(gat2.at[r], gat_other.at[r], o_s.at[r], o_r.at[r], other) for r in range(3)]

    def swap(r):
        gather2[r][1]()
        o_copies[r].start()
        unpack(r, gat2, core)

    def unpack(r, src, half):
        rows = src[r].reshape(384, 128)
        spot = pl.ds(pl.multiple_of(half * 128, 128), 128)
        for c in range(3):
            gw_out[3 * r + c, spot, :] = rows[c * 128 : (c + 1) * 128].astype(F32)

    def unpack_other(r):
        o_copies[r].wait_recv()
        unpack(r, gat_other, 1 - core)

    gi_copies = [
        [
            pltpu.make_async_copy(
                pgs.at[h, pl.ds(b * W, W), pl.ds(0, CI)], gi_out.at[b, h], gi_sem.at[h, b]
            )
            for b in range(B)
        ]
        for h in range(H)
    ]

    def back(h):
        lhs = jnp.concatenate(
            [
                ref[h + r].reshape(PIX, CO)
                for r in range(3)
                for ref in (gl, gc, gr)
            ],
            axis=1,
        )
        flipped = jnp.concatenate(
            [wgt[(TAPS - 1 - t) * CI : (TAPS - t) * CI, :] for t in range(TAPS)], axis=1
        )
        value = lax.dot_general(
            lhs, flipped, (((1,), (1,)), ((), ())), preferred_element_type=F32
        )
        pgs[h, :, 0:CI] = value
        for copy in gi_copies[h]:
            copy.start()

    lax.fori_loop(0, 2 * B, conv_grad, 0)
    ring1(0)
    ring1(1)
    ring1(2)
    lax.fori_loop(2 * B, 4 * B, conv_grad, 0)
    gedge_out[...] = gedge_f[...].astype(BF16)
    gedge_copies = edge_sends(gedge_out, gedge_in, gedge_s, gedge_r)
    for copy in gedge_copies:
        copy.start()
    ring2(0)
    ring2(1)
    ring2(2)
    grow_copies = row_sends(gc.at[1], gc.at[H], grow, grow_s, grow_r)
    for copy in grow_copies:
        copy.start()
    hd2_copy.wait_recv()
    head_pair = hd2[0] + hd2[1]
    for q in range(4):
        hdz_send[q] = head_pair[:, q * 128 : (q + 1) * 128]
    hdz_x[0]()
    for copy in gedge_copies:
        copy.wait_recv()
    set_edges_of(gl, gr, gedge_in, CO)
    back(1)
    stage2(0)
    stage2(1)
    stage2(2)
    hdz_x[1]()
    head_line = hdz_send[z]
    for k in range(1, 4):
        head_line = head_line + hdz[flip(z, k)]
    hdy[y] = head_line
    hdy_x[0]()
    back(2)
    stage3(0)
    stage3(1)
    stage3(2)
    hdy_x[1]()
    hdx[x] = add_up(hdy, 4)
    hdx_x[0]()
    collect3(0)
    collect3(1)
    collect3(2)
    for copy in grow_copies:
        copy.wait_recv()
    build_halo(grow, gedge_in, gl, gc, gr)
    back(0)
    collect2(0)
    collect2(1)
    collect2(2)
    hdx_x[1]()
    gh_out[...] = add_up(hdx, 4)
    back(3)
    swap(0)
    swap(1)
    swap(2)
    unpack_other(0)
    unpack_other(1)

    for copy in [hd2_copy] + grow_copies + gedge_copies + a_copies:
        copy.wait_send()
    for exchanged in [tot8_x, tot16_x, hdz_x, hdy_x, hdx_x] + second + third + gather3 + gather2:
        exchanged[2]()
    for r in range(3):
        for copy in ring1_copies(r) + ring2_copies(r):
            copy.wait_send()
    for line in gi_copies:
        for copy in line:
            copy.wait()
    unpack_other(2)
    for copy in o_copies:
        copy.wait_send()


def move_kernel(*refs):
    count = (len(refs) - 2) // 3
    in_sem, out_sem = refs[-2:]
    arrivals, leaves = [], []
    for src, dst, held in zip(refs[:count], refs[count : 2 * count], refs[2 * count : 3 * count]):
        size = src.shape[0] if len(src.shape) > 2 else 1
        for i in range(size):
            here, there, hold = (src.at[i], dst.at[i], held.at[i]) if size > 1 else (src, dst, held)
            slot = len(arrivals)
            arrivals.append(pltpu.make_async_copy(here, hold, in_sem.at[slot]))
            leaves.append(pltpu.make_async_copy(hold, there, out_sem.at[slot]))
    for copy in arrivals:
        copy.start()
    for arrival, leave in zip(arrivals, leaves):
        arrival.wait()
        leave.start()
    for leave in leaves:
        leave.wait()


def move_out(arrays):
    anywhere = pl.BlockSpec(memory_space=pl.ANY)
    return pl.pallas_call(
        move_kernel,
        out_shape=tuple(jax.ShapeDtypeStruct(a.shape, a.dtype) for a in arrays),
        in_specs=[anywhere] * len(arrays),
        out_specs=(anywhere,) * len(arrays),
        scratch_shapes=[pltpu.VMEM(a.shape, a.dtype) for a in arrays]
        + [pltpu.SemaphoreType.DMA((16,)), pltpu.SemaphoreType.DMA((16,))],
        compiler_params=pltpu.CompilerParams(vmem_limit_bytes=60 * 1024 * 1024),
    )(*arrays)


def per_device(features, conv_weight, bn_gain, bn_bias, head_weight, labels, raster):
    dma = pltpu.SemaphoreType.DMA
    vmem = pltpu.VMEM
    whole = pl.BlockSpec(memory_space=pltpu.VMEM)
    outs = pl.pallas_call(
        kernel,
        out_shape=(
            jax.ShapeDtypeStruct((TAPS, CI, 128), F32),
            jax.ShapeDtypeStruct((1, 128), F32),
            jax.ShapeDtypeStruct((1, 128), F32),
            jax.ShapeDtypeStruct((4, 128), F32),
            jax.ShapeDtypeStruct((B, H, W, CI), F32),
        ),
        in_specs=[whole, pl.BlockSpec(memory_space=pl.ANY)] + [whole] * 5,
        out_specs=(whole,) * 4 + (pl.BlockSpec(memory_space=pl.ANY),),
        scratch_shapes=[
            vmem((TAPS * CI, CO), BF16),
            vmem((256, 256), BF16),
            vmem((H + 2, 3 * CI, 128), F32),
            vmem((24, CI), F32),
            vmem((16, CO), F32),
            vmem((H + 2, B, W, CI), BF16),
            vmem((H + 2, B, W, CI), BF16),
            vmem((H + 2, B, W, CI), BF16),
            vmem((H + 2, 3 * CI, PIX), BF16),
            vmem((H, PIX, CO), F32),
            vmem((H, PIX, CO), F32),
            vmem((H, PIX, CO), BF16),
            vmem((H, PIX, 128), BF16),
            vmem((H, PIX, 128), BF16),
            vmem((H, PIX, 128), BF16),
            vmem((128, CO), F32),
            vmem((CO, 128), BF16),
            vmem((128, CO), BF16),
            vmem((H + 2, B, W, CO), BF16),
            vmem((H + 2, B, W, CO), BF16),
            vmem((H + 2, B, W, CO), BF16),
            vmem((2, B, W, CI), BF16),
            vmem((2, 16, CI), BF16),
            vmem((6, 16, CI), BF16),
            vmem((2, B, W, CO), BF16),
            vmem((2, 16, CO), F32),
            vmem((2, 16, CO), BF16),
            vmem((6, 16, CO), BF16),
            vmem((B, 2, CO), F32),
            vmem((8, 2, CO), F32),
            vmem((16, 2, CO), F32),
            vmem((8, 2, CO), F32),
            vmem((16, 2, CO), F32),
            vmem((2, 4, CO), F32),
            vmem((4, 4, 128), F32),
            vmem((4, 4, 128), F32),
            vmem((4, 4, 128), F32),
            vmem((4, 4, 128), F32),
            vmem((3, 3, CI, CO), F32),
            vmem((3, 3 * CI, CO), F32),
            vmem((3, 3 * CI, 128), F32),
            vmem((3, 3, 128, CO), BF16),
            vmem((3, 3, 128, CO), BF16),
            vmem((2, 192, 128), BF16),
            vmem((2, 48, CO), BF16),
            vmem((2, 48, CO), BF16),
            vmem((2, 192, 128), BF16),
            vmem((2, 48, CO), BF16),
            vmem((2, 48, CO), BF16),
            vmem((2, 384, 128), BF16),
            vmem((2, 96, CO), BF16),
            vmem((2, 96, CO), BF16),
            vmem((2, 384, 128), BF16),
            vmem((2, 96, CO), BF16),
            vmem((2, 96, CO), BF16),
            vmem((3, 4, 96, 128), F32),
            vmem((3, 4, 96, 128), BF16),
            vmem((3, 4, 96, 128), BF16),
            vmem((3, 4, 24, 128), F32),
            vmem((3, 4, 24, 128), F32),
            vmem((3, 4, 24, 128), F32),
            vmem((3, 4, 96, 128), BF16),
            vmem((3, 4, 96, 128), BF16),
            dma((TAPS,)),
            dma((2,)),
            dma((2,)),
            dma((6,)),
            dma((6,)),
            dma((2,)),
            dma((2,)),
            dma((6,)),
            dma((6,)),
        ]
        + [dma((4,))] * 4
        + [
            dma((3,)),
            dma((3,)),
            dma((3, 4)),
            dma((3, 4)),
            dma((4, 3)),
            dma((4, 3)),
            dma((3,)),
            dma((3,)),
            dma((H, B)),
        ],
        compiler_params=pltpu.CompilerParams(
            collective_id=0, has_side_effects=True, vmem_limit_bytes=60 * 1024 * 1024
        ),
        cost_estimate=pl.CostEstimate(
            flops=15_000_000_000, bytes_accessed=8_000_000, transcendentals=300_000
        ),
    )(
        features,
        conv_weight.reshape(TAPS * CI, CO),
        bn_gain.reshape(1, CO),
        bn_bias.reshape(1, CO),
        jnp.transpose(head_weight),
        labels,
        raster,
    )
    grad_weight, grad_gain, grad_bias, grad_head, grad_input = move_out(outs)
    return (
        grad_weight.reshape(3, 3, CI, 128),
        grad_gain.reshape(128),
        grad_bias.reshape(128),
        jnp.transpose(grad_head),
        grad_input,
    )


def solution(mesh):
    in_specs = (
        P(None, "rows", "cols", None),
        P(),
        P(),
        P(),
        P(),
        P(None, "rows", "cols"),
        P(None, "rows", "cols"),
    )
    out_specs = (
        P(None, None, None, "cols"),
        P("cols"),
        P("cols"),
        P("cols", None),
        P(None, "rows", "cols", None),
    )
    return jax.shard_map(
        per_device, mesh=mesh, in_specs=in_specs, out_specs=out_specs, check_vma=False
    )
```

```python
import jax
import jax.numpy as jnp
from jax import lax
from jax.experimental import pallas as pl
from jax.experimental.pallas import tpu as pltpu
from jax.sharding import PartitionSpec as P

F32 = jnp.float32
BF16 = jnp.bfloat16
MESH = pl.DeviceIdType.MESH

B = 4
H = 4
W = 128
CI = 256
CO = 512
TAPS = 9
PIX = H * W
COUNT = 4.0 * 128.0 * 512.0
EPS = 1e-05


def kernel(
    feat,
    wgt_hbm,
    gain_ref,
    bias_ref,
    head_ref,
    labels_ref,
    raster_ref,
    gat2,
    gat_other,
    gg_out,
    gb_out,
    gh_out,
    gi_out,
    wgt,
    identity,
    line_one,
    edge_f,
    edge_part,
    xl,
    xc,
    xr,
    xt,
    conv,
    pgs,
    act,
    sgs,
    onehot,
    pixw,
    head_pad,
    head_tile,
    head_t,
    gl,
    gc,
    gr,
    xrow,
    xedge_out,
    xedge_in,
    grow,
    gedge_f,
    gedge_out,
    gedge_in,
    st_local,
    st8,
    st16,
    tot8,
    tot16,
    hd2,
    hdz_send,
    hdz,
    hdy,
    hdx,
    part,
    with_conv,
    with_one,
    send_a,
    recv_a,
    ring1z_send,
    ring1x_send,
    ring1y_send,
    ring1z_recv,
    ring1x_recv,
    ring1y_recv,
    ring2z_send,
    ring2x_send,
    ring2y_send,
    ring2z_recv,
    ring2x_recv,
    ring2y_recv,
    two_own,
    two_send,
    two_recv,
    three_send,
    three_recv,
    gat3,
    wsem,
    xrow_s,
    xrow_r,
    xedge_s,
    xedge_r,
    grow_s,
    grow_r,
    gedge_s,
    gedge_r,
    st_s,
    st_r,
    hd_s,
    hd_r,
    a_s,
    a_r,
    ring_s,
    ring_r,
    dir_s,
    dir_r,
    o_s,
    o_r,
    gi_sem,
):
    me = lax.axis_index("rows")
    z = lax.axis_index("cols")
    core = lax.rem(me, 2)
    chip = me // 2
    x = chip // 4
    y = lax.rem(chip, 4)
    rank8 = z * 2 + core
    coords = {"x": x, "y": y, "z": z}

    def flip(value, bits):
        return lax.bitwise_xor(value, jnp.int32(bits)) if bits else value

    def dev8(k):
        return (flip(me, k % 2), flip(z, k // 2))

    def dev16(k):
        return (flip(me, 2 * k), z)

    def on_axis(axis, k):
        return (me, flip(z, k)) if axis == "z" else (flip(me, (2 if axis == "y" else 8) * k), z)

    other = (flip(me, 1), z)
    up = lax.rem(me + 31, 32)
    down = lax.rem(me + 1, 32)
    west = lax.rem(z + 3, 4)
    east = lax.rem(z + 1, 4)
    beyond = lax.rem(me + 31 + 2 * core, 32)

    barrier = pltpu.get_barrier_semaphore()

    def greet(device):
        pl.semaphore_signal(barrier, inc=1, device_id=device, device_id_type=MESH)

    for k in range(1, 8):
        greet(dev8(k))
    for col in (west, z, east):
        greet((beyond, col))
    for k in range(1, 16):
        greet(dev16(k))

    wcopies = []
    for t in range(TAPS):
        rows = pl.ds(t * CI, CI)
        wcopies.append(pltpu.make_async_copy(wgt_hbm.at[rows], wgt.at[rows], wsem.at[t]))
    for copy in wcopies:
        copy.start()

    row_id = lax.broadcasted_iota(jnp.int32, (16, CI), 0)
    left_edge = jnp.zeros((16, CI), F32)
    right_edge = jnp.zeros((16, CI), F32)
    for b in range(B):
        for h in range(H):
            low = feat[b, h, 0:16, :].astype(F32)[0:1, :]
            top = feat[b, h, W - 16 : W, :].astype(F32)[15:16, :]
            here = row_id == h * B + b
            left_edge = jnp.where(here, low, left_edge)
            right_edge = jnp.where(here, top, right_edge)
    xedge_out[0] = right_edge.astype(BF16)
    xedge_out[1] = left_edge.astype(BF16)

    def pick_row(ref, slot, index):
        block = ref[slot].astype(F32)
        ids = lax.broadcasted_iota(jnp.int32, block.shape, 0)
        return jnp.sum(jnp.where(ids == index, block, 0.0), axis=0, keepdims=True)

    def shifted(value, before, after):
        ids = lax.broadcasted_iota(jnp.int32, value.shape, 0)
        left = jnp.where(ids == 0, before, pltpu.roll(value, 1, 0))
        right = jnp.where(ids == W - 1, after, pltpu.roll(value, W - 1, 0))
        return left.astype(BF16), right.astype(BF16)

    def build_x(i, carry):
        b = i // H
        h = lax.rem(i, H)
        left, right = shifted(feat[b, h].astype(F32), 0.0, 0.0)
        xl[h + 1, b] = left
        xc[h + 1, b] = feat[b, h]
        xr[h + 1, b] = right
        return carry

    lax.fori_loop(0, B * H, build_x, 0)

    pl.semaphore_wait(barrier, 25)

    def remote(src, dst, ssem, rsem, device):
        return pltpu.make_async_remote_copy(
            src_ref=src,
            dst_ref=dst,
            send_sem=ssem,
            recv_sem=rsem,
            device_id=device,
            device_id_type=MESH,
        )

    def row_sends(first, last, land, ssem, rsem):
        return [
            remote(last, land.at[0], ssem.at[0], rsem.at[0], (down, z)),
            remote(first, land.at[1], ssem.at[1], rsem.at[1], (up, z)),
        ]

    def edge_sends(out, land, ssem, rsem):
        copies = []
        for side, col in ((0, east), (1, west)):
            for slot, row in ((0, down), (1, me), (2, up)):
                index = side * 3 + slot
                copies.append(
                    remote(
                        out.at[side], land.at[index], ssem.at[index], rsem.at[index], (row, col)
                    )
                )
        return copies

    xrow_copies = row_sends(feat.at[:, 0], feat.at[:, H - 1], xrow, xrow_s, xrow_r)
    for copy in xrow_copies:
        copy.start()
    xedge_copies = edge_sends(xedge_out, xedge_in, xedge_s, xedge_r)
    for copy in xedge_copies:
        copy.start()

    head_pad[...] = jnp.zeros((128, CO), F32)
    head_pad[0:4] = head_ref[...].astype(F32)
    head_t[...] = head_pad[...].astype(BF16)
    head_pad[4:8] = head_ref[...].astype(F32)
    head_tile[...] = jnp.transpose(jnp.concatenate([head_pad[0:8]] * 16, axis=0)).astype(BF16)

    lane_class = lax.rem(lax.broadcasted_iota(jnp.int32, (W, 128), 1), 4).astype(F32)
    identity[...] = jnp.where(
        lax.broadcasted_iota(jnp.int32, (256, 256), 0)
        == lax.broadcasted_iota(jnp.int32, (256, 256), 1),
        1.0,
        0.0,
    ).astype(BF16)

    def turned(value):
        size = value.shape[1]
        return lax.dot_general(
            identity[0:size, 0:size],
            value,
            (((1,), (1,)), ((), ())),
            preferred_element_type=F32,
        )

    def class_marks(i, carry):
        b = i // H
        h = lax.rem(i, H)
        spot = pl.ds(pl.multiple_of(b * W, W), W)
        code = labels_ref[b, pl.ds(h, 1), :] + 4 * raster_ref[b, pl.ds(h, 1), :]
        code = turned(jnp.broadcast_to(code.astype(F32), (128, W)).astype(BF16))
        weight = jnp.where(code > 3.5, 1.0, 0.0)
        marks = jnp.where(code - 4.0 * weight == lane_class, 1.0, 0.0)
        onehot[h, spot] = marks.astype(BF16)
        pixw[h, spot] = ((1.0 + weight) * 0.25).astype(BF16)
        return carry

    lax.fori_loop(0, B * H, class_marks, 0)

    west_ok = jnp.where(z > 0, 1.0, 0.0).astype(F32)
    east_ok = jnp.where(z < 3, 1.0, 0.0).astype(F32)
    up_ok = jnp.where(me > 0, 1.0, 0.0).astype(F32)
    down_ok = jnp.where(me < 31, 1.0, 0.0).astype(F32)

    def build_halo(land, edge_in, left_ref, mid_ref, right_ref):
        def body(b, carry):
            for side, line, ok, src in ((0, 0, up_ok, H - 1), (1, H + 1, down_ok, 0)):
                value = land[side, b].astype(F32) * ok
                slot = 2 * side
                left, right = shifted(
                    value,
                    pick_row(edge_in, slot, src * B + b) * (west_ok * ok),
                    pick_row(edge_in, slot + 3, src * B + b) * (east_ok * ok),
                )
                left_ref[line, b] = left
                mid_ref[line, b] = value.astype(BF16)
                right_ref[line, b] = right
            return carry

        lax.fori_loop(0, B, body, 0)

    for copy in wcopies:
        copy.wait()

    def conv_rows(h, first, count):
        lhs = jnp.concatenate(
            [
                ref[h + first + r].reshape(PIX, CI)
                for r in range(count)
                for ref in (xl, xc, xr)
            ],
            axis=1,
        )
        start = pl.multiple_of(first * 3 * CI, 3 * CI)
        return jnp.dot(lhs, wgt[pl.ds(start, count * 3 * CI), :], preferred_element_type=F32)

    def statistics(h, carry):
        value = conv[h]
        mid = jnp.sum(value, axis=0, keepdims=True) * (1.0 / PIX)
        st_local[h, 0:1] = mid
        st_local[h, 1:2] = jnp.sum((value - mid) ** 2, axis=0, keepdims=True)
        return carry

    def transpose_x(line):
        for c, ref in enumerate((xl, xc, xr)):
            xt[line, c * CI : (c + 1) * CI, :] = turned(ref[line].reshape(PIX, CI)).astype(BF16)
        line_one[line] = jnp.dot(
            xt[line], jnp.ones((PIX, 128), BF16), preferred_element_type=F32
        )

    def set_edges_of(left_ref, right_ref, edge_in, channels):
        def body(i, carry):
            h = i // B
            b = lax.rem(i, B)
            ids = lax.broadcasted_iota(jnp.int32, (16, channels), 0)
            low = pick_row(edge_in, 1, i) * west_ok
            top = pick_row(edge_in, 4, i) * east_ok
            block16 = left_ref[h + 1, b, 0:16].astype(F32)
            left_ref[h + 1, b, 0:16] = jnp.where(ids == 0, low, block16).astype(BF16)
            block16 = right_ref[h + 1, b, W - 16 : W].astype(F32)
            right_ref[h + 1, b, W - 16 : W] = jnp.where(ids == 15, top, block16).astype(BF16)
            return carry

        lax.fori_loop(0, B * H, body, 0)

    def inner_rows(i, carry):
        conv[1 + i] = conv_rows(1 + i, 0, 3)
        return carry

    lax.fori_loop(0, 2, inner_rows, 0)

    def outer_rows(i, carry):
        conv[3 * i] = conv_rows(3 * i, 1 - i, 2)
        return carry

    lax.fori_loop(0, 2, outer_rows, 0)

    for copy in xedge_copies:
        copy.wait_recv()
    set_edges_of(xl, xr, xedge_in, CI)
    for side, ok, c, spot in ((0, west_ok, 0, 0), (1, east_ok, 2, W - 1)):
        edge_f[...] = jnp.zeros((24, CI), F32)
        edge_f[B : B + 16] = xedge_in[3 * side + 1].astype(F32) * ok
        lhs = jnp.concatenate([edge_f[B * r : B * r + 16] for r in range(3)], axis=1)
        taps = jnp.concatenate(
            [wgt[(3 * r + c) * CI : (3 * r + c + 1) * CI, :] for r in range(3)], axis=0
        )
        edge_part[...] = jnp.dot(lhs.astype(BF16), taps, preferred_element_type=F32)

        def add_edges(i, carry, spot=spot):
            h = i // B
            place = pl.ds(lax.rem(i, B) * W + spot, 1)
            conv[h, place] += edge_part[pl.ds(i, 1)]
            return carry

        lax.fori_loop(0, B * H, add_edges, 0)

    def transpose_inner(line, carry):
        transpose_x(line)
        return carry

    lax.fori_loop(1, H + 1, transpose_inner, 0)
    for copy in xrow_copies:
        copy.wait_recv()
    build_halo(xrow, xedge_in, xl, xc, xr)

    def halo_rows(i, carry):
        conv[3 * i] += conv_rows(3 * i, 2 * i, 1)
        return carry

    lax.fori_loop(0, 2, halo_rows, 0)
    lax.fori_loop(0, H, statistics, 0)

    def combine(parts, count):
        total = parts[0][0:1]
        for item in parts[1:]:
            total = total + item[0:1]
        mid = total * (1.0 / len(parts))
        spread_sum = None
        for item in parts:
            term = item[1:2] + count * (item[0:1] - mid) ** 2
            spread_sum = term if spread_sum is None else spread_sum + term
        return mid, spread_sum

    def exchange(size, devices, src_of, land, rank, ssem, rsem):
        def all_of(sem):
            few = land.at[0 : size - 1]
            return pltpu.make_async_copy(few, few, sem)

        def start():
            for k in range(1, size):
                remote(src_of(flip(rank, k)), land.at[rank], ssem, rsem, devices(k)).start()

        return start, lambda: all_of(rsem).wait(), lambda: all_of(ssem).wait()

    def share(size, devices, land, rank, ssem, rsem):
        return exchange(size, devices, lambda j: land.at[rank], land, rank, ssem, rsem)

    def along(axis, src_of, land, ssem, rsem):
        return exchange(
            4, lambda k: on_axis(axis, k), src_of, land, coords[axis], ssem, rsem
        )

    def share_along(axis, land, ssem, rsem):
        return along(axis, lambda j: land.at[coords[axis]], land, ssem, rsem)

    st8_x = share(8, dev8, st8, rank8, st_s.at[0], st_r.at[0])
    st16_x = share(16, dev16, st16, chip, st_s.at[1], st_r.at[1])
    tot8_x = share(8, dev8, tot8, rank8, st_s.at[2], st_r.at[2])
    tot16_x = share(16, dev16, tot16, chip, st_s.at[3], st_r.at[3])
    hd2_copy = remote(hd2.at[core], hd2.at[core], hd_s.at[0], hd_r.at[0], other)
    hdz_x = along("z", lambda j: hdz_send.at[j], hdz, hd_s.at[1], hd_r.at[1])
    hdy_x = share_along("y", hdy, hd_s.at[2], hd_r.at[2])
    hdx_x = share_along("x", hdx, hd_s.at[3], hd_r.at[3])

    mid, m2 = combine([st_local[h] for h in range(H)], float(PIX))
    st8[rank8, 0:1] = mid
    st8[rank8, 1:2] = m2
    st8_x[0]()

    local_mean = mid
    transpose_x(0)
    transpose_x(H + 1)

    def center(h, carry):
        act[h] = (conv[h] - local_mean).astype(BF16)
        return carry

    lax.fori_loop(0, H, center, 0)

    def features_of(r):
        return jnp.concatenate([xt[h + r] for h in range(H)], axis=1)

    def cross_conv(r, carry):
        lhs = features_of(r)
        with_conv[r] = jnp.dot(lhs, act[...].reshape(B * PIX, CO), preferred_element_type=F32)
        with_one[r] = line_one[r] + line_one[r + 1] + line_one[r + 2] + line_one[r + 3]
        return carry

    lax.fori_loop(0, 1, cross_conv, 0)
    st8_x[1]()
    mid, m2 = combine([st8[j] for j in range(8)], float(B * PIX))
    st16[chip, 0:1] = mid
    st16[chip, 1:2] = m2
    st16_x[0]()
    lax.fori_loop(1, 3, cross_conv, 0)
    st16_x[1]()
    mean, m2 = combine([st16[j] for j in range(16)], float(8 * B * PIX))
    rstd = lax.rsqrt(m2 * (1.0 / COUNT) + EPS)
    gain = gain_ref[...]
    bias = bias_ref[...]
    scale = gain * rstd

    def middle(b, carry):
        sum_g, sum_gn = carry
        away = conv[b] - mean
        pre = away * scale + bias
        acted = jnp.maximum(pre, 0.0).astype(BF16)
        act[b] = acted
        logits = jnp.dot(acted, head_tile[...], preferred_element_type=F32)
        expo = jnp.exp(logits)
        total = expo + pltpu.roll(expo, 1, 1)
        total = total + pltpu.roll(total, 2, 1)
        score = (pixw[b].astype(F32) * (expo / total - onehot[b].astype(F32))).astype(BF16)
        sgs[b] = score
        act_grad = jnp.dot(score, head_t[...], preferred_element_type=F32)
        pre_grad = jnp.where(pre > 0.0, act_grad, 0.0)
        pgs[b] = pre_grad
        gc[b + 1] = pre_grad.astype(BF16).reshape(B, W, CO)
        sum_g = sum_g + jnp.sum(pre_grad, axis=0, keepdims=True)
        sum_gn = sum_gn + jnp.sum(pre_grad * away, axis=0, keepdims=True)
        return sum_g, sum_gn

    zero_row = jnp.zeros((1, CO), F32)
    sum_g, sum_gn = lax.fori_loop(0, B, middle, (zero_row, zero_row))

    def add_up(buf, size):
        total = buf[0]
        for j in range(1, size):
            total = total + buf[j]
        return total

    tot8[rank8, 0:1] = sum_g
    tot8[rank8, 1:2] = sum_gn * rstd
    tot8_x[0]()

    def cross_grad(r, carry):
        part[r] = jnp.dot(
            features_of(r),
            gc[1 : H + 1].reshape(B * PIX, CO),
            preferred_element_type=F32,
        ).reshape(3, CI, CO)
        return carry

    def head_part(b, total):
        return total + lax.dot_general(
            sgs[b], act[b], (((0,), (0,)), ((), ())), preferred_element_type=F32
        )

    lax.fori_loop(0, 1, cross_grad, 0)
    tot8_x[1]()
    tot16[chip] = add_up(tot8, 8)
    tot16_x[0]()
    lax.fori_loop(1, 3, cross_grad, 0)
    head_sum = lax.fori_loop(0, B, head_part, jnp.zeros((128, CO), F32))
    hd2[core] = head_sum[0:4, :]
    hd2_copy.start()
    st8_x[2]()
    st16_x[2]()
    for copy in xrow_copies + xedge_copies:
        copy.wait_send()
    tot16_x[1]()
    totals = add_up(tot16, 16)
    off = totals[0:1] * (1.0 / COUNT)
    slope = rstd * totals[1:2] * (1.0 / COUNT)
    st_local[0] = totals
    gb_out[...] = st_local[0, 0:1, pl.ds(pl.multiple_of(z * 128, 128), 128)]
    gg_out[...] = st_local[0, 1:2, pl.ds(pl.multiple_of(z * 128, 128), 128)]

    ORDERS = (("z", "y", "x"), ("x", "z", "y"), ("y", "z", "x"))
    a_copies = [remote(send_a.at[r], recv_a.at[r], a_s.at[r], a_r.at[r], other) for r in range(3)]

    shift = scale * (off + slope * (local_mean - mean))
    turn = scale * slope

    def kernel_grad(r, half):
        pieces = []
        for c in range(3):
            rows = pl.ds(pl.multiple_of(c * CI + half * 128, 128), 128)
            ones = jnp.concatenate([with_one[r, rows, :]] * 4, axis=1)
            pieces.append(
                part[r, c, pl.ds(pl.multiple_of(half * 128, 128), 128), :] * scale
                - with_conv[r, rows, :] * turn
                - ones * shift
            )
        return pieces

    for r in range(3):
        for c, piece in enumerate(kernel_grad(r, 1 - core)):
            send_a[r, c] = piece.astype(BF16)
        a_copies[r].start()

    def conv_grad(i, carry):
        b = lax.rem(i, B)
        h = lax.rem(3 * (i // B), H)
        spot = pl.ds(pl.multiple_of(b * W, W), W)
        away = conv[h, spot] - mean
        value = scale * (pgs[h, spot] - off - away * slope)
        gc[h + 1, b] = value.astype(BF16)
        gl[h + 1, b], gr[h + 1, b] = shifted(value, 0.0, 0.0)
        gedge_f[0, pl.ds(h * B + b, 1)] = value[W - 1 : W, :]
        gedge_f[1, pl.ds(h * B + b, 1)] = value[0:1, :]
        return carry

    ring1_send, ring1_recv = (ring1z_send, ring1x_send, ring1y_send), (
        ring1z_recv,
        ring1x_recv,
        ring1y_recv,
    )
    ring2_send, ring2_recv = (ring2z_send, ring2x_send, ring2y_send), (
        ring2z_recv,
        ring2x_recv,
        ring2y_recv,
    )

    def halves(r):
        return 192 if r == 0 else 48

    def block(r, q, low, high):
        q = lax.rem(q, 4)
        if r == 0:
            return with_conv[r, low:high, pl.ds(pl.multiple_of(q * 128, 128), 128)]
        return with_conv[r, pl.ds(pl.multiple_of(q * 96 + low, 16), high - low), :]

    def around(axis, way):
        step = 1 if way == 0 else 3
        if axis == "z":
            return (me, lax.rem(z + step, 4))
        stride = 2 if axis == "y" else 8
        here = coords[axis]
        return (me + stride * (lax.rem(here + step, 4) - here), z)

    def ring1_copies(r):
        axis = ORDERS[r][0]
        return [
            remote(
                ring1_send[r].at[way],
                ring1_recv[r].at[way],
                ring_s.at[r, way],
                ring_r.at[r, way],
                around(axis, way),
            )
            for way in range(2)
        ]

    def ring2_copies(r):
        axis = ORDERS[r][0]
        return [
            remote(
                ring2_send[r].at[way],
                ring2_recv[r].at[way],
                ring_s.at[r, 2 + way],
                ring_r.at[r, 2 + way],
                around(axis, way),
            )
            for way in range(2)
        ]

    def ring1(r):
        a_copies[r].wait_recv()
        for c, piece in enumerate(kernel_grad(r, core)):
            with_conv[r, c * 128 : (c + 1) * 128] = piece + recv_a[r, c].astype(F32)
        here, half = coords[ORDERS[r][0]], halves(r)
        ring1_send[r][0] = block(r, here + 2, 0, half).astype(BF16)
        ring1_send[r][1] = block(r, here + 2, half, 2 * half).astype(BF16)
        for copy in ring1_copies(r):
            copy.start()

    def ring2(r):
        for copy in ring1_copies(r):
            copy.wait_recv()
        here, half = coords[ORDERS[r][0]], halves(r)
        low = ring1_recv[r][0].astype(F32)
        high = ring1_recv[r][1].astype(F32)
        ring2_send[r][0, 0:half] = (block(r, here + 1, 0, half) + low).astype(BF16)
        ring2_send[r][0, half : 2 * half] = block(r, here + 1, half, 2 * half).astype(BF16)
        ring2_send[r][1, 0:half] = block(r, here + 3, 0, half).astype(BF16)
        ring2_send[r][1, half : 2 * half] = (
            block(r, here + 3, half, 2 * half) + high
        ).astype(BF16)
        for copy in ring2_copies(r):
            copy.start()

    row_axis = ("y", "x", "y")
    second, third, gather3, gather2 = [], [], [], []
    for r in range(3):
        second.append(
            along(
                ORDERS[r][1],
                lambda j, r=r: two_send.at[r, j],
                two_recv.at[r],
                dir_s.at[0, r],
                dir_r.at[0, r],
            )
        )
        third.append(
            along(
                ORDERS[r][2],
                lambda j, r=r: three_send.at[r, j],
                three_recv.at[r],
                dir_s.at[1, r],
                dir_r.at[1, r],
            )
        )
        gather3.append(share_along(ORDERS[r][2], gat3.at[r], dir_s.at[2, r], dir_r.at[2, r]))
        gather2.append(share_along(row_axis[r], gat2.at[r], dir_s.at[3, r], dir_r.at[3, r]))

    def stage2(r):
        for copy in ring2_copies(r):
            copy.wait_recv()
        here, half = coords[ORDERS[r][0]], halves(r)
        total = (
            block(r, here, 0, 2 * half)
            + ring2_recv[r][0].astype(F32)
            + ring2_recv[r][1].astype(F32)
        )
        for q in range(4):
            piece = (
                total[q * 96 : (q + 1) * 96] if r == 0 else total[:, q * 128 : (q + 1) * 128]
            )
            two_own[r, q] = piece
            two_send[r, q] = piece.astype(BF16)
        second[r][0]()

    def stage3(r):
        second[r][1]()
        here = coords[ORDERS[r][1]]
        total = two_own[r, here]
        for k in range(1, 4):
            total = total + two_recv[r, flip(here, k)].astype(F32)
        for q in range(4):
            three_send[r, q] = total[q * 24 : (q + 1) * 24]
        third[r][0]()

    def collect3(r):
        third[r][1]()
        here = coords[ORDERS[r][2]]
        total = three_send[r, here]
        for k in range(1, 4):
            total = total + three_recv[r, flip(here, k)]
        gat3[r, here] = total
        gather3[r][0]()

    def collect2(r):
        gather3[r][1]()
        here = coords[row_axis[r]]
        gat2[r, here] = jnp.concatenate([gat3[r, q] for q in range(4)], axis=0).astype(BF16)
        gather2[r][0]()

    o_copies = [remote(gat2.at[r], gat_other.at[r], o_s.at[r], o_r.at[r], other) for r in range(3)]

    def swap(r):
        gather2[r][1]()
        o_copies[r].start()

    gi_copies = [
        [
            pltpu.make_async_copy(
                pgs.at[h, pl.ds(b * W, W), pl.ds(0, CI)], gi_out.at[b, h], gi_sem.at[h, b]
            )
            for b in range(B)
        ]
        for h in range(H)
    ]

    def back(h):
        lhs = jnp.concatenate(
            [
                ref[h + r].reshape(PIX, CO)
                for r in range(3)
                for ref in (gl, gc, gr)
            ],
            axis=1,
        )
        flipped = jnp.concatenate(
            [wgt[(TAPS - 1 - t) * CI : (TAPS - t) * CI, :] for t in range(TAPS)], axis=1
        )
        value = lax.dot_general(
            lhs, flipped, (((1,), (1,)), ((), ())), preferred_element_type=F32
        )
        pgs[h, :, 0:CI] = value
        for copy in gi_copies[h]:
            copy.start()

    lax.fori_loop(0, 2 * B, conv_grad, 0)
    ring1(0)
    ring1(1)
    ring1(2)
    lax.fori_loop(2 * B, 4 * B, conv_grad, 0)
    gedge_out[...] = gedge_f[...].astype(BF16)
    gedge_copies = edge_sends(gedge_out, gedge_in, gedge_s, gedge_r)
    for copy in gedge_copies:
        copy.start()
    ring2(0)
    ring2(1)
    ring2(2)
    grow_copies = row_sends(gc.at[1], gc.at[H], grow, grow_s, grow_r)
    for copy in grow_copies:
        copy.start()
    hd2_copy.wait_recv()
    head_pair = hd2[0] + hd2[1]
    for q in range(4):
        hdz_send[q] = head_pair[:, q * 128 : (q + 1) * 128]
    hdz_x[0]()
    for copy in gedge_copies:
        copy.wait_recv()
    set_edges_of(gl, gr, gedge_in, CO)
    back(1)
    stage2(0)
    stage2(1)
    stage2(2)
    hdz_x[1]()
    head_line = hdz_send[z]
    for k in range(1, 4):
        head_line = head_line + hdz[flip(z, k)]
    hdy[y] = head_line
    hdy_x[0]()
    back(2)
    stage3(0)
    stage3(1)
    stage3(2)
    hdy_x[1]()
    hdx[x] = add_up(hdy, 4)
    hdx_x[0]()
    collect3(0)
    collect3(1)
    collect3(2)
    for copy in grow_copies:
        copy.wait_recv()
    build_halo(grow, gedge_in, gl, gc, gr)
    back(0)
    collect2(0)
    collect2(1)
    collect2(2)
    hdx_x[1]()
    gh_out[...] = add_up(hdx, 4)
    back(3)
    swap(0)
    swap(1)
    swap(2)

    for copy in [hd2_copy] + grow_copies + gedge_copies + a_copies:
        copy.wait_send()
    for exchanged in [tot8_x, tot16_x, hdz_x, hdy_x, hdx_x] + second + third + gather3 + gather2:
        exchanged[2]()
    for r in range(3):
        for copy in ring1_copies(r) + ring2_copies(r):
            copy.wait_send()
    for line in gi_copies:
        for copy in line:
            copy.wait()
    for copy in o_copies:
        copy.wait()


def finish_kernel(own, far, gg, gb, gh, gi, *refs):
    gw_out, gg_out, gb_out, gh_out, gi_out = refs[0:5]
    own_in, far_in, gg_in, gb_in, gh_in, gi_in, gw_in, in_sem, out_sem = refs[5:]
    core = lax.rem(lax.axis_index("rows"), 2)
    moves = [(gg, gg_in, gg_out), (gb, gb_in, gb_out), (gh, gh_in, gh_out)]
    moves += [(gi.at[b], gi_in.at[b], gi_out.at[b]) for b in range(B)]
    blocks = [pltpu.make_async_copy(a, b, in_sem.at[i]) for i, (a, b) in enumerate(((own, own_in), (far, far_in)))]
    arrivals = [pltpu.make_async_copy(a, b, in_sem.at[2 + i]) for i, (a, b, _) in enumerate(moves)]
    leaves = [pltpu.make_async_copy(b, c, out_sem.at[3 + i]) for i, (_, b, c) in enumerate(moves)]
    wide = [
        pltpu.make_async_copy(
            gw_in.at[pl.ds(3 * r, 3)], gw_out.at[pl.ds(3 * r, 3)], out_sem.at[r]
        )
        for r in range(3)
    ]
    for copy in blocks + arrivals:
        copy.start()
    for copy in blocks:
        copy.wait()

    for r in range(3):
        for src, half in ((own_in, core), (far_in, 1 - core)):
            rows = src[r].reshape(384, 128)
            spot = pl.ds(pl.multiple_of(half * 128, 128), 128)
            for c in range(3):
                gw_in[3 * r + c, spot, :] = rows[c * 128 : (c + 1) * 128].astype(F32)
        wide[r].start()
    for arrival, leave in zip(arrivals, leaves):
        arrival.wait()
        leave.start()
    for copy in wide + leaves:
        copy.wait()


def finish(arrays):
    anywhere = pl.BlockSpec(memory_space=pl.ANY)
    wide = jax.ShapeDtypeStruct((TAPS, CI, 128), F32)
    return pl.pallas_call(
        finish_kernel,
        out_shape=(wide,) + tuple(jax.ShapeDtypeStruct(a.shape, a.dtype) for a in arrays[2:]),
        in_specs=[anywhere] * 6,
        out_specs=(anywhere,) * 5,
        scratch_shapes=[pltpu.VMEM(a.shape, a.dtype) for a in arrays]
        + [
            pltpu.VMEM(wide.shape, F32),
            pltpu.SemaphoreType.DMA((9,)),
            pltpu.SemaphoreType.DMA((10,)),
        ],
        compiler_params=pltpu.CompilerParams(vmem_limit_bytes=60 * 1024 * 1024),
    )(*arrays)


def per_device(features, conv_weight, bn_gain, bn_bias, head_weight, labels, raster):
    dma = pltpu.SemaphoreType.DMA
    vmem = pltpu.VMEM
    whole = pl.BlockSpec(memory_space=pltpu.VMEM)
    outs = pl.pallas_call(
        kernel,
        out_shape=(
            jax.ShapeDtypeStruct((3, 4, 96, 128), BF16),
            jax.ShapeDtypeStruct((3, 4, 96, 128), BF16),
            jax.ShapeDtypeStruct((1, 128), F32),
            jax.ShapeDtypeStruct((1, 128), F32),
            jax.ShapeDtypeStruct((4, 128), F32),
            jax.ShapeDtypeStruct((B, H, W, CI), F32),
        ),
        in_specs=[whole, pl.BlockSpec(memory_space=pl.ANY)] + [whole] * 5,
        out_specs=(whole,) * 5 + (pl.BlockSpec(memory_space=pl.ANY),),
        scratch_shapes=[
            vmem((TAPS * CI, CO), BF16),
            vmem((256, 256), BF16),
            vmem((H + 2, 3 * CI, 128), F32),
            vmem((24, CI), F32),
            vmem((16, CO), F32),
            vmem((H + 2, B, W, CI), BF16),
            vmem((H + 2, B, W, CI), BF16),
            vmem((H + 2, B, W, CI), BF16),
            vmem((H + 2, 3 * CI, PIX), BF16),
            vmem((H, PIX, CO), F32),
            vmem((H, PIX, CO), F32),
            vmem((H, PIX, CO), BF16),
            vmem((H, PIX, 128), BF16),
            vmem((H, PIX, 128), BF16),
            vmem((H, PIX, 128), BF16),
            vmem((128, CO), F32),
            vmem((CO, 128), BF16),
            vmem((128, CO), BF16),
            vmem((H + 2, B, W, CO), BF16),
            vmem((H + 2, B, W, CO), BF16),
            vmem((H + 2, B, W, CO), BF16),
            vmem((2, B, W, CI), BF16),
            vmem((2, 16, CI), BF16),
            vmem((6, 16, CI), BF16),
            vmem((2, B, W, CO), BF16),
            vmem((2, 16, CO), F32),
            vmem((2, 16, CO), BF16),
            vmem((6, 16, CO), BF16),
            vmem((B, 2, CO), F32),
            vmem((8, 2, CO), F32),
            vmem((16, 2, CO), F32),
            vmem((8, 2, CO), F32),
            vmem((16, 2, CO), F32),
            vmem((2, 4, CO), F32),
            vmem((4, 4, 128), F32),
            vmem((4, 4, 128), F32),
            vmem((4, 4, 128), F32),
            vmem((4, 4, 128), F32),
            vmem((3, 3, CI, CO), F32),
            vmem((3, 3 * CI, CO), F32),
            vmem((3, 3 * CI, 128), F32),
            vmem((3, 3, 128, CO), BF16),
            vmem((3, 3, 128, CO), BF16),
            vmem((2, 192, 128), BF16),
            vmem((2, 48, CO), BF16),
            vmem((2, 48, CO), BF16),
            vmem((2, 192, 128), BF16),
            vmem((2, 48, CO), BF16),
            vmem((2, 48, CO), BF16),
            vmem((2, 384, 128), BF16),
            vmem((2, 96, CO), BF16),
            vmem((2, 96, CO), BF16),
            vmem((2, 384, 128), BF16),
            vmem((2, 96, CO), BF16),
            vmem((2, 96, CO), BF16),
            vmem((3, 4, 96, 128), F32),
            vmem((3, 4, 96, 128), BF16),
            vmem((3, 4, 96, 128), BF16),
            vmem((3, 4, 24, 128), F32),
            vmem((3, 4, 24, 128), F32),
            vmem((3, 4, 24, 128), F32),
            dma((TAPS,)),
            dma((2,)),
            dma((2,)),
            dma((6,)),
            dma((6,)),
            dma((2,)),
            dma((2,)),
            dma((6,)),
            dma((6,)),
        ]
        + [dma((4,))] * 4
        + [
            dma((3,)),
            dma((3,)),
            dma((3, 4)),
            dma((3, 4)),
            dma((4, 3)),
            dma((4, 3)),
            dma((3,)),
            dma((3,)),
            dma((H, B)),
        ],
        compiler_params=pltpu.CompilerParams(
            collective_id=0, has_side_effects=True, vmem_limit_bytes=60 * 1024 * 1024
        ),
        cost_estimate=pl.CostEstimate(
            flops=15_000_000_000, bytes_accessed=8_000_000, transcendentals=300_000
        ),
    )(
        features,
        conv_weight.reshape(TAPS * CI, CO),
        bn_gain.reshape(1, CO),
        bn_bias.reshape(1, CO),
        jnp.transpose(head_weight),
        labels,
        raster,
    )
    grad_weight, grad_gain, grad_bias, grad_head, grad_input = finish(outs)
    return (
        grad_weight.reshape(3, 3, CI, 128),
        grad_gain.reshape(128),
        grad_bias.reshape(128),
        jnp.transpose(grad_head),
        grad_input,
    )


def solution(mesh):
    in_specs = (
        P(None, "rows", "cols", None),
        P(),
        P(),
        P(),
        P(),
        P(None, "rows", "cols"),
        P(None, "rows", "cols"),
    )
    out_specs = (
        P(None, None, None, "cols"),
        P("cols"),
        P("cols"),
        P("cols", None),
        P(None, "rows", "cols", None),
    )
    return jax.shard_map(
        per_device, mesh=mesh, in_specs=in_specs, out_specs=out_specs, check_vma=False
    )
```

```python
import jax
import jax.numpy as jnp
from jax import lax
from jax.experimental import pallas as pl
from jax.experimental.pallas import tpu as pltpu
from jax.sharding import PartitionSpec as P

F32 = jnp.float32
BF16 = jnp.bfloat16
MESH = pl.DeviceIdType.MESH

B = 4
H = 4
W = 128
CI = 256
CO = 512
TAPS = 9
PIX = H * W
COUNT = 4.0 * 128.0 * 512.0
EPS = 1e-05


def kernel(
    feat,
    wgt_hbm,
    gain_ref,
    bias_ref,
    head_ref,
    labels_ref,
    raster_ref,
    gat2,
    gat_other,
    gg_out,
    gb_out,
    gh_out,
    gi_out,
    wgt,
    identity,
    line_one,
    edge_f,
    edge_part,
    xl,
    xc,
    xr,
    xt,
    conv,
    pgs,
    act,
    sgs,
    onehot,
    pixw,
    head_pad,
    head_tile,
    head_t,
    gl,
    gc,
    gr,
    xrow,
    xedge_out,
    xedge_in,
    grow,
    gedge_f,
    gedge_out,
    gedge_in,
    st_local,
    st8,
    st16,
    tot8,
    tot16,
    hd2,
    hdz_send,
    hdz,
    hdy,
    hdx,
    part,
    with_conv,
    with_one,
    send_a,
    recv_a,
    ring1z_send,
    ring1x_send,
    ring1y_send,
    ring1z_recv,
    ring1x_recv,
    ring1y_recv,
    ring2z_send,
    ring2x_send,
    ring2y_send,
    ring2z_recv,
    ring2x_recv,
    ring2y_recv,
    two_own,
    two_send,
    two_recv,
    three_send,
    three_recv,
    gat3,
    wsem,
    xrow_s,
    xrow_r,
    xedge_s,
    xedge_r,
    grow_s,
    grow_r,
    gedge_s,
    gedge_r,
    st_s,
    st_r,
    hd_s,
    hd_r,
    a_s,
    a_r,
    ring_s,
    ring_r,
    dir_s,
    dir_r,
    o_s,
    o_r,
    gi_sem,
):
    me = lax.axis_index("rows")
    z = lax.axis_index("cols")
    core = lax.rem(me, 2)
    chip = me // 2
    x = chip // 4
    y = lax.rem(chip, 4)
    rank8 = z * 2 + core
    coords = {"x": x, "y": y, "z": z}

    def flip(value, bits):
        return lax.bitwise_xor(value, jnp.int32(bits)) if bits else value

    def dev8(k):
        return (flip(me, k % 2), flip(z, k // 2))

    def dev16(k):
        return (flip(me, 2 * k), z)

    def on_axis(axis, k):
        return (me, flip(z, k)) if axis == "z" else (flip(me, (2 if axis == "y" else 8) * k), z)

    other = (flip(me, 1), z)

    def around(axis, way, cross=0):
        step = 1 if way == 0 else 3
        if axis == "z":
            return (flip(me, cross), lax.rem(z + step, 4))
        stride = 2 if axis == "y" else 8
        here = coords[axis]
        return (flip(me + stride * (lax.rem(here + step, 4) - here), cross), z)

    up = lax.rem(me + 31, 32)
    down = lax.rem(me + 1, 32)
    west = lax.rem(z + 3, 4)
    east = lax.rem(z + 1, 4)
    beyond = lax.rem(me + 31 + 2 * core, 32)

    barrier = pltpu.get_barrier_semaphore()

    def greet(device):
        pl.semaphore_signal(barrier, inc=1, device_id=device, device_id_type=MESH)

    for k in range(1, 8):
        greet(dev8(k))
    for col in (west, z, east):
        greet((beyond, col))
    for k in range(1, 16):
        greet(dev16(k))

    for axis in ("x", "y"):
        for way in range(2):
            greet(around(axis, way, 1))

    wcopies = []
    for t in range(TAPS):
        rows = pl.ds(t * CI, CI)
        wcopies.append(pltpu.make_async_copy(wgt_hbm.at[rows], wgt.at[rows], wsem.at[t]))
    for copy in wcopies:
        copy.start()

    row_id = lax.broadcasted_iota(jnp.int32, (16, CI), 0)
    left_edge = jnp.zeros((16, CI), F32)
    right_edge = jnp.zeros((16, CI), F32)
    for b in range(B):
        for h in range(H):
            low = feat[b, h, 0:16, :].astype(F32)[0:1, :]
            top = feat[b, h, W - 16 : W, :].astype(F32)[15:16, :]
            here = row_id == h * B + b
            left_edge = jnp.where(here, low, left_edge)
            right_edge = jnp.where(here, top, right_edge)
    xedge_out[0] = right_edge.astype(BF16)
    xedge_out[1] = left_edge.astype(BF16)

    def pick_row(ref, slot, index):
        block = ref[slot].astype(F32)
        ids = lax.broadcasted_iota(jnp.int32, block.shape, 0)
        return jnp.sum(jnp.where(ids == index, block, 0.0), axis=0, keepdims=True)

    def shifted(value, before, after):
        ids = lax.broadcasted_iota(jnp.int32, value.shape, 0)
        left = jnp.where(ids == 0, before, pltpu.roll(value, 1, 0))
        right = jnp.where(ids == W - 1, after, pltpu.roll(value, W - 1, 0))
        return left.astype(BF16), right.astype(BF16)

    def build_x(i, carry):
        b = i // H
        h = lax.rem(i, H)
        left, right = shifted(feat[b, h].astype(F32), 0.0, 0.0)
        xl[h + 1, b] = left
        xc[h + 1, b] = feat[b, h]
        xr[h + 1, b] = right
        return carry

    lax.fori_loop(0, B * H, build_x, 0)

    pl.semaphore_wait(barrier, 29)

    def remote(src, dst, ssem, rsem, device):
        return pltpu.make_async_remote_copy(
            src_ref=src,
            dst_ref=dst,
            send_sem=ssem,
            recv_sem=rsem,
            device_id=device,
            device_id_type=MESH,
        )

    def row_sends(first, last, land, ssem, rsem):
        return [
            remote(last, land.at[0], ssem.at[0], rsem.at[0], (down, z)),
            remote(first, land.at[1], ssem.at[1], rsem.at[1], (up, z)),
        ]

    def edge_sends(out, land, ssem, rsem):
        copies = []
        for side, col in ((0, east), (1, west)):
            for slot, row in ((0, down), (1, me), (2, up)):
                index = side * 3 + slot
                copies.append(
                    remote(
                        out.at[side], land.at[index], ssem.at[index], rsem.at[index], (row, col)
                    )
                )
        return copies

    xrow_copies = row_sends(feat.at[:, 0], feat.at[:, H - 1], xrow, xrow_s, xrow_r)
    for copy in xrow_copies:
        copy.start()
    xedge_copies = edge_sends(xedge_out, xedge_in, xedge_s, xedge_r)
    for copy in xedge_copies:
        copy.start()

    head_pad[...] = jnp.zeros((128, CO), F32)
    head_pad[0:4] = head_ref[...].astype(F32)
    head_t[...] = head_pad[...].astype(BF16)
    head_pad[4:8] = head_ref[...].astype(F32)
    head_tile[...] = jnp.transpose(jnp.concatenate([head_pad[0:8]] * 16, axis=0)).astype(BF16)

    lane_class = lax.rem(lax.broadcasted_iota(jnp.int32, (W, 128), 1), 4).astype(F32)
    identity[...] = jnp.where(
        lax.broadcasted_iota(jnp.int32, (256, 256), 0)
        == lax.broadcasted_iota(jnp.int32, (256, 256), 1),
        1.0,
        0.0,
    ).astype(BF16)

    def turned(value):
        size = value.shape[1]
        return lax.dot_general(
            identity[0:size, 0:size],
            value,
            (((1,), (1,)), ((), ())),
            preferred_element_type=F32,
        )

    def class_marks(i, carry):
        b = i // H
        h = lax.rem(i, H)
        spot = pl.ds(pl.multiple_of(b * W, W), W)
        code = labels_ref[b, pl.ds(h, 1), :] + 4 * raster_ref[b, pl.ds(h, 1), :]
        code = turned(jnp.broadcast_to(code.astype(F32), (128, W)).astype(BF16))
        weight = jnp.where(code > 3.5, 1.0, 0.0)
        marks = jnp.where(code - 4.0 * weight == lane_class, 1.0, 0.0)
        onehot[h, spot] = marks.astype(BF16)
        pixw[h, spot] = ((1.0 + weight) * 0.25).astype(BF16)
        return carry

    lax.fori_loop(0, B * H, class_marks, 0)

    west_ok = jnp.where(z > 0, 1.0, 0.0).astype(F32)
    east_ok = jnp.where(z < 3, 1.0, 0.0).astype(F32)
    up_ok = jnp.where(me > 0, 1.0, 0.0).astype(F32)
    down_ok = jnp.where(me < 31, 1.0, 0.0).astype(F32)

    def build_halo(land, edge_in, left_ref, mid_ref, right_ref):
        def body(b, carry):
            for side, line, ok, src in ((0, 0, up_ok, H - 1), (1, H + 1, down_ok, 0)):
                value = land[side, b].astype(F32) * ok
                slot = 2 * side
                left, right = shifted(
                    value,
                    pick_row(edge_in, slot, src * B + b) * (west_ok * ok),
                    pick_row(edge_in, slot + 3, src * B + b) * (east_ok * ok),
                )
                left_ref[line, b] = left
                mid_ref[line, b] = value.astype(BF16)
                right_ref[line, b] = right
            return carry

        lax.fori_loop(0, B, body, 0)

    for copy in wcopies:
        copy.wait()

    def conv_rows(h, first, count):
        lhs = jnp.concatenate(
            [
                ref[h + first + r].reshape(PIX, CI)
                for r in range(count)
                for ref in (xl, xc, xr)
            ],
            axis=1,
        )
        start = pl.multiple_of(first * 3 * CI, 3 * CI)
        return jnp.dot(lhs, wgt[pl.ds(start, count * 3 * CI), :], preferred_element_type=F32)

    def statistics(h, carry):
        value = conv[h]
        mid = jnp.sum(value, axis=0, keepdims=True) * (1.0 / PIX)
        st_local[h, 0:1] = mid
        st_local[h, 1:2] = jnp.sum((value - mid) ** 2, axis=0, keepdims=True)
        return carry

    def transpose_x(line):
        for c, ref in enumerate((xl, xc, xr)):
            xt[line, c * CI : (c + 1) * CI, :] = turned(ref[line].reshape(PIX, CI)).astype(BF16)
        line_one[line] = jnp.dot(
            xt[line], jnp.ones((PIX, 128), BF16), preferred_element_type=F32
        )

    def set_edges_of(left_ref, right_ref, edge_in, channels):
        def body(i, carry):
            h = i // B
            b = lax.rem(i, B)
            ids = lax.broadcasted_iota(jnp.int32, (16, channels), 0)
            low = pick_row(edge_in, 1, i) * west_ok
            top = pick_row(edge_in, 4, i) * east_ok
            block16 = left_ref[h + 1, b, 0:16].astype(F32)
            left_ref[h + 1, b, 0:16] = jnp.where(ids == 0, low, block16).astype(BF16)
            block16 = right_ref[h + 1, b, W - 16 : W].astype(F32)
            right_ref[h + 1, b, W - 16 : W] = jnp.where(ids == 15, top, block16).astype(BF16)
            return carry

        lax.fori_loop(0, B * H, body, 0)

    def inner_rows(i, carry):
        conv[1 + i] = conv_rows(1 + i, 0, 3)
        return carry

    lax.fori_loop(0, 2, inner_rows, 0)

    def outer_rows(i, carry):
        conv[3 * i] = conv_rows(3 * i, 1 - i, 2)
        return carry

    lax.fori_loop(0, 2, outer_rows, 0)

    for copy in xedge_copies:
        copy.wait_recv()
    set_edges_of(xl, xr, xedge_in, CI)
    for side, ok, c, spot in ((0, west_ok, 0, 0), (1, east_ok, 2, W - 1)):
        edge_f[...] = jnp.zeros((24, CI), F32)
        edge_f[B : B + 16] = xedge_in[3 * side + 1].astype(F32) * ok
        lhs = jnp.concatenate([edge_f[B * r : B * r + 16] for r in range(3)], axis=1)
        taps = jnp.concatenate(
            [wgt[(3 * r + c) * CI : (3 * r + c + 1) * CI, :] for r in range(3)], axis=0
        )
        edge_part[...] = jnp.dot(lhs.astype(BF16), taps, preferred_element_type=F32)

        def add_edges(i, carry, spot=spot):
            h = i // B
            place = pl.ds(lax.rem(i, B) * W + spot, 1)
            conv[h, place] += edge_part[pl.ds(i, 1)]
            return carry

        lax.fori_loop(0, B * H, add_edges, 0)

    def transpose_inner(line, carry):
        transpose_x(line)
        return carry

    lax.fori_loop(1, H + 1, transpose_inner, 0)
    for copy in xrow_copies:
        copy.wait_recv()
    build_halo(xrow, xedge_in, xl, xc, xr)

    def halo_rows(i, carry):
        conv[3 * i] += conv_rows(3 * i, 2 * i, 1)
        return carry

    lax.fori_loop(0, 2, halo_rows, 0)
    lax.fori_loop(0, H, statistics, 0)

    def combine(parts, count):
        total = parts[0][0:1]
        for item in parts[1:]:
            total = total + item[0:1]
        mid = total * (1.0 / len(parts))
        spread_sum = None
        for item in parts:
            term = item[1:2] + count * (item[0:1] - mid) ** 2
            spread_sum = term if spread_sum is None else spread_sum + term
        return mid, spread_sum

    def exchange(size, devices, src_of, land, rank, ssem, rsem):
        def all_of(sem):
            few = land.at[0 : size - 1]
            return pltpu.make_async_copy(few, few, sem)

        def start():
            for k in range(1, size):
                remote(src_of(flip(rank, k)), land.at[rank], ssem, rsem, devices(k)).start()

        return start, lambda: all_of(rsem).wait(), lambda: all_of(ssem).wait()

    def share(size, devices, land, rank, ssem, rsem):
        return exchange(size, devices, lambda j: land.at[rank], land, rank, ssem, rsem)

    def along(axis, src_of, land, ssem, rsem):
        return exchange(
            4, lambda k: on_axis(axis, k), src_of, land, coords[axis], ssem, rsem
        )

    def share_along(axis, land, ssem, rsem):
        return along(axis, lambda j: land.at[coords[axis]], land, ssem, rsem)

    st8_x = share(8, dev8, st8, rank8, st_s.at[0], st_r.at[0])
    st16_x = share(16, dev16, st16, chip, st_s.at[1], st_r.at[1])
    tot8_x = share(8, dev8, tot8, rank8, st_s.at[2], st_r.at[2])
    tot16_x = share(16, dev16, tot16, chip, st_s.at[3], st_r.at[3])
    hd2_copy = remote(hd2.at[core], hd2.at[core], hd_s.at[0], hd_r.at[0], other)
    hdz_x = along("z", lambda j: hdz_send.at[j], hdz, hd_s.at[1], hd_r.at[1])
    hdy_x = share_along("y", hdy, hd_s.at[2], hd_r.at[2])
    hdx_x = share_along("x", hdx, hd_s.at[3], hd_r.at[3])

    mid, m2 = combine([st_local[h] for h in range(H)], float(PIX))
    st8[rank8, 0:1] = mid
    st8[rank8, 1:2] = m2
    st8_x[0]()

    local_mean = mid
    transpose_x(0)
    transpose_x(H + 1)

    def center(h, carry):
        act[h] = (conv[h] - local_mean).astype(BF16)
        return carry

    lax.fori_loop(0, H, center, 0)

    def features_of(r):
        return jnp.concatenate([xt[h + r] for h in range(H)], axis=1)

    def cross_conv(r, carry):
        lhs = features_of(r)
        with_conv[r] = jnp.dot(lhs, act[...].reshape(B * PIX, CO), preferred_element_type=F32)
        with_one[r] = line_one[r] + line_one[r + 1] + line_one[r + 2] + line_one[r + 3]
        return carry

    lax.fori_loop(0, 1, cross_conv, 0)
    st8_x[1]()
    mid, m2 = combine([st8[j] for j in range(8)], float(B * PIX))
    st16[chip, 0:1] = mid
    st16[chip, 1:2] = m2
    st16_x[0]()
    lax.fori_loop(1, 3, cross_conv, 0)
    st16_x[1]()
    mean, m2 = combine([st16[j] for j in range(16)], float(8 * B * PIX))
    rstd = lax.rsqrt(m2 * (1.0 / COUNT) + EPS)
    gain = gain_ref[...]
    bias = bias_ref[...]
    scale = gain * rstd

    def middle(b, carry):
        sum_g, sum_gn = carry
        away = conv[b] - mean
        pre = away * scale + bias
        acted = jnp.maximum(pre, 0.0).astype(BF16)
        act[b] = acted
        logits = jnp.dot(acted, head_tile[...], preferred_element_type=F32)
        expo = jnp.exp(logits)
        total = expo + pltpu.roll(expo, 1, 1)
        total = total + pltpu.roll(total, 2, 1)
        score = (pixw[b].astype(F32) * (expo / total - onehot[b].astype(F32))).astype(BF16)
        sgs[b] = score
        act_grad = jnp.dot(score, head_t[...], preferred_element_type=F32)
        pre_grad = jnp.where(pre > 0.0, act_grad, 0.0)
        pgs[b] = pre_grad
        gc[b + 1] = pre_grad.astype(BF16).reshape(B, W, CO)
        sum_g = sum_g + jnp.sum(pre_grad, axis=0, keepdims=True)
        sum_gn = sum_gn + jnp.sum(pre_grad * away, axis=0, keepdims=True)
        return sum_g, sum_gn

    zero_row = jnp.zeros((1, CO), F32)
    sum_g, sum_gn = lax.fori_loop(0, B, middle, (zero_row, zero_row))

    def add_up(buf, size):
        total = buf[0]
        for j in range(1, size):
            total = total + buf[j]
        return total

    tot8[rank8, 0:1] = sum_g
    tot8[rank8, 1:2] = sum_gn * rstd
    tot8_x[0]()

    def cross_grad(r, carry):
        part[r] = jnp.dot(
            features_of(r),
            gc[1 : H + 1].reshape(B * PIX, CO),
            preferred_element_type=F32,
        ).reshape(3, CI, CO)
        return carry

    def head_part(b, total):
        return total + lax.dot_general(
            sgs[b], act[b], (((0,), (0,)), ((), ())), preferred_element_type=F32
        )

    lax.fori_loop(0, 1, cross_grad, 0)
    tot8_x[1]()
    tot16[chip] = add_up(tot8, 8)
    tot16_x[0]()
    lax.fori_loop(1, 3, cross_grad, 0)
    head_sum = lax.fori_loop(0, B, head_part, jnp.zeros((128, CO), F32))
    hd2[core] = head_sum[0:4, :]
    hd2_copy.start()
    st8_x[2]()
    st16_x[2]()
    for copy in xrow_copies + xedge_copies:
        copy.wait_send()
    tot16_x[1]()
    totals = add_up(tot16, 16)
    off = totals[0:1] * (1.0 / COUNT)
    slope = rstd * totals[1:2] * (1.0 / COUNT)
    st_local[0] = totals
    gb_out[...] = st_local[0, 0:1, pl.ds(pl.multiple_of(z * 128, 128), 128)]
    gg_out[...] = st_local[0, 1:2, pl.ds(pl.multiple_of(z * 128, 128), 128)]

    ORDERS = (("z", "y", "x"), ("x", "z", "y"), ("y", "z", "x"))
    a_copies = [remote(send_a.at[r], recv_a.at[r], a_s.at[r], a_r.at[r], other) for r in range(3)]

    shift = scale * (off + slope * (local_mean - mean))
    turn = scale * slope

    def kernel_grad(r, half):
        pieces = []
        for c in range(3):
            rows = pl.ds(pl.multiple_of(c * CI + half * 128, 128), 128)
            ones = jnp.concatenate([with_one[r, rows, :]] * 4, axis=1)
            pieces.append(
                part[r, c, pl.ds(pl.multiple_of(half * 128, 128), 128), :] * scale
                - with_conv[r, rows, :] * turn
                - ones * shift
            )
        return pieces

    for r in range(3):
        for c, piece in enumerate(kernel_grad(r, 1 - core)):
            send_a[r, c * 128 : (c + 1) * 128] = piece.astype(BF16)
        a_copies[r].start()

    def conv_grad(i, carry):
        b = lax.rem(i, B)
        h = lax.rem(3 * (i // B), H)
        spot = pl.ds(pl.multiple_of(b * W, W), W)
        away = conv[h, spot] - mean
        value = scale * (pgs[h, spot] - off - away * slope)
        gc[h + 1, b] = value.astype(BF16)
        gl[h + 1, b], gr[h + 1, b] = shifted(value, 0.0, 0.0)
        gedge_f[0, pl.ds(h * B + b, 1)] = value[W - 1 : W, :]
        gedge_f[1, pl.ds(h * B + b, 1)] = value[0:1, :]
        return carry

    ring1_send, ring1_recv = (ring1z_send, ring1x_send, ring1y_send), (
        ring1z_recv,
        ring1x_recv,
        ring1y_recv,
    )
    ring2_send, ring2_recv = (ring2z_send, ring2x_send, ring2y_send), (
        ring2z_recv,
        ring2x_recv,
        ring2y_recv,
    )

    def halves(r):
        return 192 if r == 0 else 48

    def block(r, q, low, high):
        q = lax.rem(q, 4)
        if r == 0:
            return with_conv[r, low:high, pl.ds(pl.multiple_of(q * 128, 128), 128)]
        return with_conv[r, pl.ds(pl.multiple_of(q * 96 + low, 16), high - low), :]

    def first_block(r, way):
        q, half = lax.rem(coords[ORDERS[r][0]] + 2, 4), halves(r)
        if r == 0:
            cols = pl.ds(pl.multiple_of(q * 128, 128), 128)
            return send_a.at[r, pl.ds(way * half, half), cols]
        return send_a.at[r, pl.ds(pl.multiple_of(q * 96 + way * half, 16), half)]

    def ring1_copies(r):
        axis = ORDERS[r][0]
        copies = []
        for way in range(2):
            for cross in range(2):
                copies.append(
                    remote(
                        first_block(r, way) if cross else ring1_send[r].at[way],
                        ring1_recv[r].at[way, cross],
                        ring_s.at[r, 4 * cross + way],
                        ring_r.at[r, 4 * cross + way],
                        around(axis, way, cross),
                    )
                )
        return copies

    def ring2_copies(r):
        axis = ORDERS[r][0]
        return [
            remote(
                ring2_send[r].at[way],
                ring2_recv[r].at[way],
                ring_s.at[r, 2 + way],
                ring_r.at[r, 2 + way],
                around(axis, way),
            )
            for way in range(2)
        ]

    def ring1(r):
        for c, piece in enumerate(kernel_grad(r, core)):
            with_conv[r, c * 128 : (c + 1) * 128] = piece
        here, half = coords[ORDERS[r][0]], halves(r)
        ring1_send[r][0] = block(r, here + 2, 0, half).astype(BF16)
        ring1_send[r][1] = block(r, here + 2, half, 2 * half).astype(BF16)
        for copy in ring1_copies(r):
            copy.start()

    def ring2(r):
        a_copies[r].wait_recv()
        with_conv[r, 0:384] += recv_a[r].astype(F32)
        for copy in ring1_copies(r):
            copy.wait_recv()
        here, half = coords[ORDERS[r][0]], halves(r)
        low = ring1_recv[r][0, 0].astype(F32) + ring1_recv[r][0, 1].astype(F32)
        high = ring1_recv[r][1, 0].astype(F32) + ring1_recv[r][1, 1].astype(F32)
        ring2_send[r][0, 0:half] = (block(r, here + 1, 0, half) + low).astype(BF16)
        ring2_send[r][0, half : 2 * half] = block(r, here + 1, half, 2 * half).astype(BF16)
        ring2_send[r][1, 0:half] = block(r, here + 3, 0, half).astype(BF16)
        ring2_send[r][1, half : 2 * half] = (
            block(r, here + 3, half, 2 * half) + high
        ).astype(BF16)
        for copy in ring2_copies(r):
            copy.start()

    row_axis = ("y", "x", "y")
    second, third, gather3, gather2 = [], [], [], []
    for r in range(3):
        second.append(
            along(
                ORDERS[r][1],
                lambda j, r=r: two_send.at[r, j],
                two_recv.at[r],
                dir_s.at[0, r],
                dir_r.at[0, r],
            )
        )
        third.append(
            along(
                ORDERS[r][2],
                lambda j, r=r: three_send.at[r, j],
                three_recv.at[r],
                dir_s.at[1, r],
                dir_r.at[1, r],
            )
        )
        gather3.append(share_along(ORDERS[r][2], gat3.at[r], dir_s.at[2, r], dir_r.at[2, r]))
        gather2.append(share_along(row_axis[r], gat2.at[r], dir_s.at[3, r], dir_r.at[3, r]))

    def stage2(r):
        for copy in ring2_copies(r):
            copy.wait_recv()
        here, half = coords[ORDERS[r][0]], halves(r)
        total = (
            block(r, here, 0, 2 * half)
            + ring2_recv[r][0].astype(F32)
            + ring2_recv[r][1].astype(F32)
        )
        for q in range(4):
            piece = (
                total[q * 96 : (q + 1) * 96] if r == 0 else total[:, q * 128 : (q + 1) * 128]
            )
            two_own[r, q] = piece
            two_send[r, q] = piece.astype(BF16)
        second[r][0]()

    def stage3(r):
        second[r][1]()
        here = coords[ORDERS[r][1]]
        total = two_own[r, here]
        for k in range(1, 4):
            total = total + two_recv[r, flip(here, k)].astype(F32)
        for q in range(4):
            three_send[r, q] = total[q * 24 : (q + 1) * 24]
        third[r][0]()

    def collect3(r):
        third[r][1]()
        here = coords[ORDERS[r][2]]
        total = three_send[r, here]
        for k in range(1, 4):
            total = total + three_recv[r, flip(here, k)]
        gat3[r, here] = total
        gather3[r][0]()

    def collect2(r):
        gather3[r][1]()
        here = coords[row_axis[r]]
        gat2[r, here] = jnp.concatenate([gat3[r, q] for q in range(4)], axis=0).astype(BF16)
        gather2[r][0]()

    o_copies = [remote(gat2.at[r], gat_other.at[r], o_s.at[r], o_r.at[r], other) for r in range(3)]

    def swap(r):
        gather2[r][1]()
        o_copies[r].start()

    gi_copies = [
        [
            pltpu.make_async_copy(
                pgs.at[h, pl.ds(b * W, W), pl.ds(0, CI)], gi_out.at[b, h], gi_sem.at[h, b]
            )
            for b in range(B)
        ]
        for h in range(H)
    ]

    def back(h):
        lhs = jnp.concatenate(
            [
                ref[h + r].reshape(PIX, CO)
                for r in range(3)
                for ref in (gl, gc, gr)
            ],
            axis=1,
        )
        flipped = jnp.concatenate(
            [wgt[(TAPS - 1 - t) * CI : (TAPS - t) * CI, :] for t in range(TAPS)], axis=1
        )
        value = lax.dot_general(
            lhs, flipped, (((1,), (1,)), ((), ())), preferred_element_type=F32
        )
        pgs[h, :, 0:CI] = value
        for copy in gi_copies[h]:
            copy.start()

    ring1(0)
    ring1(1)
    ring1(2)
    lax.fori_loop(0, 2 * B, conv_grad, 0)
    lax.fori_loop(2 * B, 4 * B, conv_grad, 0)
    gedge_out[...] = gedge_f[...].astype(BF16)
    gedge_copies = edge_sends(gedge_out, gedge_in, gedge_s, gedge_r)
    for copy in gedge_copies:
        copy.start()
    ring2(0)
    ring2(1)
    ring2(2)
    grow_copies = row_sends(gc.at[1], gc.at[H], grow, grow_s, grow_r)
    for copy in grow_copies:
        copy.start()
    hd2_copy.wait_recv()
    head_pair = hd2[0] + hd2[1]
    for q in range(4):
        hdz_send[q] = head_pair[:, q * 128 : (q + 1) * 128]
    hdz_x[0]()
    for copy in gedge_copies:
        copy.wait_recv()
    set_edges_of(gl, gr, gedge_in, CO)
    back(1)
    stage2(0)
    stage2(1)
    stage2(2)
    hdz_x[1]()
    head_line = hdz_send[z]
    for k in range(1, 4):
        head_line = head_line + hdz[flip(z, k)]
    hdy[y] = head_line
    hdy_x[0]()
    back(2)
    stage3(0)
    stage3(1)
    stage3(2)
    hdy_x[1]()
    hdx[x] = add_up(hdy, 4)
    hdx_x[0]()
    collect3(0)
    collect3(1)
    collect3(2)
    for copy in grow_copies:
        copy.wait_recv()
    build_halo(grow, gedge_in, gl, gc, gr)
    back(0)
    collect2(0)
    collect2(1)
    collect2(2)
    hdx_x[1]()
    gh_out[...] = add_up(hdx, 4)
    back(3)
    swap(0)
    swap(1)
    swap(2)

    for copy in [hd2_copy] + grow_copies + gedge_copies + a_copies:
        copy.wait_send()
    for exchanged in [tot8_x, tot16_x, hdz_x, hdy_x, hdx_x] + second + third + gather3 + gather2:
        exchanged[2]()
    for r in range(3):
        for copy in ring1_copies(r) + ring2_copies(r):
            copy.wait_send()
    for line in gi_copies:
        for copy in line:
            copy.wait()
    for copy in o_copies:
        copy.wait()


def finish_kernel(own, far, gg, gb, gh, gi, *refs):
    gw_out, gg_out, gb_out, gh_out, gi_out = refs[0:5]
    own_in, far_in, gg_in, gb_in, gh_in, gi_in, gw_in, in_sem, out_sem = refs[5:]
    core = lax.rem(lax.axis_index("rows"), 2)
    moves = [(gg, gg_in, gg_out), (gb, gb_in, gb_out), (gh, gh_in, gh_out)]
    moves += [(gi.at[b], gi_in.at[b], gi_out.at[b]) for b in range(B)]
    blocks = [pltpu.make_async_copy(a, b, in_sem.at[i]) for i, (a, b) in enumerate(((own, own_in), (far, far_in)))]
    arrivals = [pltpu.make_async_copy(a, b, in_sem.at[2 + i]) for i, (a, b, _) in enumerate(moves)]
    leaves = [pltpu.make_async_copy(b, c, out_sem.at[3 + i]) for i, (_, b, c) in enumerate(moves)]
    wide = [
        pltpu.make_async_copy(
            gw_in.at[pl.ds(3 * r, 3)], gw_out.at[pl.ds(3 * r, 3)], out_sem.at[r]
        )
        for r in range(3)
    ]
    for copy in blocks + arrivals:
        copy.start()
    for copy in blocks:
        copy.wait()

    for r in range(3):
        for src, half in ((own_in, core), (far_in, 1 - core)):
            rows = src[r].reshape(384, 128)
            spot = pl.ds(pl.multiple_of(half * 128, 128), 128)
            for c in range(3):
                gw_in[3 * r + c, spot, :] = rows[c * 128 : (c + 1) * 128].astype(F32)
        wide[r].start()
    for arrival, leave in zip(arrivals, leaves):
        arrival.wait()
        leave.start()
    for copy in wide + leaves:
        copy.wait()


def finish(arrays):
    anywhere = pl.BlockSpec(memory_space=pl.ANY)
    wide = jax.ShapeDtypeStruct((TAPS, CI, 128), F32)
    return pl.pallas_call(
        finish_kernel,
        out_shape=(wide,) + tuple(jax.ShapeDtypeStruct(a.shape, a.dtype) for a in arrays[2:]),
        in_specs=[anywhere] * 6,
        out_specs=(anywhere,) * 5,
        scratch_shapes=[pltpu.VMEM(a.shape, a.dtype) for a in arrays]
        + [
            pltpu.VMEM(wide.shape, F32),
            pltpu.SemaphoreType.DMA((9,)),
            pltpu.SemaphoreType.DMA((10,)),
        ],
        compiler_params=pltpu.CompilerParams(vmem_limit_bytes=60 * 1024 * 1024),
    )(*arrays)


def per_device(features, conv_weight, bn_gain, bn_bias, head_weight, labels, raster):
    dma = pltpu.SemaphoreType.DMA
    vmem = pltpu.VMEM
    whole = pl.BlockSpec(memory_space=pltpu.VMEM)
    outs = pl.pallas_call(
        kernel,
        out_shape=(
            jax.ShapeDtypeStruct((3, 4, 96, 128), BF16),
            jax.ShapeDtypeStruct((3, 4, 96, 128), BF16),
            jax.ShapeDtypeStruct((1, 128), F32),
            jax.ShapeDtypeStruct((1, 128), F32),
            jax.ShapeDtypeStruct((4, 128), F32),
            jax.ShapeDtypeStruct((B, H, W, CI), F32),
        ),
        in_specs=[whole, pl.BlockSpec(memory_space=pl.ANY)] + [whole] * 5,
        out_specs=(whole,) * 5 + (pl.BlockSpec(memory_space=pl.ANY),),
        scratch_shapes=[
            vmem((TAPS * CI, CO), BF16),
            vmem((256, 256), BF16),
            vmem((H + 2, 3 * CI, 128), F32),
            vmem((24, CI), F32),
            vmem((16, CO), F32),
            vmem((H + 2, B, W, CI), BF16),
            vmem((H + 2, B, W, CI), BF16),
            vmem((H + 2, B, W, CI), BF16),
            vmem((H + 2, 3 * CI, PIX), BF16),
            vmem((H, PIX, CO), F32),
            vmem((H, PIX, CO), F32),
            vmem((H, PIX, CO), BF16),
            vmem((H, PIX, 128), BF16),
            vmem((H, PIX, 128), BF16),
            vmem((H, PIX, 128), BF16),
            vmem((128, CO), F32),
            vmem((CO, 128), BF16),
            vmem((128, CO), BF16),
            vmem((H + 2, B, W, CO), BF16),
            vmem((H + 2, B, W, CO), BF16),
            vmem((H + 2, B, W, CO), BF16),
            vmem((2, B, W, CI), BF16),
            vmem((2, 16, CI), BF16),
            vmem((6, 16, CI), BF16),
            vmem((2, B, W, CO), BF16),
            vmem((2, 16, CO), F32),
            vmem((2, 16, CO), BF16),
            vmem((6, 16, CO), BF16),
            vmem((B, 2, CO), F32),
            vmem((8, 2, CO), F32),
            vmem((16, 2, CO), F32),
            vmem((8, 2, CO), F32),
            vmem((16, 2, CO), F32),
            vmem((2, 4, CO), F32),
            vmem((4, 4, 128), F32),
            vmem((4, 4, 128), F32),
            vmem((4, 4, 128), F32),
            vmem((4, 4, 128), F32),
            vmem((3, 3, CI, CO), F32),
            vmem((3, 3 * CI, CO), F32),
            vmem((3, 3 * CI, 128), F32),
            vmem((3, 384, CO), BF16),
            vmem((3, 384, CO), BF16),
            vmem((2, 192, 128), BF16),
            vmem((2, 48, CO), BF16),
            vmem((2, 48, CO), BF16),
            vmem((2, 2, 192, 128), BF16),
            vmem((2, 2, 48, CO), BF16),
            vmem((2, 2, 48, CO), BF16),
            vmem((2, 384, 128), BF16),
            vmem((2, 96, CO), BF16),
            vmem((2, 96, CO), BF16),
            vmem((2, 384, 128), BF16),
            vmem((2, 96, CO), BF16),
            vmem((2, 96, CO), BF16),
            vmem((3, 4, 96, 128), F32),
            vmem((3, 4, 96, 128), BF16),
            vmem((3, 4, 96, 128), BF16),
            vmem((3, 4, 24, 128), F32),
            vmem((3, 4, 24, 128), F32),
            vmem((3, 4, 24, 128), F32),
            dma((TAPS,)),
            dma((2,)),
            dma((2,)),
            dma((6,)),
            dma((6,)),
            dma((2,)),
            dma((2,)),
            dma((6,)),
            dma((6,)),
        ]
        + [dma((4,))] * 4
        + [
            dma((3,)),
            dma((3,)),
            dma((3, 6)),
            dma((3, 6)),
            dma((4, 3)),
            dma((4, 3)),
            dma((3,)),
            dma((3,)),
            dma((H, B)),
        ],
        compiler_params=pltpu.CompilerParams(
            collective_id=0, has_side_effects=True, vmem_limit_bytes=60 * 1024 * 1024
        ),
        cost_estimate=pl.CostEstimate(
            flops=15_000_000_000, bytes_accessed=8_000_000, transcendentals=300_000
        ),
    )(
        features,
        conv_weight.reshape(TAPS * CI, CO),
        bn_gain.reshape(1, CO),
        bn_bias.reshape(1, CO),
        jnp.transpose(head_weight),
        labels,
        raster,
    )
    grad_weight, grad_gain, grad_bias, grad_head, grad_input = finish(outs)
    return (
        grad_weight.reshape(3, 3, CI, 128),
        grad_gain.reshape(128),
        grad_bias.reshape(128),
        jnp.transpose(grad_head),
        grad_input,
    )


def solution(mesh):
    in_specs = (
        P(None, "rows", "cols", None),
        P(),
        P(),
        P(),
        P(),
        P(None, "rows", "cols"),
        P(None, "rows", "cols"),
    )
    out_specs = (
        P(None, None, None, "cols"),
        P("cols"),
        P("cols"),
        P("cols", None),
        P(None, "rows", "cols", None),
    )
    return jax.shard_map(
        per_device, mesh=mesh, in_specs=in_specs, out_specs=out_specs, check_vma=False
    )
```
